128 devices in a mesh: dp: 8 (over x_hi, y), tensor: 16 (over z, x_lo, core).
Axes of the slice: x: 4 (x_hi: 2, x_lo: 2; x = x_hi * 2 + x_lo), y: 4, z: 4, core: 2. Of those that a mesh axis runs over, the one named last changes fastest.
Arguments:
- tokens: bfloat16 [16384, 2048], P(('dp', 'tensor')), may hold values from -6 to 6
- segments: int32 [16, 1024], P('dp'), may hold values from 0 to 3, never falling along the last dimension, each value on 1 to 768 neighbouring positions
- first_gain: float32 [2048], P('dp'), may hold values from 0.1 to 1.9
- first_shift: float32 [2048], P('dp'), may hold values from -2 to 2
- heads_weight: float32 [2048, 3, 2048], P('dp', None, 'tensor'), may hold values from -0.125 to 0.125
- heads_bias: float32 [3, 32, 64], P(None, 'tensor', 'dp'), may hold values from -3 to 3
- output_weight: float32 [2048, 2048], P('tensor', 'dp'), may hold values from -1 to 1
- second_gain: float32 [2048], P('dp'), may hold values from 0.1 to 1.9
- second_shift: float32 [2048], P('dp'), may hold values from -2 to 2
- gate_up_weight: float32 [2048, 2, 5632], P('dp', None, 'tensor'), may hold values from -0.125 to 0.125
- down_weight: float32 [5632, 2048], P('tensor', 'dp'), may hold values from -0.078125 to 0.078125
- cotangent: bfloat16 [16384, 2048], P(('dp', 'tensor')), may hold values from -6 to 6
Outputs:
- mixed: float32 [16384, 2048], P(('dp', 'tensor'))
- grad_tokens: float32 [16384, 2048], P(('dp', 'tensor'))
- grad_first_gain: float32 [2048], P(('dp', 'tensor'))
- grad_first_shift: float32 [2048], P(('dp', 'tensor'))
- grad_heads_weight: float32 [2048, 3, 2048], P('dp', None, 'tensor')
- grad_heads_bias: float32 [3, 32, 64], P(None, 'tensor', 'dp')
- grad_output_weight: float32 [2048, 2048], P('tensor', 'dp')
- grad_second_gain: float32 [2048], P(('dp', 'tensor'))
- grad_second_shift: float32 [2048], P(('dp', 'tensor'))
- grad_gate_up_weight: float32 [2048, 2, 5632], P('dp', None, 'tensor')
- grad_down_weight: float32 [5632, 2048], P('tensor', 'dp')
The draws below stay inside these ranges and needn't reach their ends.
Inputs may be any that keep to these rules, and one draw needn't show every extreme that they name: `segments`: within each sequence of 1024 tokens the segment numbers never fall; each document has 1 to 768 tokens, and one of each sequence has exactly that many.
All inputs are finite; a program needn't handle non-finite values.
Results may differ from the reference program's by a relative error of at most 0.012.
The reference program's roundings to bfloat16 on the way count: a program that leaves them out, or rounds other values in their place, can miss the bound.
Values may be sent and summed in bfloat16 or wider, within the bound.
A program may use at most 256 MiB of HBM per device.

```python
import math
import jax
import jax.numpy as jnp
import numpy as np
from jax import lax

D = 2048
H = 32
HD = 64
ROT = 16
FF = 5632
WINDOW = 512
QB = 512
LEN = 1024
SEQS = 16
TOKENS = 16384


def level_of(stream_key, extent, pieces, smallest, largest):
    level = 1.0
    for axis_at, blocks in pieces:
        draws = jax.random.uniform(jax.random.fold_in(jax.random.fold_in(stream_key, 6), axis_at), (blocks,), jnp.float32, smallest / len(pieces), largest / len(pieces))
        level = level * jnp.repeat(jnp.exp(draws), extent[axis_at] // blocks).reshape((-1,) + (1,) * (len(extent) - 1 - axis_at))
    return level


def split_up(count, total, most, lean):
    weights = [(1 << 20) // math.isqrt(grade ** lean) + 1 for grade in range(2, count + 1)]
    rest, counts = total - most - (count - 1), [1] * (count - 1)
    while rest > 0:
        movable = [i for i in range(count - 1) if counts[i] < most]
        mass, budget = sum([weights[i] for i in movable]), rest
        for i in movable:
            more = min(most - counts[i], max(1, budget * weights[i] // mass), rest)
            counts[i] = counts[i] + more
            rest = rest - more
    return np.array([most] + counts)


def ragged_sizes(key, amount, total, bound, lean):
    if amount == 2:
        one = jax.random.randint(key, (), max(1, total - bound), min(bound, total - 1) + 1)
        return jnp.stack([one, total - one])
    tallies = jnp.asarray(split_up(amount, total, bound, lean), jnp.int32)
    couples = (amount - 1) // 2
    source_of, sink = tallies[1:1 + 2 * couples:2], tallies[2:2 + 2 * couples:2]
    slack = jnp.minimum(source_of - 1, bound - sink)
    passed = jax.random.randint(jax.random.fold_in(key, 1), (couples,), 0, 1 << 20) % (slack + 1)
    tallies = tallies.at[1:1 + 2 * couples:2].set(source_of - passed).at[2:2 + 2 * couples:2].set(sink + passed)
    return tallies[jax.random.permutation(jax.random.fold_in(key, 2), amount)]


def centred(rng, extent, scale, bound, split=(), held_as=jnp.bfloat16):
    values = scale * jax.random.normal(rng, extent, jnp.float32)
    if split:
        values = values * level_of(rng, extent, split, -0.22, 0.18)
    return jnp.clip(values, -bound, bound).astype(held_as)


def setup_inputs(seed: int = 0) -> dict:
    streams_of = jax.random.split(jax.random.key(seed), 13)
    tokens = centred(streams_of[0], (TOKENS, D), 1.0, 6.0, ((0, 128),))
    segments = jax.vmap(lambda own: jnp.searchsorted(jnp.cumsum(ragged_sizes(own, 4, LEN, 3 * LEN // 4, 1)), jnp.arange(LEN), side="right"))(jax.random.split(streams_of[1], SEQS)).reshape((SEQS, LEN)).astype(jnp.int32)
    first_gain = jnp.clip(1.0 + 0.18 * jax.random.normal(streams_of[2], (D,), jnp.float32), 0.1, 1.9)
    first_shift = centred(streams_of[3], (D,), 0.3, 2.0, ((0, 8),), jnp.float32)
    heads_weight = centred(streams_of[4], (D, 3, D), D ** -0.5, 0.125, ((0, 8), (2, 16)), jnp.float32)
    heads_bias = centred(streams_of[5], (3, H, HD), 0.5, 3.0, ((1, 16), (2, 8)), jnp.float32)
    output_weight = centred(streams_of[6], (D, D), (D // 64) ** -0.5, 1.0, ((0, 16), (1, 8)), jnp.float32)
    second_gain = jnp.clip(1.0 + 0.18 * jax.random.normal(streams_of[7], (D,), jnp.float32), 0.1, 1.9)
    second_shift = centred(streams_of[8], (D,), 0.3, 2.0, ((0, 8),), jnp.float32)
    gate_up_weight = centred(streams_of[9], (D, 2, FF), D ** -0.5, 0.125, ((0, 8), (2, 16)), jnp.float32)
    down_weight = centred(streams_of[10], (FF, D), FF ** -0.5, 0.078125, ((0, 16), (1, 8)), jnp.float32)
    cotangent = centred(streams_of[11], (TOKENS, D), 1.0, 6.0, ((0, 128),))
    return dict(tokens=tokens, segments=segments, first_gain=first_gain, first_shift=first_shift, heads_weight=heads_weight, heads_bias=heads_bias, output_weight=output_weight, second_gain=second_gain, second_shift=second_shift, gate_up_weight=gate_up_weight, down_weight=down_weight, cotangent=cotangent)


NORM_EPS = 1e-05
BASE_FREQ = 10000.0
FAR_NEGATIVE = -1e+30
HIGHEST = lax.Precision.HIGHEST

@jax.custom_vjp
def low(v):
    return lax.optimization_barrier(v.astype(jnp.bfloat16)).astype(jnp.float32)

@jax.custom_vjp
def low_back(v):
    return v

def low_keep(v):
    return (low(v), None)

def low_pass(kept, grad):
    return (grad,)

def back_keep(v):
    return (v, None)

def back_low(kept, grad):
    return (low(grad),)
low.defvjp(low_keep, low_pass)
low_back.defvjp(back_keep, back_low)

def layer_norm(values, gain, shift):
    centre = values - lax.optimization_barrier(jnp.mean(values, axis=-1, keepdims=True))
    spread = lax.optimization_barrier(jnp.mean(centre * centre, axis=-1, keepdims=True))
    return centre * lax.rsqrt(spread + NORM_EPS) * gain + shift

def doc_positions(seg_ids):
    length = seg_ids.shape[-1]
    places = jnp.arange(length, dtype=jnp.int32)
    is_start = jnp.concatenate([jnp.ones_like(seg_ids[..., :1]), (seg_ids[..., 1:] != seg_ids[..., :-1]).astype(jnp.int32)], axis=-1)
    starts = lax.cummax(jnp.where(is_start > 0, places, 0), axis=seg_ids.ndim - 1)
    return places - starts

def rotate(values, places, sign):
    half_rot = ROT // 2
    inverse = jnp.exp(jnp.arange(half_rot, dtype=jnp.float32) * (-2.0 * math.log(BASE_FREQ) / ROT))
    angles = places.astype(jnp.float32)[..., None] * inverse
    cosine = jnp.cos(angles)[..., None, :]
    sine_part = sign * jnp.sin(angles)[..., None, :]
    first_half = values[..., :half_rot]
    second_half = values[..., half_rot:ROT]
    return jnp.concatenate([first_half * cosine - second_half * sine_part, second_half * cosine + first_half * sine_part, values[..., ROT:]], axis=-1)

def attend(query, keys, values, seg_ids):
    groups = query.shape[0]
    padding = jnp.zeros((groups, QB) + query.shape[2:], jnp.float32)
    key_pad = jnp.concatenate([padding, keys], axis=1)
    value_pad = jnp.concatenate([padding, values], axis=1)
    seg_pad = jnp.concatenate([jnp.full((groups, QB), -1, jnp.int32), seg_ids], axis=1)

    def one_block(block_id):
        first_row = block_id * QB
        row_ids = first_row + jnp.arange(QB, dtype=jnp.int32)
        col_ids = first_row - QB + jnp.arange(2 * QB, dtype=jnp.int32)
        distance = row_ids[:, None] - col_ids[None, :]
        in_window = (distance >= 0) & (distance < WINDOW)
        seg_rows = lax.dynamic_slice_in_dim(seg_ids, first_row, QB, 1)
        seg_cols = lax.dynamic_slice_in_dim(seg_pad, first_row, 2 * QB, 1)
        allowed = in_window[None] & (seg_rows[:, :, None] == seg_cols[:, None, :])
        q_block = lax.dynamic_slice_in_dim(query, first_row, QB, 1)
        k_block = lax.dynamic_slice_in_dim(key_pad, first_row, 2 * QB, 1)
        v_block = lax.dynamic_slice_in_dim(value_pad, first_row, 2 * QB, 1)
        scores = low_back(jnp.einsum('gqhd,gkhd->ghqk', q_block, k_block, precision=HIGHEST))
        scores = jnp.where(allowed[:, None], scores, FAR_NEGATIVE)
        maxima = lax.optimization_barrier(jnp.max(scores, axis=-1, keepdims=True))
        weights = jnp.exp(scores - maxima)
        probabilities = weights / lax.optimization_barrier(jnp.sum(weights, axis=-1, keepdims=True))
        return jnp.einsum('ghqk,gkhd->gqhd', low(probabilities), v_block, precision=HIGHEST)
    blocks = lax.map(jax.checkpoint(one_block), jnp.arange(LEN // QB, dtype=jnp.int32))
    return jnp.moveaxis(blocks, 0, 1).reshape(query.shape)

def forward(inputs, seg_ids, params):
    gain_one, shift_one, w_heads, b_heads, w_output, gain_two, shift_two, w_gate_up, w_down = [low(parameter) for parameter in params]
    groups = inputs.shape[0]
    places = doc_positions(seg_ids)
    normed_one = low(layer_norm(inputs, gain_one, shift_one))
    projected = jnp.einsum('gtd,dje->gtje', normed_one, w_heads, precision=HIGHEST) + b_heads.reshape(3, H * HD)
    projected = low_back(projected).reshape(groups, LEN, 3, H, HD)
    query = low(rotate(projected[:, :, 0], places, 1.0) * HD ** (-0.5))
    keys = low(rotate(projected[:, :, 1], places, 1.0))
    values = low(projected[:, :, 2])
    attended = low(low_back(attend(query, keys, values, seg_ids).reshape(groups, LEN, H * HD)))
    residual = inputs + low_back(jnp.einsum('gtd,de->gte', attended, w_output, precision=HIGHEST))
    normed_two = low(layer_norm(residual, gain_two, shift_two))
    gate_up = low_back(jnp.einsum('gtd,dje->gtje', normed_two, w_gate_up, precision=HIGHEST))
    hidden = low(jax.nn.silu(gate_up[:, :, 0]) * gate_up[:, :, 1])
    return residual + low_back(jnp.einsum('gtf,fd->gtd', hidden, w_down, precision=HIGHEST))

def reference(tokens, segments, first_gain, first_shift, heads_weight, heads_bias, output_weight, second_gain, second_shift, gate_up_weight, down_weight, cotangent):
    params = (first_gain, first_shift, heads_weight, heads_bias, output_weight, second_gain, second_shift, gate_up_weight, down_weight)
    inputs = tokens.astype(jnp.float32).reshape(-1, 2, LEN, D)
    upstream = cotangent.astype(jnp.float32).reshape(-1, 2, LEN, D)
    seg_groups = segments.reshape(-1, 2, LEN)

    def one_group(running, group_data):
        group_in, group_seg, group_up = group_data

        def run_layer(group_x, *weights):
            return forward(group_x, group_seg, weights)
        result, pullback = jax.vjp(run_layer, group_in, *params)
        gradients = pullback(group_up)
        summed = tuple((before + fresh_grad for before, fresh_grad in zip(running, gradients[1:])))
        return (summed, (result, gradients[0]))
    zeros = tuple((jnp.zeros_like(parameter) for parameter in params))
    totals, (results, input_grads) = lax.scan(one_group, zeros, (inputs, seg_groups, upstream))
    mixed = results.reshape(-1, D)
    grad_tokens = input_grads.reshape(-1, D)
    return (mixed, grad_tokens, totals[0], totals[1], totals[2], totals[3], totals[4], totals[5], totals[6], totals[7], totals[8])
```

```python
import math

import jax
import jax.numpy as jnp
import numpy as np
from jax import lax
from jax.sharding import Mesh, PartitionSpec as P

D = 2048
HD = 64
ROT = 16
WINDOW = 512
QB = 512
LEN = 1024

NORM_EPS = 1e-05
BASE_FREQ = 10000.0
FAR_NEGATIVE = -1e30
BF = jnp.bfloat16
F32 = jnp.float32


def layer_norm_parts(values):
    centre = values - jnp.mean(values, axis=-1, keepdims=True)
    inverse = lax.rsqrt(jnp.mean(centre * centre, axis=-1, keepdims=True) + NORM_EPS)
    return (centre * inverse, inverse)


def norm_back(upstream, normed, inverse, gain):
    scaled = upstream * gain
    inner = (
        scaled
        - jnp.mean(scaled, axis=-1, keepdims=True)
        - normed * jnp.mean(scaled * normed, axis=-1, keepdims=True)
    )
    return (inner * inverse, jnp.sum(upstream * normed, axis=0), jnp.sum(upstream, axis=0))


def doc_starts(seg):
    places = jnp.arange(LEN, dtype=jnp.int32)
    before = jnp.concatenate([jnp.full((1,), -1, jnp.int32), seg[:-1]])
    return lax.cummax(jnp.where(seg != before, places, 0), axis=0)


def rotate(values, places, sign):
    half_rot = ROT // 2
    inverse = jnp.exp(jnp.arange(half_rot, dtype=F32) * (-2.0 * math.log(BASE_FREQ) / ROT))
    angles = places.astype(F32)[..., None] * inverse
    cosine = jnp.cos(angles)[..., None, :]
    sine_part = sign * jnp.sin(angles)[..., None, :]
    first_half = values[..., :half_rot]
    second_half = values[..., half_rot:ROT]
    return jnp.concatenate(
        [
            first_half * cosine - second_half * sine_part,
            second_half * cosine + first_half * sine_part,
            values[..., ROT:],
        ],
        axis=-1,
    )


def nt(left, right):
    return lax.dot_general(left, right, (((1,), (1,)), ((), ())), preferred_element_type=F32)


def tn(left, right):
    return lax.dot_general(left, right, (((0,), (0,)), ((), ())), preferred_element_type=F32)


def mm(left, right):
    return jnp.dot(left, right, preferred_element_type=F32)


def gather_w(w):
    return lax.all_gather(w, ("zhi", "dp"), axis=0, tiled=False)


def gather_b(v):
    return lax.all_gather(v, "b", axis=0, tiled=True)


def scatter_b(v):
    return lax.psum_scatter(v.astype(BF), "b", scatter_dimension=0, tiled=True).astype(F32)


def attention(query, keys, values, allowed):
    scores = jnp.einsum("qhd,khd->hqk", query, keys, preferred_element_type=F32)
    scores = jnp.where(allowed[None], scores, FAR_NEGATIVE)
    maxima = jnp.max(scores, axis=-1, keepdims=True)
    weights = jnp.exp(scores - maxima)
    return weights / jnp.sum(weights, axis=-1, keepdims=True)


def per_device(
    tokens,
    segments,
    first_gain,
    first_shift,
    heads_weight,
    heads_bias,
    output_weight,
    second_gain,
    second_shift,
    gate_up_weight,
    down_weight,
    cotangent,
):
    zhi = lax.axis_index("zhi")
    rows = tokens.shape[0]
    seg = lax.dynamic_index_in_dim(segments, zhi, 0, keepdims=False)
    starts = doc_starts(seg)
    index = jnp.arange(LEN, dtype=jnp.int32)
    places = index - starts
    lowest = jnp.maximum(starts, index - (WINDOW - 1))
    allowed = (index[None, :] <= index[:, None]) & (index[None, :] >= lowest[:, None])

    small = jnp.stack([first_gain, first_shift, second_gain, second_shift]).astype(BF)
    small = lax.all_gather(small, "dp", axis=1, tiled=True).astype(F32)
    gain_one, shift_one, gain_two, shift_two = small[0], small[1], small[2], small[3]
    bias = gather_w(heads_bias.astype(BF).reshape(6, 8)).astype(F32)
    bias = bias.reshape(2, 8, 3, 2, 8).transpose(2, 0, 3, 1, 4).reshape(3, 4, HD)
    w_heads = gather_w(heads_weight.astype(BF)).reshape(2, D, 3, 128)
    w_out = gather_w(output_weight.astype(BF))
    w_gate_up = gather_w(gate_up_weight.astype(BF)).reshape(2, D, 2, 352)
    w_down = gather_w(down_weight.astype(BF))
    w_heads = w_heads.transpose(1, 2, 0, 3).reshape(D, 768)
    w_out = w_out.reshape(2, 8, 128, 256).transpose(0, 2, 1, 3).reshape(256, D)
    w_gate_up = w_gate_up.transpose(1, 2, 0, 3).reshape(D, 1408)
    w_down = w_down.reshape(2, 8, 352, 256).transpose(0, 2, 1, 3).reshape(704, D)

    inputs = tokens.astype(F32)
    normed_one, inverse_one = layer_norm_parts(inputs)
    first_all = gather_b((normed_one * gain_one + shift_one).astype(BF))
    up_all = gather_b(cotangent)
    projected = (mm(first_all, w_heads) + bias.reshape(768)).reshape(LEN, 3, 4, HD)
    query = (rotate(projected[:, 0], places, 1.0) * HD ** (-0.5)).astype(BF)
    keys = rotate(projected[:, 1], places, 1.0).astype(BF)
    values = projected[:, 2].astype(BF)
    probabilities = attention(query, keys, values, allowed)
    prob_low = probabilities.astype(BF)
    attended = (
        jnp.einsum("hqk,khd->qhd", prob_low, values, preferred_element_type=F32)
        .astype(BF)
        .reshape(LEN, 256)
    )
    residual = inputs + scatter_b(mm(attended, w_out))
    normed_two, inverse_two = layer_norm_parts(residual)
    second_all = gather_b((normed_two * gain_two + shift_two).astype(BF))
    gate_up = mm(second_all, w_gate_up)
    gate_pre, up_pre = gate_up[:, :704], gate_up[:, 704:]
    sigmoid_gate = jax.nn.sigmoid(gate_pre)
    silu_gate = gate_pre * sigmoid_gate
    hidden = (silu_gate * up_pre).astype(BF)
    mixed = residual + scatter_b(mm(hidden, w_down))

    hidden_grad = nt(up_all, w_down)
    grad_down = tn(hidden, up_all)
    gate_grad = hidden_grad * up_pre * sigmoid_gate * (1.0 + gate_pre * (1.0 - sigmoid_gate))
    up_grad = hidden_grad * silu_gate
    gate_up_grad = jnp.concatenate([gate_grad, up_grad], axis=1).astype(BF)
    grad_gate_up = tn(second_all, gate_up_grad)
    second_grad = scatter_b(nt(gate_up_grad, w_gate_up))
    residual_part, grad_gain_two, grad_shift_two = norm_back(
        second_grad, normed_two, inverse_two, gain_two
    )
    residual_grad = cotangent.astype(F32) + residual_part
    branch_all = gather_b(residual_grad.astype(BF))
    attended_grad = nt(branch_all, w_out).astype(BF).reshape(LEN, 4, HD)
    grad_output = tn(attended, branch_all)

    prob_grad = jnp.einsum("qhd,khd->hqk", attended_grad, values, preferred_element_type=F32)
    row_inner = jnp.sum(probabilities * prob_grad, axis=-1, keepdims=True)
    score_grad = (probabilities * (prob_grad - row_inner)).astype(BF)
    query_grad = jnp.einsum("hqk,khd->qhd", score_grad, keys, preferred_element_type=F32)
    key_grad = jnp.einsum("hqk,qhd->khd", score_grad, query, preferred_element_type=F32)
    value_grad = jnp.einsum("hqk,qhd->khd", prob_low, attended_grad, preferred_element_type=F32)
    projected_grad = jnp.stack(
        [
            rotate(query_grad * HD ** (-0.5), places, -1.0),
            rotate(key_grad, places, -1.0),
            value_grad,
        ],
        axis=1,
    )
    projected_grad = projected_grad.astype(BF).reshape(LEN, 768)
    grad_bias = jnp.sum(projected_grad.astype(F32), axis=0)
    grad_heads = tn(first_all, projected_grad)
    first_grad = scatter_b(nt(projected_grad, w_heads))
    input_part, grad_gain_one, grad_shift_one = norm_back(
        first_grad, normed_one, inverse_one, gain_one
    )
    grad_tokens = residual_grad + input_part

    def scatter_w(v):
        return lax.psum_scatter(v, ("zhi", "dp"), scatter_dimension=0, tiled=False)

    grad_heads = grad_heads.astype(BF).reshape(8, 256, 3, 2, 128).transpose(3, 0, 1, 2, 4)
    grad_gate_up = grad_gate_up.astype(BF).reshape(8, 256, 2, 2, 352).transpose(3, 0, 1, 2, 4)
    grad_output = grad_output.astype(BF).reshape(2, 128, 8, 256).transpose(0, 2, 1, 3)
    grad_down = grad_down.astype(BF).reshape(2, 352, 8, 256).transpose(0, 2, 1, 3)
    grad_heads = scatter_w(grad_heads.reshape(16, 256, 3, 128)).astype(F32)
    grad_gate_up = scatter_w(grad_gate_up.reshape(16, 256, 2, 352)).astype(F32)
    grad_output = scatter_w(grad_output.reshape(16, 128, 256)).astype(F32)
    grad_down = scatter_w(grad_down.reshape(16, 352, 256)).astype(F32)
    grad_bias = grad_bias.reshape(3, 2, 2, 8, 8).transpose(1, 3, 0, 2, 4).reshape(16, 3, 2, 8)
    grad_bias = scatter_w(grad_bias)
    norms = jnp.stack([grad_gain_one, grad_shift_one, grad_gain_two, grad_shift_two])
    norms = lax.psum_scatter(norms, ("dp", "zhi", "b"), scatter_dimension=1, tiled=True)
    return (
        mixed,
        grad_tokens,
        norms[0],
        norms[1],
        grad_heads,
        grad_bias,
        grad_output,
        norms[2],
        norms[3],
        grad_gate_up,
        grad_down,
    )


T = ("zhi", "b")
ALL = ("dp", "zhi", "b")


def solution(mesh):
    fine = Mesh(np.asarray(mesh.devices).reshape(8, 2, 8), ("dp", "zhi", "b"))
    return jax.shard_map(
        per_device,
        mesh=fine,
        in_specs=(
            P(ALL, None),
            P("dp", None),
            P("dp"),
            P("dp"),
            P("dp", None, T),
            P(None, T, "dp"),
            P(T, "dp"),
            P("dp"),
            P("dp"),
            P("dp", None, T),
            P(T, "dp"),
            P(ALL, None),
        ),
        out_specs=(
            P(ALL, None),
            P(ALL, None),
            P(ALL),
            P(ALL),
            P("dp", None, T),
            P(None, T, "dp"),
            P(T, "dp"),
            P(ALL),
            P(ALL),
            P("dp", None, T),
            P(T, "dp"),
        ),
        check_vma=False,
    )
```

```python
import functools
import math

import jax
import jax.numpy as jnp
from jax import lax
from jax.experimental import pallas as pl
from jax.experimental.pallas import tpu as pltpu
from jax.sharding import PartitionSpec as P

D = 2048
HD = 64
ROT = 16
WINDOW = 512
LEN = 1024
OWN = 128
HALF = OWN // 2
CHIP = 2 * OWN
UNITS = 352
PAD = 384
QB = 256

NORM_EPS = 1e-05
BASE_FREQ = 10000.0
FAR_NEGATIVE = -1e30
BF = jnp.bfloat16
F32 = jnp.float32
MESH = pl.DeviceIdType.MESH
VMEM_LIMIT = 60 * 2**20
DMA = pltpu.SemaphoreType.DMA


def spot(z, x, c):
    return (z % 2) * 4 + x * 2 + c


class Near:
    def __init__(self):
        t = lax.axis_index("tensor")
        z, x, c = t // 4, (t // 2) % 2, t % 2
        oz = (z // 2) * 2 + (z + 1) % 2
        ox, oc = 1 - x, 1 - c
        self.c, self.oc = c, oc
        self.me = spot(z, x, c)
        self.dev = {
            "x": {"tensor": z * 4 + ox * 2 + c},
            "z": {"tensor": oz * 4 + x * 2 + c},
            "s": {"tensor": z * 4 + x * 2 + oc},
        }
        self.same = {"o": spot(z, x, c), "x": spot(z, ox, c), "z": spot(oz, x, c), "d": spot(oz, ox, c)}
        self.other = {
            "o": spot(z, x, oc),
            "x": spot(z, ox, oc),
            "z": spot(oz, x, oc),
            "d": spot(oz, ox, oc),
        }
        self.chip = {"o": (z % 2) * 2 + x, "x": (z % 2) * 2 + ox, "z": (oz % 2) * 2 + x, "d": (oz % 2) * 2 + ox}


def remote(src, dst, send, recv, device):
    return pltpu.make_async_remote_copy(
        src_ref=src, dst_ref=dst, send_sem=send, recv_sem=recv, device_id=device, device_id_type=MESH
    )


def greet(devices):
    barrier = pltpu.get_barrier_semaphore()
    for device in devices:
        pl.semaphore_signal(barrier, inc=1, device_id=device, device_id_type=MESH)
    pl.semaphore_wait(barrier, len(devices))


def block_rows(block, half=None):
    if half is None:
        return pl.ds(pl.multiple_of(block * OWN, OWN), OWN)
    return pl.ds(pl.multiple_of(block * OWN + half * HALF, HALF), HALF)


def chip_rows(chip):
    return pl.ds(pl.multiple_of(chip * CHIP, CHIP), CHIP)


class Gather:
    COPIES = 13

    def __init__(self, near, buf, send, recv):
        self.near, self.buf, self.send, self.recv = near, buf, send, recv
        self.sent = []

    def copy(self, index, block, half, to):
        view = self.buf.at[block_rows(block, half)]
        return remote(view, view, self.send.at[index], self.recv.at[index], self.near.dev[to])

    def go(self, index, block, half, to):
        copy = self.copy(index, block, half, to)
        copy.start()
        self.sent.append(copy)

    def take(self, index, block, half, to="s"):
        self.copy(index, block, half, to).wait_recv()

    def start(self):
        me = self.near.me
        self.go(0, me, 0, "z")
        self.go(1, me, 1, "x")
        self.go(4, me, None, "s")
        self.go(2, me, 0, "x")
        self.go(3, me, 1, "z")

    def first(self):
        same = self.near.same
        self.take(0, same["z"], 0)
        self.go(5, same["z"], 0, "x")
        self.go(7, same["z"], 0, "s")
        self.take(1, same["x"], 1)
        self.go(6, same["x"], 1, "z")
        self.go(8, same["x"], 1, "s")

    def second(self):
        same = self.near.same
        self.take(2, same["x"], 0)
        self.go(9, same["x"], 0, "s")
        self.take(3, same["z"], 1)
        self.go(10, same["z"], 1, "s")

    def third(self):
        same = self.near.same
        self.take(5, same["d"], 0)
        self.go(11, same["d"], 0, "s")
        self.take(6, same["d"], 1)
        self.go(12, same["d"], 1, "s")

    def own_chip(self):
        self.take(4, self.near.other["o"], None)

    def x_chip(self):
        self.take(8, self.near.other["x"], 1)
        self.take(9, self.near.other["x"], 0)

    def z_chip(self):
        self.take(7, self.near.other["z"], 0)
        self.take(10, self.near.other["z"], 1)

    def d_chip(self):
        self.take(11, self.near.other["d"], 0)
        self.take(12, self.near.other["d"], 1)

    def finish(self):
        for copy in self.sent:
            copy.wait_send()

    def run(self, use):
        self.own_chip()
        use("o")
        self.first()
        self.second()
        self.x_chip()
        use("x")
        self.third()
        self.z_chip()
        use("z")
        self.d_chip()
        use("d")


class Scatter:
    COPIES = 10

    @staticmethod
    def scratch(width=D):
        return [
            pltpu.VMEM((CHIP, width), F32),
            pltpu.VMEM((4, OWN, width), F32),
            pltpu.VMEM((4, OWN, width), BF),
            pltpu.VMEM((4, OWN, width), BF),
            pltpu.VMEM((OWN, width), BF),
            pltpu.VMEM((4, HALF, width), BF),
            pltpu.VMEM((2, HALF, width), BF),
            pltpu.VMEM((4, HALF, width), BF),
            DMA((Scatter.COPIES,)),
            DMA((Scatter.COPIES,)),
        ]

    KEYS = ("d", "z", "x", "o")

    def __init__(self, near, refs):
        self.near = near
        (
            self.part,
            self.mine,
            self.core_out,
            self.core_in,
            self.far_out,
            self.out,
            self.through,
            self.last,
            self.send,
            self.recv,
        ) = refs
        self.sent = []

    def copy(self, index, src, dst, to):
        return remote(src, dst, self.send.at[index], self.recv.at[index], self.near.dev[to])

    def go(self, index, src, dst, to):
        copy = self.copy(index, src, dst, to)
        copy.start()
        self.sent.append(copy)

    def take(self, index, dst, to="s"):
        self.copy(index, dst, dst, to).wait_recv()

    def produce(self, key, make):
        i = self.KEYS.index(key)
        make(self.near.chip[key])
        self.core_out[i] = self.part[block_rows(self.near.oc), :].astype(BF)
        self.go(i, self.core_out.at[i], self.core_in.at[i], "s")
        self.mine[i] = self.part[block_rows(self.near.c), :]

    def join(self, key):
        i = self.KEYS.index(key)
        self.take(i, self.core_in.at[i])

    def summed(self, key, half):
        i = self.KEYS.index(key)
        rows = slice(half * HALF, (half + 1) * HALF)
        return self.mine[i, rows, :] + self.core_in[i, rows, :].astype(F32)

    def far(self):
        self.join("d")
        self.far_out[:HALF, :] = self.summed("d", 0).astype(BF)
        self.go(4, self.far_out.at[pl.ds(0, HALF)], self.through.at[0], "z")
        self.far_out[HALF:, :] = self.summed("d", 1).astype(BF)
        self.go(5, self.far_out.at[pl.ds(HALF, HALF)], self.through.at[1], "x")

    def z_direct(self):
        self.join("z")
        self.out[0] = self.summed("z", 0).astype(BF)
        self.go(6, self.out.at[0], self.last.at[0], "z")

    def x_direct(self):
        self.join("x")
        self.out[1] = self.summed("x", 1).astype(BF)
        self.go(7, self.out.at[1], self.last.at[1], "x")

    def relays(self):
        self.take(4, self.through.at[0])
        self.out[2] = (self.summed("x", 0) + self.through[0].astype(F32)).astype(BF)
        self.go(8, self.out.at[2], self.last.at[2], "x")
        self.take(5, self.through.at[1])
        self.out[3] = (self.summed("z", 1) + self.through[1].astype(F32)).astype(BF)
        self.go(9, self.out.at[3], self.last.at[3], "z")

    def result(self):
        self.join("o")
        for index in range(4):
            self.take(6 + index, self.last.at[index])
        first = self.summed("o", 0) + self.last[0].astype(F32) + self.last[2].astype(F32)
        second = self.summed("o", 1) + self.last[1].astype(F32) + self.last[3].astype(F32)
        for copy in self.sent:
            copy.wait_send()
        self.sent = []
        return first, second

    def run(self, make):
        self.produce("d", make)
        self.produce("z", make)
        self.far()
        self.produce("x", make)
        self.z_direct()
        self.produce("o", make)
        self.x_direct()
        self.relays()
        return self.result()


def dot(left, right):
    return jnp.dot(left, right, preferred_element_type=F32)


def dot_nt(left, right):
    return lax.dot_general(left, right, (((1,), (1,)), ((), ())), preferred_element_type=F32)


def dot_tn(left, right):
    return lax.dot_general(left, right, (((0,), (0,)), ((), ())), preferred_element_type=F32)


def layer_norm_parts(values):
    centre = values - jnp.mean(values, axis=-1, keepdims=True)
    inverse = lax.rsqrt(jnp.mean(centre * centre, axis=-1, keepdims=True) + NORM_EPS)
    return (centre * inverse, inverse)


def norm_back(upstream, normed, inverse, gain):
    scaled = upstream * gain
    inner = (
        scaled
        - jnp.mean(scaled, axis=-1, keepdims=True)
        - normed * jnp.mean(scaled * normed, axis=-1, keepdims=True)
    )
    return (
        inner * inverse,
        jnp.sum(upstream * normed, axis=0, keepdims=True),
        jnp.sum(upstream, axis=0, keepdims=True),
    )


def params(collective=None):
    if collective is None:
        return pltpu.CompilerParams(vmem_limit_bytes=VMEM_LIMIT)
    return pltpu.CompilerParams(
        collective_id=collective, has_side_effects=True, vmem_limit_bytes=VMEM_LIMIT
    )


def cost(flops, moved):
    return pl.CostEstimate(flops=flops, bytes_accessed=moved, transcendentals=0)


IN_VMEM = pl.BlockSpec(memory_space=pltpu.VMEM)
ANYWHERE = pl.BlockSpec(memory_space=pl.ANY)


def shape(dims, dtype):
    return jax.ShapeDtypeStruct(dims, dtype)


def copy_all(pairs, sems):
    copies = [pltpu.make_async_copy(src, dst, sems.at[i]) for i, (src, dst) in enumerate(pairs)]
    for copy in copies:
        copy.start()
    return copies


def dp_of(k, h):
    dp = lax.axis_index("dp")
    return ((dp // 4 + h) % 2) * 4 + (dp % 4 - k + 4) % 4


def weight_pairs(blocks, buf):
    pairs = []
    if len(blocks) == 4:
        for k in range(4):
            for h in range(2):
                for s in range(2):
                    row = pl.ds(pl.multiple_of(dp_of(k, h) * 256, 256), 256)
                    pairs.append((blocks[k].at[h * 2 + s], buf.at[s, row]))
    else:
        for k in range(4):
            for h in range(2):
                row = pl.ds(pl.multiple_of(dp_of(k, h) * 256, 256), 256)
                pairs.append((blocks[k].at[h], buf.at[0, row]))
                pairs.append((blocks[4].at[k * 2 + h], buf.at[1, row]))
    return pairs


def open_kernel(
    tok, cot, small, head, first_out, cot_out, gains_out, head_out,
    fa, ca, gbuf, ga_send, ga_recv, gc_send, gc_recv, sm_send, sm_recv, hd_send, hd_recv, out_sem,
):
    near = Near()
    t, dp = lax.axis_index("tensor"), lax.axis_index("dp")
    h, y = dp // 4, dp % 4
    over = {"dp": (1 - h) * 4 + y}
    ring = [{"dp": h * 4 + (y + k) % 4} for k in (1, 2, 3)]
    partner = {"tensor": (3 - t // 4) * 4 + t % 4}
    greet([near.dev["x"], near.dev["z"], near.dev["s"], over, partner] + ring)

    small_sent = []

    def send_small(index, slot_from, slot_to, device, src=None):
        copy = remote(
            gbuf.at[slot_from] if src is None else src,
            gbuf.at[slot_to],
            sm_send.at[index],
            sm_recv.at[index],
            device,
        )
        copy.start()
        small_sent.append(copy)

    def take_small(index, slot):
        remote(gbuf.at[slot], gbuf.at[slot], sm_send.at[index], sm_recv.at[index], over).wait_recv()

    send_small(0, 0, 1, over, small)
    for k in (1, 2, 3):
        send_small(k, 0, k * 2, ring[k - 1], small)

    head_sent = []

    def send_head(index, slot_from, slot_to, device, src=None):
        copy = remote(
            head_out.at[slot_from] if src is None else src,
            head_out.at[slot_to],
            hd_send.at[index],
            hd_recv.at[index],
            device,
        )
        copy.start()
        head_sent.append(copy)

    def take_head(index, slot):
        remote(head_out.at[slot], head_out.at[slot], hd_send.at[index], hd_recv.at[index], over).wait_recv()

    send_head(0, 0, 1, partner, head)
    send_head(1, 0, 2, over, head)
    for k in (1, 2, 3):
        send_head(3 + (k - 1) * 4, 0, k * 4, ring[k - 1], head)

    ca[block_rows(near.me), :] = cot[...]
    cots = Gather(near, ca, gc_send, gc_recv)
    cots.start()
    gbuf[0] = small[...]
    own_head = pltpu.make_async_copy(head, head_out.at[0], out_sem.at[8])
    own_head.start()

    normed, _ = layer_norm_parts(tok[...].astype(F32))
    take_small(0, 1)
    for k in (1, 2, 3):
        send_small(3 + k, 1, k * 2 + 1, ring[k - 1])
    for k in (1, 2, 3):
        take_small(k, k * 2)
    for k in (1, 2, 3):
        take_small(3 + k, k * 2 + 1)
    for d in range(8):
        slot = ((y - d % 4 + 4) % 4) * 2 + (h + d // 4) % 2
        gains_out[:, d * 256 : (d + 1) * 256] = gbuf[slot]
    first = normed * gains_out[0:1, :] + gains_out[1:2, :]
    fa[block_rows(near.me), :] = first.astype(BF)
    firsts = Gather(near, fa, ga_send, ga_recv)
    firsts.start()

    take_head(0, 1)
    send_head(2, 1, 3, over)
    for k in (1, 2, 3):
        send_head(4 + (k - 1) * 4, 1, k * 4 + 1, ring[k - 1])
    take_head(1, 2)
    for k in (1, 2, 3):
        send_head(5 + (k - 1) * 4, 2, k * 4 + 2, ring[k - 1])

    cots.first()
    cots.second()
    take_head(2, 3)
    for k in (1, 2, 3):
        send_head(6 + (k - 1) * 4, 3, k * 4 + 3, ring[k - 1])
    cots.third()
    firsts.first()
    firsts.second()
    firsts.third()
    copies = []

    def out(index, buf, target, chip):
        rows = chip_rows(chip)
        copy = pltpu.make_async_copy(buf.at[rows], target.at[rows], out_sem.at[index])
        copy.start()
        copies.append(copy)

    for i, (gather, buf, target) in enumerate(((cots, ca, cot_out), (firsts, fa, first_out))):
        gather.own_chip()
        out(i * 4, buf, target, near.chip["o"])
        gather.x_chip()
        out(i * 4 + 1, buf, target, near.chip["x"])
        gather.z_chip()
        out(i * 4 + 2, buf, target, near.chip["z"])
        gather.d_chip()
        out(i * 4 + 3, buf, target, near.chip["d"])
    for k in (1, 2, 3):
        for j in range(4):
            take_head(3 + (k - 1) * 4 + j, k * 4 + j)
    cots.finish()
    firsts.finish()
    for copy in small_sent + head_sent:
        copy.wait_send()
    own_head.wait()
    for copy in copies:
        copy.wait()


def open_call(tokens, cotangent, small, head):
    return pl.pallas_call(
        open_kernel,
        out_shape=(
            shape((LEN, D), BF),
            shape((LEN, D), BF),
            shape((8, D), F32),
            shape((16,) + head.shape, BF),
        ),
        in_specs=[IN_VMEM, IN_VMEM, IN_VMEM, ANYWHERE],
        out_specs=(ANYWHERE, ANYWHERE, IN_VMEM, ANYWHERE),
        scratch_shapes=[
            pltpu.VMEM((LEN, D), BF),
            pltpu.VMEM((LEN, D), BF),
            pltpu.VMEM((8, 8, 256), F32),
            DMA((Gather.COPIES,)),
            DMA((Gather.COPIES,)),
            DMA((Gather.COPIES,)),
            DMA((Gather.COPIES,)),
            DMA((7,)),
            DMA((7,)),
            DMA((15,)),
            DMA((15,)),
            DMA((9,)),
        ],
        compiler_params=params(1),
        cost_estimate=cost(10**9, 60 * 2**20),
        name="open",
    )(tokens, cotangent, small, head)


def roll_rotate(values, cos, sin_up, sin_down):
    return (
        values * cos + pltpu.roll(values, 128 - ROT // 2, 1) * sin_up + pltpu.roll(values, ROT // 2, 1) * sin_down
    )


def window(block):
    start = max(0, block * QB - WINDOW)
    return start, (block + 1) * QB


def mask_bias(lowest, start, stop, block):
    keys = lax.broadcasted_iota(jnp.int32, (stop - start, QB), 0) + start
    queries = lax.broadcasted_iota(jnp.int32, (stop - start, QB), 1) + block * QB
    return jnp.where((keys <= queries) & (keys >= lowest), 0.0, FAR_NEGATIVE)


def head_lanes(rows, head):
    lanes = lax.broadcasted_iota(jnp.int32, (rows, 128), 1)
    return (lanes >= HD) if head else (lanes < HD)


def attend_kernel(
    first, head, cos, sin_up, sin_down, lowest,
    query, keys, values, attended, log_sum,
    wv, extra, vt, w_sem,
):
    copies = []
    for k in range(4):
        for h in range(2):
            for s in range(2):
                slot, dp = k * 4 + h * 2 + s, dp_of(k, h)
                row = pl.ds(pl.multiple_of(dp * 256, 256), 256)
                tail = pl.ds((k * 2 + h) * 16, 16)
                copies.append(
                    pltpu.make_async_copy(head.at[slot, pl.ds(0, 256)], wv.at[s, row], w_sem.at[2 * slot])
                )
                copies.append(
                    pltpu.make_async_copy(head.at[slot, pl.ds(256, 16)], extra.at[s, tail], w_sem.at[2 * slot + 1])
                )
    for copy in copies:
        copy.start()
    for copy in copies:
        copy.wait()
    bias = [jnp.sum(extra[s].astype(F32), axis=0, keepdims=True) for s in range(2)]

    @pl.loop(0, LEN // CHIP)
    def _(step):
        rows = chip_rows(step)
        c, up, down = cos[rows, :], sin_up[rows, :], sin_down[rows, :]
        for s in range(2):
            lanes = slice(s * 128, (s + 1) * 128)
            made = dot(first[rows, :], wv[s]) + bias[s]
            query[rows, lanes] = (roll_rotate(made[:, :128], c, up, down) * HD ** (-0.5)).astype(BF)
            keys[rows, lanes] = roll_rotate(made[:, 128:256], c, up, down).astype(BF)
            values[rows, lanes] = made[:, 256:].astype(BF)
            vt[s, :, rows] = made[:, 256:].T.astype(BF)

    for block in range(LEN // QB):
        start, stop = window(block)
        rows = slice(block * QB, (block + 1) * QB)
        bias_t = mask_bias(lowest[:, rows], start, stop, block)
        for s in range(2):
            lanes = slice(s * 128, (s + 1) * 128)
            q, k = query[rows, lanes], keys[start:stop, lanes]
            v_t = vt[s, :, start:stop]
            halves = []
            for head_id in range(2):
                q_one = jnp.where(head_lanes(QB, head_id), q, jnp.zeros_like(q))
                scores = dot_nt(k, q_one) + bias_t
                top = jnp.max(scores, axis=0, keepdims=True)
                weights = jnp.exp(scores - top)
                total = jnp.sum(weights, axis=0, keepdims=True)
                made = dot(v_t, weights.astype(BF))
                halves.append(made[head_id * HD : (head_id + 1) * HD] * (1.0 / total))
                log_sum[s * 2 + head_id : s * 2 + head_id + 1, rows] = top + jnp.log(total)
            attended[rows, lanes] = jnp.concatenate(halves, axis=0).T.astype(BF)


def attend_call(first_all, head, cos, sin_up, sin_down, lowest):
    narrow = shape((LEN, 256), BF)
    return pl.pallas_call(
        attend_kernel,
        out_shape=(narrow, narrow, narrow, narrow, shape((8, LEN), F32)),
        in_specs=[IN_VMEM, ANYWHERE] + [IN_VMEM] * 4,
        out_specs=(IN_VMEM,) * 5,
        scratch_shapes=[
            pltpu.VMEM((2, D, 384), BF),
            pltpu.VMEM((2, 128, 384), BF),
            pltpu.VMEM((2, 128, LEN), BF),
            DMA((32,)),
        ],
        compiler_params=params(),
        cost_estimate=cost(5 * 10**9, 12 * 2**20),
        name="attend",
    )(first_all, head, cos, sin_up, sin_down, lowest)


def silu_parts(gate, up, grad):
    sig = 1.0 / (1.0 + jnp.exp(-gate))
    silu = gate * sig
    return silu * up, grad * up * sig * (1.0 + gate * (1.0 - sig)), grad * silu


def middle_kernel(
    attended, tok, gains, cot_all, *rest,
):
    wo_in, wg_in, wd_in = rest[0:5], rest[5:9], rest[9:14]
    residual, second_out, hidden_out, grads_out = rest[14:18]
    wo, wg, wd, cots, hg, second, hidden, grads = rest[18:26]
    scatter_refs, (ga_send, ga_recv, w_sem, o_sem) = rest[26:36], rest[36:40]
    near = Near()
    out_copies = copy_all(weight_pairs(wo_in, wo), w_sem.at[pl.ds(0, 16)])
    cot_copy = copy_all([(cot_all, cots)], w_sem.at[pl.ds(48, 1)])
    down_copies = copy_all(weight_pairs(wd_in, wd), w_sem.at[pl.ds(16, 16)])
    gate_copies = copy_all(weight_pairs(wg_in, wg), w_sem.at[pl.ds(32, 16)])
    greet([near.dev["x"], near.dev["z"], near.dev["s"]])
    for copy in out_copies:
        copy.wait()
    scatter = Scatter(near, scatter_refs)

    def make(chip):
        rows = chip_rows(chip)
        scatter.part[...] = dot_nt(attended[rows, :128], wo[0]) + dot_nt(attended[rows, 128:], wo[1])

    scatter.produce("d", make)
    scatter.produce("z", make)
    scatter.far()
    scatter.produce("x", make)
    scatter.z_direct()
    scatter.produce("o", make)
    scatter.x_direct()
    for copy in cot_copy + down_copies:
        copy.wait()
    for chip in range(2):
        for s in range(2):
            hg[s, chip_rows(chip), :] = dot(cots[chip_rows(chip), :], wd[s])
    scatter.relays()
    for chip in range(2, 4):
        for s in range(2):
            hg[s, chip_rows(chip), :] = dot(cots[chip_rows(chip), :], wd[s])
    for copy in gate_copies:
        copy.wait()
    first, second_half = scatter.result()
    residual[:HALF, :] = tok[:HALF, :].astype(F32) + first
    residual[HALF:, :] = tok[HALF:, :].astype(F32) + second_half
    normed, _ = layer_norm_parts(residual[...])
    second[block_rows(near.me), :] = (normed * gains[2:3, :] + gains[3:4, :]).astype(BF)
    gather = Gather(near, second, ga_send, ga_recv)
    gather.start()
    copies = []

    def use(key):
        chip = near.chip[key]
        rows = chip_rows(chip)
        for s in range(2):
            made = dot(second[rows, :], wg[s])
            h, g, u = silu_parts(made[:, :PAD], made[:, PAD:], hg[s, rows, :])
            hidden[rows, s * PAD : (s + 1) * PAD] = h.astype(BF)
            grads[rows, s * 2 * PAD : s * 2 * PAD + PAD] = g.astype(BF)
            grads[rows, s * 2 * PAD + PAD : (s + 1) * 2 * PAD] = u.astype(BF)
        i = "oxzd".index(key) * 3
        copies.extend(
            copy_all(
                [
                    (second.at[rows], second_out.at[rows]),
                    (hidden.at[rows], hidden_out.at[rows]),
                    (grads.at[rows], grads_out.at[rows]),
                ],
                o_sem.at[pl.ds(i, 3)],
            )
        )

    gather.run(use)
    gather.finish()
    for copy in copies:
        copy.wait()


def middle_call(attended, tokens, gains, cot_all, wo, wg, wd):
    return pl.pallas_call(
        middle_kernel,
        out_shape=(
            shape((OWN, D), F32),
            shape((LEN, D), BF),
            shape((LEN, 2 * PAD), BF),
            shape((LEN, 4 * PAD), BF),
        ),
        in_specs=[IN_VMEM, IN_VMEM, IN_VMEM] + [ANYWHERE] * 15,
        out_specs=(IN_VMEM, ANYWHERE, ANYWHERE, ANYWHERE),
        scratch_shapes=[
            pltpu.VMEM((2, D, 128), BF),
            pltpu.VMEM((2, D, 2 * PAD), BF),
            pltpu.VMEM((2, D, PAD), BF),
            pltpu.VMEM((LEN, D), BF),
            pltpu.VMEM((2, LEN, PAD), F32),
            pltpu.VMEM((LEN, D), BF),
            pltpu.VMEM((LEN, 2 * PAD), BF),
            pltpu.VMEM((LEN, 4 * PAD), BF),
            *Scatter.scratch(),
            DMA((Gather.COPIES,)),
            DMA((Gather.COPIES,)),
            DMA((49,)),
            DMA((12,)),
        ],
        compiler_params=params(2),
        cost_estimate=cost(20 * 10**9, 60 * 2**20),
        name="middle",
    )(attended, tokens, gains, cot_all, *wo, *wg, *wd)


def back_kernel(grads, residual, cot, gains, *rest):
    wo_in, wg_in = rest[0:5], rest[5:9]
    residual_grad, branch_out, attended_grad, norm_sums = rest[9:13]
    wo, wg, branch = rest[13:16]
    scatter_refs, (ga_send, ga_recv, w_sem, o_sem) = rest[16:26], rest[26:30]
    near = Near()
    gate_copies = copy_all(weight_pairs(wg_in, wg), w_sem.at[pl.ds(0, 16)])
    out_copies = copy_all(weight_pairs(wo_in, wo), w_sem.at[pl.ds(16, 16)])
    greet([near.dev["x"], near.dev["z"], near.dev["s"]])
    for copy in gate_copies:
        copy.wait()
    scatter = Scatter(near, scatter_refs)

    def make(chip):
        rows = chip_rows(chip)
        scatter.part[...] = dot_nt(grads[rows, : 2 * PAD], wg[0]) + dot_nt(grads[rows, 2 * PAD :], wg[1])

    first, second_half = scatter.run(make)
    normed, inverse = layer_norm_parts(residual[...])
    upstream = jnp.concatenate([first, second_half], axis=0)
    part, gain_sum, shift_sum = norm_back(upstream, normed, inverse, gains[2:3, :])
    made = cot[...].astype(F32) + part
    residual_grad[...] = made
    norm_sums[0:1, :] = gain_sum
    norm_sums[1:2, :] = shift_sum
    branch[block_rows(near.me), :] = made.astype(BF)
    gather = Gather(near, branch, ga_send, ga_recv)
    gather.start()
    for copy in out_copies:
        copy.wait()
    copies = []

    def use(key):
        rows = chip_rows(near.chip[key])
        for s in range(2):
            attended_grad[rows, s * 128 : (s + 1) * 128] = dot(branch[rows, :], wo[s]).astype(BF)
        i = "oxzd".index(key)
        copies.extend(copy_all([(branch.at[rows], branch_out.at[rows])], o_sem.at[pl.ds(i, 1)]))

    gather.run(use)
    gather.finish()
    for copy in copies:
        copy.wait()


def back_call(grads, residual, cotangent, gains, wo, wg):
    return pl.pallas_call(
        back_kernel,
        out_shape=(shape((OWN, D), F32), shape((LEN, D), BF), shape((LEN, 256), BF), shape((8, D), F32)),
        in_specs=[IN_VMEM] * 4 + [ANYWHERE] * 9,
        out_specs=(IN_VMEM, ANYWHERE, IN_VMEM, IN_VMEM),
        scratch_shapes=[
            pltpu.VMEM((2, D, 128), BF),
            pltpu.VMEM((2, D, 2 * PAD), BF),
            pltpu.VMEM((LEN, D), BF),
            *Scatter.scratch(),
            DMA((Gather.COPIES,)),
            DMA((Gather.COPIES,)),
            DMA((32,)),
            DMA((4,)),
        ],
        compiler_params=params(3),
        cost_estimate=cost(12 * 10**9, 60 * 2**20),
        name="back",
    )(grads, residual, cotangent, gains, *wo, *wg)


def attend_back_kernel(
    query, keys, values, attended_grad, log_sum, cos, sin_up, sin_down, lowest,
    projected_grad, bias_sum, kt, key_acc, value_acc,
):
    for s in range(2):
        kt[s] = keys[:, s * 128 : (s + 1) * 128].astype(F32).T.astype(BF)
    key_acc[...] = jnp.zeros_like(key_acc)
    value_acc[...] = jnp.zeros_like(value_acc)
    for block in range(LEN // QB):
        start, stop = window(block)
        rows = slice(block * QB, (block + 1) * QB)
        bias_t = mask_bias(lowest[:, rows], start, stop, block)
        for s in range(2):
            lanes = slice(s * 128, (s + 1) * 128)
            q, k, v = query[rows, lanes], keys[start:stop, lanes], values[start:stop, lanes]
            grad, k_t = attended_grad[rows, lanes], kt[s, :, start:stop]
            halves, key_sum, value_sum = [], None, None
            for head_id in range(2):
                mine = head_lanes(QB, head_id)
                q_one = jnp.where(mine, q, jnp.zeros_like(q))
                g_one = jnp.where(mine, grad, jnp.zeros_like(grad))
                index = s * 2 + head_id
                probs = jnp.exp(dot_nt(k, q_one) + bias_t - log_sum[index : index + 1, rows])
                prob_grad = dot_nt(v, g_one)
                inner = jnp.sum(probs * prob_grad, axis=0, keepdims=True)
                score_grad = (probs * (prob_grad - inner)).astype(BF)
                made = dot(k_t, score_grad)
                halves.append(made[head_id * HD : (head_id + 1) * HD])
                key_part = dot(score_grad, q_one)
                value_part = dot(probs.astype(BF), g_one)
                key_sum = key_part if key_sum is None else key_sum + key_part
                value_sum = value_part if value_sum is None else value_sum + value_part
            query_grad = jnp.concatenate(halves, axis=0).T * HD ** (-0.5)
            query_grad = roll_rotate(query_grad, cos[rows, :], -sin_up[rows, :], -sin_down[rows, :])
            projected_grad[rows, s * 384 : s * 384 + 128] = query_grad.astype(BF)
            key_acc[s, start:stop, :] += key_sum
            value_acc[s, start:stop, :] += value_sum
    for s in range(2):
        made = roll_rotate(key_acc[s], cos[...], -sin_up[...], -sin_down[...])
        projected_grad[:, s * 384 + 128 : s * 384 + 256] = made.astype(BF)
        projected_grad[:, s * 384 + 256 : s * 384 + 384] = value_acc[s].astype(BF)
    bias_sum[...] = jnp.broadcast_to(
        jnp.sum(projected_grad[...].astype(F32), axis=0, keepdims=True), bias_sum.shape
    )


def attend_back_call(query, keys, values, attended_grad, log_sum, cos, sin_up, sin_down, lowest):
    return pl.pallas_call(
        attend_back_kernel,
        out_shape=(shape((LEN, 768), BF), shape((8, 768), F32)),
        in_specs=[IN_VMEM] * 9,
        out_specs=(IN_VMEM, IN_VMEM),
        scratch_shapes=[
            pltpu.VMEM((2, 128, LEN), BF),
            pltpu.VMEM((2, LEN, 128), F32),
            pltpu.VMEM((2, LEN, 128), F32),
        ],
        compiler_params=params(),
        cost_estimate=cost(15 * 10**9, 12 * 2**20),
        name="attend_back",
    )(query, keys, values, attended_grad, log_sum, cos, sin_up, sin_down, lowest)


def close_kernel(projected_grad, hidden, tok, residual, residual_grad, gains, head, *rest):
    wd_in, (mixed, grad_tokens, norm_sums) = rest[0:5], rest[5:8]
    wv, wd = rest[8:10]
    a_refs, b_refs, (w_sem,) = rest[10:20], rest[20:30], rest[30:31]
    near = Near()
    pairs = []
    for k in range(4):
        for h in range(2):
            for s in range(2):
                row = pl.ds(pl.multiple_of(dp_of(k, h) * 256, 256), 256)
                pairs.append((head.at[k * 4 + h * 2 + s, pl.ds(0, 256)], wv.at[s, row]))
    head_copies = copy_all(pairs, w_sem.at[pl.ds(0, 16)])
    down_copies = copy_all(weight_pairs(wd_in, wd), w_sem.at[pl.ds(16, 16)])
    greet([near.dev["x"], near.dev["z"], near.dev["s"]])
    one, two = Scatter(near, a_refs), Scatter(near, b_refs)

    def make_one(chip):
        rows = chip_rows(chip)
        one.part[...] = dot_nt(projected_grad[rows, :384], wv[0]) + dot_nt(projected_grad[rows, 384:], wv[1])

    def make_two(chip):
        rows = chip_rows(chip)
        two.part[...] = dot_nt(hidden[rows, :PAD], wd[0]) + dot_nt(hidden[rows, PAD:], wd[1])

    for copy in head_copies:
        copy.wait()
    one.produce("d", make_one)
    one.produce("z", make_one)
    one.far()
    one.produce("x", make_one)
    one.z_direct()
    one.produce("o", make_one)
    one.x_direct()
    for copy in down_copies:
        copy.wait()
    two.produce("d", make_two)
    two.produce("z", make_two)
    one.relays()
    two.far()
    two.produce("x", make_two)
    two.z_direct()
    two.produce("o", make_two)
    two.x_direct()
    first, second = one.result()
    normed, inverse = layer_norm_parts(tok[...].astype(F32))
    part, gain_sum, shift_sum = norm_back(
        jnp.concatenate([first, second], axis=0), normed, inverse, gains[0:1, :]
    )
    grad_tokens[...] = residual_grad[...] + part
    norm_sums[0:1, :] = gain_sum
    norm_sums[1:2, :] = shift_sum
    two.relays()
    first, second = two.result()
    mixed[:HALF, :] = residual[:HALF, :] + first
    mixed[HALF:, :] = residual[HALF:, :] + second


def close_call(projected_grad, hidden, tokens, residual, residual_grad, gains, head, wd):
    return pl.pallas_call(
        close_kernel,
        out_shape=(shape((OWN, D), F32), shape((OWN, D), F32), shape((8, D), F32)),
        in_specs=[IN_VMEM] * 6 + [ANYWHERE] * 6,
        out_specs=(IN_VMEM,) * 3,
        scratch_shapes=[
            pltpu.VMEM((2, D, 384), BF),
            pltpu.VMEM((2, D, PAD), BF),
            *Scatter.scratch(),
            *Scatter.scratch(),
            DMA((32,)),
        ],
        compiler_params=params(4),
        cost_estimate=cost(10 * 10**9, 60 * 2**20),
        name="close",
    )(projected_grad, hidden, tokens, residual, residual_grad, gains, head, *wd)


def over_y(v, k):
    pairs = [(h * 4 + y, h * 4 + (y + k) % 4) for h in range(2) for y in range(4)]
    return lax.ppermute(v, "dp", pairs)


def over_x(v):
    return lax.ppermute(v, "dp", [(d, (d + 4) % 8) for d in range(8)])


def over_z(v):
    return lax.ppermute(v, "tensor", [(t, (3 - t // 4) * 4 + t % 4) for t in range(16)])


def y_last(base):
    return (base, over_y(base, 1), over_y(base, 2), over_y(base, 3))


def z_last(base):
    rings = y_last(base)
    return rings + (over_z(jnp.concatenate(rings, axis=0)),)


def around(v, axis, k):
    y = lax.axis_index("dp") % 4
    return lax.dynamic_index_in_dim(v, (y + k) % 4, axis, keepdims=False)


def sum_y(v):
    total = around(v, 1, 0).astype(F32)
    for k in (1, 2, 3):
        total = total + over_y(around(v, 1, k), k).astype(F32)
    return total


def sum_x(v):
    h = lax.axis_index("dp") // 4
    theirs = lax.dynamic_index_in_dim(v, 1 - h, 0, keepdims=False).astype(BF)
    mine = lax.dynamic_index_in_dim(v, h, 0, keepdims=False).astype(F32)
    return mine + over_x(theirs).astype(F32)


def tables(segments):
    z = lax.axis_index("tensor") // 4
    seg = lax.dynamic_index_in_dim(segments, z // 2, 0, keepdims=True)
    index = jnp.arange(LEN, dtype=jnp.int32)[None]
    before = jnp.concatenate([jnp.full((1, 1), -1, jnp.int32), seg[:, :-1]], axis=1)
    starts = lax.cummax(jnp.where(seg != before, index, 0), axis=1)
    lowest = jnp.maximum(starts, index - (WINDOW - 1))
    half_rot = ROT // 2
    inverse = jnp.exp(jnp.arange(half_rot, dtype=F32) * (-2.0 * math.log(BASE_FREQ) / ROT))
    angles = (index - starts).astype(F32) * inverse[:, None]
    cosine, sine = lax.optimization_barrier((jnp.cos(angles).T, jnp.sin(angles).T))
    none = jnp.zeros((LEN, half_rot), F32)
    rest = jnp.zeros((LEN, HD - ROT), F32)
    cos = jnp.concatenate([cosine, cosine, rest + 1.0] * 2, axis=1)
    sin_up = jnp.concatenate([-sine, none, rest] * 2, axis=1)
    sin_down = jnp.concatenate([none, sine, rest] * 2, axis=1)
    return cos, sin_up, sin_down, lowest


def wide(w):
    return jnp.pad(w, [(0, 0)] * (w.ndim - 1) + [(0, PAD - UNITS)])


def per_device(
    tokens,
    segments,
    first_gain,
    first_shift,
    heads_weight,
    heads_bias,
    output_weight,
    second_gain,
    second_shift,
    gate_up_weight,
    down_weight,
    cotangent,
):
    dp = lax.axis_index("dp")
    small = jnp.stack([first_gain, first_shift, second_gain, second_shift]).astype(BF).astype(F32)
    small = jnp.pad(small, [(0, 4), (0, 0)])
    here = (jnp.arange(8) == dp).astype(BF)[None, None, :, None]
    bias = (heads_bias.astype(BF)[:, :, None, :] * here).reshape(1, 384)
    head = jnp.concatenate([heads_weight.astype(BF).reshape(256, 384), jnp.pad(bias, [(0, 15), (0, 0)])], axis=0)

    out_t = output_weight.T.astype(BF)
    down_t = wide(down_weight.T.astype(BF))
    gate_up = wide(gate_up_weight.astype(BF)).reshape(256, 2 * PAD)
    gate_two = jnp.stack([gate_up, over_z(gate_up)])
    gate_four = jnp.concatenate([gate_two, over_x(gate_two)], axis=0)
    down_two = jnp.stack([down_t, over_x(down_t)])
    out_two = jnp.stack([out_t, over_x(out_t)])

    cos, sin_up, sin_down, lowest = tables(segments)
    first_all, cot_all, gains, head_all = open_call(tokens, cotangent, small, head)
    gate_four, down_two, out_two, first_all = lax.optimization_barrier((gate_four, down_two, out_two, first_all))
    wo = z_last(out_two)
    wg = y_last(gate_four)
    wd = z_last(down_two)

    query, keys, values, attended, log_sum = attend_call(first_all, head_all, cos, sin_up, sin_down, lowest)
    residual, second_all, hidden, grads = middle_call(attended, tokens, gains, cot_all, wo, wg, wd)

    grad_gate = dot_tn(second_all, grads).astype(BF).reshape(2, 4, 256, 4 * PAD)
    grad_down = dot_tn(cot_all, hidden).astype(BF).reshape(2, 4, 256, 2 * PAD)
    grad_gate = sum_y(grad_gate)
    grad_gate = grad_gate[..., : 2 * PAD] + over_z(grad_gate[..., 2 * PAD :].astype(BF)).astype(F32)
    grad_gate = sum_x(grad_gate)
    grad_down = grad_down[..., :PAD].astype(F32) + over_z(grad_down[..., PAD:]).astype(F32)
    grad_down = sum_x(sum_y(grad_down.astype(BF)))

    residual_grad, branch_all, attended_grad, sums_two = back_call(grads, residual, cotangent, gains, wo, wg)
    grad_out = dot_tn(branch_all, attended).astype(BF)
    projected_grad, bias_sum = attend_back_call(
        query, keys, values, attended_grad, log_sum, cos, sin_up, sin_down, lowest
    )
    grad_heads = dot_tn(first_all, projected_grad).astype(BF)
    bias_rows = jnp.pad(bias_sum[:1].astype(BF), [(0, 15), (0, 0)])
    parts = []
    for s in range(2):
        rows = jnp.concatenate(
            [grad_heads[:, s * 384 : (s + 1) * 384], grad_out[:, s * 128 : (s + 1) * 128]], axis=1
        ).reshape(2, 4, 256, 512)
        tail = jnp.pad(bias_rows[:, s * 384 : (s + 1) * 384], [(0, 0), (0, 128)])
        tail = jnp.broadcast_to(tail, (2, 4, 16, 512))
        parts.append(jnp.concatenate([rows, tail], axis=2))
    last = sum_y(jnp.concatenate(parts, axis=3))
    last = last[..., :512] + over_z(last[..., 512:].astype(BF)).astype(F32)
    last = sum_x(last)

    mixed, grad_tokens, sums_one = close_call(
        projected_grad, hidden, tokens, residual, residual_grad, gains, head_all, wd
    )
    norms = jnp.concatenate([sums_one[:2], sums_two[:2]], axis=0).reshape(64, 128)
    norms = lax.psum(norms, ("dp", "tensor")).reshape(4, D)
    place = dp * 256 + lax.axis_index("tensor") * 16
    norms = lax.dynamic_slice_in_dim(norms, place, 16, 1)

    grad_heads = last[:256, :384].reshape(256, 3, 128)
    grad_bias = lax.dynamic_slice_in_dim(last[256, :384].reshape(3, 2, HD), dp * 8, 8, 2)
    grad_output = last[:256, 384:].T
    grad_gate_up = grad_gate.reshape(256, 2, PAD)[..., :UNITS]
    grad_down = grad_down[:, :UNITS].T
    return (
        mixed,
        grad_tokens,
        norms[0],
        norms[1],
        grad_heads,
        grad_bias,
        grad_output,
        norms[2],
        norms[3],
        grad_gate_up,
        grad_down,
    )


ALL = ("dp", "tensor")


def solution(mesh):
    return jax.shard_map(
        per_device,
        mesh=mesh,
        in_specs=(
            P(ALL, None),
            P("dp", None),
            P("dp"),
            P("dp"),
            P("dp", None, "tensor"),
            P(None, "tensor", "dp"),
            P("tensor", "dp"),
            P("dp"),
            P("dp"),
            P("dp", None, "tensor"),
            P("tensor", "dp"),
            P(ALL, None),
        ),
        out_specs=(
            P(ALL, None),
            P(ALL, None),
            P(ALL),
            P(ALL),
            P("dp", None, "tensor"),
            P(None, "tensor", "dp"),
            P("tensor", "dp"),
            P(ALL),
            P(ALL),
            P("dp", None, "tensor"),
            P("tensor", "dp"),
        ),
        check_vma=False,
    )
```

```python
import functools
import math

import jax
import jax.numpy as jnp
from jax import lax
from jax.experimental import pallas as pl
from jax.experimental.pallas import tpu as pltpu
from jax.sharding import PartitionSpec as P

D = 2048
HD = 64
ROT = 16
WINDOW = 512
LEN = 1024
OWN = 128
HALF = OWN // 2
CHIP = 2 * OWN
UNITS = 352
PAD = 384
QB = 256

NORM_EPS = 1e-05
BASE_FREQ = 10000.0
FAR_NEGATIVE = -1e30
BF = jnp.bfloat16
F32 = jnp.float32
MESH = pl.DeviceIdType.MESH
VMEM_LIMIT = 60 * 2**20
DMA = pltpu.SemaphoreType.DMA


def spot(z, x, c):
    return (z % 2) * 4 + x * 2 + c


class Near:
    def __init__(self):
        t = lax.axis_index("tensor")
        z, x, c = t // 4, (t // 2) % 2, t % 2
        oz = (z // 2) * 2 + (z + 1) % 2
        ox, oc = 1 - x, 1 - c
        self.c, self.oc = c, oc
        self.me = spot(z, x, c)
        self.dev = {
            "x": {"tensor": z * 4 + ox * 2 + c},
            "z": {"tensor": oz * 4 + x * 2 + c},
            "s": {"tensor": z * 4 + x * 2 + oc},
        }
        self.same = {"o": spot(z, x, c), "x": spot(z, ox, c), "z": spot(oz, x, c), "d": spot(oz, ox, c)}
        self.other = {
            "o": spot(z, x, oc),
            "x": spot(z, ox, oc),
            "z": spot(oz, x, oc),
            "d": spot(oz, ox, oc),
        }
        self.chip = {"o": (z % 2) * 2 + x, "x": (z % 2) * 2 + ox, "z": (oz % 2) * 2 + x, "d": (oz % 2) * 2 + ox}


def remote(src, dst, send, recv, device):
    return pltpu.make_async_remote_copy(
        src_ref=src, dst_ref=dst, send_sem=send, recv_sem=recv, device_id=device, device_id_type=MESH
    )


def greet(devices):
    barrier = pltpu.get_barrier_semaphore()
    for device in devices:
        pl.semaphore_signal(barrier, inc=1, device_id=device, device_id_type=MESH)
    pl.semaphore_wait(barrier, len(devices))


def block_rows(block, half=None):
    if half is None:
        return pl.ds(pl.multiple_of(block * OWN, OWN), OWN)
    return pl.ds(pl.multiple_of(block * OWN + half * HALF, HALF), HALF)


def chip_rows(chip):
    return pl.ds(pl.multiple_of(chip * CHIP, CHIP), CHIP)


class Gather:
    COPIES = 13

    def __init__(self, near, buf, send, recv):
        self.near, self.buf, self.send, self.recv = near, buf, send, recv
        self.sent = []

    def copy(self, index, block, half, to):
        view = self.buf.at[block_rows(block, half)]
        return remote(view, view, self.send.at[index], self.recv.at[index], self.near.dev[to])

    def go(self, index, block, half, to):
        copy = self.copy(index, block, half, to)
        copy.start()
        self.sent.append(copy)

    def take(self, index, block, half, to="s"):
        self.copy(index, block, half, to).wait_recv()

    def start(self):
        me = self.near.me
        self.go(0, me, 0, "z")
        self.go(1, me, 1, "x")
        self.go(4, me, None, "s")
        self.go(2, me, 0, "x")
        self.go(3, me, 1, "z")

    def first(self):
        same = self.near.same
        self.take(0, same["z"], 0)
        self.go(5, same["z"], 0, "x")
        self.go(7, same["z"], 0, "s")
        self.take(1, same["x"], 1)
        self.go(6, same["x"], 1, "z")
        self.go(8, same["x"], 1, "s")

    def second(self):
        same = self.near.same
        self.take(2, same["x"], 0)
        self.go(9, same["x"], 0, "s")
        self.take(3, same["z"], 1)
        self.go(10, same["z"], 1, "s")

    def third(self):
        same = self.near.same
        self.take(5, same["d"], 0)
        self.go(11, same["d"], 0, "s")
        self.take(6, same["d"], 1)
        self.go(12, same["d"], 1, "s")

    def own_chip(self):
        self.take(4, self.near.other["o"], None)

    def x_chip(self):
        self.take(8, self.near.other["x"], 1)
        self.take(9, self.near.other["x"], 0)

    def z_chip(self):
        self.take(7, self.near.other["z"], 0)
        self.take(10, self.near.other["z"], 1)

    def d_chip(self):
        self.take(11, self.near.other["d"], 0)
        self.take(12, self.near.other["d"], 1)

    def finish(self):
        for copy in self.sent:
            copy.wait_send()

    def run(self, use):
        self.own_chip()
        use("o")
        self.first()
        self.second()
        self.x_chip()
        use("x")
        self.third()
        self.z_chip()
        use("z")
        self.d_chip()
        use("d")


class Scatter:
    COPIES = 10

    @staticmethod
    def scratch(width=D):
        return [
            pltpu.VMEM((CHIP, width), F32),
            pltpu.VMEM((4, OWN, width), F32),
            pltpu.VMEM((4, OWN, width), BF),
            pltpu.VMEM((4, OWN, width), BF),
            pltpu.VMEM((OWN, width), BF),
            pltpu.VMEM((4, HALF, width), BF),
            pltpu.VMEM((2, HALF, width), BF),
            pltpu.VMEM((4, HALF, width), BF),
            DMA((Scatter.COPIES,)),
            DMA((Scatter.COPIES,)),
        ]

    KEYS = ("d", "z", "x", "o")

    def __init__(self, near, refs):
        self.near = near
        (
            self.part,
            self.mine,
            self.core_out,
            self.core_in,
            self.far_out,
            self.out,
            self.through,
            self.last,
            self.send,
            self.recv,
        ) = refs
        self.sent = []

    def copy(self, index, src, dst, to):
        return remote(src, dst, self.send.at[index], self.recv.at[index], self.near.dev[to])

    def go(self, index, src, dst, to):
        copy = self.copy(index, src, dst, to)
        copy.start()
        self.sent.append(copy)

    def take(self, index, dst, to="s"):
        self.copy(index, dst, dst, to).wait_recv()

    def produce(self, key, make):
        i = self.KEYS.index(key)
        make(self.near.chip[key])
        self.core_out[i] = self.part[block_rows(self.near.oc), :].astype(BF)
        self.go(i, self.core_out.at[i], self.core_in.at[i], "s")
        self.mine[i] = self.part[block_rows(self.near.c), :]

    def join(self, key):
        i = self.KEYS.index(key)
        self.take(i, self.core_in.at[i])

    def summed(self, key, half):
        i = self.KEYS.index(key)
        rows = slice(half * HALF, (half + 1) * HALF)
        return self.mine[i, rows, :] + self.core_in[i, rows, :].astype(F32)

    def far(self):
        self.join("d")
        self.far_out[:HALF, :] = self.summed("d", 0).astype(BF)
        self.go(4, self.far_out.at[pl.ds(0, HALF)], self.through.at[0], "z")
        self.far_out[HALF:, :] = self.summed("d", 1).astype(BF)
        self.go(5, self.far_out.at[pl.ds(HALF, HALF)], self.through.at[1], "x")

    def z_direct(self):
        self.join("z")
        self.out[0] = self.summed("z", 0).astype(BF)
        self.go(6, self.out.at[0], self.last.at[0], "z")

    def x_direct(self):
        self.join("x")
        self.out[1] = self.summed("x", 1).astype(BF)
        self.go(7, self.out.at[1], self.last.at[1], "x")

    def relays(self):
        self.take(4, self.through.at[0])
        self.out[2] = (self.summed("x", 0) + self.through[0].astype(F32)).astype(BF)
        self.go(8, self.out.at[2], self.last.at[2], "x")
        self.take(5, self.through.at[1])
        self.out[3] = (self.summed("z", 1) + self.through[1].astype(F32)).astype(BF)
        self.go(9, self.out.at[3], self.last.at[3], "z")

    def result(self):
        self.join("o")
        for index in range(4):
            self.take(6 + index, self.last.at[index])
        first = self.summed("o", 0) + self.last[0].astype(F32) + self.last[2].astype(F32)
        second = self.summed("o", 1) + self.last[1].astype(F32) + self.last[3].astype(F32)
        for copy in self.sent:
            copy.wait_send()
        self.sent = []
        return first, second

    def run(self, make):
        self.produce("d", make)
        self.produce("z", make)
        self.far()
        self.produce("x", make)
        self.z_direct()
        self.produce("o", make)
        self.x_direct()
        self.relays()
        return self.result()


def dot(left, right):
    return jnp.dot(left, right, preferred_element_type=F32)


def dot_nt(left, right):
    return lax.dot_general(left, right, (((1,), (1,)), ((), ())), preferred_element_type=F32)


def dot_tn(left, right):
    return lax.dot_general(left, right, (((0,), (0,)), ((), ())), preferred_element_type=F32)


def layer_norm_parts(values):
    centre = values - jnp.mean(values, axis=-1, keepdims=True)
    inverse = lax.rsqrt(jnp.mean(centre * centre, axis=-1, keepdims=True) + NORM_EPS)
    return (centre * inverse, inverse)


def norm_back(upstream, normed, inverse, gain):
    scaled = upstream * gain
    inner = (
        scaled
        - jnp.mean(scaled, axis=-1, keepdims=True)
        - normed * jnp.mean(scaled * normed, axis=-1, keepdims=True)
    )
    return (
        inner * inverse,
        jnp.sum(upstream * normed, axis=0, keepdims=True),
        jnp.sum(upstream, axis=0, keepdims=True),
    )


def params(collective=None):
    if collective is None:
        return pltpu.CompilerParams(vmem_limit_bytes=VMEM_LIMIT)
    return pltpu.CompilerParams(
        collective_id=collective, has_side_effects=True, vmem_limit_bytes=VMEM_LIMIT
    )


def cost(flops, moved):
    return pl.CostEstimate(flops=flops, bytes_accessed=moved, transcendentals=0)


IN_VMEM = pl.BlockSpec(memory_space=pltpu.VMEM)
ANYWHERE = pl.BlockSpec(memory_space=pl.ANY)


def shape(dims, dtype):
    return jax.ShapeDtypeStruct(dims, dtype)


def copy_all(pairs, sems):
    copies = [pltpu.make_async_copy(src, dst, sems.at[i]) for i, (src, dst) in enumerate(pairs)]
    for copy in copies:
        copy.start()
    return copies


class Far:
    def __init__(self):
        t, dp = lax.axis_index("tensor"), lax.axis_index("dp")
        self.h, self.y = dp // 4, dp % 4
        self.over = {"dp": (1 - self.h) * 4 + self.y}
        self.partner = {"tensor": (3 - t // 4) * 4 + t % 4}
        self.ring = {k: {"dp": self.h * 4 + (self.y + k) % 4} for k in (1, 2, 3)}

    def dp(self, k, h):
        return ((self.h + h) % 2) * 4 + (self.y - k + 4) % 4

    def rows(self, k, h):
        return pl.ds(pl.multiple_of(self.dp(k, h) * 256, 256), 256)

    def ahead(self, k, h):
        return pl.ds(pl.multiple_of((h * 4 + (self.y + k) % 4) * 256, 256), 256)


class Copies:
    def __init__(self, send, recv):
        self.send, self.recv, self.sent = send, recv, []

    def go(self, index, src, dst, device):
        copy = remote(src, dst, self.send.at[index], self.recv.at[index], device)
        copy.start()
        self.sent.append(copy)

    def take(self, index, dst, device):
        remote(dst, dst, self.send.at[index], self.recv.at[index], device).wait_recv()

    def finish(self):
        for copy in self.sent:
            copy.wait_send()
        self.sent = []


class Ring:
    def __init__(self, far, n, place, send, recv):
        self.far, self.n, self.place = far, n, place
        self.copies = Copies(send, recv)

    def start(self, j, src=None):
        own = self.place(0, j)
        src = own if src is None else src
        self.copies.go(j, src, own, self.far.ring[1])
        self.copies.go(self.n + j, src, own, self.far.ring[3])

    def relay(self, j):
        if j < self.n // 2:
            view = self.place(1, j)
            self.copies.take(j, view, self.far.ring[1])
            self.copies.go(2 * self.n + j, view, view, self.far.ring[1])
        else:
            view = self.place(3, j)
            self.copies.take(self.n + j, view, self.far.ring[3])
            self.copies.go(2 * self.n + j, view, view, self.far.ring[3])

    def rest(self, j):
        if j < self.n // 2:
            self.copies.take(self.n + j, self.place(3, j), self.far.ring[3])
        else:
            self.copies.take(j, self.place(1, j), self.far.ring[1])
        self.copies.take(2 * self.n + j, self.place(2, j), self.far.ring[1])

    def finish(self):
        for j in range(self.n):
            self.rest(j)
        self.copies.finish()


class SumY:
    COPIES = 15

    def __init__(self, far, send, recv):
        self.far, self.copies = far, Copies(send, recv)

    def start_y(self, src, lanes, own, land, own_sems):
        self.own, self.land = own, land
        self.local = []
        for k in (1, 2, 3):
            for h in range(2):
                for s in range(2):
                    j = h * 2 + s
                    self.copies.go(
                        (k - 1) * 4 + j, src.at[self.far.ahead(k, h), lanes(s)], land.at[k - 1, j], self.far.ring[k]
                    )
        for h in range(2):
            for s in range(2):
                j = h * 2 + s
                copy = pltpu.make_async_copy(src.at[self.far.ahead(0, h), lanes(s)], own.at[j], own_sems.at[j])
                copy.start()
                self.local.append(copy)

    def add_y(self, out):
        for copy in self.local:
            copy.wait()
        for j in range(4):
            total = self.own[j].astype(F32)
            for k in (1, 2, 3):
                self.copies.take((k - 1) * 4 + j, self.land.at[k - 1, j], self.far.ring[k])
                total = total + self.land[k - 1, j].astype(F32)
            out[j] = total.astype(BF)

    def start_z(self, sums, land):
        self.z_land = land
        for h in range(2):
            self.copies.go(12 + h, sums.at[h * 2 + 1], land.at[h], self.far.partner)

    def add_z(self, sums, out):
        for h in range(2):
            self.copies.take(12 + h, self.z_land.at[h], self.far.partner)
            out[h] = (sums[h * 2].astype(F32) + self.z_land[h].astype(F32)).astype(BF)


class SumZ:
    COPIES = 8

    def __init__(self, far, send, recv):
        self.far, self.copies = far, Copies(send, recv)

    def start_z(self, src, lanes, own, land, own_sem):
        self.own, self.land = own, land
        self.copies.go(0, src.at[:, lanes(1)], land, self.far.partner)
        self.local = pltpu.make_async_copy(src.at[:, lanes(0)], own, own_sem)
        self.local.start()

    def add_z(self, out):
        self.local.wait()
        self.copies.take(0, self.land, self.far.partner)
        out[...] = (self.own[...].astype(F32) + self.land[...].astype(F32)).astype(BF)

    def start_y(self, sums, land):
        self.y_land = land
        for k in (1, 2, 3):
            for h in range(2):
                self.copies.go(
                    1 + (k - 1) * 2 + h, sums.at[self.far.ahead(k, h)], land.at[k - 1, h], self.far.ring[k]
                )

    def add_y(self, sums, out):
        for h in range(2):
            total = sums[self.far.ahead(0, h), :].astype(F32)
            for k in (1, 2, 3):
                self.copies.take(1 + (k - 1) * 2 + h, self.y_land.at[k - 1, h], self.far.ring[k])
                total = total + self.y_land[k - 1, h].astype(F32)
            out[h] = total.astype(BF)


class SumX:
    def __init__(self, far, send, recv):
        self.far, self.copies = far, Copies(send, recv)

    def start(self, sums, land):
        self.land = land
        self.copies.go(0, sums.at[1 - self.far.h], land, self.far.over)

    def add(self, sums, out):
        self.copies.take(0, self.land, self.far.over)
        out[...] = sums[self.far.h].astype(F32) + self.land[...].astype(F32)


def rotary_tables(starts, cos_out, up_out, down_out):
    index = lax.broadcasted_iota(jnp.int32, (8, LEN), 1)
    power = lax.broadcasted_iota(jnp.int32, (8, LEN), 0).astype(F32)
    angles = (index - starts).astype(F32) * jnp.exp(power * (-2.0 * math.log(BASE_FREQ) / ROT))
    cosine, sine = jnp.cos(angles), jnp.sin(angles)
    none, rest = jnp.zeros((8, LEN), F32), jnp.zeros((HD - ROT, LEN), F32)
    cos_out[...] = jnp.concatenate([cosine, cosine, rest + 1.0] * 2, axis=0).T
    up_out[...] = jnp.concatenate([-sine, none, rest] * 2, axis=0).T
    down_out[...] = jnp.concatenate([none, sine, rest] * 2, axis=0).T


def document_starts(seg):
    index = lax.broadcasted_iota(jnp.int32, (8, LEN), 1)
    new = (index == 0) | (pltpu.roll(seg, 1, 1) != seg)
    starts = jnp.where(new, index, 0)
    step = 1
    while step < LEN:
        starts = jnp.maximum(starts, jnp.where(index >= step, pltpu.roll(starts, step, 1), 0))
        step *= 2
    return starts


def open_kernel(
    tok, seg, small, head, out_t, down_t, gate,
    first_out, gains_out, bias_out, head_out, wo_out, down_out, gate_out, cos_out, up_out, sdown_out, lowest_out,
    fa, gbuf, gbuf_two, ga_send, ga_recv, sm_send, sm_recv, hd_send, hd_recv, hr_send, hr_recv,
    oo_send, oo_recv, or_send, or_recv, dn_send, dn_recv, dr_send, dr_recv, gt_send, gt_recv,
    sr_send, sr_recv, out_sem,
):
    near, far = Near(), Far()
    greet([near.dev["x"], near.dev["z"], near.dev["s"], far.over, far.partner, far.ring[1], far.ring[3]])
    locals_ = []

    def keep(index, src, dst):
        copy = pltpu.make_async_copy(src, dst, out_sem.at[index])
        copy.start()
        locals_.append(copy)

    smalls = Copies(sm_send, sm_recv)
    small_ring = Ring(far, 2, lambda k, j: gbuf.at[far.dp(k, j)], sr_send, sr_recv)
    smalls.go(0, small, gbuf.at[far.dp(0, 0)], far.over)
    small_ring.start(0, small)

    def head_at(k, j):
        return head_out.at[j % 2, far.rows(k, j // 2)]

    heads = Copies(hd_send, hd_recv)
    head_ring = Ring(far, 4, head_at, hr_send, hr_recv)
    heads.go(0, head, head_at(0, 0), far.over)
    heads.go(1, head, head_at(0, 1), far.partner)
    head_ring.start(0, head)

    outs, downs, gates = Copies(oo_send, oo_recv), Copies(dn_send, dn_recv), Copies(gt_send, gt_recv)
    out_ring = Ring(far, 2, lambda k, j: wo_out.at[0, far.rows(k, j)], or_send, or_recv)
    down_ring = Ring(far, 2, lambda k, j: down_out.at[far.rows(k, j)], dr_send, dr_recv)
    outs.go(0, out_t, wo_out.at[0, far.rows(0, 0)], far.over)
    downs.go(0, down_t, down_out.at[far.rows(0, 0)], far.over)

    gbuf[far.dp(0, 0)] = small[...]
    keep(0, head, head_at(0, 0))
    keep(1, out_t, wo_out.at[0, far.rows(0, 0)])
    keep(2, down_t, down_out.at[far.rows(0, 0)])
    keep(3, gate, gate_out.at[0])

    normed, _ = layer_norm_parts(tok[...].astype(F32))
    smalls.take(0, gbuf.at[far.dp(0, 1)], far.over)
    small_ring.start(1)
    heads.take(0, head_at(0, 2), far.over)
    heads.go(2, head_at(0, 2), head_at(0, 3), far.partner)
    head_ring.start(2)
    small_ring.relay(0)
    small_ring.relay(1)
    heads.take(1, head_at(0, 1), far.partner)
    head_ring.start(1)
    small_ring.finish()
    smalls.go(1, gbuf, gbuf_two, far.partner)
    for d in range(8):
        gains_out[:, d * 256 : (d + 1) * 256] = gbuf[d, :, :256]
    first = normed * gains_out[0:1, :] + gains_out[1:2, :]
    fa[block_rows(near.me), :] = first.astype(BF)
    firsts = Gather(near, fa, ga_send, ga_recv)
    firsts.start()
    heads.take(2, head_at(0, 3), far.partner)
    head_ring.start(3)

    gates.go(0, gate, gate_out.at[2], far.over)
    gates.go(1, gate, gate_out.at[1], far.partner)
    outs.take(0, wo_out.at[0, far.rows(0, 1)], far.over)
    out_ring.start(0, out_t)
    out_ring.start(1)
    downs.take(0, down_out.at[far.rows(0, 1)], far.over)
    down_ring.start(0, down_t)
    down_ring.start(1)

    starts = document_starts(jnp.broadcast_to(seg[pl.ds(lax.axis_index("tensor") // 8, 1), :], (8, LEN)))
    index = lax.broadcasted_iota(jnp.int32, (8, LEN), 1)
    lowest_out[...] = jnp.maximum(starts, index - (WINDOW - 1))

    head_ring.relay(0)
    head_ring.relay(2)
    firsts.first()
    firsts.second()
    rotary_tables(starts, cos_out, up_out, sdown_out)
    gates.take(0, gate_out.at[2], far.over)
    gates.go(2, gate_out.at[2], gate_out.at[3], far.partner)
    head_ring.relay(1)
    head_ring.relay(3)
    out_ring.relay(0)
    out_ring.relay(1)
    firsts.third()
    down_ring.relay(0)
    down_ring.relay(1)
    firsts.own_chip()
    keep(4, fa.at[chip_rows(near.chip["o"])], first_out.at[chip_rows(near.chip["o"])])
    firsts.x_chip()
    keep(5, fa.at[chip_rows(near.chip["x"])], first_out.at[chip_rows(near.chip["x"])])
    firsts.z_chip()
    keep(6, fa.at[chip_rows(near.chip["z"])], first_out.at[chip_rows(near.chip["z"])])
    firsts.d_chip()
    keep(7, fa.at[chip_rows(near.chip["d"])], first_out.at[chip_rows(near.chip["d"])])
    smalls.take(1, gbuf_two, far.partner)
    bias_out[:, :384] = jnp.broadcast_to(jnp.sum(gbuf[:, 4, :], axis=0, keepdims=True), (8, 384))
    bias_out[:, 384:] = jnp.broadcast_to(jnp.sum(gbuf_two[:, 4, :], axis=0, keepdims=True), (8, 384))
    out_ring.finish()
    locals_[1].wait()
    outs.go(1, wo_out.at[0], wo_out.at[1], far.partner)
    head_ring.finish()
    down_ring.finish()
    gates.take(1, gate_out.at[1], far.partner)
    gates.take(2, gate_out.at[3], far.partner)
    outs.take(1, wo_out.at[1], far.partner)
    for group in (smalls, heads, outs, downs, gates):
        group.finish()
    firsts.finish()
    for i, copy in enumerate(locals_):
        if i != 1:
            copy.wait()


def sems(*counts):
    return [DMA((n,)) for n in counts for _ in range(2)]


def open_call(tokens, segments, small, head, out_t, down_t, gate):
    return pl.pallas_call(
        open_kernel,
        out_shape=(
            shape((LEN, D), BF),
            shape((8, D), F32),
            shape((8, 768), F32),
            shape((2, D, 384), BF),
            shape((2, D, 128), BF),
            shape((D, PAD), BF),
            shape((4, 256, 2 * PAD), BF),
            shape((LEN, 128), F32),
            shape((LEN, 128), F32),
            shape((LEN, 128), F32),
            shape((8, LEN), jnp.int32),
        ),
        in_specs=[IN_VMEM] * 7,
        out_specs=(ANYWHERE, IN_VMEM, IN_VMEM) + (ANYWHERE,) * 4 + (IN_VMEM,) * 4,
        scratch_shapes=[
            pltpu.VMEM((LEN, D), BF),
            pltpu.VMEM((8, 8, 384), F32),
            pltpu.VMEM((8, 8, 384), F32),
            *sems(Gather.COPIES, 2, 3, 12, 2, 6, 1, 6, 3, 6),
            DMA((8,)),
        ],
        compiler_params=params(1),
        cost_estimate=cost(10**9, 60 * 2**20),
        name="open",
    )(tokens, segments, small, head, out_t, down_t, gate)


def roll_rotate(values, cos, sin_up, sin_down):
    return (
        values * cos + pltpu.roll(values, 128 - ROT // 2, 1) * sin_up + pltpu.roll(values, ROT // 2, 1) * sin_down
    )


def window(block):
    start = max(0, block * QB - WINDOW)
    return start, (block + 1) * QB


def mask_bias(lowest, start, stop, block):
    keys = lax.broadcasted_iota(jnp.int32, (stop - start, QB), 0) + start
    queries = lax.broadcasted_iota(jnp.int32, (stop - start, QB), 1) + block * QB
    return jnp.where((keys <= queries) & (keys >= lowest), 0.0, FAR_NEGATIVE)


def head_lanes(rows, head):
    lanes = lax.broadcasted_iota(jnp.int32, (rows, 128), 1)
    return (lanes >= HD) if head else (lanes < HD)


def attend_kernel(
    first, head, bias, cos, sin_up, sin_down, lowest, cot, gate_base, down_half,
    query, keys, values, attended, log_sum, cot_out, gate_half, down_two,
    wv, vt, ca, gc_send, gc_recv, gr_send, gr_recv, dz_send, dz_recv, w_sem, out_sem,
):
    near, far = Near(), Far()
    load = copy_all([(head, wv)], w_sem)
    greet([near.dev["x"], near.dev["z"], near.dev["s"], far.partner, far.ring[1], far.ring[3]])
    gates = Ring(far, 4, lambda k, j: gate_half.at[j % 2, far.rows(k, j // 2)], gr_send, gr_recv)
    for j in range(4):
        gates.start(j, gate_base.at[j, :, pl.ds(0, PAD)])
    ca[block_rows(near.me), :] = cot[...]
    cots = Gather(near, ca, gc_send, gc_recv)
    cots.start()
    downs = Copies(dz_send, dz_recv)
    downs.go(0, down_half.at[pl.ds(0, LEN)], down_two, far.partner)
    load[0].wait()

    def project(step):
        rows = slice(step * CHIP, (step + 1) * CHIP)
        c, up, down = cos[rows, :], sin_up[rows, :], sin_down[rows, :]
        for s in range(2):
            lanes = slice(s * 128, (s + 1) * 128)
            made = dot(first[rows, :], wv[s]) + bias[0:1, s * 384 : (s + 1) * 384]
            query[rows, lanes] = (roll_rotate(made[:, :128], c, up, down) * HD ** (-0.5)).astype(BF)
            keys[rows, lanes] = roll_rotate(made[:, 128:256], c, up, down).astype(BF)
            values[rows, lanes] = made[:, 256:].astype(BF)
            vt[s, :, rows] = made[:, 256:].T.astype(BF)

    def look(block):
        start, stop = window(block)
        rows = slice(block * QB, (block + 1) * QB)
        bias_t = mask_bias(lowest[0:1, rows], start, stop, block)
        for s in range(2):
            lanes = slice(s * 128, (s + 1) * 128)
            q, k = query[rows, lanes], keys[start:stop, lanes]
            v_t = vt[s, :, start:stop]
            halves = []
            for head_id in range(2):
                q_one = jnp.where(head_lanes(QB, head_id), q, jnp.zeros_like(q))
                scores = dot_nt(k, q_one) + bias_t
                top = jnp.max(scores, axis=0, keepdims=True)
                weights = jnp.exp(scores - top)
                total = jnp.sum(weights, axis=0, keepdims=True)
                made = dot(v_t, weights.astype(BF))
                halves.append(made[head_id * HD : (head_id + 1) * HD] * (1.0 / total))
                log_sum[s * 2 + head_id : s * 2 + head_id + 1, rows] = top + jnp.log(total)
            attended[rows, lanes] = jnp.concatenate(halves, axis=0).T.astype(BF)

    for step in range(4):
        project(step)
    cots.first()
    gates.relay(0)
    look(0)
    cots.second()
    gates.relay(1)
    look(1)
    gates.relay(2)
    look(2)
    cots.third()
    gates.relay(3)
    look(3)
    copies = []
    for i, (key, done) in enumerate(
        (("o", cots.own_chip), ("x", cots.x_chip), ("z", cots.z_chip), ("d", cots.d_chip))
    ):
        done()
        rows = chip_rows(near.chip[key])
        copies.extend(copy_all([(ca.at[rows], cot_out.at[rows])], out_sem.at[pl.ds(i, 1)]))
    downs.take(0, down_two, far.partner)
    downs.finish()
    gates.finish()
    cots.finish()
    for copy in copies:
        copy.wait()


def attend_call(first_all, head, bias, cos, sin_up, sin_down, lowest, cotangent, gate_base, down_half):
    narrow = shape((LEN, 256), BF)
    return pl.pallas_call(
        attend_kernel,
        out_shape=(
            narrow, narrow, narrow, narrow, shape((8, LEN), F32),
            shape((LEN, D), BF), shape((2, D, PAD), BF), shape((LEN, PAD), BF),
        ),
        in_specs=[IN_VMEM, ANYWHERE] + [IN_VMEM] * 6 + [ANYWHERE] * 2,
        out_specs=(IN_VMEM,) * 5 + (ANYWHERE,) * 3,
        scratch_shapes=[
            pltpu.VMEM((2, D, 384), BF),
            pltpu.VMEM((2, 128, LEN), BF),
            pltpu.VMEM((LEN, D), BF),
            *sems(Gather.COPIES, 12, 1),
            DMA((1,)),
            DMA((4,)),
        ],
        compiler_params=params(2),
        cost_estimate=cost(5 * 10**9, 12 * 2**20),
        name="attend",
    )(first_all, head, bias, cos, sin_up, sin_down, lowest, cotangent, gate_base, down_half)


def silu_parts(gate, up, grad):
    sig = 1.0 / (1.0 + jnp.exp(-gate))
    silu = gate * sig
    return silu * up, grad * up * sig * (1.0 + gate * (1.0 - sig)), grad * silu


def middle_kernel(
    attended, tok, gains, cot_all, wo_all, gate_base, gate_half, down_half, down_two,
    residual, second_out, hidden_out, grads_out, wg_out, wd_out,
    wo, wg, wd, cots, hg, second, hidden, grads, *rest,
):
    scatter_refs = rest[:10]
    ga_send, ga_recv, ur_send, ur_recv, dz_send, dz_recv, w_sem, o_sem = rest[10:]
    near, far = Near(), Far()
    lower, upper = pl.ds(0, LEN), pl.ds(LEN, LEN)
    out_copy = copy_all([(wo_all, wo)], w_sem.at[pl.ds(0, 1)])
    greet([near.dev["x"], near.dev["z"], near.dev["s"], far.partner, far.ring[1], far.ring[3]])
    up_lanes = pl.ds(PAD, PAD)
    ups = Ring(far, 4, lambda k, j: wg.at[j % 2, far.rows(k, j // 2), up_lanes], ur_send, ur_recv)
    for j in range(4):
        ups.start(j, gate_base.at[j, :, up_lanes])
    downs = Copies(dz_send, dz_recv)
    downs.go(0, down_half.at[upper], wd.at[1, upper], far.partner)
    cot_copy = copy_all([(cot_all, cots)], w_sem.at[pl.ds(1, 1)])
    down_copies = copy_all([(down_half, wd.at[0]), (down_two, wd.at[1, lower])], w_sem.at[pl.ds(2, 2)])
    pairs = []
    for j in range(4):
        pairs.append((gate_base.at[j], wg.at[j % 2, far.rows(0, j // 2)]))
        for k in (1, 2, 3):
            rows = far.rows(k, j // 2)
            pairs.append((gate_half.at[j % 2, rows], wg.at[j % 2, rows, pl.ds(0, PAD)]))
    gate_copies = copy_all(pairs, w_sem.at[pl.ds(4, 16)])
    out_copy[0].wait()
    scatter = Scatter(near, scatter_refs)

    def make(chip):
        rows = chip_rows(chip)
        scatter.part[...] = dot_nt(attended[rows, :128], wo[0]) + dot_nt(attended[rows, 128:], wo[1])

    scatter.produce("d", make)
    scatter.produce("z", make)
    scatter.far()
    scatter.produce("x", make)
    scatter.z_direct()
    scatter.produce("o", make)
    scatter.x_direct()
    ups.relay(0)
    ups.relay(1)
    scatter.relays()
    ups.relay(2)
    ups.relay(3)
    for copy in cot_copy + down_copies:
        copy.wait()
    downs.take(0, wd.at[1, upper], far.partner)
    for chip in range(4):
        for s in range(2):
            hg[s, chip * CHIP : (chip + 1) * CHIP, :] = dot(cots[chip * CHIP : (chip + 1) * CHIP, :], wd[s])
    first, second_half = scatter.result()
    residual[:HALF, :] = tok[:HALF, :].astype(F32) + first
    residual[HALF:, :] = tok[HALF:, :].astype(F32) + second_half
    normed, _ = layer_norm_parts(residual[...])
    second[block_rows(near.me), :] = (normed * gains[2:3, :] + gains[3:4, :]).astype(BF)
    gather = Gather(near, second, ga_send, ga_recv)
    gather.start()
    for copy in gate_copies:
        copy.wait()
    ups.finish()
    downs.finish()
    copies = copy_all([(wg, wg_out), (wd, wd_out)], o_sem.at[pl.ds(12, 2)])

    def use(key):
        chip = near.chip[key]
        rows = chip_rows(chip)
        for s in range(2):
            made = dot(second[rows, :], wg[s])
            h, g, u = silu_parts(made[:, :PAD], made[:, PAD:], hg[s, rows, :])
            hidden[rows, s * PAD : (s + 1) * PAD] = h.astype(BF)
            grads[rows, s * 2 * PAD : s * 2 * PAD + PAD] = g.astype(BF)
            grads[rows, s * 2 * PAD + PAD : (s + 1) * 2 * PAD] = u.astype(BF)
        i = "oxzd".index(key) * 3
        copies.extend(
            copy_all(
                [
                    (second.at[rows], second_out.at[rows]),
                    (hidden.at[rows], hidden_out.at[rows]),
                    (grads.at[rows], grads_out.at[rows]),
                ],
                o_sem.at[pl.ds(i, 3)],
            )
        )

    gather.run(use)
    gather.finish()
    for copy in copies:
        copy.wait()


def middle_call(attended, tokens, gains, cot_all, wo, gate_base, gate_half, down_half, down_two):
    return pl.pallas_call(
        middle_kernel,
        out_shape=(
            shape((OWN, D), F32),
            shape((LEN, D), BF),
            shape((LEN, 2 * PAD), BF),
            shape((LEN, 4 * PAD), BF),
            shape((2, D, 2 * PAD), BF),
            shape((2, D, PAD), BF),
        ),
        in_specs=[IN_VMEM, IN_VMEM, IN_VMEM] + [ANYWHERE] * 6,
        out_specs=(IN_VMEM,) + (ANYWHERE,) * 5,
        scratch_shapes=[
            pltpu.VMEM((2, D, 128), BF),
            pltpu.VMEM((2, D, 2 * PAD), BF),
            pltpu.VMEM((2, D, PAD), BF),
            pltpu.VMEM((LEN, D), BF),
            pltpu.VMEM((2, LEN, PAD), F32),
            pltpu.VMEM((LEN, D), BF),
            pltpu.VMEM((LEN, 2 * PAD), BF),
            pltpu.VMEM((LEN, 4 * PAD), BF),
            *Scatter.scratch(),
            *sems(Gather.COPIES, 12, 1),
            DMA((20,)),
            DMA((14,)),
        ],
        compiler_params=params(3),
        cost_estimate=cost(20 * 10**9, 60 * 2**20),
        name="middle",
    )(attended, tokens, gains, cot_all, wo, gate_base, gate_half, down_half, down_two)


A_LANES = 640
B_LANES = 2 * PAD - A_LANES


def back_kernel(
    grads, residual, cot, gains, wo_all, wg_all, grad_gate, grad_down,
    residual_grad, branch_out, attended_grad, norm_sums, a_sum, b_sum, c_sum,
    wo, wg, branch, a_own, a_land, b_own, b_land, c_own, c_land, *rest,
):
    scatter_refs = rest[:10]
    ga_send, ga_recv, ay_send, ay_recv, bz_send, bz_recv, cz_send, cz_recv, w_sem, o_sem = rest[10:]
    near, far = Near(), Far()
    load = copy_all([(wg_all, wg), (wo_all, wo)], w_sem.at[pl.ds(0, 2)])
    greet([near.dev["x"], near.dev["z"], near.dev["s"], far.partner, far.ring[1], far.ring[2], far.ring[3]])
    a = SumY(far, ay_send, ay_recv)
    b, c = SumZ(far, bz_send, bz_recv), SumZ(far, cz_send, cz_recv)
    a.start_y(grad_gate, lambda s: pl.ds(s * 2 * PAD, A_LANES), a_own, a_land, w_sem.at[pl.ds(2, 4)])
    c.start_z(grad_down, lambda s: pl.ds(s * PAD, PAD), c_own, c_land, w_sem.at[6])
    b.start_z(grad_gate, lambda s: pl.ds(s * 2 * PAD + A_LANES, B_LANES), b_own, b_land, w_sem.at[7])
    load[0].wait()
    scatter = Scatter(near, scatter_refs)

    def make(chip):
        rows = chip_rows(chip)
        scatter.part[...] = dot_nt(grads[rows, : 2 * PAD], wg[0]) + dot_nt(grads[rows, 2 * PAD :], wg[1])

    first, second_half = scatter.run(make)
    normed, inverse = layer_norm_parts(residual[...])
    upstream = jnp.concatenate([first, second_half], axis=0)
    part, gain_sum, shift_sum = norm_back(upstream, normed, inverse, gains[2:3, :])
    made = cot[...].astype(F32) + part
    residual_grad[...] = made
    norm_sums[...] = jnp.concatenate([gain_sum, shift_sum] * 4, axis=0)
    branch[block_rows(near.me), :] = made.astype(BF)
    gather = Gather(near, branch, ga_send, ga_recv)
    gather.start()
    load[1].wait()
    copies = []

    def use(key):
        rows = chip_rows(near.chip[key])
        for s in range(2):
            attended_grad[rows, s * 128 : (s + 1) * 128] = dot(branch[rows, :], wo[s]).astype(BF)
        i = "oxzd".index(key)
        copies.extend(copy_all([(branch.at[rows], branch_out.at[rows])], o_sem.at[pl.ds(i, 1)]))

    gather.run(use)
    gather.finish()
    c.add_z(c_sum)
    b.add_z(b_sum)
    a.add_y(a_sum)
    for job in (a, b, c):
        job.copies.finish()
    for copy in copies:
        copy.wait()


def back_call(grads, residual, cotangent, gains, wo, wg, grad_gate, grad_down):
    return pl.pallas_call(
        back_kernel,
        out_shape=(
            shape((OWN, D), F32),
            shape((LEN, D), BF),
            shape((LEN, 256), BF),
            shape((8, D), F32),
            shape((4, 256, A_LANES), BF),
            shape((D, B_LANES), BF),
            shape((D, PAD), BF),
        ),
        in_specs=[IN_VMEM] * 4 + [ANYWHERE] * 4,
        out_specs=(IN_VMEM, ANYWHERE) + (IN_VMEM,) * 5,
        scratch_shapes=[
            pltpu.VMEM((2, D, 128), BF),
            pltpu.VMEM((2, D, 2 * PAD), BF),
            pltpu.VMEM((LEN, D), BF),
            pltpu.VMEM((4, 256, A_LANES), BF),
            pltpu.VMEM((3, 4, 256, A_LANES), BF),
            pltpu.VMEM((D, B_LANES), BF),
            pltpu.VMEM((D, B_LANES), BF),
            pltpu.VMEM((D, PAD), BF),
            pltpu.VMEM((D, PAD), BF),
            *Scatter.scratch(),
            *sems(Gather.COPIES, SumY.COPIES, SumZ.COPIES, SumZ.COPIES),
            DMA((8,)),
            DMA((4,)),
        ],
        compiler_params=params(4),
        cost_estimate=cost(12 * 10**9, 60 * 2**20),
        name="back",
    )(grads, residual, cotangent, gains, wo, wg, grad_gate, grad_down)


def attend_back_kernel(
    query, keys, values, attended_grad, log_sum, cos, sin_up, sin_down, lowest,
    hidden, residual, a_sum, b_sum, c_sum, wd_all, grad_out,
    projected_grad, bias_sum, mixed, a_two, b_two, c_two, o_sum,
    kt, key_acc, value_acc, wd, a_land, b_land, c_land, o_own, o_land, *rest,
):
    scatter_refs = rest[:10]
    a_send, a_recv, b_send, b_recv, c_send, c_recv, o_send, o_recv, w_sem = rest[10:]
    near, far = Near(), Far()
    load = copy_all([(wd_all, wd)], w_sem.at[pl.ds(0, 1)])
    greet([near.dev["x"], near.dev["z"], near.dev["s"], far.partner, far.ring[1], far.ring[2], far.ring[3]])
    a, b, c = SumY(far, a_send, a_recv), SumZ(far, b_send, b_recv), SumZ(far, c_send, c_recv)
    o = SumZ(far, o_send, o_recv)
    c.start_y(c_sum, c_land)
    b.start_y(b_sum, b_land)
    a.start_z(a_sum, a_land)
    o.start_z(grad_out, lambda s: pl.ds(s * 128, 128), o_own, o_land, w_sem.at[1])

    for s in range(2):
        kt[s] = keys[:, s * 128 : (s + 1) * 128].astype(F32).T.astype(BF)
    key_acc[...] = jnp.zeros_like(key_acc)
    value_acc[...] = jnp.zeros_like(value_acc)
    scatter = Scatter(near, scatter_refs)
    load[0].wait()

    def make(chip):
        rows = chip_rows(chip)
        scatter.part[...] = dot_nt(hidden[rows, :PAD], wd[0]) + dot_nt(hidden[rows, PAD:], wd[1])

    def look(block):
        start, stop = window(block)
        rows = slice(block * QB, (block + 1) * QB)
        bias_t = mask_bias(lowest[0:1, rows], start, stop, block)
        for s in range(2):
            lanes = slice(s * 128, (s + 1) * 128)
            q, k, v = query[rows, lanes], keys[start:stop, lanes], values[start:stop, lanes]
            grad, k_t = attended_grad[rows, lanes], kt[s, :, start:stop]
            halves, key_sum, value_sum = [], None, None
            for head_id in range(2):
                mine = head_lanes(QB, head_id)
                q_one = jnp.where(mine, q, jnp.zeros_like(q))
                g_one = jnp.where(mine, grad, jnp.zeros_like(grad))
                index = s * 2 + head_id
                probs = jnp.exp(dot_nt(k, q_one) + bias_t - log_sum[index : index + 1, rows])
                prob_grad = dot_nt(v, g_one)
                inner = jnp.sum(probs * prob_grad, axis=0, keepdims=True)
                score_grad = (probs * (prob_grad - inner)).astype(BF)
                made = dot(k_t, score_grad)
                halves.append(made[head_id * HD : (head_id + 1) * HD])
                key_part = dot(score_grad, q_one)
                value_part = dot(probs.astype(BF), g_one)
                key_sum = key_part if key_sum is None else key_sum + key_part
                value_sum = value_part if value_sum is None else value_sum + value_part
            query_grad = jnp.concatenate(halves, axis=0).T * HD ** (-0.5)
            query_grad = roll_rotate(query_grad, cos[rows, :], -sin_up[rows, :], -sin_down[rows, :])
            projected_grad[rows, s * 384 : s * 384 + 128] = query_grad.astype(BF)
            key_acc[s, start:stop, :] += key_sum
            value_acc[s, start:stop, :] += value_sum

    scatter.produce("d", make)
    scatter.produce("z", make)
    scatter.far()
    scatter.produce("x", make)
    scatter.z_direct()
    scatter.produce("o", make)
    scatter.x_direct()
    look(0)
    look(1)
    scatter.relays()
    look(2)
    look(3)
    for s in range(2):
        made = roll_rotate(key_acc[s], cos[...], -sin_up[...], -sin_down[...])
        projected_grad[:, s * 384 + 128 : s * 384 + 256] = made.astype(BF)
        projected_grad[:, s * 384 + 256 : s * 384 + 384] = value_acc[s].astype(BF)
    bias_sum[...] = jnp.broadcast_to(
        jnp.sum(projected_grad[...].astype(F32), axis=0, keepdims=True), bias_sum.shape
    )
    first, second = scatter.result()
    mixed[:HALF, :] = residual[:HALF, :] + first
    mixed[HALF:, :] = residual[HALF:, :] + second
    a.add_z(a_sum, a_two)
    o.add_z(o_sum)
    b.add_y(b_sum, b_two)
    c.add_y(c_sum, c_two)
    for job in (a, b, c, o):
        job.copies.finish()


def attend_back_call(query, keys, values, attended_grad, log_sum, cos, sin_up, sin_down, lowest, *more):
    return pl.pallas_call(
        attend_back_kernel,
        out_shape=(
            shape((LEN, 768), BF),
            shape((8, 768), F32),
            shape((OWN, D), F32),
            shape((2, 256, A_LANES), BF),
            shape((2, 256, B_LANES), BF),
            shape((2, 256, PAD), BF),
            shape((D, 128), BF),
        ),
        in_specs=[IN_VMEM] * 14 + [ANYWHERE] * 2,
        out_specs=(IN_VMEM,) * 7,
        scratch_shapes=[
            pltpu.VMEM((2, 128, LEN), BF),
            pltpu.VMEM((2, LEN, 128), F32),
            pltpu.VMEM((2, LEN, 128), F32),
            pltpu.VMEM((2, D, PAD), BF),
            pltpu.VMEM((2, 256, A_LANES), BF),
            pltpu.VMEM((3, 2, 256, B_LANES), BF),
            pltpu.VMEM((3, 2, 256, PAD), BF),
            pltpu.VMEM((D, 128), BF),
            pltpu.VMEM((D, 128), BF),
            *Scatter.scratch(),
            *sems(SumY.COPIES, SumZ.COPIES, SumZ.COPIES, SumZ.COPIES),
            DMA((2,)),
        ],
        compiler_params=params(5),
        cost_estimate=cost(15 * 10**9, 12 * 2**20),
        name="attend_back",
    )(query, keys, values, attended_grad, log_sum, cos, sin_up, sin_down, lowest, *more)


def close_kernel(
    projected_grad, tok, residual_grad, gains, sums_two, bias_sum, a_two, b_two, c_two, o_sum, head, grad_heads,
    grad_tokens, norms, gate_up, down, output, heads,
    wv, q_own, q_land, q_sum, q_zland, q_two, v_own, v_land, v_sum, v_yland, v_two, o_yland, o_two,
    a_xland, b_xland, c_xland, o_xland, q_xland, v_xland, pack, pack_land, pack_y, *rest,
):
    scatter_refs = rest[:10]
    q_send, q_recv, v_send, v_recv, o_send, o_recv, x_send, x_recv, p_send, p_recv, w_sem = rest[10:]
    near, far = Near(), Far()
    load = copy_all([(head, wv)], w_sem.at[pl.ds(0, 1)])
    greet(
        [near.dev["x"], near.dev["z"], near.dev["s"], far.over, far.partner]
        + [far.ring[1], far.ring[2], far.ring[3]]
    )
    q, v, o = SumY(far, q_send, q_recv), SumZ(far, v_send, v_recv), SumZ(far, o_send, o_recv)
    q.start_y(grad_heads, lambda s: pl.ds(s * 384, 256), q_own, q_land, w_sem.at[pl.ds(1, 4)])
    v.start_z(grad_heads, lambda s: pl.ds(s * 384 + 256, 128), v_own, v_land, w_sem.at[5])
    o.start_y(o_sum, o_yland)
    xs = [SumX(far, x_send.at[pl.ds(i, 1)], x_recv.at[pl.ds(i, 1)]) for i in range(6)]
    packs = Copies(p_send, p_recv)
    scatter = Scatter(near, scatter_refs)

    def make(chip):
        rows = chip_rows(chip)
        scatter.part[...] = dot_nt(projected_grad[rows, :384], wv[0]) + dot_nt(projected_grad[rows, 384:], wv[1])

    load[0].wait()
    scatter.produce("d", make)
    scatter.produce("z", make)
    scatter.far()
    scatter.produce("x", make)
    scatter.z_direct()
    scatter.produce("o", make)
    scatter.x_direct()
    normed, inverse = layer_norm_parts(tok[...].astype(F32))
    scatter.relays()
    xs[0].start(a_two, a_xland)
    xs[1].start(b_two, b_xland)
    xs[2].start(c_two, c_xland)
    v.add_z(v_sum)
    v.start_y(v_sum, v_yland)
    o.add_y(o_sum, o_two)
    xs[3].start(o_two, o_xland)
    first, second = scatter.result()
    part, gain_sum, shift_sum = norm_back(
        jnp.concatenate([first, second], axis=0), normed, inverse, gains[0:1, :]
    )
    grad_tokens[...] = residual_grad[...] + part
    pack[0] = jnp.concatenate([gain_sum, shift_sum, sums_two[0:2, :], jnp.zeros((4, D), F32)], axis=0)

    def swap(stage, device):
        packs.go(stage, pack.at[stage], pack_land.at[stage], device)

    def join(stage, device):
        packs.take(stage, pack_land.at[stage], device)
        pack[stage + 1] = pack[stage] + pack_land[stage]

    swap(0, near.dev["s"])
    q.add_y(q_sum)
    q.start_z(q_sum, q_zland)
    join(0, near.dev["s"])
    swap(1, near.dev["x"])
    xs[0].add(a_two, gate_up.at[:, pl.ds(0, A_LANES)])
    join(1, near.dev["x"])
    swap(2, near.dev["z"])
    xs[1].add(b_two, gate_up.at[:, pl.ds(A_LANES, B_LANES)])
    xs[2].add(c_two, down)
    v.add_y(v_sum, v_two)
    xs[5].start(v_two, v_xland)
    join(2, near.dev["z"])
    pack[3, 4:5, :768] = bias_sum[0:1, :]
    swap(3, far.partner)
    q.add_z(q_sum, q_two)
    xs[4].start(q_two, q_xland)
    xs[3].add(o_two, output)
    packs.take(3, pack_land.at[3], far.partner)
    pack[4] = pack[3] + pack_land[3]
    pack[4, 4:5, :384] = pack[3, 4:5, :384] + pack_land[3, 4:5, 384:768]
    swap(4, far.over)
    join(4, far.over)
    for k in (1, 2, 3):
        packs.go(4 + k, pack.at[5], pack_y.at[k - 1], far.ring[k])
    xs[5].add(v_two, heads.at[:, pl.ds(256, 128)])
    xs[4].add(q_two, heads.at[:, pl.ds(0, 256)])
    total = pack[5]
    for k in (1, 2, 3):
        packs.take(4 + k, pack_y.at[k - 1], far.ring[k])
        total = total + pack_y[k - 1]
    norms[...] = total
    for job in [q, v, o] + xs:
        job.copies.finish()
    packs.finish()


def close_call(projected_grad, tokens, residual_grad, gains, sums_two, bias_sum, a, b, c, o, head, grad_heads):
    return pl.pallas_call(
        close_kernel,
        out_shape=(
            shape((OWN, D), F32),
            shape((8, D), F32),
            shape((256, 2 * PAD), F32),
            shape((256, PAD), F32),
            shape((256, 128), F32),
            shape((256, 384), F32),
        ),
        in_specs=[IN_VMEM] * 10 + [ANYWHERE] * 2,
        out_specs=(IN_VMEM,) * 6,
        scratch_shapes=[
            pltpu.VMEM((2, D, 384), BF),
            pltpu.VMEM((4, 256, 256), BF),
            pltpu.VMEM((3, 4, 256, 256), BF),
            pltpu.VMEM((4, 256, 256), BF),
            pltpu.VMEM((2, 256, 256), BF),
            pltpu.VMEM((2, 256, 256), BF),
            pltpu.VMEM((D, 128), BF),
            pltpu.VMEM((D, 128), BF),
            pltpu.VMEM((D, 128), BF),
            pltpu.VMEM((3, 2, 256, 128), BF),
            pltpu.VMEM((2, 256, 128), BF),
            pltpu.VMEM((3, 2, 256, 128), BF),
            pltpu.VMEM((2, 256, 128), BF),
            pltpu.VMEM((256, A_LANES), BF),
            pltpu.VMEM((256, B_LANES), BF),
            pltpu.VMEM((256, PAD), BF),
            pltpu.VMEM((256, 128), BF),
            pltpu.VMEM((256, 256), BF),
            pltpu.VMEM((256, 128), BF),
            pltpu.VMEM((6, 8, D), F32),
            pltpu.VMEM((5, 8, D), F32),
            pltpu.VMEM((3, 8, D), F32),
            *Scatter.scratch(),
            *sems(SumY.COPIES, SumZ.COPIES, SumZ.COPIES, 6, 8),
            DMA((6,)),
        ],
        compiler_params=params(6),
        cost_estimate=cost(10 * 10**9, 60 * 2**20),
        name="close",
    )(projected_grad, tokens, residual_grad, gains, sums_two, bias_sum, a, b, c, o, head, grad_heads)


def wide(w):
    return jnp.pad(w, [(0, 0)] * (w.ndim - 1) + [(0, PAD - UNITS)])


def per_device(
    tokens,
    segments,
    first_gain,
    first_shift,
    heads_weight,
    heads_bias,
    output_weight,
    second_gain,
    second_shift,
    gate_up_weight,
    down_weight,
    cotangent,
):
    dp = lax.axis_index("dp")
    here = (jnp.arange(8) == dp).astype(BF)[None, None, :, None]
    bias = (heads_bias.astype(BF)[:, :, None, :] * here).reshape(1, 384).astype(F32)
    small = jnp.stack([first_gain, first_shift, second_gain, second_shift]).astype(BF).astype(F32)
    small = jnp.concatenate([jnp.pad(small, [(0, 0), (0, 128)]), bias, jnp.zeros((3, 384), F32)], axis=0)
    head = heads_weight.astype(BF).reshape(256, 384)
    out_t = output_weight.T.astype(BF)
    down_t = wide(down_weight.T.astype(BF))
    gate_up = wide(gate_up_weight.astype(BF)).reshape(256, 2 * PAD)

    first_all, gains, bias_all, head_all, wo, down_half, gate_base, cos, sin_up, sin_down, lowest = open_call(
        tokens, segments, small, head, out_t, down_t, gate_up
    )
    query, keys, values, attended, log_sum, cot_all, gate_half, down_two = attend_call(
        first_all, head_all, bias_all, cos, sin_up, sin_down, lowest, cotangent, gate_base, down_half
    )
    residual, second_all, hidden, grads, wg, wd = middle_call(
        attended, tokens, gains, cot_all, wo, gate_base, gate_half, down_half, down_two
    )
    grad_gate = dot_tn(second_all, grads).astype(BF)
    grad_down = dot_tn(cot_all, hidden).astype(BF)
    residual_grad, branch_all, attended_grad, sums_two, a, b, c = back_call(
        grads, residual, cotangent, gains, wo, wg, grad_gate, grad_down
    )
    grad_out = dot_tn(branch_all, attended).astype(BF)
    projected_grad, bias_sum, mixed, a, b, c, o = attend_back_call(
        query, keys, values, attended_grad, log_sum, cos, sin_up, sin_down, lowest,
        hidden, residual, a, b, c, wd, grad_out,
    )
    grad_heads = dot_tn(first_all, projected_grad).astype(BF)
    grad_tokens, norms, gate_up, down, output, heads = close_call(
        projected_grad, tokens, residual_grad, gains, sums_two, bias_sum, a, b, c, o, head_all, grad_heads
    )
    place = dp * 256 + lax.axis_index("tensor") * 16
    norm_parts = lax.dynamic_slice_in_dim(norms[:4], place, 16, 1)
    return (
        mixed,
        grad_tokens,
        norm_parts[0],
        norm_parts[1],
        heads.reshape(256, 3, 128),
        lax.dynamic_slice_in_dim(norms[4, :384].reshape(3, 2, HD), dp * 8, 8, 2),
        output.T,
        norm_parts[2],
        norm_parts[3],
        gate_up.reshape(256, 2, PAD)[..., :UNITS],
        down[:, :UNITS].T,
    )


ALL = ("dp", "tensor")


def solution(mesh):
    return jax.shard_map(
        per_device,
        mesh=mesh,
        in_specs=(
            P(ALL, None),
            P("dp", None),
            P("dp"),
            P("dp"),
            P("dp", None, "tensor"),
            P(None, "tensor", "dp"),
            P("tensor", "dp"),
            P("dp"),
            P("dp"),
            P("dp", None, "tensor"),
            P("tensor", "dp"),
            P(ALL, None),
        ),
        out_specs=(
            P(ALL, None),
            P(ALL, None),
            P(ALL),
            P(ALL),
            P("dp", None, "tensor"),
            P(None, "tensor", "dp"),
            P("tensor", "dp"),
            P(ALL),
            P(ALL),
            P("dp", None, "tensor"),
            P("tensor", "dp"),
        ),
        check_vma=False,
    )
```

```python
import functools
import math

import jax
import jax.numpy as jnp
from jax import lax
from jax.experimental import pallas as pl
from jax.experimental.pallas import tpu as pltpu
from jax.sharding import PartitionSpec as P

D = 2048
HD = 64
ROT = 16
WINDOW = 512
LEN = 1024
OWN = 128
HALF = OWN // 2
CHIP = 2 * OWN
UNITS = 352
PAD = 384
QB = 256

NORM_EPS = 1e-05
BASE_FREQ = 10000.0
FAR_NEGATIVE = -1e30
BF = jnp.bfloat16
F32 = jnp.float32
MESH = pl.DeviceIdType.MESH
VMEM_LIMIT = 60 * 2**20
DMA = pltpu.SemaphoreType.DMA


def spot(z, x, c):
    return (z % 2) * 4 + x * 2 + c


class Near:
    def __init__(self):
        t = lax.axis_index("tensor")
        z, x, c = t // 4, (t // 2) % 2, t % 2
        oz = (z // 2) * 2 + (z + 1) % 2
        ox, oc = 1 - x, 1 - c
        self.c, self.oc = c, oc
        self.me = spot(z, x, c)
        self.dev = {
            "x": {"tensor": z * 4 + ox * 2 + c},
            "z": {"tensor": oz * 4 + x * 2 + c},
            "s": {"tensor": z * 4 + x * 2 + oc},
        }
        self.same = {"o": spot(z, x, c), "x": spot(z, ox, c), "z": spot(oz, x, c), "d": spot(oz, ox, c)}
        self.other = {
            "o": spot(z, x, oc),
            "x": spot(z, ox, oc),
            "z": spot(oz, x, oc),
            "d": spot(oz, ox, oc),
        }
        self.chip = {"o": (z % 2) * 2 + x, "x": (z % 2) * 2 + ox, "z": (oz % 2) * 2 + x, "d": (oz % 2) * 2 + ox}


def remote(src, dst, send, recv, device):
    return pltpu.make_async_remote_copy(
        src_ref=src, dst_ref=dst, send_sem=send, recv_sem=recv, device_id=device, device_id_type=MESH
    )


def greet(devices):
    barrier = pltpu.get_barrier_semaphore()
    for device in devices:
        pl.semaphore_signal(barrier, inc=1, device_id=device, device_id_type=MESH)
    pl.semaphore_wait(barrier, len(devices))


def block_rows(block, half=None):
    if half is None:
        return pl.ds(pl.multiple_of(block * OWN, OWN), OWN)
    return pl.ds(pl.multiple_of(block * OWN + half * HALF, HALF), HALF)


def chip_rows(chip):
    return pl.ds(pl.multiple_of(chip * CHIP, CHIP), CHIP)


class Gather:
    COPIES = 13

    def __init__(self, near, buf, send, recv):
        self.near, self.buf, self.send, self.recv = near, buf, send, recv
        self.sent = []

    def copy(self, index, block, half, to):
        view = self.buf.at[block_rows(block, half)]
        return remote(view, view, self.send.at[index], self.recv.at[index], self.near.dev[to])

    def go(self, index, block, half, to):
        copy = self.copy(index, block, half, to)
        copy.start()
        self.sent.append(copy)

    def take(self, index, block, half, to="s"):
        self.copy(index, block, half, to).wait_recv()

    def start(self):
        me = self.near.me
        self.go(0, me, 0, "z")
        self.go(1, me, 1, "x")
        self.go(4, me, None, "s")
        self.go(2, me, 0, "x")
        self.go(3, me, 1, "z")

    def first(self):
        same = self.near.same
        self.take(0, same["z"], 0)
        self.go(5, same["z"], 0, "x")
        self.go(7, same["z"], 0, "s")
        self.take(1, same["x"], 1)
        self.go(6, same["x"], 1, "z")
        self.go(8, same["x"], 1, "s")

    def second(self):
        same = self.near.same
        self.take(2, same["x"], 0)
        self.go(9, same["x"], 0, "s")
        self.take(3, same["z"], 1)
        self.go(10, same["z"], 1, "s")

    def third(self):
        same = self.near.same
        self.take(5, same["d"], 0)
        self.go(11, same["d"], 0, "s")
        self.take(6, same["d"], 1)
        self.go(12, same["d"], 1, "s")

    def own_chip(self):
        self.take(4, self.near.other["o"], None)

    def x_chip(self):
        self.take(8, self.near.other["x"], 1)
        self.take(9, self.near.other["x"], 0)

    def z_chip(self):
        self.take(7, self.near.other["z"], 0)
        self.take(10, self.near.other["z"], 1)

    def d_chip(self):
        self.take(11, self.near.other["d"], 0)
        self.take(12, self.near.other["d"], 1)

    def finish(self):
        for copy in self.sent:
            copy.wait_send()

    def run(self, use):
        self.own_chip()
        use("o")
        self.first()
        self.second()
        self.x_chip()
        use("x")
        self.third()
        self.z_chip()
        use("z")
        self.d_chip()
        use("d")


class Scatter:
    COPIES = 10

    @staticmethod
    def scratch(width=D):
        return [
            pltpu.VMEM((CHIP, width), F32),
            pltpu.VMEM((4, OWN, width), F32),
            pltpu.VMEM((4, OWN, width), BF),
            pltpu.VMEM((4, OWN, width), BF),
            pltpu.VMEM((OWN, width), BF),
            pltpu.VMEM((4, HALF, width), BF),
            pltpu.VMEM((2, HALF, width), BF),
            pltpu.VMEM((4, HALF, width), BF),
            DMA((Scatter.COPIES,)),
            DMA((Scatter.COPIES,)),
        ]

    @staticmethod
    def again(width=D):
        return [
            pltpu.VMEM((4, OWN, width), BF),
            pltpu.VMEM((2, HALF, width), BF),
            pltpu.VMEM((4, HALF, width), BF),
            DMA((Scatter.COPIES,)),
            DMA((Scatter.COPIES,)),
        ]

    @staticmethod
    def second(refs, more):
        return list(refs[:3]) + [more[0]] + list(refs[4:6]) + list(more[1:])

    KEYS = ("d", "z", "x", "o")

    def __init__(self, near, refs):
        self.near = near
        (
            self.part,
            self.mine,
            self.core_out,
            self.core_in,
            self.far_out,
            self.out,
            self.through,
            self.last,
            self.send,
            self.recv,
        ) = refs
        self.sent = []

    def copy(self, index, src, dst, to):
        return remote(src, dst, self.send.at[index], self.recv.at[index], self.near.dev[to])

    def go(self, index, src, dst, to):
        copy = self.copy(index, src, dst, to)
        copy.start()
        self.sent.append(copy)

    def take(self, index, dst, to="s"):
        self.copy(index, dst, dst, to).wait_recv()

    def produce(self, key, make):
        i = self.KEYS.index(key)
        make(self.near.chip[key])
        self.core_out[i] = self.part[block_rows(self.near.oc), :].astype(BF)
        self.go(i, self.core_out.at[i], self.core_in.at[i], "s")
        self.mine[i] = self.part[block_rows(self.near.c), :]

    def join(self, key):
        i = self.KEYS.index(key)
        self.take(i, self.core_in.at[i])

    def summed(self, key, half):
        i = self.KEYS.index(key)
        rows = slice(half * HALF, (half + 1) * HALF)
        return self.mine[i, rows, :] + self.core_in[i, rows, :].astype(F32)

    def far(self):
        self.join("d")
        self.far_out[:HALF, :] = self.summed("d", 0).astype(BF)
        self.go(4, self.far_out.at[pl.ds(0, HALF)], self.through.at[0], "z")
        self.far_out[HALF:, :] = self.summed("d", 1).astype(BF)
        self.go(5, self.far_out.at[pl.ds(HALF, HALF)], self.through.at[1], "x")

    def z_direct(self):
        self.join("z")
        self.out[0] = self.summed("z", 0).astype(BF)
        self.go(6, self.out.at[0], self.last.at[0], "z")

    def x_direct(self):
        self.join("x")
        self.out[1] = self.summed("x", 1).astype(BF)
        self.go(7, self.out.at[1], self.last.at[1], "x")

    def relays(self):
        self.take(4, self.through.at[0])
        self.out[2] = (self.summed("x", 0) + self.through[0].astype(F32)).astype(BF)
        self.go(8, self.out.at[2], self.last.at[2], "x")
        self.take(5, self.through.at[1])
        self.out[3] = (self.summed("z", 1) + self.through[1].astype(F32)).astype(BF)
        self.go(9, self.out.at[3], self.last.at[3], "z")

    def result(self):
        self.join("o")
        for index in range(4):
            self.take(6 + index, self.last.at[index])
        first = self.summed("o", 0) + self.last[0].astype(F32) + self.last[2].astype(F32)
        second = self.summed("o", 1) + self.last[1].astype(F32) + self.last[3].astype(F32)
        for copy in self.sent:
            copy.wait_send()
        self.sent = []
        return first, second

    def run(self, make):
        self.produce("d", make)
        self.produce("z", make)
        self.far()
        self.produce("x", make)
        self.z_direct()
        self.produce("o", make)
        self.x_direct()
        self.relays()
        return self.result()


def dot(left, right):
    return jnp.dot(left, right, preferred_element_type=F32)


def dot_nt(left, right):
    return lax.dot_general(left, right, (((1,), (1,)), ((), ())), preferred_element_type=F32)


def dot_tn(left, right):
    return lax.dot_general(left, right, (((0,), (0,)), ((), ())), preferred_element_type=F32)


def layer_norm_parts(values):
    centre = values - jnp.mean(values, axis=-1, keepdims=True)
    inverse = lax.rsqrt(jnp.mean(centre * centre, axis=-1, keepdims=True) + NORM_EPS)
    return (centre * inverse, inverse)


def norm_back(upstream, normed, inverse, gain):
    scaled = upstream * gain
    inner = (
        scaled
        - jnp.mean(scaled, axis=-1, keepdims=True)
        - normed * jnp.mean(scaled * normed, axis=-1, keepdims=True)
    )
    return (
        inner * inverse,
        jnp.sum(upstream * normed, axis=0, keepdims=True),
        jnp.sum(upstream, axis=0, keepdims=True),
    )


def params(collective=None):
    if collective is None:
        return pltpu.CompilerParams(vmem_limit_bytes=VMEM_LIMIT)
    return pltpu.CompilerParams(
        collective_id=collective, has_side_effects=True, vmem_limit_bytes=VMEM_LIMIT
    )


def cost(flops, moved):
    return pl.CostEstimate(flops=flops, bytes_accessed=moved, transcendentals=0)


IN_VMEM = pl.BlockSpec(memory_space=pltpu.VMEM)
ANYWHERE = pl.BlockSpec(memory_space=pl.ANY)


def shape(dims, dtype):
    return jax.ShapeDtypeStruct(dims, dtype)


def copy_all(pairs, sems):
    copies = [pltpu.make_async_copy(src, dst, sems.at[i]) for i, (src, dst) in enumerate(pairs)]
    for copy in copies:
        copy.start()
    return copies


class Far:
    def __init__(self):
        t, dp = lax.axis_index("tensor"), lax.axis_index("dp")
        self.h, self.y = dp // 4, dp % 4
        self.over = {"dp": (1 - self.h) * 4 + self.y}
        self.partner = {"tensor": (3 - t // 4) * 4 + t % 4}
        self.ring = {k: {"dp": self.h * 4 + (self.y + k) % 4} for k in (1, 2, 3)}

    def dp(self, k, h):
        return ((self.h + h) % 2) * 4 + (self.y - k + 4) % 4

    def rows(self, k, h):
        return pl.ds(pl.multiple_of(self.dp(k, h) * 256, 256), 256)

    def ahead(self, k, h):
        return pl.ds(pl.multiple_of((h * 4 + (self.y + k) % 4) * 256, 256), 256)


class Copies:
    def __init__(self, send, recv):
        self.send, self.recv, self.sent = send, recv, []

    def go(self, index, src, dst, device):
        copy = remote(src, dst, self.send.at[index], self.recv.at[index], device)
        copy.start()
        self.sent.append(copy)

    def take(self, index, dst, device):
        remote(dst, dst, self.send.at[index], self.recv.at[index], device).wait_recv()

    def finish(self):
        for copy in self.sent:
            copy.wait_send()
        self.sent = []


class Ring:
    def __init__(self, far, n, place, send, recv):
        self.far, self.n, self.place = far, n, place
        self.copies = Copies(send, recv)

    def start(self, j, src=None):
        own = self.place(0, j)
        src = own if src is None else src
        self.copies.go(j, src, own, self.far.ring[1])
        self.copies.go(self.n + j, src, own, self.far.ring[3])

    def relay(self, j):
        if j < self.n // 2:
            view = self.place(1, j)
            self.copies.take(j, view, self.far.ring[1])
            self.copies.go(2 * self.n + j, view, view, self.far.ring[1])
        else:
            view = self.place(3, j)
            self.copies.take(self.n + j, view, self.far.ring[3])
            self.copies.go(2 * self.n + j, view, view, self.far.ring[3])

    def rest(self, j):
        if j < self.n // 2:
            self.copies.take(self.n + j, self.place(3, j), self.far.ring[3])
        else:
            self.copies.take(j, self.place(1, j), self.far.ring[1])
        self.copies.take(2 * self.n + j, self.place(2, j), self.far.ring[1])

    def finish(self):
        for j in range(self.n):
            self.rest(j)
        self.copies.finish()


class SumY:
    COPIES = 12

    @staticmethod
    def scratch(lanes):
        return [
            pltpu.VMEM((4, 256, lanes), BF),
            pltpu.VMEM((4, 256, lanes), BF),
            pltpu.VMEM((2, 4, 256, lanes), BF),
        ]

    def __init__(self, far, block, refs, send, recv):
        self.far, self.block = far, block
        self.through, self.out, self.last = refs
        self.copies = Copies(send, recv)

    def to(self, j):
        return self.far.ring[1] if j < 2 else self.far.ring[3]

    def start_far(self, h):
        for j in (h * 2, h * 2 + 1):
            self.copies.go(j, self.block(2, j), self.through.at[j], self.to(j))

    def start_near(self, k, h):
        if (k == 1) == (h == 1):
            side = 0 if k == 1 else 1
            for j in (h * 2, h * 2 + 1):
                self.copies.go(4 + side * 4 + j, self.block(k, j), self.last.at[side, j], self.far.ring[k])

    def relay(self, h):
        k, side = (1, 0) if h == 0 else (3, 1)
        for j in (h * 2, h * 2 + 1):
            self.copies.take(j, self.through.at[j], self.to(j))
            self.out[j] = (self.block(k, j)[...].astype(F32) + self.through[j].astype(F32)).astype(BF)
            self.copies.go(4 + side * 4 + j, self.out.at[j], self.last.at[side, j], self.far.ring[k])

    def add(self, out):
        for j in range(4):
            total = self.block(0, j)[...].astype(F32)
            for side, k in ((0, 1), (1, 3)):
                self.copies.take(4 + side * 4 + j, self.last.at[side, j], self.far.ring[k])
                total = total + self.last[side, j].astype(F32)
            out[j] = total.astype(BF)


class PairZ:
    COPIES = 2

    def __init__(self, far, send, recv):
        self.far, self.copies = far, Copies(send, recv)

    def start(self, sums, land):
        self.sums, self.land = sums, land
        for h in range(2):
            self.copies.go(h, sums.at[h * 2 + 1], land.at[h], self.far.partner)

    def add(self, out):
        for h in range(2):
            self.copies.take(h, self.land.at[h], self.far.partner)
            out[h] = (self.sums[h * 2].astype(F32) + self.land[h].astype(F32)).astype(BF)


class SumZ:
    COPIES = 8

    def __init__(self, far, block, land, send, recv):
        self.far, self.block, self.land = far, block, land
        self.copies = Copies(send, recv)

    def start(self, k, h):
        rows = self.far.ahead(k, h)
        self.copies.go(k * 2 + h, self.block(rows, 1), self.land.at[rows], self.far.partner)

    def add(self, out):
        for k in range(4):
            for h in range(2):
                rows = self.far.ahead(k, h)
                self.copies.take(k * 2 + h, self.land.at[rows], self.far.partner)
                out[rows, :] = (self.block(rows, 0)[...].astype(F32) + self.land[rows, :].astype(F32)).astype(BF)


class RingY:
    COPIES = 6

    def __init__(self, far, send, recv):
        self.far, self.copies = far, Copies(send, recv)

    def start(self, sums, land):
        self.sums, self.land = sums, land
        for k in (1, 2, 3):
            for h in range(2):
                self.copies.go(
                    (k - 1) * 2 + h, sums.at[self.far.ahead(k, h)], land.at[k - 1, h], self.far.ring[k]
                )

    def add(self, out):
        for h in range(2):
            total = self.sums[self.far.ahead(0, h), :].astype(F32)
            for k in (1, 2, 3):
                self.copies.take((k - 1) * 2 + h, self.land.at[k - 1, h], self.far.ring[k])
                total = total + self.land[k - 1, h].astype(F32)
            out[h] = total.astype(BF)


class SumX:
    def __init__(self, far, send, recv):
        self.far, self.copies = far, Copies(send, recv)

    def start(self, sums, land):
        self.land = land
        self.copies.go(0, sums.at[1 - self.far.h], land, self.far.over)

    def add(self, sums, out):
        self.copies.take(0, self.land, self.far.over)
        out[...] = sums[self.far.h].astype(F32) + self.land[...].astype(F32)


def rotary_tables(starts, cos_out, up_out, down_out):
    index = lax.broadcasted_iota(jnp.int32, (8, LEN), 1)
    power = lax.broadcasted_iota(jnp.int32, (8, LEN), 0).astype(F32)
    angles = (index - starts).astype(F32) * jnp.exp(power * (-2.0 * math.log(BASE_FREQ) / ROT))
    cosine, sine = jnp.cos(angles), jnp.sin(angles)
    none, rest = jnp.zeros((8, LEN), F32), jnp.zeros((HD - ROT, LEN), F32)
    cos_out[...] = jnp.concatenate([cosine, cosine, rest + 1.0] * 2, axis=0).T
    up_out[...] = jnp.concatenate([-sine, none, rest] * 2, axis=0).T
    down_out[...] = jnp.concatenate([none, sine, rest] * 2, axis=0).T


def document_starts(seg):
    index = lax.broadcasted_iota(jnp.int32, (8, LEN), 1)
    new = (index == 0) | (pltpu.roll(seg, 1, 1) != seg)
    starts = jnp.where(new, index, 0)
    step = 1
    while step < LEN:
        starts = jnp.maximum(starts, jnp.where(index >= step, pltpu.roll(starts, step, 1), 0))
        step *= 2
    return starts


def roll_rotate(values, cos, sin_up, sin_down):
    return (
        values * cos + pltpu.roll(values, 128 - ROT // 2, 1) * sin_up + pltpu.roll(values, ROT // 2, 1) * sin_down
    )


def window(block):
    start = max(0, block * QB - WINDOW)
    return start, (block + 1) * QB


def mask_bias(lowest, start, stop, block):
    keys = lax.broadcasted_iota(jnp.int32, (stop - start, QB), 0) + start
    queries = lax.broadcasted_iota(jnp.int32, (stop - start, QB), 1) + block * QB
    return jnp.where((keys <= queries) & (keys >= lowest), 0.0, FAR_NEGATIVE)


def head_lanes(rows, head):
    lanes = lax.broadcasted_iota(jnp.int32, (rows, 128), 1)
    return (lanes >= HD) if head else (lanes < HD)


def silu_parts(gate, up, grad):
    sig = 1.0 / (1.0 + jnp.exp(-gate))
    silu = gate * sig
    return silu * up, grad * up * sig * (1.0 + gate * (1.0 - sig)), grad * silu


def sems(*counts):
    return [DMA((n,)) for n in counts for _ in range(2)]


class Quad:
    def __init__(self, far, place, send, recv):
        self.far, self.place = far, place
        self.copies = Copies(send, recv)

    def over(self, src):
        self.copies.go(0, src, self.place(0, 0), self.far.over)

    def partner(self, src):
        self.copies.go(1, src, self.place(0, 1), self.far.partner)

    def take_over(self):
        self.copies.take(0, self.place(0, 2), self.far.over)
        self.copies.go(2, self.place(0, 2), self.place(0, 3), self.far.partner)

    def take_partner(self):
        self.copies.take(1, self.place(0, 1), self.far.partner)

    def take_last(self):
        self.copies.take(2, self.place(0, 3), self.far.partner)


class Across:
    def __init__(self, far, buf, send, recv):
        self.far, self.buf = far, buf
        self.copies = Copies(send, recv)

    def start(self, k, h, src=None):
        rows = self.far.rows(k, h)
        src = self.buf.at[0, rows] if src is None else src
        self.copies.go(k * 2 + h, src, self.buf.at[1, rows], self.far.partner)

    def finish(self):
        for k in range(4):
            for h in range(2):
                self.copies.take(k * 2 + h, self.buf.at[1, self.far.rows(k, h)], self.far.partner)
        self.copies.finish()


def forward_kernel(
    tok, cot, seg, small, head, out_t, down_t, gate,
    first_out, cot_out, query_out, keys_out, values_out, attended_out, log_sum, residual, second_out, hidden_out,
    grads_out, wh_out, wo_out, wg_out, wd_out, gains, cos, sin_up, sin_down, lowest,
    fa, ca, wv, wo, wd, wg, query, keys, values, attended, vt, hg, second, hidden, grads, gbuf, gbuf_two, bias,
    *rest,
):
    scatter_refs, rest = rest[:10], rest[10:]
    (
        ga_send, ga_recv, gc_send, gc_recv, gs_send, gs_recv, sm_send, sm_recv, sr_send, sr_recv,
        hq_send, hq_recv, hr_send, hr_recv, oo_send, oo_recv, or_send, or_recv, dn_send, dn_recv, dr_send, dr_recv,
        gq_send, gq_recv, gr_send, gr_recv, ur_send, ur_recv, oz_send, oz_recv, dz_send, dz_recv, out_sem,
    ) = rest
    near, far = Near(), Far()
    greet([near.dev["x"], near.dev["z"], near.dev["s"], far.over, far.partner, far.ring[1], far.ring[3]])
    written = []

    def write(src, dst):
        copy = pltpu.make_async_copy(src, dst, out_sem.at[len(written)])
        copy.start()
        written.append(copy)

    def head_at(k, j):
        return wv.at[j % 2, far.rows(k, j // 2)]

    def gate_at(k, j):
        return wg.at[j % 2, far.rows(k, j // 2)]

    gate_lanes, up_lanes = pl.ds(0, PAD), pl.ds(PAD, PAD)
    smalls = Copies(sm_send, sm_recv)
    small_ring = Ring(far, 2, lambda k, j: gbuf.at[far.dp(k, j)], sr_send, sr_recv)
    head_quad, gate_quad = Quad(far, head_at, hq_send, hq_recv), Quad(far, gate_at, gq_send, gq_recv)
    head_ring = Ring(far, 4, head_at, hr_send, hr_recv)
    outs, downs = Copies(oo_send, oo_recv), Copies(dn_send, dn_recv)
    out_ring = Ring(far, 2, lambda k, j: wo.at[0, far.rows(k, j)], or_send, or_recv)
    down_ring = Ring(far, 2, lambda k, j: wd.at[0, far.rows(k, j)], dr_send, dr_recv)
    gate_ring = Ring(far, 4, lambda k, j: wg.at[j % 2, far.rows(k, j // 2), gate_lanes], gr_send, gr_recv)
    up_ring = Ring(far, 4, lambda k, j: wg.at[j % 2, far.rows(k, j // 2), up_lanes], ur_send, ur_recv)
    firsts = Gather(near, fa, ga_send, ga_recv)
    cots = Gather(near, ca, gc_send, gc_recv)
    seconds = Gather(near, second, gs_send, gs_recv)

    out_z, down_z = Across(far, wo, oz_send, oz_recv), Across(far, wd, dz_send, dz_recv)

    smalls.go(0, small, gbuf.at[far.dp(0, 0)], far.over)
    small_ring.start(0, small)
    head_quad.over(head)
    head_quad.partner(head)
    head_ring.start(0, head)
    gbuf[far.dp(0, 0)] = small[...]
    normed, _ = layer_norm_parts(tok[...].astype(F32))
    smalls.take(0, gbuf.at[far.dp(0, 1)], far.over)
    small_ring.start(1)
    head_quad.take_over()
    head_ring.start(2)
    small_ring.relay(0)
    small_ring.relay(1)
    head_quad.take_partner()
    head_ring.start(1)
    small_ring.finish()
    for d in range(8):
        gains[:, d * 256 : (d + 1) * 256] = gbuf[d, :, :256]
    first = normed * gains[0:1, :] + gains[1:2, :]
    fa[block_rows(near.me), :] = first.astype(BF)
    firsts.start()
    smalls.go(1, gbuf, gbuf_two, far.partner)
    head_ring.relay(0)
    head_quad.take_last()
    head_ring.start(3)
    outs.go(0, out_t, wo.at[0, far.rows(0, 0)], far.over)
    downs.go(0, down_t, wd.at[0, far.rows(0, 0)], far.over)
    gate_quad.partner(gate)
    out_z.start(0, 0, out_t)
    down_z.start(0, 0, down_t)
    wv[0, far.rows(0, 0), :] = head[...]
    wo[0, far.rows(0, 0), :] = out_t[...]
    wd[0, far.rows(0, 0), :] = down_t[...]
    wg[0, far.rows(0, 0), :] = gate[...]
    head_ring.relay(2)
    starts = document_starts(jnp.broadcast_to(seg[pl.ds(lax.axis_index("tensor") // 8, 1), :], (8, LEN)))
    index = lax.broadcasted_iota(jnp.int32, (8, LEN), 1)
    lowest[...] = jnp.maximum(starts, index - (WINDOW - 1))
    head_ring.relay(1)
    head_ring.relay(3)
    outs.take(0, wo.at[0, far.rows(0, 1)], far.over)
    out_z.start(0, 1)
    downs.take(0, wd.at[0, far.rows(0, 1)], far.over)
    down_z.start(0, 1)
    out_ring.start(0)
    out_ring.start(1)
    rotary_tables(starts, cos, sin_up, sin_down)
    firsts.first()
    firsts.second()
    gate_quad.over(gate)
    ca[block_rows(near.me), :] = cot[...]
    cots.start()
    down_ring.start(0)
    down_ring.start(1)
    firsts.third()
    smalls.take(1, gbuf_two, far.partner)
    bias[0:1, :384] = jnp.sum(gbuf[:, 4, :], axis=0, keepdims=True)
    bias[0:1, 384:] = jnp.sum(gbuf_two[:, 4, :], axis=0, keepdims=True)
    head_ring.finish()
    out_ring.relay(0)
    out_ring.relay(1)

    def project(chip):
        rows = chip_rows(chip)
        c, up, down = cos[rows, :], sin_up[rows, :], sin_down[rows, :]
        for s in range(2):
            lanes = slice(s * 128, (s + 1) * 128)
            made = dot(fa[rows, :], wv[s]) + bias[0:1, s * 384 : (s + 1) * 384]
            query[rows, lanes] = (roll_rotate(made[:, :128], c, up, down) * HD ** (-0.5)).astype(BF)
            keys[rows, lanes] = roll_rotate(made[:, 128:256], c, up, down).astype(BF)
            values[rows, lanes] = made[:, 256:].astype(BF)
            vt[chip, s] = made[:, 256:].T.astype(BF)

    def look(block):
        start, stop = window(block)
        rows = slice(block * QB, (block + 1) * QB)
        bias_t = mask_bias(lowest[0:1, rows], start, stop, block)
        for s in range(2):
            lanes = slice(s * 128, (s + 1) * 128)
            q, k = query[rows, lanes], keys[start:stop, lanes]
            v_t = jnp.concatenate([vt[i, s] for i in range(start // CHIP, stop // CHIP)], axis=1)
            halves = []
            for head_id in range(2):
                q_one = jnp.where(head_lanes(QB, head_id), q, jnp.zeros_like(q))
                scores = dot_nt(k, q_one) + bias_t
                top = jnp.max(scores, axis=0, keepdims=True)
                weights = jnp.exp(scores - top)
                total = jnp.sum(weights, axis=0, keepdims=True)
                made = dot(v_t, weights.astype(BF))
                halves.append(made[head_id * HD : (head_id + 1) * HD] * (1.0 / total))
                log_sum[s * 2 + head_id : s * 2 + head_id + 1, rows] = top + jnp.log(total)
            attended[rows, lanes] = jnp.concatenate(halves, axis=0).T.astype(BF)

    firsts.own_chip()
    project(near.chip["o"])
    down_ring.relay(0)
    down_ring.relay(1)
    firsts.x_chip()
    project(near.chip["x"])
    gate_ring.start(0)
    gate_quad.take_over()
    gate_ring.start(2)
    out_ring.finish()
    for k in (1, 2, 3):
        out_z.start(k, 0)
        out_z.start(k, 1)
    firsts.z_chip()
    project(near.chip["z"])
    firsts.d_chip()
    project(near.chip["d"])
    for src, dst in ((fa, first_out), (wv, wh_out), (query, query_out), (keys, keys_out), (values, values_out)):
        write(src, dst)
    down_ring.finish()
    for k in (1, 2, 3):
        down_z.start(k, 0)
        down_z.start(k, 1)
    gate_quad.take_partner()
    gate_ring.start(1)
    look(0)
    cots.first()
    cots.second()
    gate_quad.take_last()
    gate_ring.start(3)
    gate_ring.relay(0)
    look(1)
    cots.third()
    gate_ring.relay(2)
    up_ring.start(0)
    up_ring.start(1)
    look(2)
    gate_ring.relay(1)
    up_ring.start(2)
    up_ring.start(3)
    look(3)
    gate_ring.relay(3)

    out_z.finish()
    scatter = Scatter(near, scatter_refs)

    def make(chip):
        rows = chip_rows(chip)
        scatter.part[...] = dot_nt(attended[rows, :128], wo[0]) + dot_nt(attended[rows, 128:], wo[1])

    scatter.produce("d", make)
    scatter.produce("z", make)
    scatter.far()
    scatter.produce("x", make)
    scatter.z_direct()
    scatter.produce("o", make)
    scatter.x_direct()
    write(attended, attended_out)
    write(wo, wo_out)
    cots.own_chip()
    cots.x_chip()
    cots.z_chip()
    cots.d_chip()
    write(ca, cot_out)
    scatter.relays()
    up_ring.relay(0)
    up_ring.relay(1)
    one, two = scatter.result()
    residual[:HALF, :] = tok[:HALF, :].astype(F32) + one
    residual[HALF:, :] = tok[HALF:, :].astype(F32) + two
    normed, _ = layer_norm_parts(residual[...])
    second[block_rows(near.me), :] = (normed * gains[2:3, :] + gains[3:4, :]).astype(BF)
    seconds.start()
    up_ring.relay(2)
    up_ring.relay(3)
    down_z.finish()
    write(wd, wd_out)
    for chip in range(4):
        for s in range(2):
            hg[s, chip * CHIP : (chip + 1) * CHIP, :] = dot(ca[chip * CHIP : (chip + 1) * CHIP, :], wd[s])
    seconds.first()
    seconds.second()
    gate_ring.finish()
    up_ring.finish()
    write(wg, wg_out)

    def use(key):
        chip = near.chip[key]
        rows = chip_rows(chip)
        for s in range(2):
            made = dot(second[rows, :], wg[s])
            h, g, u = silu_parts(made[:, :PAD], made[:, PAD:], hg[s, rows, :])
            hidden[rows, s * PAD : (s + 1) * PAD] = h.astype(BF)
            grads[rows, s * 2 * PAD : s * 2 * PAD + PAD] = g.astype(BF)
            grads[rows, s * 2 * PAD + PAD : (s + 1) * 2 * PAD] = u.astype(BF)
        write(second.at[rows], second_out.at[rows])
        write(hidden.at[rows], hidden_out.at[rows])
        write(grads.at[rows], grads_out.at[rows])

    seconds.own_chip()
    use("o")
    seconds.x_chip()
    use("x")
    seconds.third()
    seconds.z_chip()
    use("z")
    seconds.d_chip()
    use("d")
    for group in (smalls, head_quad.copies, gate_quad.copies, outs, downs, firsts, cots, seconds):
        group.finish()
    for copy in written:
        copy.wait()


def forward_call(tokens, cotangent, segments, small, head, out_t, down_t, gate):
    narrow = shape((LEN, 256), BF)
    return pl.pallas_call(
        forward_kernel,
        out_shape=(
            shape((LEN, D), BF),
            shape((LEN, D), BF),
            narrow,
            narrow,
            narrow,
            narrow,
            shape((8, LEN), F32),
            shape((OWN, D), F32),
            shape((LEN, D), BF),
            shape((LEN, 2 * PAD), BF),
            shape((LEN, 4 * PAD), BF),
            shape((2, D, 384), BF),
            shape((2, D, 128), BF),
            shape((2, D, 2 * PAD), BF),
            shape((2, D, PAD), BF),
            shape((8, D), F32),
            shape((LEN, 128), F32),
            shape((LEN, 128), F32),
            shape((LEN, 128), F32),
            shape((8, LEN), jnp.int32),
        ),
        in_specs=[IN_VMEM] * 8,
        out_specs=(ANYWHERE,) * 6 + (IN_VMEM,) * 2 + (ANYWHERE,) * 7 + (IN_VMEM,) * 5,
        scratch_shapes=[
            pltpu.VMEM((LEN, D), BF),
            pltpu.VMEM((LEN, D), BF),
            pltpu.VMEM((2, D, 384), BF),
            pltpu.VMEM((2, D, 128), BF),
            pltpu.VMEM((2, D, PAD), BF),
            pltpu.VMEM((2, D, 2 * PAD), BF),
            pltpu.VMEM((LEN, 256), BF),
            pltpu.VMEM((LEN, 256), BF),
            pltpu.VMEM((LEN, 256), BF),
            pltpu.VMEM((LEN, 256), BF),
            pltpu.VMEM((4, 2, 128, CHIP), BF),
            pltpu.VMEM((2, LEN, PAD), F32),
            pltpu.VMEM((LEN, D), BF),
            pltpu.VMEM((LEN, 2 * PAD), BF),
            pltpu.VMEM((LEN, 4 * PAD), BF),
            pltpu.VMEM((8, 8, 384), F32),
            pltpu.VMEM((8, 8, 384), F32),
            pltpu.VMEM((8, 768), F32),
            *Scatter.scratch(),
            *sems(*[Gather.COPIES] * 3, 2, 6, 3, 12, 1, 6, 1, 6, 3, 12, 12, 8, 8),
            DMA((22,)),
        ],
        compiler_params=params(1),
        cost_estimate=cost(40 * 10**9, 80 * 2**20),
        name="forward",
    )(tokens, cotangent, segments, small, head, out_t, down_t, gate)


A_LANES = 640
B_LANES = 2 * PAD - A_LANES


def back_kernel(
    residual, cot, gains, grads_in, second_in, hidden_in, cot_in, wo_in, wg_in,
    residual_grad, branch_out, attended_grad, norm_sums, a_sum, b_sum, c_sum,
    wo, wg, branch, grads, second, hidden, cots, gate_part, down_part, b_land, c_land, *rest,
):
    scatter_refs, a_refs, rest = rest[:10], rest[10:13], rest[13:]
    ga_send, ga_recv, ay_send, ay_recv, bz_send, bz_recv, cz_send, cz_recv, w_sem, o_sem = rest
    near, far = Near(), Far()
    load = copy_all(
        [(wg_in, wg), (grads_in, grads), (second_in, second), (hidden_in, hidden), (cot_in, cots), (wo_in, wo)], w_sem
    )
    greet([near.dev["x"], near.dev["z"], near.dev["s"], far.partner, far.ring[1], far.ring[3]])

    def gate_block(k, j):
        return gate_part.at[far.ahead(k, j // 2), pl.ds((j % 2) * 2 * PAD, A_LANES)]

    a = SumY(far, gate_block, a_refs, ay_send, ay_recv)
    b = SumZ(
        far, lambda rows, s: gate_part.at[rows, pl.ds(s * 2 * PAD + A_LANES, B_LANES)], b_land, bz_send, bz_recv
    )
    c = SumZ(far, lambda rows, s: down_part.at[rows, pl.ds(s * PAD, PAD)], c_land, cz_send, cz_recv)
    scatter = Scatter(near, scatter_refs)

    def make(chip):
        rows = chip_rows(chip)
        scatter.part[...] = dot_nt(grads[rows, : 2 * PAD], wg[0]) + dot_nt(grads[rows, 2 * PAD :], wg[1])

    def weight_part(k, h):
        rows = far.ahead(k, h)
        gate_part[rows, :] = dot_tn(second[:, rows], grads[...]).astype(BF)
        if k == 2:
            a.start_far(h)
        elif k != 0:
            a.start_near(k, h)
        down_part[rows, :] = dot_tn(cots[:, rows], hidden[...]).astype(BF)
        c.start(k, h)
        b.start(k, h)

    load[0].wait()
    load[1].wait()
    scatter.produce("d", make)
    scatter.produce("z", make)
    scatter.far()
    scatter.produce("x", make)
    scatter.z_direct()
    scatter.produce("o", make)
    scatter.x_direct()
    for copy in load[2:5]:
        copy.wait()
    weight_part(2, 0)
    weight_part(2, 1)
    scatter.relays()
    weight_part(1, 0)
    weight_part(1, 1)
    weight_part(3, 0)
    a.relay(0)
    weight_part(3, 1)
    a.relay(1)
    first, second_half = scatter.result()
    normed, inverse = layer_norm_parts(residual[...])
    upstream = jnp.concatenate([first, second_half], axis=0)
    part, gain_sum, shift_sum = norm_back(upstream, normed, inverse, gains[2:3, :])
    made = cot[...].astype(F32) + part
    residual_grad[...] = made
    norm_sums[...] = jnp.concatenate([gain_sum, shift_sum] * 4, axis=0)
    branch[block_rows(near.me), :] = made.astype(BF)
    gather = Gather(near, branch, ga_send, ga_recv)
    gather.start()
    load[5].wait()
    weight_part(0, 0)
    weight_part(0, 1)
    copies = []

    def use(key):
        rows = chip_rows(near.chip[key])
        for s in range(2):
            attended_grad[rows, s * 128 : (s + 1) * 128] = dot(branch[rows, :], wo[s]).astype(BF)
        i = "oxzd".index(key)
        copies.extend(copy_all([(branch.at[rows], branch_out.at[rows])], o_sem.at[pl.ds(i, 1)]))

    gather.run(use)
    gather.finish()
    a.add(a_sum)
    c.add(c_sum)
    b.add(b_sum)
    for job in (a, b, c):
        job.copies.finish()
    for copy in copies:
        copy.wait()


def back_call(residual, cotangent, gains, grads, second, hidden, cot_all, wo, wg):
    return pl.pallas_call(
        back_kernel,
        out_shape=(
            shape((OWN, D), F32),
            shape((LEN, D), BF),
            shape((LEN, 256), BF),
            shape((8, D), F32),
            shape((4, 256, A_LANES), BF),
            shape((D, B_LANES), BF),
            shape((D, PAD), BF),
        ),
        in_specs=[IN_VMEM] * 3 + [ANYWHERE] * 6,
        out_specs=(IN_VMEM, ANYWHERE) + (IN_VMEM,) * 5,
        scratch_shapes=[
            pltpu.VMEM((2, D, 128), BF),
            pltpu.VMEM((2, D, 2 * PAD), BF),
            pltpu.VMEM((LEN, D), BF),
            pltpu.VMEM((LEN, 4 * PAD), BF),
            pltpu.VMEM((LEN, D), BF),
            pltpu.VMEM((LEN, 2 * PAD), BF),
            pltpu.VMEM((LEN, D), BF),
            pltpu.VMEM((D, 4 * PAD), BF),
            pltpu.VMEM((D, 2 * PAD), BF),
            pltpu.VMEM((D, B_LANES), BF),
            pltpu.VMEM((D, PAD), BF),
            *Scatter.scratch(),
            *SumY.scratch(A_LANES),
            *sems(Gather.COPIES, SumY.COPIES, SumZ.COPIES, SumZ.COPIES),
            DMA((6,)),
            DMA((4,)),
        ],
        compiler_params=params(2),
        cost_estimate=cost(25 * 10**9, 60 * 2**20),
        name="back",
    )(residual, cotangent, gains, grads, second, hidden, cot_all, wo, wg)


Q_LANES = 256
V_LANES = 384 - Q_LANES


def close_kernel(
    query, keys, values, attended_grad, log_sum, cos, sin_up, sin_down, lowest,
    residual, residual_grad, tok, gains, sums_two, a_sum, b_sum, c_sum, grad_out, hidden_in, first_in, wd_in, wh_in,
    mixed, grad_tokens, norms, gate_up, down, output, heads,
    kt, key_acc, value_acc, projected, wd, wh, hidden, first, head_part, bias_sum,
    a_zland, a_two, b_yland, b_two, c_yland, c_two, o_zland, o_sum, o_yland, o_two,
    q_sum, q_zland, q_two, v_zland, v_sum, v_yland, v_two,
    a_xland, b_xland, c_xland, o_xland, q_xland, v_xland, pack, pack_land, pack_y, *rest,
):
    scatter_refs, more_refs, q_refs, rest = rest[:10], rest[10:15], rest[15:18], rest[18:]
    (
        az_send, az_recv, by_send, by_recv, cy_send, cy_recv, oz_send, oz_recv, oy_send, oy_recv,
        qy_send, qy_recv, qz_send, qz_recv, vz_send, vz_recv, vy_send, vy_recv, x_send, x_recv, p_send, p_recv, w_sem,
    ) = rest
    near, far = Near(), Far()
    load = copy_all([(wd_in, wd), (hidden_in, hidden), (wh_in, wh), (first_in, first)], w_sem)
    greet(
        [near.dev["x"], near.dev["z"], near.dev["s"], far.over, far.partner]
        + [far.ring[1], far.ring[2], far.ring[3]]
    )
    b, c, a = RingY(far, by_send, by_recv), RingY(far, cy_send, cy_recv), PairZ(far, az_send, az_recv)
    o = SumZ(far, lambda rows, s: grad_out.at[rows, pl.ds(s * 128, 128)], o_zland, oz_send, oz_recv)
    o_y = RingY(far, oy_send, oy_recv)
    c.start(c_sum, c_yland)
    b.start(b_sum, b_yland)
    a.start(a_sum, a_zland)
    for k in range(4):
        for h in range(2):
            o.start(k, h)
    xs = [SumX(far, x_send.at[pl.ds(i, 1)], x_recv.at[pl.ds(i, 1)]) for i in range(6)]
    packs = Copies(p_send, p_recv)

    for s in range(2):
        kt[s] = keys[:, s * 128 : (s + 1) * 128].astype(F32).T.astype(BF)
    key_acc[...] = jnp.zeros_like(key_acc)
    value_acc[...] = jnp.zeros_like(value_acc)
    scatter = Scatter(near, scatter_refs)
    load[0].wait()
    load[1].wait()

    def make(chip):
        rows = chip_rows(chip)
        scatter.part[...] = dot_nt(hidden[rows, :PAD], wd[0]) + dot_nt(hidden[rows, PAD:], wd[1])

    def look(block):
        start, stop = window(block)
        rows = slice(block * QB, (block + 1) * QB)
        bias_t = mask_bias(lowest[0:1, rows], start, stop, block)
        for s in range(2):
            lanes = slice(s * 128, (s + 1) * 128)
            q, k, v = query[rows, lanes], keys[start:stop, lanes], values[start:stop, lanes]
            grad, k_t = attended_grad[rows, lanes], kt[s, :, start:stop]
            halves, key_sum, value_sum = [], None, None
            for head_id in range(2):
                mine = head_lanes(QB, head_id)
                q_one = jnp.where(mine, q, jnp.zeros_like(q))
                g_one = jnp.where(mine, grad, jnp.zeros_like(grad))
                index = s * 2 + head_id
                probs = jnp.exp(dot_nt(k, q_one) + bias_t - log_sum[index : index + 1, rows])
                prob_grad = dot_nt(v, g_one)
                inner = jnp.sum(probs * prob_grad, axis=0, keepdims=True)
                score_grad = (probs * (prob_grad - inner)).astype(BF)
                made = dot(k_t, score_grad)
                halves.append(made[head_id * HD : (head_id + 1) * HD])
                key_part = dot(score_grad, q_one)
                value_part = dot(probs.astype(BF), g_one)
                key_sum = key_part if key_sum is None else key_sum + key_part
                value_sum = value_part if value_sum is None else value_sum + value_part
            query_grad = jnp.concatenate(halves, axis=0).T * HD ** (-0.5)
            query_grad = roll_rotate(query_grad, cos[rows, :], -sin_up[rows, :], -sin_down[rows, :])
            projected[rows, s * 384 : s * 384 + 128] = query_grad.astype(BF)
            key_acc[s, start:stop, :] += key_sum
            value_acc[s, start:stop, :] += value_sum

    scatter.produce("d", make)
    scatter.produce("z", make)
    scatter.far()
    scatter.produce("x", make)
    scatter.z_direct()
    scatter.produce("o", make)
    scatter.x_direct()
    look(0)
    look(1)
    scatter.relays()
    look(2)
    look(3)
    for s in range(2):
        made = roll_rotate(key_acc[s], cos[...], -sin_up[...], -sin_down[...])
        projected[:, s * 384 + 128 : s * 384 + 256] = made.astype(BF)
        projected[:, s * 384 + 256 : s * 384 + 384] = value_acc[s].astype(BF)
    one, two = scatter.result()
    mixed[:HALF, :] = residual[:HALF, :] + one
    mixed[HALF:, :] = residual[HALF:, :] + two

    q = SumY(
        far, lambda k, j: head_part.at[far.ahead(k, j // 2), pl.ds((j % 2) * 384, Q_LANES)], q_refs, qy_send, qy_recv
    )
    v = SumZ(
        far, lambda rows, s: head_part.at[rows, pl.ds(s * 384 + Q_LANES, V_LANES)], v_zland, vz_send, vz_recv
    )
    q_z, v_y = PairZ(far, qz_send, qz_recv), RingY(far, vy_send, vy_recv)
    last = Scatter(near, Scatter.second(scatter_refs, more_refs))

    def make_last(chip):
        rows = chip_rows(chip)
        last.part[...] = dot_nt(projected[rows, :384], wh[0]) + dot_nt(projected[rows, 384:], wh[1])

    def weight_part(k, h):
        rows = far.ahead(k, h)
        head_part[rows, :] = dot_tn(first[:, rows], projected[...]).astype(BF)
        if k == 2:
            q.start_far(h)
        elif k != 0:
            q.start_near(k, h)
        v.start(k, h)

    load[2].wait()
    load[3].wait()
    weight_part(2, 0)
    weight_part(2, 1)
    last.produce("d", make_last)
    last.produce("z", make_last)
    last.far()
    weight_part(1, 0)
    weight_part(1, 1)
    last.produce("x", make_last)
    last.z_direct()
    weight_part(3, 0)
    weight_part(3, 1)
    last.produce("o", make_last)
    last.x_direct()
    q.relay(0)
    q.relay(1)
    weight_part(0, 0)
    weight_part(0, 1)
    a.add(a_two)
    xs[0].start(a_two, a_xland)
    last.relays()
    o.add(o_sum)
    o_y.start(o_sum, o_yland)
    b.add(b_two)
    c.add(c_two)
    xs[1].start(b_two, b_xland)
    xs[2].start(c_two, c_xland)
    bias_sum[...] = jnp.broadcast_to(jnp.sum(projected[...].astype(F32), axis=0, keepdims=True), bias_sum.shape)
    normed, inverse = layer_norm_parts(tok[...].astype(F32))
    one, two = last.result()
    part, gain_sum, shift_sum = norm_back(jnp.concatenate([one, two], axis=0), normed, inverse, gains[0:1, :])
    grad_tokens[...] = residual_grad[...] + part
    pack[0] = jnp.concatenate([gain_sum, shift_sum, sums_two[0:2, :], jnp.zeros((4, D), F32)], axis=0)

    def swap(stage, device):
        packs.go(stage, pack.at[stage], pack_land.at[stage], device)

    def join(stage, device):
        packs.take(stage, pack_land.at[stage], device)
        pack[stage + 1] = pack[stage] + pack_land[stage]

    swap(0, near.dev["s"])
    v.add(v_sum)
    v_y.start(v_sum, v_yland)
    q.add(q_sum)
    q_z.start(q_sum, q_zland)
    join(0, near.dev["s"])
    swap(1, near.dev["x"])
    xs[0].add(a_two, gate_up.at[:, pl.ds(0, A_LANES)])
    o_y.add(o_two)
    xs[3].start(o_two, o_xland)
    join(1, near.dev["x"])
    swap(2, near.dev["z"])
    xs[1].add(b_two, gate_up.at[:, pl.ds(A_LANES, B_LANES)])
    v_y.add(v_two)
    xs[5].start(v_two, v_xland)
    join(2, near.dev["z"])
    pack[3, 4:5, :768] = bias_sum[0:1, :]
    swap(3, far.partner)
    q_z.add(q_two)
    xs[4].start(q_two, q_xland)
    packs.take(3, pack_land.at[3], far.partner)
    pack[4] = pack[3] + pack_land[3]
    pack[4, 4:5, :384] = pack[3, 4:5, :384] + pack_land[3, 4:5, 384:768]
    swap(4, far.over)
    xs[2].add(c_two, down)
    xs[3].add(o_two, output)
    join(4, far.over)
    for k in (1, 2, 3):
        packs.go(4 + k, pack.at[5], pack_y.at[k - 1], far.ring[k])
    xs[5].add(v_two, heads.at[:, pl.ds(Q_LANES, V_LANES)])
    xs[4].add(q_two, heads.at[:, pl.ds(0, Q_LANES)])
    total = pack[5]
    for k in (1, 2, 3):
        packs.take(4 + k, pack_y.at[k - 1], far.ring[k])
        total = total + pack_y[k - 1]
    norms[...] = total
    for job in [a, b, c, o, o_y, q, q_z, v, v_y] + xs:
        job.copies.finish()
    packs.finish()


def close_call(*args):
    def two(lanes):
        return pltpu.VMEM((2, 256, lanes), BF)

    def ring(lanes):
        return pltpu.VMEM((3, 2, 256, lanes), BF)

    def whole(lanes):
        return pltpu.VMEM((D, lanes), BF)

    return pl.pallas_call(
        close_kernel,
        out_shape=(
            shape((OWN, D), F32),
            shape((OWN, D), F32),
            shape((8, D), F32),
            shape((256, 2 * PAD), F32),
            shape((256, PAD), F32),
            shape((256, 128), F32),
            shape((256, 384), F32),
        ),
        in_specs=[IN_VMEM] * 18 + [ANYWHERE] * 4,
        out_specs=(IN_VMEM,) * 7,
        scratch_shapes=[
            pltpu.VMEM((2, 128, LEN), BF),
            pltpu.VMEM((2, LEN, 128), F32),
            pltpu.VMEM((2, LEN, 128), F32),
            pltpu.VMEM((LEN, 768), BF),
            pltpu.VMEM((2, D, PAD), BF),
            pltpu.VMEM((2, D, 384), BF),
            pltpu.VMEM((LEN, 2 * PAD), BF),
            pltpu.VMEM((LEN, D), BF),
            pltpu.VMEM((D, 768), BF),
            pltpu.VMEM((8, 768), F32),
            two(A_LANES), two(A_LANES),
            ring(B_LANES), two(B_LANES), ring(PAD), two(PAD),
            whole(128), whole(128), ring(128), two(128),
            pltpu.VMEM((4, 256, Q_LANES), BF), two(Q_LANES), two(Q_LANES),
            whole(V_LANES), whole(V_LANES), ring(V_LANES), two(V_LANES),
            *[pltpu.VMEM((256, n), BF) for n in (A_LANES, B_LANES, PAD, 128, Q_LANES, V_LANES)],
            pltpu.VMEM((6, 8, D), F32),
            pltpu.VMEM((5, 8, D), F32),
            pltpu.VMEM((3, 8, D), F32),
            *Scatter.scratch(),
            *Scatter.again(),
            *SumY.scratch(Q_LANES),
            *sems(2, 6, 6, 8, 6, 12, 2, 8, 6, 6, 8),
            DMA((4,)),
        ],
        compiler_params=params(3),
        cost_estimate=cost(25 * 10**9, 60 * 2**20),
        name="close",
    )(*args)


def wide(w):
    return jnp.pad(w, [(0, 0)] * (w.ndim - 1) + [(0, PAD - UNITS)])


def per_device(
    tokens,
    segments,
    first_gain,
    first_shift,
    heads_weight,
    heads_bias,
    output_weight,
    second_gain,
    second_shift,
    gate_up_weight,
    down_weight,
    cotangent,
):
    dp = lax.axis_index("dp")
    here = (jnp.arange(8) == dp).astype(BF)[None, None, :, None]
    bias = (heads_bias.astype(BF)[:, :, None, :] * here).reshape(1, 384).astype(F32)
    small = jnp.stack([first_gain, first_shift, second_gain, second_shift]).astype(BF).astype(F32)
    small = jnp.concatenate([jnp.pad(small, [(0, 0), (0, 128)]), bias, jnp.zeros((3, 384), F32)], axis=0)
    head = heads_weight.astype(BF).reshape(256, 384)
    out_t = output_weight.T.astype(BF)
    down_t = wide(down_weight.T.astype(BF))
    gate_up = wide(gate_up_weight.astype(BF)).reshape(256, 2 * PAD)

    (
        first_all, cot_all, query, keys, values, attended, log_sum, residual, second_all, hidden, grads,
        head_all, wo, wg, wd, gains, cos, sin_up, sin_down, lowest,
    ) = forward_call(tokens, cotangent, segments, small, head, out_t, down_t, gate_up)
    residual_grad, branch_all, attended_grad, sums_two, a, b, c = back_call(
        residual, cotangent, gains, grads, second_all, hidden, cot_all, wo, wg
    )
    grad_out = dot_tn(branch_all, attended).astype(BF)
    mixed, grad_tokens, norms, gate_up, down, output, heads = close_call(
        query, keys, values, attended_grad, log_sum, cos, sin_up, sin_down, lowest,
        residual, residual_grad, tokens, gains, sums_two, a, b, c, grad_out, hidden, first_all, wd, head_all,
    )
    place = dp * 256 + lax.axis_index("tensor") * 16
    norm_parts = lax.dynamic_slice_in_dim(norms[:4], place, 16, 1)
    return (
        mixed,
        grad_tokens,
        norm_parts[0],
        norm_parts[1],
        heads.reshape(256, 3, 128),
        lax.dynamic_slice_in_dim(norms[4, :384].reshape(3, 2, HD), dp * 8, 8, 2),
        output.T,
        norm_parts[2],
        norm_parts[3],
        gate_up.reshape(256, 2, PAD)[..., :UNITS],
        down[:, :UNITS].T,
    )


ALL = ("dp", "tensor")


def solution(mesh):
    return jax.shard_map(
        per_device,
        mesh=mesh,
        in_specs=(
            P(ALL, None),
            P("dp", None),
            P("dp"),
            P("dp"),
            P("dp", None, "tensor"),
            P(None, "tensor", "dp"),
            P("tensor", "dp"),
            P("dp"),
            P("dp"),
            P("dp", None, "tensor"),
            P("tensor", "dp"),
            P(ALL, None),
        ),
        out_specs=(
            P(ALL, None),
            P(ALL, None),
            P(ALL),
            P(ALL),
            P("dp", None, "tensor"),
            P(None, "tensor", "dp"),
            P("tensor", "dp"),
            P(ALL),
            P(ALL),
            P("dp", None, "tensor"),
            P("tensor", "dp"),
        ),
        check_vma=False,
    )
```

```python
import functools
import math

import jax
import jax.numpy as jnp
from jax import lax
from jax.experimental import pallas as pl
from jax.experimental.pallas import tpu as pltpu
from jax.sharding import PartitionSpec as P

D = 2048
HD = 64
ROT = 16
WINDOW = 512
LEN = 1024
OWN = 128
HALF = OWN // 2
CHIP = 2 * OWN
UNITS = 352
PAD = 384
QB = 256

NORM_EPS = 1e-05
BASE_FREQ = 10000.0
FAR_NEGATIVE = -1e30
BF = jnp.bfloat16
F32 = jnp.float32
MESH = pl.DeviceIdType.MESH
VMEM_LIMIT = 62 * 2**20
DMA = pltpu.SemaphoreType.DMA


def spot(z, x, c):
    return (z % 2) * 4 + x * 2 + c


class Near:
    def __init__(self):
        t = lax.axis_index("tensor")
        z, x, c = t // 4, (t // 2) % 2, t % 2
        oz = (z // 2) * 2 + (z + 1) % 2
        ox, oc = 1 - x, 1 - c
        self.c, self.oc = c, oc
        self.me = spot(z, x, c)
        self.dev = {
            "x": {"tensor": z * 4 + ox * 2 + c},
            "z": {"tensor": oz * 4 + x * 2 + c},
            "s": {"tensor": z * 4 + x * 2 + oc},
        }
        self.same = {"o": spot(z, x, c), "x": spot(z, ox, c), "z": spot(oz, x, c), "d": spot(oz, ox, c)}
        self.other = {
            "o": spot(z, x, oc),
            "x": spot(z, ox, oc),
            "z": spot(oz, x, oc),
            "d": spot(oz, ox, oc),
        }
        self.chip = {"o": (z % 2) * 2 + x, "x": (z % 2) * 2 + ox, "z": (oz % 2) * 2 + x, "d": (oz % 2) * 2 + ox}


def remote(src, dst, send, recv, device):
    return pltpu.make_async_remote_copy(
        src_ref=src, dst_ref=dst, send_sem=send, recv_sem=recv, device_id=device, device_id_type=MESH
    )


def greet(devices):
    barrier = pltpu.get_barrier_semaphore()
    for device in devices:
        pl.semaphore_signal(barrier, inc=1, device_id=device, device_id_type=MESH)
    pl.semaphore_wait(barrier, len(devices))


def block_rows(block, half=None):
    if half is None:
        return pl.ds(pl.multiple_of(block * OWN, OWN), OWN)
    return pl.ds(pl.multiple_of(block * OWN + half * HALF, HALF), HALF)


def chip_rows(chip):
    return pl.ds(pl.multiple_of(chip * CHIP, CHIP), CHIP)


class Gather:
    COPIES = 13

    def __init__(self, near, buf, send, recv):
        self.near, self.buf, self.send, self.recv = near, buf, send, recv
        self.sent = []

    def copy(self, index, block, half, to):
        view = self.buf.at[block_rows(block, half)]
        return remote(view, view, self.send.at[index], self.recv.at[index], self.near.dev[to])

    def go(self, index, block, half, to):
        copy = self.copy(index, block, half, to)
        copy.start()
        self.sent.append(copy)

    def take(self, index, block, half, to="s"):
        self.copy(index, block, half, to).wait_recv()

    def start(self):
        me = self.near.me
        self.go(0, me, 0, "z")
        self.go(1, me, 1, "x")
        self.go(4, me, None, "s")
        self.go(2, me, 0, "x")
        self.go(3, me, 1, "z")

    def first(self):
        same = self.near.same
        self.take(0, same["z"], 0)
        self.go(5, same["z"], 0, "x")
        self.go(7, same["z"], 0, "s")
        self.take(1, same["x"], 1)
        self.go(6, same["x"], 1, "z")
        self.go(8, same["x"], 1, "s")

    def second(self):
        same = self.near.same
        self.take(2, same["x"], 0)
        self.go(9, same["x"], 0, "s")
        self.take(3, same["z"], 1)
        self.go(10, same["z"], 1, "s")

    def third(self):
        same = self.near.same
        self.take(5, same["d"], 0)
        self.go(11, same["d"], 0, "s")
        self.take(6, same["d"], 1)
        self.go(12, same["d"], 1, "s")

    def own_chip(self):
        self.take(4, self.near.other["o"], None)

    def x_chip(self):
        self.take(8, self.near.other["x"], 1)
        self.take(9, self.near.other["x"], 0)

    def z_chip(self):
        self.take(7, self.near.other["z"], 0)
        self.take(10, self.near.other["z"], 1)

    def d_chip(self):
        self.take(11, self.near.other["d"], 0)
        self.take(12, self.near.other["d"], 1)

    def finish(self):
        for copy in self.sent:
            copy.wait_send()

    def run(self, use):
        self.own_chip()
        use("o")
        self.first()
        self.second()
        self.x_chip()
        use("x")
        self.third()
        self.z_chip()
        use("z")
        self.d_chip()
        use("d")


class Scatter:
    COPIES = 10

    @staticmethod
    def scratch(width=D):
        return [
            pltpu.VMEM((CHIP, width), F32),
            pltpu.VMEM((4, OWN, width), F32),
            pltpu.VMEM((4, OWN, width), BF),
            pltpu.VMEM((4, OWN, width), BF),
            pltpu.VMEM((OWN, width), BF),
            pltpu.VMEM((4, HALF, width), BF),
            pltpu.VMEM((2, HALF, width), BF),
            pltpu.VMEM((4, HALF, width), BF),
            DMA((Scatter.COPIES,)),
            DMA((Scatter.COPIES,)),
        ]

    @staticmethod
    def again(width=D):
        return [
            pltpu.VMEM((4, OWN, width), BF),
            pltpu.VMEM((2, HALF, width), BF),
            pltpu.VMEM((4, HALF, width), BF),
            DMA((Scatter.COPIES,)),
            DMA((Scatter.COPIES,)),
        ]

    @staticmethod
    def second(refs, more):
        return list(refs[:3]) + [more[0]] + list(refs[4:6]) + list(more[1:])

    KEYS = ("d", "z", "x", "o")

    def __init__(self, near, refs):
        self.near = near
        (
            self.part,
            self.mine,
            self.core_out,
            self.core_in,
            self.far_out,
            self.out,
            self.through,
            self.last,
            self.send,
            self.recv,
        ) = refs
        self.sent = []

    def copy(self, index, src, dst, to):
        return remote(src, dst, self.send.at[index], self.recv.at[index], self.near.dev[to])

    def go(self, index, src, dst, to):
        copy = self.copy(index, src, dst, to)
        copy.start()
        self.sent.append(copy)

    def take(self, index, dst, to="s"):
        self.copy(index, dst, dst, to).wait_recv()

    def produce(self, key, make):
        i = self.KEYS.index(key)
        make(self.near.chip[key])
        self.core_out[i] = self.part[block_rows(self.near.oc), :].astype(BF)
        self.go(i, self.core_out.at[i], self.core_in.at[i], "s")
        self.mine[i] = self.part[block_rows(self.near.c), :]

    def join(self, key):
        i = self.KEYS.index(key)
        self.take(i, self.core_in.at[i])

    def summed(self, key, half):
        i = self.KEYS.index(key)
        rows = slice(half * HALF, (half + 1) * HALF)
        return self.mine[i, rows, :] + self.core_in[i, rows, :].astype(F32)

    def far(self):
        self.join("d")
        self.far_out[:HALF, :] = self.summed("d", 0).astype(BF)
        self.go(4, self.far_out.at[pl.ds(0, HALF)], self.through.at[0], "z")
        self.far_out[HALF:, :] = self.summed("d", 1).astype(BF)
        self.go(5, self.far_out.at[pl.ds(HALF, HALF)], self.through.at[1], "x")

    def z_direct(self):
        self.join("z")
        self.out[0] = self.summed("z", 0).astype(BF)
        self.go(6, self.out.at[0], self.last.at[0], "z")

    def x_direct(self):
        self.join("x")
        self.out[1] = self.summed("x", 1).astype(BF)
        self.go(7, self.out.at[1], self.last.at[1], "x")

    def relays(self):
        self.take(4, self.through.at[0])
        self.out[2] = (self.summed("x", 0) + self.through[0].astype(F32)).astype(BF)
        self.go(8, self.out.at[2], self.last.at[2], "x")
        self.take(5, self.through.at[1])
        self.out[3] = (self.summed("z", 1) + self.through[1].astype(F32)).astype(BF)
        self.go(9, self.out.at[3], self.last.at[3], "z")

    def result(self):
        self.join("o")
        for index in range(4):
            self.take(6 + index, self.last.at[index])
        first = self.summed("o", 0) + self.last[0].astype(F32) + self.last[2].astype(F32)
        second = self.summed("o", 1) + self.last[1].astype(F32) + self.last[3].astype(F32)
        for copy in self.sent:
            copy.wait_send()
        self.sent = []
        return first, second

    def run(self, make):
        self.produce("d", make)
        self.produce("z", make)
        self.far()
        self.produce("x", make)
        self.z_direct()
        self.x_direct()
        self.relays()
        self.produce("o", make)
        return self.result()


def dot(left, right):
    return jnp.dot(left, right, preferred_element_type=F32)


def dot_nt(left, right):
    return lax.dot_general(left, right, (((1,), (1,)), ((), ())), preferred_element_type=F32)


def dot_tn(left, right):
    return lax.dot_general(left, right, (((0,), (0,)), ((), ())), preferred_element_type=F32)


def layer_norm_parts(values):
    centre = values - jnp.mean(values, axis=-1, keepdims=True)
    inverse = lax.rsqrt(jnp.mean(centre * centre, axis=-1, keepdims=True) + NORM_EPS)
    return (centre * inverse, inverse)


def norm_back(upstream, normed, inverse, gain):
    scaled = upstream * gain
    inner = (
        scaled
        - jnp.mean(scaled, axis=-1, keepdims=True)
        - normed * jnp.mean(scaled * normed, axis=-1, keepdims=True)
    )
    return (
        inner * inverse,
        jnp.sum(upstream * normed, axis=0, keepdims=True),
        jnp.sum(upstream, axis=0, keepdims=True),
    )


def params(collective=None):
    if collective is None:
        return pltpu.CompilerParams(vmem_limit_bytes=VMEM_LIMIT)
    return pltpu.CompilerParams(
        collective_id=collective, has_side_effects=True, vmem_limit_bytes=VMEM_LIMIT
    )


def cost(flops, moved):
    return pl.CostEstimate(flops=flops, bytes_accessed=moved, transcendentals=0)


IN_VMEM = pl.BlockSpec(memory_space=pltpu.VMEM)
ANYWHERE = pl.BlockSpec(memory_space=pl.ANY)


def shape(dims, dtype):
    return jax.ShapeDtypeStruct(dims, dtype)


def copy_all(pairs, sems):
    copies = [pltpu.make_async_copy(src, dst, sems.at[i]) for i, (src, dst) in enumerate(pairs)]
    for copy in copies:
        copy.start()
    return copies


class Far:
    def __init__(self):
        t, dp = lax.axis_index("tensor"), lax.axis_index("dp")
        self.h, self.y = dp // 4, dp % 4
        self.over = {"dp": (1 - self.h) * 4 + self.y}
        self.partner = {"tensor": (3 - t // 4) * 4 + t % 4}
        self.ring = {k: {"dp": self.h * 4 + (self.y + k) % 4} for k in (1, 2, 3)}

    def dp(self, k, h):
        return ((self.h + h) % 2) * 4 + (self.y - k + 4) % 4

    def dp_of(self, i):
        return (self.h + i // 4) % 2 * 4 + (self.y + i % 4) % 4

    def span(self, k, h):
        return pl.ds(pl.multiple_of(self.dp(k, h) * 256, 256), 256)

    def ahead(self, k, h):
        return pl.ds(pl.multiple_of((h * 4 + (self.y + k) % 4) * 256, 256), 256)


class Copies:
    def __init__(self, send, recv):
        self.send, self.recv, self.sent = send, recv, []

    def go(self, index, src, dst, device):
        copy = remote(src, dst, self.send.at[index], self.recv.at[index], device)
        copy.start()
        self.sent.append(copy)

    def take(self, index, dst, device):
        remote(dst, dst, self.send.at[index], self.recv.at[index], device).wait_recv()

    def finish(self):
        for copy in self.sent:
            copy.wait_send()
        self.sent = []


class Ring:
    def __init__(self, far, n, place, send, recv):
        self.far, self.n, self.place = far, n, place
        self.copies = Copies(send, recv)

    def start(self, j, src=None):
        own = self.place(0, j)
        src = own if src is None else src
        self.copies.go(j, src, own, self.far.ring[1])
        self.copies.go(self.n + j, src, own, self.far.ring[3])

    def relay(self, j):
        if j < self.n // 2:
            view = self.place(1, j)
            self.copies.take(j, view, self.far.ring[1])
            self.copies.go(2 * self.n + j, view, view, self.far.ring[1])
        else:
            view = self.place(3, j)
            self.copies.take(self.n + j, view, self.far.ring[3])
            self.copies.go(2 * self.n + j, view, view, self.far.ring[3])

    def near(self, j):
        if j < self.n // 2:
            self.copies.take(self.n + j, self.place(3, j), self.far.ring[3])
        else:
            self.copies.take(j, self.place(1, j), self.far.ring[1])

    def finish(self, near=True):
        for j in range(self.n):
            if near:
                self.near(j)
            self.copies.take(2 * self.n + j, self.place(2, j), self.far.ring[1])
        self.copies.finish()


class SumY:
    COPIES = 12

    @staticmethod
    def scratch(dims):
        return [
            pltpu.VMEM((4,) + dims, BF),
            pltpu.VMEM((4,) + dims, BF),
            pltpu.VMEM((2, 4) + dims, BF),
        ]

    def __init__(self, far, block, refs, send, recv):
        self.far, self.block = far, block
        self.through, self.out, self.last = refs
        self.copies = Copies(send, recv)

    def to(self, j):
        return self.far.ring[1] if j < 2 else self.far.ring[3]

    def start(self, s):
        for j in (s, 2 + s):
            self.copies.go(j, self.block(2, j), self.through.at[j], self.to(j))
        self.copies.go(4 + 2 + s, self.block(1, 2 + s), self.last.at[0, 2 + s], self.far.ring[1])
        self.copies.go(8 + s, self.block(3, s), self.last.at[1, s], self.far.ring[3])

    def relay(self, s):
        for j, k, side in ((s, 1, 0), (2 + s, 3, 1)):
            self.copies.take(j, self.through.at[j], self.to(j))
            self.out[j] = (self.block(k, j)[...].astype(F32) + self.through[j].astype(F32)).astype(BF)
            self.copies.go(4 + side * 4 + j, self.out.at[j], self.last.at[side, j], self.far.ring[k])

    def add(self, out):
        for j in range(4):
            total = self.block(0, j)[...].astype(F32)
            for side, k in ((0, 1), (1, 3)):
                self.copies.take(4 + side * 4 + j, self.last.at[side, j], self.far.ring[k])
                total = total + self.last[side, j].astype(F32)
            out[j] = total.astype(BF)


class PairZ:
    COPIES = 2

    def __init__(self, far, send, recv):
        self.far, self.copies = far, Copies(send, recv)

    def start(self, sums, land):
        self.sums, self.land = sums, land
        for h in range(2):
            self.copies.go(h, sums.at[h * 2 + 1], land.at[h], self.far.partner)

    def add(self, out):
        for h in range(2):
            self.copies.take(h, self.land.at[h], self.far.partner)
            out[h] = (self.sums[h * 2].astype(F32) + self.land[h].astype(F32)).astype(BF)


class SumZ:
    COPIES = 8

    def __init__(self, far, block, land, out, send, recv):
        self.far, self.block, self.land, self.out = far, block, land, out
        self.copies = Copies(send, recv)

    def start(self, k, h):
        self.copies.go(k * 2 + h, self.block(k, h, 1), self.land(k, h), self.far.partner)

    def start_all(self):
        for k in (2, 1, 3, 0):
            for h in range(2):
                self.start(k, h)

    def add(self):
        for k in (2, 1, 3, 0):
            for h in range(2):
                self.copies.take(k * 2 + h, self.land(k, h), self.far.partner)
                total = self.block(k, h, 0)[...].astype(F32) + self.land(k, h)[...].astype(F32)
                self.out(k, h)[...] = total.astype(BF)


class RingY:
    COPIES = 6

    def __init__(self, far, block, land, send, recv):
        self.far, self.block, self.land = far, block, land
        self.copies = Copies(send, recv)

    def start(self):
        for k in (2, 1, 3):
            for h in range(2):
                self.copies.go((k - 1) * 2 + h, self.block(k, h), self.land.at[k - 1, h], self.far.ring[k])

    def add(self, out):
        for h in range(2):
            total = self.block(0, h)[...].astype(F32)
            for k in (1, 2, 3):
                self.copies.take((k - 1) * 2 + h, self.land.at[k - 1, h], self.far.ring[k])
                total = total + self.land[k - 1, h].astype(F32)
            out[h] = total.astype(BF)


class SumX:
    def __init__(self, far, send, recv):
        self.far, self.copies = far, Copies(send, recv)

    def start(self, sums, land):
        self.sums, self.land = sums, land
        self.copies.go(0, sums.at[1 - self.far.h], land, self.far.over)

    def add(self):
        self.copies.take(0, self.land, self.far.over)
        return self.sums[self.far.h].astype(F32) + self.land[...].astype(F32)


def rotary_tables(starts, cos_out, up_out, down_out):
    index = lax.broadcasted_iota(jnp.int32, (8, LEN), 1)
    power = lax.broadcasted_iota(jnp.int32, (8, LEN), 0).astype(F32)
    angles = (index - starts).astype(F32) * jnp.exp(power * (-2.0 * math.log(BASE_FREQ) / ROT))
    cosine, sine = jnp.cos(angles), jnp.sin(angles)
    none, rest = jnp.zeros((8, LEN), F32), jnp.zeros((HD - ROT, LEN), F32)
    cos_out[...] = jnp.concatenate([cosine, cosine, rest + 1.0] * 2, axis=0).T
    up_out[...] = jnp.concatenate([-sine, none, rest] * 2, axis=0).T
    down_out[...] = jnp.concatenate([none, sine, rest] * 2, axis=0).T


def document_starts(seg):
    index = lax.broadcasted_iota(jnp.int32, (8, LEN), 1)
    new = (index == 0) | (pltpu.roll(seg, 1, 1) != seg)
    starts = jnp.where(new, index, 0)
    step = 1
    while step < LEN:
        starts = jnp.maximum(starts, jnp.where(index >= step, pltpu.roll(starts, step, 1), 0))
        step *= 2
    return starts


def roll_rotate(values, cos, sin_up, sin_down):
    return (
        values * cos + pltpu.roll(values, 128 - ROT // 2, 1) * sin_up + pltpu.roll(values, ROT // 2, 1) * sin_down
    )


def window(block):
    start = max(0, block * QB - WINDOW)
    return start, (block + 1) * QB


def mask_bias(lowest, start, stop, block):
    keys = lax.broadcasted_iota(jnp.int32, (stop - start, QB), 0) + start
    queries = lax.broadcasted_iota(jnp.int32, (stop - start, QB), 1) + block * QB
    return jnp.where((keys <= queries) & (keys >= lowest), 0.0, FAR_NEGATIVE)


def head_lanes(rows, head):
    lanes = lax.broadcasted_iota(jnp.int32, (rows, 128), 1)
    return (lanes >= HD) if head else (lanes < HD)


def silu_parts(gate, up, grad):
    sig = 1.0 / (1.0 + jnp.exp(-gate))
    silu = gate * sig
    return silu * up, grad * up * sig * (1.0 + gate * (1.0 - sig)), grad * silu


def sems(*counts):
    return [DMA((n,)) for n in counts for _ in range(2)]


class Quad:
    def __init__(self, far, place, send, recv):
        self.far, self.place = far, place
        self.copies = Copies(send, recv)

    def over(self, src):
        self.copies.go(0, src, self.place(0, 0), self.far.over)

    def partner(self, src):
        self.copies.go(1, src, self.place(0, 1), self.far.partner)

    def take_over(self):
        self.copies.take(0, self.place(0, 2), self.far.over)
        self.copies.go(2, self.place(0, 2), self.place(0, 3), self.far.partner)

    def take_partner(self):
        self.copies.take(1, self.place(0, 1), self.far.partner)

    def take_last(self):
        self.copies.take(2, self.place(0, 3), self.far.partner)


class Across:
    def __init__(self, far, place, send, recv):
        self.far, self.place = far, place
        self.copies = Copies(send, recv)

    def start(self, k, h, src=None):
        src = self.place(k, h, 0) if src is None else src
        self.copies.go(k * 2 + h, src, self.place(k, h, 1), self.far.partner)

    def finish(self):
        for k in range(4):
            for h in range(2):
                self.copies.take(k * 2 + h, self.place(k, h, 1), self.far.partner)
        self.copies.finish()


class ZLast:
    def __init__(self, far, place, refs):
        x_send, x_recv, r_send, r_recv, z_send, z_recv = refs
        self.far, self.place = far, place
        self.copies = Copies(x_send, x_recv)
        self.ring = Ring(far, 2, lambda k, j: place(k, j, 0), r_send, r_recv)
        self.across = Across(far, place, z_send, z_recv)

    def over(self, src):
        self.src = src
        self.copies.go(0, src, self.place(0, 0, 0), self.far.over)

    def take_over(self):
        self.copies.take(0, self.place(0, 1, 0), self.far.over)

    def partner(self):
        self.across.start(0, 0, self.src)
        self.across.start(0, 1)

    def start(self):
        self.ring.start(0, self.src)
        self.ring.start(1)

    def ring_done(self):
        self.ring.finish(near=False)
        self.across.start(2, 0)
        self.across.start(2, 1)

    def relay(self):
        self.ring.relay(0)
        self.ring.relay(1)
        self.ring.near(0)
        self.ring.near(1)
        for k in (1, 3):
            self.across.start(k, 0)
            self.across.start(k, 1)

    def finish(self):
        self.across.finish()
        self.copies.finish()


Q_LANES = 256
V_LANES = 384 - Q_LANES
UP_ROWS = 176


def bias_lanes(bias, dp):
    j = lax.broadcasted_iota(jnp.int32, (8, 384), 0)
    lane = lax.broadcasted_iota(jnp.int32, (8, 384), 1)
    pick = jnp.where(lane % HD == dp * 8 + j, 1.0, 0.0).astype(BF)
    total = jnp.zeros((1, 384), F32)
    lane = lax.broadcasted_iota(jnp.int32, (1, 384), 1)
    for p in range(3):
        for h in range(2):
            made = dot(bias[p, h : h + 1, :].astype(BF), pick)
            total = total + jnp.where(lane // HD == p * 2 + h, made, 0.0)
    return total


def forward_kernel(
    tok, cot, seg, gain_one, shift_one, gain_two, shift_two, head_in, bias_in, out_in, gate_in, down_in,
    first_out, cot_out, query_out, keys_out, values_out, attended_out, log_sum, residual, second_out, hidden_out,
    grads_out, wh_out, wo_out, wg_out, wd_out, gains, cos, sin_up, sin_down, lowest,
    fa, ca, wv, wo, wd, wg, query, keys, values, attended, vt, hg, second, hidden, grads, gbuf, gbuf_two, bias,
    small, head, outw, gate, down, wh_turned, wo_turned, first_turned, *rest,
):
    scatter_refs, rest = rest[:10], rest[10:]
    (
        ga_send, ga_recv, gc_send, gc_recv, gs_send, gs_recv, sm_send, sm_recv, sr_send, sr_recv,
        hq_send, hq_recv, hr_send, hr_recv, gq_send, gq_recv, gr_send, gr_recv, uq_send, uq_recv, ur_send, ur_recv,
    ) = rest[:22]
    out_refs, down_refs, tail_refs, value_refs, (out_sem,) = rest[22:28], rest[28:34], rest[34:40], rest[40:46], rest[46:]
    near, far = Near(), Far()
    greet([near.dev["x"], near.dev["z"], near.dev["s"], far.over, far.partner, far.ring[1], far.ring[3]])
    written = []

    def write(src, dst):
        copy = pltpu.make_async_copy(src, dst, out_sem.at[len(written)])
        copy.start()
        written.append(copy)

    def head_at(k, j):
        return wv.at[j % 2, far.span(k, j // 2), pl.ds(0, Q_LANES)]

    def value_at(k, h, s):
        return wv.at[s, far.span(k, h), pl.ds(Q_LANES, V_LANES)]

    def gate_at(k, j):
        return wg.at[(j % 2) * 2, pl.ds(0, UNITS), far.span(k, j // 2)]

    def up_at(k, j):
        return wg.at[(j % 2) * 2 + 1, pl.ds(0, UP_ROWS), far.span(k, j // 2)]

    def tail_at(k, h, s):
        return wg.at[s * 2 + 1, pl.ds(UP_ROWS, UNITS - UP_ROWS), far.span(k, h)]

    def out_at(k, h, s):
        return wo.at[pl.ds(s * 128, 128), far.span(k, h)]

    def down_at(k, h, s):
        return wd.at[pl.ds(s * PAD, UNITS), far.span(k, h)]

    smalls = Copies(sm_send, sm_recv)
    small_ring = Ring(far, 2, lambda k, j: gbuf.at[far.dp(k, j)], sr_send, sr_recv)
    head_quad, head_ring = Quad(far, head_at, hq_send, hq_recv), Ring(far, 4, head_at, hr_send, hr_recv)
    gate_quad, gate_ring = Quad(far, gate_at, gq_send, gq_recv), Ring(far, 4, gate_at, gr_send, gr_recv)
    up_quad, up_ring = Quad(far, up_at, uq_send, uq_recv), Ring(far, 4, up_at, ur_send, ur_recv)
    outs, downs, tails = ZLast(far, out_at, out_refs), ZLast(far, down_at, down_refs), ZLast(far, tail_at, tail_refs)
    vals = ZLast(far, value_at, value_refs)
    firsts = Gather(near, fa, ga_send, ga_recv)
    cots = Gather(near, ca, gc_send, gc_recv)
    seconds = Gather(near, second, gs_send, gs_recv)

    small[0:1, :256] = gain_one[...].astype(BF).astype(F32)
    small[1:2, :256] = shift_one[...].astype(BF).astype(F32)
    small[2:3, :256] = gain_two[...].astype(BF).astype(F32)
    small[3:4, :256] = shift_two[...].astype(BF).astype(F32)
    small[4:5, :] = bias_lanes(bias_in, lax.axis_index("dp"))
    for p in range(3):
        head[:, p * 128 : (p + 1) * 128] = head_in[p].astype(BF)
    smalls.go(0, small, gbuf.at[far.dp(0, 0)], far.over)
    small_ring.start(0, small)
    own_qk, own_v = head.at[:, pl.ds(0, Q_LANES)], head.at[:, pl.ds(Q_LANES, V_LANES)]
    head_quad.over(own_qk)
    head_quad.partner(own_qk)
    vals.over(own_v)
    vals.ring.start(0, own_v)
    head_ring.start(0, own_qk)
    gbuf[far.dp(0, 0)] = small[...]
    normed, _ = layer_norm_parts(tok[...].astype(F32))
    smalls.take(0, gbuf.at[far.dp(0, 1)], far.over)
    small_ring.start(1)
    vals.take_over()
    vals.ring.start(1)
    vals.partner()
    head_quad.take_over()
    head_ring.start(2)
    small_ring.relay(0)
    small_ring.relay(1)
    head_quad.take_partner()
    head_ring.start(1)
    small_ring.finish()
    for d in range(8):
        gains[:, d * 256 : (d + 1) * 256] = gbuf[d, :, :256]
    first = normed * gains[0:1, :] + gains[1:2, :]
    fa[block_rows(near.me), :] = first.astype(BF)
    firsts.start()
    vals.relay()
    head_ring.relay(0)
    head_quad.take_last()
    head_ring.start(3)
    smalls.go(1, gbuf, gbuf_two, far.partner)
    outw[...] = out_in[...].astype(BF)
    down[...] = down_in[...].astype(BF)
    gate[...] = gate_in[...].astype(BF)
    up_own, tail_own = gate.at[1, pl.ds(0, UP_ROWS)], gate.at[1, pl.ds(UP_ROWS, UNITS - UP_ROWS)]
    outs.over(outw)
    outs.ring.start(0, outw)
    downs.over(down)
    tails.over(tail_own)
    gate_quad.over(gate.at[0])
    up_quad.over(up_own)
    wv[0, far.span(0, 0), :] = head[...]
    vals.ring_done()
    head_ring.relay(2)
    wo[:128, far.span(0, 0)] = outw[...]
    wd[:UNITS, far.span(0, 0)] = down[...]
    wg[0, :UNITS, far.span(0, 0)] = gate[0]
    wg[1, :UNITS, far.span(0, 0)] = gate[1]
    for i in range(4):
        wg[i, UNITS:, :] = jnp.zeros((PAD - UNITS, D), BF)
    for i in range(2):
        wd[i * PAD + UNITS : (i + 1) * PAD, :] = jnp.zeros((PAD - UNITS, D), BF)
    head_ring.relay(1)
    head_ring.relay(3)
    outs.take_over()
    outs.ring.start(1)
    outs.partner()
    gate_quad.partner(gate.at[0])
    up_quad.partner(up_own)
    starts = document_starts(jnp.broadcast_to(seg[pl.ds(lax.axis_index("tensor") // 8, 1), :], (8, LEN)))
    index = lax.broadcasted_iota(jnp.int32, (8, LEN), 1)
    lowest[...] = jnp.maximum(starts, index - (WINDOW - 1))
    firsts.first()
    firsts.second()
    rotary_tables(starts, cos, sin_up, sin_down)
    downs.take_over()
    downs.partner()
    tails.take_over()
    tails.partner()
    firsts.third()
    gate_quad.take_over()
    up_quad.take_over()
    smalls.take(1, gbuf_two, far.partner)
    bias[0:1, :384] = jnp.sum(gbuf[:, 4, :], axis=0, keepdims=True)
    bias[0:1, 384:] = jnp.sum(gbuf_two[:, 4, :], axis=0, keepdims=True)
    head_ring.finish()
    downs.start()
    tails.start()
    ca[block_rows(near.me), :] = cot[...]
    cots.start()
    outs.relay()
    vals.across.finish()

    def project(chip):
        rows = chip_rows(chip)
        c, up, down = cos[rows, :], sin_up[rows, :], sin_down[rows, :]
        for s in range(2):
            lanes = slice(s * 128, (s + 1) * 128)
            made = dot(fa[rows, :], wv[s]) + bias[0:1, s * 384 : (s + 1) * 384]
            query[rows, lanes] = (roll_rotate(made[:, :128], c, up, down) * HD ** (-0.5)).astype(BF)
            keys[rows, lanes] = roll_rotate(made[:, 128:256], c, up, down).astype(BF)
            values[rows, lanes] = made[:, 256:].astype(BF)
            vt[chip, s] = made[:, 256:].T.astype(BF)

    def look(block):
        start, stop = window(block)
        rows = slice(block * QB, (block + 1) * QB)
        bias_t = mask_bias(lowest[0:1, rows], start, stop, block)
        for s in range(2):
            lanes = slice(s * 128, (s + 1) * 128)
            q, k = query[rows, lanes], keys[start:stop, lanes]
            v_t = jnp.concatenate([vt[i, s] for i in range(start // CHIP, stop // CHIP)], axis=1)
            halves = []
            for head_id in range(2):
                q_one = jnp.where(head_lanes(QB, head_id), q, jnp.zeros_like(q))
                scores = dot_nt(k, q_one) + bias_t
                top = jnp.max(scores, axis=0, keepdims=True)
                weights = jnp.exp(scores - top)
                total = jnp.sum(weights, axis=0, keepdims=True)
                made = dot(v_t, weights.astype(BF))
                halves.append(made[head_id * HD : (head_id + 1) * HD] * (1.0 / total))
                log_sum[s * 2 + head_id : s * 2 + head_id + 1, rows] = top + jnp.log(total)
            attended[rows, lanes] = jnp.concatenate(halves, axis=0).T.astype(BF)

    firsts.own_chip()
    project(near.chip["o"])
    firsts.x_chip()
    project(near.chip["x"])
    firsts.z_chip()
    project(near.chip["z"])
    firsts.d_chip()
    project(near.chip["d"])
    for src, dst in ((query, query_out), (keys, keys_out), (values, values_out)):
        write(src, dst)
    outs.ring_done()
    look(0)
    gate_quad.take_partner()
    gate_quad.take_last()
    up_quad.take_partner()
    up_quad.take_last()
    look(1)
    gate_ring.start(0, gate.at[0])
    gate_ring.start(1)
    gate_ring.start(2)
    gate_ring.start(3)
    cots.first()
    cots.second()
    look(2)
    downs.relay()
    tails.relay()
    look(3)
    cots.third()
    outs.finish()
    scatter = Scatter(near, scatter_refs)

    def make(chip):
        rows = chip_rows(chip)
        scatter.part[...] = dot(attended[rows, :], wo[...])

    scatter.produce("d", make)
    scatter.produce("z", make)
    scatter.far()
    scatter.produce("x", make)
    scatter.z_direct()
    scatter.x_direct()
    up_ring.start(0, up_own)
    up_ring.start(1)
    up_ring.start(2)
    up_ring.start(3)
    scatter.relays()
    scatter.produce("o", make)
    downs.ring_done()
    tails.ring_done()
    write(attended, attended_out)
    wo_turned[...] = wo[...].T
    write(wo_turned, wo_out)
    gate_ring.relay(0)
    gate_ring.relay(1)
    gate_ring.relay(2)
    gate_ring.relay(3)
    cots.own_chip()
    cots.x_chip()
    cots.z_chip()
    cots.d_chip()
    write(ca, cot_out)
    one, two = scatter.result()
    residual[:HALF, :] = tok[:HALF, :].astype(F32) + one
    residual[HALF:, :] = tok[HALF:, :].astype(F32) + two
    normed, _ = layer_norm_parts(residual[...])
    second[block_rows(near.me), :] = (normed * gains[2:3, :] + gains[3:4, :]).astype(BF)
    seconds.start()
    for half in range(2):
        wh_turned[half * 384 : (half + 1) * 384, :] = wv[half].T
    write(wh_turned, wh_out)
    for chip in range(4):
        first_turned[:, chip * CHIP : (chip + 1) * CHIP] = fa[chip * CHIP : (chip + 1) * CHIP, :].T
    write(first_turned, first_out)
    for j in range(4):
        up_ring.relay(j)
    seconds.first()
    seconds.second()
    downs.finish()
    write(wd, wd_out)
    for chip in range(4):
        rows = slice(chip * CHIP, (chip + 1) * CHIP)
        hg[:, rows] = dot_nt(wd[...], ca[rows, :])
    seconds.third()
    gate_ring.finish()
    up_ring.finish()
    tails.finish()
    write(wg, wg_out)

    def use(key):
        chip = near.chip[key]
        rows = chip_rows(chip)
        for s in range(2):
            made = dot_nt(wg[s * 2 : s * 2 + 2].reshape(2 * PAD, D), second[rows, :])
            h, g, u = silu_parts(made[:PAD], made[PAD:], hg[s * PAD : (s + 1) * PAD, rows])
            hidden[s * PAD : (s + 1) * PAD, rows] = h.astype(BF)
            grads[s * 2 * PAD : s * 2 * PAD + PAD, rows] = g.astype(BF)
            grads[s * 2 * PAD + PAD : (s + 1) * 2 * PAD, rows] = u.astype(BF)
        write(second.at[rows], second_out.at[rows])
        write(hidden.at[:, rows], hidden_out.at[:, rows])
        write(grads.at[:, rows], grads_out.at[:, rows])

    seconds.own_chip()
    use("o")
    seconds.x_chip()
    use("x")
    seconds.z_chip()
    use("z")
    seconds.d_chip()
    use("d")
    for group in (smalls, head_quad.copies, gate_quad.copies, up_quad.copies, vals.copies, firsts, cots, seconds):
        group.finish()
    for copy in written:
        copy.wait()


def forward_call(*args):
    narrow = shape((LEN, 256), BF)
    return pl.pallas_call(
        forward_kernel,
        out_shape=(
            shape((D, LEN), BF),
            shape((LEN, D), BF),
            narrow,
            narrow,
            narrow,
            narrow,
            shape((8, LEN), F32),
            shape((OWN, D), F32),
            shape((LEN, D), BF),
            shape((2 * PAD, LEN), BF),
            shape((4 * PAD, LEN), BF),
            shape((768, D), BF),
            shape((D, 256), BF),
            shape((4, PAD, D), BF),
            shape((2 * PAD, D), BF),
            shape((8, D), F32),
            shape((LEN, 128), F32),
            shape((LEN, 128), F32),
            shape((LEN, 128), F32),
            shape((8, LEN), jnp.int32),
        ),
        in_specs=[IN_VMEM] * 12,
        out_specs=(ANYWHERE,) * 6 + (IN_VMEM,) * 2 + (ANYWHERE,) * 7 + (IN_VMEM,) * 5,
        scratch_shapes=[
            pltpu.VMEM((LEN, D), BF),
            pltpu.VMEM((LEN, D), BF),
            pltpu.VMEM((2, D, 384), BF),
            pltpu.VMEM((256, D), BF),
            pltpu.VMEM((2 * PAD, D), BF),
            pltpu.VMEM((4, PAD, D), BF),
            pltpu.VMEM((LEN, 256), BF),
            pltpu.VMEM((LEN, 256), BF),
            pltpu.VMEM((LEN, 256), BF),
            pltpu.VMEM((LEN, 256), BF),
            pltpu.VMEM((4, 2, 128, CHIP), BF),
            pltpu.VMEM((2 * PAD, LEN), F32),
            pltpu.VMEM((LEN, D), BF),
            pltpu.VMEM((2 * PAD, LEN), BF),
            pltpu.VMEM((4 * PAD, LEN), BF),
            pltpu.VMEM((8, 8, 384), F32),
            pltpu.VMEM((8, 8, 384), F32),
            pltpu.VMEM((8, 768), F32),
            pltpu.VMEM((8, 384), F32),
            pltpu.VMEM((256, 384), BF),
            pltpu.VMEM((128, 256), BF),
            pltpu.VMEM((2, UNITS, 256), BF),
            pltpu.VMEM((UNITS, 256), BF),
            pltpu.VMEM((768, D), BF),
            pltpu.VMEM((D, 256), BF),
            pltpu.VMEM((D, LEN), BF),
            *Scatter.scratch(),
            *sems(*[Gather.COPIES] * 3, 2, 6, 3, 12, 3, 12, 3, 12, *[1, 6, 8] * 4),
            DMA((22,)),
        ],
        compiler_params=params(1),
        cost_estimate=cost(40 * 10**9, 80 * 2**20),
        name="forward",
    )(*args)


ROWS = 3 * UNITS
A_ROWS = 608
B_ROWS = ROWS - A_ROWS


def back_kernel(
    residual, cot, gains, grads_in, second_in, hidden_in, cot_in, wo_in, wg_in, attended_in,
    residual_grad, attended_grad, norm_sums, a_sum, b_sum, grad_out,
    wo, wg, branch, grads, second, hidden, cots, attended, parts, b_land, *rest,
):
    scatter_refs, a_refs, rest = rest[:10], rest[10:13], rest[13:]
    ga_send, ga_recv, ay_send, ay_recv, bz_send, bz_recv, w_sem = rest
    near, far = Near(), Far()
    load = copy_all(
        [
            (wg_in, wg),
            (grads_in, grads),
            (second_in, second),
            (hidden_in, hidden),
            (cot_in, cots),
            (wo_in, wo),
            (attended_in, attended),
        ],
        w_sem,
    )
    greet([near.dev["x"], near.dev["z"], near.dev["s"], far.partner, far.ring[1], far.ring[3]])
    a_rows, b_rows = pl.ds(0, A_ROWS), pl.ds(A_ROWS, B_ROWS)
    a = SumY(far, lambda k, j: parts.at[j % 2, a_rows, far.ahead(k, j // 2)], a_refs, ay_send, ay_recv)
    b = SumZ(
        far,
        lambda k, h, s: parts.at[s, b_rows, far.ahead(k, h)],
        lambda k, h: b_land.at[:, far.ahead(k, h)],
        lambda k, h: b_sum.at[:, far.ahead(k, h)],
        bz_send,
        bz_recv,
    )
    scatter = Scatter(near, scatter_refs)

    def make(chip):
        scatter.part[...] = dot_tn(grads[:, chip_rows(chip)], wg[...].reshape(4 * PAD, D))

    def gate_part(s):
        start = s * 2 * PAD
        parts[s, :UNITS, :] = dot(grads[start : start + UNITS, :], second[...]).astype(BF)

    def up_part(s):
        start = s * 2 * PAD + PAD
        parts[s, UNITS : 2 * UNITS, :] = dot(grads[start : start + UNITS, :], second[...]).astype(BF)

    def down_part(s):
        start = s * PAD
        parts[s, 2 * UNITS :, :] = dot(hidden[start : start + UNITS, :], cots[...]).astype(BF)

    load[0].wait()
    load[1].wait()
    scatter.produce("d", make)
    scatter.produce("z", make)
    scatter.far()
    scatter.produce("x", make)
    scatter.z_direct()
    for copy in load[2:5]:
        copy.wait()
    up_part(1)
    scatter.x_direct()
    gate_part(1)
    a.start(1)
    scatter.relays()
    scatter.produce("o", make)
    down_part(1)
    b.start_all()
    gate_part(0)
    up_part(0)
    a.start(0)
    a.relay(1)
    first, second_half = scatter.result()
    normed, inverse = layer_norm_parts(residual[...])
    upstream = jnp.concatenate([first, second_half], axis=0)
    part, gain_sum, shift_sum = norm_back(upstream, normed, inverse, gains[2:3, :])
    made = cot[...].astype(F32) + part
    residual_grad[...] = made
    norm_sums[...] = jnp.concatenate([gain_sum, shift_sum] * 4, axis=0)
    branch[block_rows(near.me), :] = made.astype(BF)
    gather = Gather(near, branch, ga_send, ga_recv)
    gather.start()
    load[5].wait()
    load[6].wait()
    down_part(0)
    a.relay(0)

    def use(key):
        rows = chip_rows(near.chip[key])
        attended_grad[rows, :] = dot(branch[rows, :], wo[...]).astype(BF)

    gather.run(use)
    grad_out[...] = dot_tn(attended[...], branch[...]).astype(BF)
    gather.finish()
    b.add()
    a.add(a_sum)
    for job in (a, b):
        job.copies.finish()


def back_call(*args):
    return pl.pallas_call(
        back_kernel,
        out_shape=(
            shape((OWN, D), F32),
            shape((LEN, 256), BF),
            shape((8, D), F32),
            shape((4, A_ROWS, 256), BF),
            shape((B_ROWS, D), BF),
            shape((256, D), BF),
        ),
        in_specs=[IN_VMEM] * 3 + [ANYWHERE] * 7,
        out_specs=(IN_VMEM,) * 6,
        scratch_shapes=[
            pltpu.VMEM((D, 256), BF),
            pltpu.VMEM((4, PAD, D), BF),
            pltpu.VMEM((LEN, D), BF),
            pltpu.VMEM((4 * PAD, LEN), BF),
            pltpu.VMEM((LEN, D), BF),
            pltpu.VMEM((2 * PAD, LEN), BF),
            pltpu.VMEM((LEN, D), BF),
            pltpu.VMEM((LEN, 256), BF),
            pltpu.VMEM((2, ROWS, D), BF),
            pltpu.VMEM((B_ROWS, D), BF),
            *Scatter.scratch(),
            *SumY.scratch((A_ROWS, 256)),
            *sems(Gather.COPIES, SumY.COPIES, SumZ.COPIES),
            DMA((7,)),
        ],
        compiler_params=params(2),
        cost_estimate=cost(25 * 10**9, 60 * 2**20),
        name="back",
    )(*args)


def close_kernel(
    query, keys, values, attended_grad, log_sum, cos, sin_up, sin_down, lowest,
    residual, residual_grad, tok, gains, sums_two, a_sum, b_sum, grad_out, hidden_in, first_in, wd_in, wh_in,
    mixed, grad_tokens, norms, bias_grad, gate_up, down, output, heads,
    kt, key_acc, value_acc, projected, wd, wh, hidden, first, head_part, bias_sum,
    a_zland, a_two, b_yland, b_two, o_zland, o_sum, o_yland, o_two,
    q_sum, q_zland, q_two, v_zland, v_sum, v_yland, v_two,
    a_xland, b_xland, o_xland, q_xland, v_xland, pack, pack_dp, pack_one, pack_chip, pack_two, pack_z, *rest,
):
    scatter_refs, more_refs, q_refs, rest = rest[:10], rest[10:15], rest[15:18], rest[18:]
    (
        az_send, az_recv, by_send, by_recv, oz_send, oz_recv, oy_send, oy_recv,
        qy_send, qy_recv, qz_send, qz_recv, vz_send, vz_recv, vy_send, vy_recv, x_send, x_recv, p_send, p_recv, w_sem,
    ) = rest
    near, far = Near(), Far()
    load = copy_all([(wd_in, wd), (hidden_in, hidden), (wh_in, wh), (first_in, first)], w_sem)
    t = lax.axis_index("tensor")
    dp_peers = [{"dp": far.dp_of(i)} for i in range(1, 8)]
    chip_peers = [near.dev["s"], near.dev["x"], {"tensor": (t // 4) * 4 + 3 - t % 4}]
    z_peers = [far.partner, near.dev["z"], {"tensor": ((t // 4 + 2) % 4) * 4 + t % 4}]
    greet(dp_peers + chip_peers + z_peers)
    a = PairZ(far, az_send, az_recv)
    b = RingY(far, lambda k, h: b_sum.at[:, far.ahead(k, h)], b_yland, by_send, by_recv)
    o = SumZ(
        far,
        lambda k, h, s: grad_out.at[pl.ds(s * 128, 128), far.ahead(k, h)],
        lambda k, h: o_zland.at[:, far.ahead(k, h)],
        lambda k, h: o_sum.at[:, far.ahead(k, h)],
        oz_send,
        oz_recv,
    )
    o_y = RingY(far, lambda k, h: o_sum.at[:, far.ahead(k, h)], o_yland, oy_send, oy_recv)
    b.start()
    a.start(a_sum, a_zland)
    o.start_all()
    xs = [SumX(far, x_send.at[pl.ds(i, 1)], x_recv.at[pl.ds(i, 1)]) for i in range(5)]
    packs = Copies(p_send, p_recv)

    for s in range(2):
        kt[s] = keys[:, s * 128 : (s + 1) * 128].astype(F32).T.astype(BF)
    key_acc[...] = jnp.zeros_like(key_acc)
    value_acc[...] = jnp.zeros_like(value_acc)
    scatter = Scatter(near, scatter_refs)
    load[0].wait()
    load[1].wait()

    def make(chip):
        scatter.part[...] = dot_tn(hidden[:, chip_rows(chip)], wd[...])

    def look(block):
        start, stop = window(block)
        rows = slice(block * QB, (block + 1) * QB)
        bias_t = mask_bias(lowest[0:1, rows], start, stop, block)
        for s in range(2):
            lanes = slice(s * 128, (s + 1) * 128)
            q, k, v = query[rows, lanes], keys[start:stop, lanes], values[start:stop, lanes]
            grad, k_t = attended_grad[rows, lanes], kt[s, :, start:stop]
            halves, key_sum, value_sum = [], None, None
            for head_id in range(2):
                mine = head_lanes(QB, head_id)
                q_one = jnp.where(mine, q, jnp.zeros_like(q))
                g_one = jnp.where(mine, grad, jnp.zeros_like(grad))
                index = s * 2 + head_id
                probs = jnp.exp(dot_nt(k, q_one) + bias_t - log_sum[index : index + 1, rows])
                prob_grad = dot_nt(v, g_one)
                inner = jnp.sum(probs * prob_grad, axis=0, keepdims=True)
                score_grad = (probs * (prob_grad - inner)).astype(BF)
                made = dot(k_t, score_grad)
                halves.append(made[head_id * HD : (head_id + 1) * HD])
                key_part = dot(score_grad, q_one)
                value_part = dot(probs.astype(BF), g_one)
                key_sum = key_part if key_sum is None else key_sum + key_part
                value_sum = value_part if value_sum is None else value_sum + value_part
            query_grad = jnp.concatenate(halves, axis=0).T * HD ** (-0.5)
            query_grad = roll_rotate(query_grad, cos[rows, :], -sin_up[rows, :], -sin_down[rows, :])
            projected[rows, s * 384 : s * 384 + 128] = query_grad.astype(BF)
            key_acc[s, start:stop, :] += key_sum
            value_acc[s, start:stop, :] += value_sum

    scatter.produce("d", make)
    scatter.produce("z", make)
    scatter.far()
    scatter.produce("x", make)
    scatter.z_direct()
    scatter.x_direct()
    scatter.produce("o", make)
    look(0)
    scatter.relays()
    look(1)
    look(2)
    look(3)
    for s in range(2):
        made = roll_rotate(key_acc[s], cos[...], -sin_up[...], -sin_down[...])
        projected[:, s * 384 + 128 : s * 384 + 256] = made.astype(BF)
        projected[:, s * 384 + 256 : s * 384 + 384] = value_acc[s].astype(BF)
    one, two = scatter.result()
    mixed[:HALF, :] = residual[:HALF, :] + one
    mixed[HALF:, :] = residual[HALF:, :] + two

    def query_key_part(k, j):
        return head_part.at[far.ahead(k, j // 2), pl.ds((j % 2) * 384, Q_LANES)]

    q = SumY(far, query_key_part, q_refs, qy_send, qy_recv)
    v = SumZ(
        far,
        lambda k, h, s: head_part.at[far.ahead(k, h), pl.ds(s * 384 + Q_LANES, V_LANES)],
        lambda k, h: v_zland.at[far.ahead(k, h)],
        lambda k, h: v_sum.at[far.ahead(k, h)],
        vz_send,
        vz_recv,
    )
    q_z = PairZ(far, qz_send, qz_recv)
    v_y = RingY(far, lambda k, h: v_sum.at[far.ahead(k, h)], v_yland, vy_send, vy_recv)
    last = Scatter(near, Scatter.second(scatter_refs, more_refs))

    def make_last(chip):
        rows = chip_rows(chip)
        last.part[...] = dot(projected[rows, :], wh[...])

    def weight_part(k, h):
        rows = far.ahead(k, h)
        head_part[rows, :] = dot(first[rows, :], projected[...]).astype(BF)
        v.start(k, h)

    load[2].wait()
    load[3].wait()
    weight_part(2, 0)
    weight_part(2, 1)
    weight_part(1, 1)
    weight_part(3, 0)
    q.start(0)
    q.start(1)
    last.produce("d", make_last)
    last.produce("z", make_last)
    last.far()
    weight_part(1, 0)
    weight_part(3, 1)
    last.produce("x", make_last)
    last.z_direct()
    q.relay(0)
    last.x_direct()
    q.relay(1)
    last.relays()
    last.produce("o", make_last)
    weight_part(0, 0)
    weight_part(0, 1)
    a.add(a_two)
    xs[0].start(a_two, a_xland)
    o.add()
    o_y.start()
    b.add(b_two)
    xs[1].start(b_two, b_xland)
    bias_sum[...] = jnp.broadcast_to(jnp.sum(projected[...].astype(F32), axis=0, keepdims=True), bias_sum.shape)
    normed, inverse = layer_norm_parts(tok[...].astype(F32))
    one, two = last.result()
    part, gain_sum, shift_sum = norm_back(jnp.concatenate([one, two], axis=0), normed, inverse, gains[0:1, :])
    grad_tokens[...] = residual_grad[...] + part
    sums = jnp.concatenate([gain_sum, shift_sum, sums_two[0:2, :]], axis=0)
    pack[...] = jnp.zeros_like(pack)
    for d in range(8):
        pack[d, 0:4, :256] = sums[:, d * 256 : (d + 1) * 256]
        pack[d, 4:5, :] = bias_sum[0:1, :384]
        pack[d, 5:6, :] = bias_sum[0:1, 384:]
    for i, device in enumerate(dp_peers):
        packs.go(i, pack.at[far.dp_of(i + 1)], pack_dp.at[i], device)
    v.add()
    v_y.start()
    q.add(q_sum)
    q_z.start(q_sum, q_zland)
    total = pack[far.dp(0, 0)]
    for i, device in enumerate(dp_peers):
        packs.take(i, pack_dp.at[i], device)
        total = total + pack_dp[i]
    pack_one[...] = total
    for i, device in enumerate(chip_peers):
        packs.go(7 + i, pack_one, pack_chip.at[i], device)
    gate_up[:A_ROWS, :] = xs[0].add()
    o_y.add(o_two)
    xs[2].start(o_two, o_xland)
    made = xs[1].add()
    gate_up[A_ROWS:, :] = made[: 2 * UNITS - A_ROWS]
    down[...] = made[2 * UNITS - A_ROWS :]
    for i, device in enumerate(chip_peers):
        packs.take(7 + i, pack_chip.at[i], device)
        total = jnp.concatenate([total[:4] + pack_chip[i, :4, :], total[4:]], axis=0)
    pack_two[...] = total
    for i, device in enumerate(z_peers):
        packs.go(10 + i, pack_two, pack_z.at[i], device)
    v_y.add(v_two)
    xs[4].start(v_two, v_xland)
    q_z.add(q_two)
    xs[3].start(q_two, q_xland)
    output[...] = xs[2].add()
    own_bias = total[4:5]
    for i, device in enumerate(z_peers):
        packs.take(10 + i, pack_z.at[i], device)
        total = total + pack_z[i]
    own_bias = own_bias + pack_z[0, 5:6, :]
    dp, tensor = lax.axis_index("dp"), lax.axis_index("tensor")
    norms[...] = pltpu.roll(total[:, :256], 256 - tensor * 16, 1)[:, :128]
    own_bias = pltpu.roll(jnp.broadcast_to(own_bias, (8, 384)), 384 - dp * 8, 1)
    for i in range(6):
        bias_grad[i : i + 1, :] = own_bias[0:1, i * HD : i * HD + 8]
    heads[2] = xs[4].add()
    made = xs[3].add()
    heads[0] = made[:, :128]
    heads[1] = made[:, 128:]
    packs.finish()
    for job in [a, b, o, o_y, q, q_z, v, v_y] + xs:
        job.copies.finish()


def close_call(*args):
    def block(*lead):
        return pltpu.VMEM(lead, BF)

    return pl.pallas_call(
        close_kernel,
        out_shape=(
            shape((OWN, D), F32),
            shape((OWN, D), F32),
            shape((8, 128), F32),
            shape((6, 8), F32),
            shape((2 * UNITS, 256), F32),
            shape((UNITS, 256), F32),
            shape((128, 256), F32),
            shape((3, 256, 128), F32),
        ),
        in_specs=[IN_VMEM] * 17 + [ANYWHERE] * 4,
        out_specs=(IN_VMEM,) * 8,
        scratch_shapes=[
            pltpu.VMEM((2, 128, LEN), BF),
            pltpu.VMEM((2, LEN, 128), F32),
            pltpu.VMEM((2, LEN, 128), F32),
            pltpu.VMEM((LEN, 768), BF),
            pltpu.VMEM((2 * PAD, D), BF),
            pltpu.VMEM((768, D), BF),
            pltpu.VMEM((2 * PAD, LEN), BF),
            pltpu.VMEM((D, LEN), BF),
            pltpu.VMEM((D, 768), BF),
            pltpu.VMEM((8, 768), F32),
            block(2, A_ROWS, 256), block(2, A_ROWS, 256),
            block(3, 2, B_ROWS, 256), block(2, B_ROWS, 256),
            block(128, D), block(128, D), block(3, 2, 128, 256), block(2, 128, 256),
            block(4, 256, Q_LANES), block(2, 256, Q_LANES), block(2, 256, Q_LANES),
            block(D, V_LANES), block(D, V_LANES), block(3, 2, 256, V_LANES), block(2, 256, V_LANES),
            block(A_ROWS, 256), block(B_ROWS, 256), block(128, 256), block(256, Q_LANES), block(256, V_LANES),
            *[pltpu.VMEM(lead + (8, 384), F32) for lead in ((8,), (7,), (), (3,), (), (3,))],
            *Scatter.scratch(),
            *Scatter.again(),
            *SumY.scratch((256, Q_LANES)),
            *sems(2, 6, 8, 6, 12, 2, 8, 6, 5, 13),
            DMA((4,)),
        ],
        compiler_params=params(3),
        cost_estimate=cost(25 * 10**9, 60 * 2**20),
        name="close",
    )(*args)


def per_device(
    tokens,
    segments,
    first_gain,
    first_shift,
    heads_weight,
    heads_bias,
    output_weight,
    second_gain,
    second_shift,
    gate_up_weight,
    down_weight,
    cotangent,
):
    (
        first_all, cot_all, query, keys, values, attended, log_sum, residual, second_all, hidden, grads,
        wh, wo, wg, wd, gains, cos, sin_up, sin_down, lowest,
    ) = forward_call(
        tokens,
        cotangent,
        segments,
        *[v.reshape(1, 256) for v in (first_gain, first_shift, second_gain, second_shift)],
        heads_weight.transpose(1, 0, 2),
        heads_bias,
        output_weight,
        gate_up_weight.transpose(1, 2, 0),
        down_weight,
    )
    residual_grad, attended_grad, sums_two, a, b, grad_out = back_call(
        residual, cotangent, gains, grads, second_all, hidden, cot_all, wo, wg, attended
    )
    mixed, grad_tokens, norms, bias_grad, gate_up, down, output, heads = close_call(
        query, keys, values, attended_grad, log_sum, cos, sin_up, sin_down, lowest,
        residual, residual_grad, tokens, gains, sums_two, a, b, grad_out, hidden, first_all, wd, wh,
    )
    return (
        mixed,
        grad_tokens,
        norms[0, :16],
        norms[1, :16],
        heads.transpose(1, 0, 2),
        bias_grad.reshape(3, 2, 8),
        output,
        norms[2, :16],
        norms[3, :16],
        gate_up.reshape(2, UNITS, 256).transpose(2, 0, 1),
        down,
    )


ALL = ("dp", "tensor")


def solution(mesh):
    return jax.shard_map(
        per_device,
        mesh=mesh,
        in_specs=(
            P(ALL, None),
            P("dp", None),
            P("dp"),
            P("dp"),
            P("dp", None, "tensor"),
            P(None, "tensor", "dp"),
            P("tensor", "dp"),
            P("dp"),
            P("dp"),
            P("dp", None, "tensor"),
            P("tensor", "dp"),
            P(ALL, None),
        ),
        out_specs=(
            P(ALL, None),
            P(ALL, None),
            P(ALL),
            P(ALL),
            P("dp", None, "tensor"),
            P(None, "tensor", "dp"),
            P("tensor", "dp"),
            P(ALL),
            P(ALL),
            P("dp", None, "tensor"),
            P("tensor", "dp"),
        ),
        check_vma=False,
    )
```

```python
import functools
import math

import jax
import jax.numpy as jnp
from jax import lax
from jax.experimental import pallas as pl
from jax.experimental.pallas import tpu as pltpu
from jax.sharding import PartitionSpec as P

D = 2048
HD = 64
ROT = 16
WINDOW = 512
LEN = 1024
OWN = 128
HALF = OWN // 2
CHIP = 2 * OWN
UNITS = 352
PAD = 384
QB = 256

NORM_EPS = 1e-05
BASE_FREQ = 10000.0
FAR_NEGATIVE = -1e30
BF = jnp.bfloat16
F32 = jnp.float32
MESH = pl.DeviceIdType.MESH
VMEM_LIMIT = 62 * 2**20
DMA = pltpu.SemaphoreType.DMA


def spot(z, x, c):
    return (z % 2) * 4 + x * 2 + c


class Near:
    def __init__(self):
        t = lax.axis_index("tensor")
        z, x, c = t // 4, (t // 2) % 2, t % 2
        oz = (z // 2) * 2 + (z + 1) % 2
        ox, oc = 1 - x, 1 - c
        self.c, self.oc = c, oc
        self.me = spot(z, x, c)
        self.dev = {
            "x": {"tensor": z * 4 + ox * 2 + c},
            "z": {"tensor": oz * 4 + x * 2 + c},
            "s": {"tensor": z * 4 + x * 2 + oc},
        }
        self.same = {"o": spot(z, x, c), "x": spot(z, ox, c), "z": spot(oz, x, c), "d": spot(oz, ox, c)}
        self.other = {
            "o": spot(z, x, oc),
            "x": spot(z, ox, oc),
            "z": spot(oz, x, oc),
            "d": spot(oz, ox, oc),
        }
        self.chip = {"o": (z % 2) * 2 + x, "x": (z % 2) * 2 + ox, "z": (oz % 2) * 2 + x, "d": (oz % 2) * 2 + ox}


def remote(src, dst, send, recv, device):
    return pltpu.make_async_remote_copy(
        src_ref=src, dst_ref=dst, send_sem=send, recv_sem=recv, device_id=device, device_id_type=MESH
    )


def greet(devices):
    barrier = pltpu.get_barrier_semaphore()
    for device in devices:
        pl.semaphore_signal(barrier, inc=1, device_id=device, device_id_type=MESH)
    pl.semaphore_wait(barrier, len(devices))


def block_rows(block, half=None):
    if half is None:
        return pl.ds(pl.multiple_of(block * OWN, OWN), OWN)
    return pl.ds(pl.multiple_of(block * OWN + half * HALF, HALF), HALF)


def chip_rows(chip):
    return pl.ds(pl.multiple_of(chip * CHIP, CHIP), CHIP)


class Gather:
    COPIES = 13

    def __init__(self, near, buf, send, recv):
        self.near, self.buf, self.send, self.recv = near, buf, send, recv
        self.sent = []

    def copy(self, index, block, half, to):
        view = self.buf.at[block_rows(block, half)]
        return remote(view, view, self.send.at[index], self.recv.at[index], self.near.dev[to])

    def go(self, index, block, half, to):
        copy = self.copy(index, block, half, to)
        copy.start()
        self.sent.append(copy)

    def take(self, index, block, half, to="s"):
        self.copy(index, block, half, to).wait_recv()

    def start(self):
        me = self.near.me
        self.go(0, me, 0, "z")
        self.go(1, me, 1, "x")
        self.go(4, me, None, "s")
        self.go(2, me, 0, "x")
        self.go(3, me, 1, "z")

    def first(self):
        same = self.near.same
        self.take(0, same["z"], 0)
        self.go(5, same["z"], 0, "x")
        self.go(7, same["z"], 0, "s")
        self.take(1, same["x"], 1)
        self.go(6, same["x"], 1, "z")
        self.go(8, same["x"], 1, "s")

    def second(self):
        same = self.near.same
        self.take(2, same["x"], 0)
        self.go(9, same["x"], 0, "s")
        self.take(3, same["z"], 1)
        self.go(10, same["z"], 1, "s")

    def third(self):
        same = self.near.same
        self.take(5, same["d"], 0)
        self.go(11, same["d"], 0, "s")
        self.take(6, same["d"], 1)
        self.go(12, same["d"], 1, "s")

    def own_chip(self):
        self.take(4, self.near.other["o"], None)

    def x_chip(self):
        self.take(8, self.near.other["x"], 1)
        self.take(9, self.near.other["x"], 0)

    def z_chip(self):
        self.take(7, self.near.other["z"], 0)
        self.take(10, self.near.other["z"], 1)

    def d_chip(self):
        self.take(11, self.near.other["d"], 0)
        self.take(12, self.near.other["d"], 1)

    def finish(self):
        for copy in self.sent:
            copy.wait_send()

    def run(self, use):
        self.own_chip()
        use("o")
        self.first()
        self.second()
        self.x_chip()
        use("x")
        self.third()
        self.z_chip()
        use("z")
        self.d_chip()
        use("d")


class Scatter:
    COPIES = 10

    @staticmethod
    def scratch(width=D):
        return [
            pltpu.VMEM((CHIP, width), F32),
            pltpu.VMEM((4, OWN, width), F32),
            pltpu.VMEM((4, OWN, width), BF),
            pltpu.VMEM((4, OWN, width), BF),
            pltpu.VMEM((OWN, width), BF),
            pltpu.VMEM((4, HALF, width), BF),
            pltpu.VMEM((2, HALF, width), BF),
            pltpu.VMEM((4, HALF, width), BF),
            DMA((Scatter.COPIES,)),
            DMA((Scatter.COPIES,)),
        ]

    @staticmethod
    def again(width=D):
        return [
            pltpu.VMEM((4, OWN, width), BF),
            pltpu.VMEM((2, HALF, width), BF),
            pltpu.VMEM((4, HALF, width), BF),
            DMA((Scatter.COPIES,)),
            DMA((Scatter.COPIES,)),
        ]

    @staticmethod
    def second(refs, more):
        return list(refs[:3]) + [more[0]] + list(refs[4:6]) + list(more[1:])

    KEYS = ("d", "z", "x", "o")

    def __init__(self, near, refs):
        self.near = near
        (
            self.part,
            self.mine,
            self.core_out,
            self.core_in,
            self.far_out,
            self.out,
            self.through,
            self.last,
            self.send,
            self.recv,
        ) = refs
        self.sent = []

    def copy(self, index, src, dst, to):
        return remote(src, dst, self.send.at[index], self.recv.at[index], self.near.dev[to])

    def go(self, index, src, dst, to):
        copy = self.copy(index, src, dst, to)
        copy.start()
        self.sent.append(copy)

    def take(self, index, dst, to="s"):
        self.copy(index, dst, dst, to).wait_recv()

    def produce(self, key, make):
        i = self.KEYS.index(key)
        make(self.near.chip[key])
        self.core_out[i] = self.part[block_rows(self.near.oc), :].astype(BF)
        self.go(i, self.core_out.at[i], self.core_in.at[i], "s")
        self.mine[i] = self.part[block_rows(self.near.c), :]

    def join(self, key):
        i = self.KEYS.index(key)
        self.take(i, self.core_in.at[i])

    def summed(self, key, half):
        i = self.KEYS.index(key)
        rows = slice(half * HALF, (half + 1) * HALF)
        return self.mine[i, rows, :] + self.core_in[i, rows, :].astype(F32)

    def far(self):
        self.join("d")
        self.far_out[:HALF, :] = self.summed("d", 0).astype(BF)
        self.go(4, self.far_out.at[pl.ds(0, HALF)], self.through.at[0], "z")
        self.far_out[HALF:, :] = self.summed("d", 1).astype(BF)
        self.go(5, self.far_out.at[pl.ds(HALF, HALF)], self.through.at[1], "x")

    def z_direct(self):
        self.join("z")
        self.out[0] = self.summed("z", 0).astype(BF)
        self.go(6, self.out.at[0], self.last.at[0], "z")

    def x_direct(self):
        self.join("x")
        self.out[1] = self.summed("x", 1).astype(BF)
        self.go(7, self.out.at[1], self.last.at[1], "x")

    def relays(self):
        self.take(4, self.through.at[0])
        self.out[2] = (self.summed("x", 0) + self.through[0].astype(F32)).astype(BF)
        self.go(8, self.out.at[2], self.last.at[2], "x")
        self.take(5, self.through.at[1])
        self.out[3] = (self.summed("z", 1) + self.through[1].astype(F32)).astype(BF)
        self.go(9, self.out.at[3], self.last.at[3], "z")

    def result(self):
        self.join("o")
        for index in range(4):
            self.take(6 + index, self.last.at[index])
        first = self.summed("o", 0) + self.last[0].astype(F32) + self.last[2].astype(F32)
        second = self.summed("o", 1) + self.last[1].astype(F32) + self.last[3].astype(F32)
        for copy in self.sent:
            copy.wait_send()
        self.sent = []
        return first, second

    def run(self, make):
        self.produce("d", make)
        self.produce("z", make)
        self.far()
        self.produce("x", make)
        self.z_direct()
        self.x_direct()
        self.relays()
        self.produce("o", make)
        return self.result()


def dot(left, right):
    return jnp.dot(left, right, preferred_element_type=F32)


def dot_nt(left, right):
    return lax.dot_general(left, right, (((1,), (1,)), ((), ())), preferred_element_type=F32)


def dot_tn(left, right):
    return lax.dot_general(left, right, (((0,), (0,)), ((), ())), preferred_element_type=F32)


def layer_norm_parts(values):
    centre = values - jnp.mean(values, axis=-1, keepdims=True)
    inverse = lax.rsqrt(jnp.mean(centre * centre, axis=-1, keepdims=True) + NORM_EPS)
    return (centre * inverse, inverse)


def norm_back(upstream, normed, inverse, gain):
    scaled = upstream * gain
    inner = (
        scaled
        - jnp.mean(scaled, axis=-1, keepdims=True)
        - normed * jnp.mean(scaled * normed, axis=-1, keepdims=True)
    )
    return (
        inner * inverse,
        jnp.sum(upstream * normed, axis=0, keepdims=True),
        jnp.sum(upstream, axis=0, keepdims=True),
    )


def params(collective=None):
    if collective is None:
        return pltpu.CompilerParams(vmem_limit_bytes=VMEM_LIMIT)
    return pltpu.CompilerParams(
        collective_id=collective, has_side_effects=True, vmem_limit_bytes=VMEM_LIMIT
    )


def cost(flops, moved):
    return pl.CostEstimate(flops=flops, bytes_accessed=moved, transcendentals=0)


IN_VMEM = pl.BlockSpec(memory_space=pltpu.VMEM)
ANYWHERE = pl.BlockSpec(memory_space=pl.ANY)


def shape(dims, dtype):
    return jax.ShapeDtypeStruct(dims, dtype)


def copy_all(pairs, sems):
    copies = [pltpu.make_async_copy(src, dst, sems.at[i]) for i, (src, dst) in enumerate(pairs)]
    for copy in copies:
        copy.start()
    return copies


class Far:
    def __init__(self):
        t, dp = lax.axis_index("tensor"), lax.axis_index("dp")
        self.h, self.y = dp // 4, dp % 4
        self.over = {"dp": (1 - self.h) * 4 + self.y}
        self.partner = {"tensor": (3 - t // 4) * 4 + t % 4}
        self.ring = {k: {"dp": self.h * 4 + (self.y + k) % 4} for k in (1, 2, 3)}

    def dp(self, k, h):
        return ((self.h + h) % 2) * 4 + (self.y - k + 4) % 4

    def dp_of(self, i):
        return (self.h + i // 4) % 2 * 4 + (self.y + i % 4) % 4

    def span(self, k, h):
        return pl.ds(pl.multiple_of(self.dp(k, h) * 256, 256), 256)

    def ahead(self, k, h):
        return pl.ds(pl.multiple_of((h * 4 + (self.y + k) % 4) * 256, 256), 256)


class Copies:
    def __init__(self, send, recv):
        self.send, self.recv, self.sent = send, recv, []

    def go(self, index, src, dst, device):
        copy = remote(src, dst, self.send.at[index], self.recv.at[index], device)
        copy.start()
        self.sent.append(copy)

    def take(self, index, dst, device):
        remote(dst, dst, self.send.at[index], self.recv.at[index], device).wait_recv()

    def finish(self):
        for copy in self.sent:
            copy.wait_send()
        self.sent = []


class Ring:
    def __init__(self, far, n, place, send, recv):
        self.far, self.n, self.place = far, n, place
        self.copies = Copies(send, recv)

    def start(self, j, src=None):
        own = self.place(0, j)
        src = own if src is None else src
        self.copies.go(j, src, own, self.far.ring[1])
        self.copies.go(self.n + j, src, own, self.far.ring[3])

    def relay(self, j):
        if j < self.n // 2:
            view = self.place(1, j)
            self.copies.take(j, view, self.far.ring[1])
            self.copies.go(2 * self.n + j, view, view, self.far.ring[1])
        else:
            view = self.place(3, j)
            self.copies.take(self.n + j, view, self.far.ring[3])
            self.copies.go(2 * self.n + j, view, view, self.far.ring[3])

    def near(self, j):
        if j < self.n // 2:
            self.copies.take(self.n + j, self.place(3, j), self.far.ring[3])
        else:
            self.copies.take(j, self.place(1, j), self.far.ring[1])

    def done(self, j):
        self.near(j)
        self.copies.take(2 * self.n + j, self.place(2, j), self.far.ring[1])

    def finish(self, near=True):
        for j in range(self.n):
            if near:
                self.near(j)
            self.copies.take(2 * self.n + j, self.place(2, j), self.far.ring[1])
        self.copies.finish()


class SumY:
    COPIES = 12

    @staticmethod
    def scratch(dims):
        return [
            pltpu.VMEM((4,) + dims, BF),
            pltpu.VMEM((4,) + dims, BF),
            pltpu.VMEM((2, 4) + dims, BF),
        ]

    def __init__(self, far, block, refs, send, recv):
        self.far, self.block = far, block
        self.through, self.out, self.last = refs
        self.copies = Copies(send, recv)

    def to(self, j):
        return self.far.ring[1] if j < 2 else self.far.ring[3]

    def start(self, s):
        for j in (s, 2 + s):
            self.copies.go(j, self.block(2, j), self.through.at[j], self.to(j))
        self.copies.go(4 + 2 + s, self.block(1, 2 + s), self.last.at[0, 2 + s], self.far.ring[1])
        self.copies.go(8 + s, self.block(3, s), self.last.at[1, s], self.far.ring[3])

    def relay(self, s):
        for j, k, side in ((s, 1, 0), (2 + s, 3, 1)):
            self.copies.take(j, self.through.at[j], self.to(j))
            self.out[j] = (self.block(k, j)[...].astype(F32) + self.through[j].astype(F32)).astype(BF)
            self.copies.go(4 + side * 4 + j, self.out.at[j], self.last.at[side, j], self.far.ring[k])

    def add(self, out):
        for j in range(4):
            total = self.block(0, j)[...].astype(F32)
            for side, k in ((0, 1), (1, 3)):
                self.copies.take(4 + side * 4 + j, self.last.at[side, j], self.far.ring[k])
                total = total + self.last[side, j].astype(F32)
            out[j] = total.astype(BF)


class PairZ:
    COPIES = 2

    def __init__(self, far, send, recv):
        self.far, self.copies = far, Copies(send, recv)

    def start(self, sums, land):
        self.sums, self.land = sums, land
        for h in range(2):
            self.copies.go(h, sums.at[h * 2 + 1], land.at[h], self.far.partner)

    def add(self, out):
        for h in range(2):
            self.copies.take(h, self.land.at[h], self.far.partner)
            out[h] = (self.sums[h * 2].astype(F32) + self.land[h].astype(F32)).astype(BF)


class SumZ:
    COPIES = 8

    def __init__(self, far, block, land, out, send, recv):
        self.far, self.block, self.land, self.out = far, block, land, out
        self.copies = Copies(send, recv)

    def start(self, k, h):
        self.copies.go(k * 2 + h, self.block(k, h, 1), self.land(k, h), self.far.partner)

    def start_all(self):
        for k in (2, 1, 3, 0):
            for h in range(2):
                self.start(k, h)

    def add(self):
        for k in (2, 1, 3, 0):
            for h in range(2):
                self.copies.take(k * 2 + h, self.land(k, h), self.far.partner)
                total = self.block(k, h, 0)[...].astype(F32) + self.land(k, h)[...].astype(F32)
                self.out(k, h)[...] = total.astype(BF)


class RingY:
    COPIES = 6

    def __init__(self, far, block, land, send, recv):
        self.far, self.block, self.land = far, block, land
        self.copies = Copies(send, recv)

    def start(self):
        for k in (2, 1, 3):
            for h in range(2):
                self.copies.go((k - 1) * 2 + h, self.block(k, h), self.land.at[k - 1, h], self.far.ring[k])

    def add(self, out):
        for h in range(2):
            total = self.block(0, h)[...].astype(F32)
            for k in (1, 2, 3):
                self.copies.take((k - 1) * 2 + h, self.land.at[k - 1, h], self.far.ring[k])
                total = total + self.land[k - 1, h].astype(F32)
            out[h] = total.astype(BF)


class SumX:
    def __init__(self, far, send, recv):
        self.far, self.copies = far, Copies(send, recv)

    def start(self, sums, land):
        self.sums, self.land = sums, land
        self.copies.go(0, sums.at[1 - self.far.h], land, self.far.over)

    def add(self):
        self.copies.take(0, self.land, self.far.over)
        return self.sums[self.far.h].astype(F32) + self.land[...].astype(F32)


def rotary_tables(starts, cos_out, up_out, down_out):
    index = lax.broadcasted_iota(jnp.int32, (8, LEN), 1)
    power = lax.broadcasted_iota(jnp.int32, (8, LEN), 0).astype(F32)
    angles = (index - starts).astype(F32) * jnp.exp(power * (-2.0 * math.log(BASE_FREQ) / ROT))
    cosine, sine = jnp.cos(angles), jnp.sin(angles)
    none, rest = jnp.zeros((8, LEN), F32), jnp.zeros((HD - ROT, LEN), F32)
    cos_out[...] = jnp.concatenate([cosine, cosine, rest + 1.0] * 2, axis=0).T
    up_out[...] = jnp.concatenate([-sine, none, rest] * 2, axis=0).T
    down_out[...] = jnp.concatenate([none, sine, rest] * 2, axis=0).T


def document_starts(seg):
    index = lax.broadcasted_iota(jnp.int32, (8, LEN), 1)
    new = (index == 0) | (pltpu.roll(seg, 1, 1) != seg)
    starts = jnp.where(new, index, 0)
    step = 1
    while step < LEN:
        starts = jnp.maximum(starts, jnp.where(index >= step, pltpu.roll(starts, step, 1), 0))
        step *= 2
    return starts


def roll_rotate(values, cos, sin_up, sin_down):
    return (
        values * cos + pltpu.roll(values, 128 - ROT // 2, 1) * sin_up + pltpu.roll(values, ROT // 2, 1) * sin_down
    )


def window(block):
    start = max(0, block * QB - WINDOW)
    return start, (block + 1) * QB


def mask_bias(lowest, start, stop, block):
    keys = lax.broadcasted_iota(jnp.int32, (stop - start, QB), 0) + start
    queries = lax.broadcasted_iota(jnp.int32, (stop - start, QB), 1) + block * QB
    return jnp.where((keys <= queries) & (keys >= lowest), 0.0, FAR_NEGATIVE)


def head_lanes(rows, head):
    lanes = lax.broadcasted_iota(jnp.int32, (rows, 128), 1)
    return (lanes >= HD) if head else (lanes < HD)


def silu_parts(gate, up, grad):
    sig = 1.0 / (1.0 + jnp.exp(-gate))
    silu = gate * sig
    return silu * up, grad * up * sig * (1.0 + gate * (1.0 - sig)), grad * silu


def sems(*counts):
    return [DMA((n,)) for n in counts for _ in range(2)]


class Quad:
    def __init__(self, far, place, send, recv):
        self.far, self.place = far, place
        self.copies = Copies(send, recv)

    def over(self, src):
        self.copies.go(0, src, self.place(0, 0), self.far.over)

    def partner(self, src):
        self.copies.go(1, src, self.place(0, 1), self.far.partner)

    def take_over(self):
        self.copies.take(0, self.place(0, 2), self.far.over)
        self.copies.go(2, self.place(0, 2), self.place(0, 3), self.far.partner)

    def take_partner(self):
        self.copies.take(1, self.place(0, 1), self.far.partner)

    def take_last(self):
        self.copies.take(2, self.place(0, 3), self.far.partner)


class Across:
    def __init__(self, far, place, send, recv):
        self.far, self.place = far, place
        self.copies = Copies(send, recv)

    def start(self, k, h, src=None):
        src = self.place(k, h, 0) if src is None else src
        self.copies.go(k * 2 + h, src, self.place(k, h, 1), self.far.partner)

    def finish(self):
        for k in range(4):
            for h in range(2):
                self.copies.take(k * 2 + h, self.place(k, h, 1), self.far.partner)
        self.copies.finish()


class ZLast:
    def __init__(self, far, place, refs):
        x_send, x_recv, r_send, r_recv, z_send, z_recv = refs
        self.far, self.place = far, place
        self.copies = Copies(x_send, x_recv)
        self.ring = Ring(far, 2, lambda k, j: place(k, j, 0), r_send, r_recv)
        self.across = Across(far, place, z_send, z_recv)

    def over(self, src):
        self.src = src
        self.copies.go(0, src, self.place(0, 0, 0), self.far.over)

    def take_over(self):
        self.copies.take(0, self.place(0, 1, 0), self.far.over)

    def partner(self):
        self.across.start(0, 0, self.src)
        self.across.start(0, 1)

    def start(self):
        self.ring.start(0, self.src)
        self.ring.start(1)

    def ring_done(self):
        self.ring.finish(near=False)
        self.across.start(2, 0)
        self.across.start(2, 1)

    def relay(self):
        self.ring.relay(0)
        self.ring.relay(1)
        self.ring.near(0)
        self.ring.near(1)
        for k in (1, 3):
            self.across.start(k, 0)
            self.across.start(k, 1)

    def finish(self):
        self.across.finish()
        self.copies.finish()


Q_LANES = 256
V_LANES = 384 - Q_LANES
UP_ROWS = 176


def bias_lanes(bias, dp):
    j = lax.broadcasted_iota(jnp.int32, (8, 384), 0)
    lane = lax.broadcasted_iota(jnp.int32, (8, 384), 1)
    pick = jnp.where(lane % HD == dp * 8 + j, 1.0, 0.0).astype(BF)
    total = jnp.zeros((1, 384), F32)
    lane = lax.broadcasted_iota(jnp.int32, (1, 384), 1)
    for p in range(3):
        for h in range(2):
            made = dot(bias[p, h : h + 1, :].astype(BF), pick)
            total = total + jnp.where(lane // HD == p * 2 + h, made, 0.0)
    return total


def forward_kernel(
    tok, cot, seg, gain_one, shift_one, gain_two, shift_two, head_in, bias_in, out_in, gate_in, down_in,
    first_out, cot_out, query_out, keys_out, values_out, attended_out, log_sum, residual_out, second_out, hidden_out,
    grads_out, wh_out, wo_out, wg_out, wd_out, gains, cos_out, up_out, sdown_out, lowest,
    fa, ca, wv, wo, wd, wg, query, keys, values, attended, vt, hg, second, hidden, grads, gbuf, gbuf_two, bias,
    small, head, outw, gate, down, wh_turned, wo_turned, first_turned, residual, cos, sin_up, sin_down, *rest,
):
    scatter_refs, rest = rest[:10], rest[10:]
    (
        ga_send, ga_recv, gc_send, gc_recv, gs_send, gs_recv, sm_send, sm_recv, sr_send, sr_recv,
        hq_send, hq_recv, hr_send, hr_recv, gq_send, gq_recv, gr_send, gr_recv, uq_send, uq_recv, ur_send, ur_recv,
    ) = rest[:22]
    out_refs, down_refs, tail_refs, value_refs, (out_sem,) = rest[22:28], rest[28:34], rest[34:40], rest[40:46], rest[46:]
    near, far = Near(), Far()
    greet([near.dev["x"], near.dev["z"], near.dev["s"], far.over, far.partner, far.ring[1], far.ring[3]])
    written = []

    def write(src, dst):
        copy = pltpu.make_async_copy(src, dst, out_sem.at[len(written)])
        copy.start()
        written.append(copy)

    def head_at(k, j):
        return wv.at[j % 2, far.span(k, j // 2), pl.ds(0, Q_LANES)]

    def value_at(k, h, s):
        return wv.at[s, far.span(k, h), pl.ds(Q_LANES, V_LANES)]

    def gate_at(k, j):
        return wg.at[(j % 2) * 2, pl.ds(0, UNITS), far.span(k, j // 2)]

    def up_at(k, j):
        return wg.at[(j % 2) * 2 + 1, pl.ds(0, UP_ROWS), far.span(k, j // 2)]

    def tail_at(k, h, s):
        return wg.at[s * 2 + 1, pl.ds(UP_ROWS, UNITS - UP_ROWS), far.span(k, h)]

    def out_at(k, h, s):
        return wo.at[pl.ds(s * 128, 128), far.span(k, h)]

    def down_at(k, h, s):
        return wd.at[pl.ds(s * PAD, UNITS), far.span(k, h)]

    smalls = Copies(sm_send, sm_recv)
    small_ring = Ring(far, 2, lambda k, j: gbuf.at[far.dp(k, j)], sr_send, sr_recv)
    head_quad, head_ring = Quad(far, head_at, hq_send, hq_recv), Ring(far, 4, head_at, hr_send, hr_recv)
    gate_quad, gate_ring = Quad(far, gate_at, gq_send, gq_recv), Ring(far, 4, gate_at, gr_send, gr_recv)
    up_quad, up_ring = Quad(far, up_at, uq_send, uq_recv), Ring(far, 4, up_at, ur_send, ur_recv)
    outs, downs, tails = ZLast(far, out_at, out_refs), ZLast(far, down_at, down_refs), ZLast(far, tail_at, tail_refs)
    vals = ZLast(far, value_at, value_refs)
    firsts = Gather(near, fa, ga_send, ga_recv)
    cots = Gather(near, ca, gc_send, gc_recv)
    seconds = Gather(near, second, gs_send, gs_recv)

    small[0:1, :256] = gain_one[...].astype(BF).astype(F32)
    small[1:2, :256] = shift_one[...].astype(BF).astype(F32)
    small[2:3, :256] = gain_two[...].astype(BF).astype(F32)
    small[3:4, :256] = shift_two[...].astype(BF).astype(F32)
    small[4:5, :] = bias_lanes(bias_in, lax.axis_index("dp"))
    for p in range(3):
        head[:, p * 128 : (p + 1) * 128] = head_in[p].astype(BF)
    smalls.go(0, small, gbuf.at[far.dp(0, 0)], far.over)
    small_ring.start(0, small)
    own_qk, own_v = head.at[:, pl.ds(0, Q_LANES)], head.at[:, pl.ds(Q_LANES, V_LANES)]
    head_quad.over(own_qk)
    head_quad.partner(own_qk)
    vals.over(own_v)
    vals.ring.start(0, own_v)
    head_ring.start(0, own_qk)
    gbuf[far.dp(0, 0)] = small[...]
    normed, _ = layer_norm_parts(tok[...].astype(F32))
    smalls.take(0, gbuf.at[far.dp(0, 1)], far.over)
    small_ring.start(1)
    vals.take_over()
    vals.ring.start(1)
    vals.partner()
    head_quad.take_over()
    head_ring.start(2)
    small_ring.relay(0)
    small_ring.relay(1)
    small_ring.finish()
    for d in range(8):
        gains[:, d * 256 : (d + 1) * 256] = gbuf[d, :, :256]
    first = normed * gains[0:1, :] + gains[1:2, :]
    fa[block_rows(near.me), :] = first.astype(BF)
    firsts.start()
    vals.relay()
    head_ring.relay(0)
    head_ring.relay(2)
    head_quad.take_partner()
    head_ring.start(1)
    head_quad.take_last()
    head_ring.start(3)
    smalls.go(1, gbuf, gbuf_two, far.partner)
    outw[...] = out_in[...].astype(BF)
    down[...] = down_in[...].astype(BF)
    gate[...] = gate_in[...].astype(BF)
    up_own, tail_own = gate.at[1, pl.ds(0, UP_ROWS)], gate.at[1, pl.ds(UP_ROWS, UNITS - UP_ROWS)]
    outs.over(outw)
    gate_quad.partner(gate.at[0])
    up_quad.partner(up_own)
    wv[0, far.span(0, 0), :] = head[...]
    vals.ring_done()
    wo[:128, far.span(0, 0)] = outw[...]
    wd[:UNITS, far.span(0, 0)] = down[...]
    wg[0, :UNITS, far.span(0, 0)] = gate[0]
    wg[1, :UNITS, far.span(0, 0)] = gate[1]
    for i in range(4):
        wg[i, UNITS:, :] = jnp.zeros((PAD - UNITS, D), BF)
    for i in range(2):
        wd[i * PAD + UNITS : (i + 1) * PAD, :] = jnp.zeros((PAD - UNITS, D), BF)
    starts = document_starts(jnp.broadcast_to(seg[pl.ds(lax.axis_index("tensor") // 8, 1), :], (8, LEN)))
    index = lax.broadcasted_iota(jnp.int32, (8, LEN), 1)
    lowest[...] = jnp.maximum(starts, index - (WINDOW - 1))
    head_ring.relay(1)
    head_ring.relay(3)
    firsts.first()
    firsts.second()
    rotary_tables(starts, cos, sin_up, sin_down)
    for src, dst in ((cos, cos_out), (sin_up, up_out), (sin_down, sdown_out)):
        write(src, dst)
    smalls.take(1, gbuf_two, far.partner)
    bias[0:1, :384] = jnp.sum(gbuf[:, 4, :], axis=0, keepdims=True)
    bias[0:1, 384:] = jnp.sum(gbuf_two[:, 4, :], axis=0, keepdims=True)
    outs.take_over()
    outs.ring.start(0, outw)
    outs.ring.start(1)
    outs.partner()
    firsts.third()
    gate_quad.over(gate.at[0])
    up_quad.over(up_own)
    downs.over(down)
    tails.over(tail_own)
    head_ring.done(0)
    head_ring.done(2)

    def project(chip, s):
        rows = chip_rows(chip)
        c, up, down = cos[rows, :], sin_up[rows, :], sin_down[rows, :]
        lanes = slice(s * 128, (s + 1) * 128)
        made = dot(fa[rows, :], wv[s]) + bias[0:1, s * 384 : (s + 1) * 384]
        query[rows, lanes] = (roll_rotate(made[:, :128], c, up, down) * HD ** (-0.5)).astype(BF)
        keys[rows, lanes] = roll_rotate(made[:, 128:256], c, up, down).astype(BF)
        values[rows, lanes] = made[:, 256:].astype(BF)
        vt[chip, s] = made[:, 256:].T.astype(BF)

    def look(block, s):
        start, stop = window(block)
        rows = slice(block * QB, (block + 1) * QB)
        bias_t = mask_bias(lowest[0:1, rows], start, stop, block)
        lanes = slice(s * 128, (s + 1) * 128)
        q, k = query[rows, lanes], keys[start:stop, lanes]
        v_t = jnp.concatenate([vt[i, s] for i in range(start // CHIP, stop // CHIP)], axis=1)
        halves = []
        for head_id in range(2):
            q_one = jnp.where(head_lanes(QB, head_id), q, jnp.zeros_like(q))
            scores = dot_nt(k, q_one) + bias_t
            top = jnp.max(scores, axis=0, keepdims=True)
            weights = jnp.exp(scores - top)
            total = jnp.sum(weights, axis=0, keepdims=True)
            made = dot(v_t, weights.astype(BF))
            halves.append(made[head_id * HD : (head_id + 1) * HD] * (1.0 / total))
            log_sum[s * 2 + head_id : s * 2 + head_id + 1, rows] = top + jnp.log(total)
        attended[rows, lanes] = jnp.concatenate(halves, axis=0).T.astype(BF)

    firsts.own_chip()
    project(near.chip["o"], 0)
    firsts.x_chip()
    project(near.chip["x"], 0)
    firsts.z_chip()
    project(near.chip["z"], 0)
    firsts.d_chip()
    project(near.chip["d"], 0)
    ca[block_rows(near.me), :] = cot[...]
    cots.start()
    look(0, 0)
    downs.ring.start(0, down)
    tails.ring.start(0, tail_own)
    outs.relay()
    look(1, 0)
    look(2, 0)
    gate_quad.take_over()
    up_quad.take_over()
    downs.take_over()
    downs.ring.start(1)
    downs.partner()
    tails.take_over()
    tails.ring.start(1)
    tails.partner()
    look(3, 0)
    head_ring.done(1)
    head_ring.done(3)
    vals.across.finish()
    gate_ring.start(0, gate.at[0])
    gate_ring.start(2)
    for key in "oxzd":
        project(near.chip[key], 1)
    outs.ring_done()
    for src, dst in ((query, query_out), (keys, keys_out), (values, values_out)):
        write(src, dst)
    look(0, 1)
    gate_quad.take_partner()
    gate_ring.start(1)
    look(1, 1)
    downs.relay()
    tails.relay()
    gate_quad.take_last()
    gate_ring.start(3)
    cots.first()
    cots.second()
    look(2, 1)
    up_quad.take_partner()
    up_quad.take_last()
    look(3, 1)
    cots.third()
    outs.finish()
    scatter = Scatter(near, scatter_refs)

    def make(chip):
        rows = chip_rows(chip)
        scatter.part[...] = dot(attended[rows, :], wo[...])

    scatter.produce("d", make)
    scatter.produce("z", make)
    scatter.far()
    scatter.produce("x", make)
    scatter.z_direct()
    scatter.x_direct()
    up_ring.start(0, up_own)
    up_ring.start(1)
    up_ring.start(2)
    up_ring.start(3)
    scatter.relays()
    scatter.produce("o", make)
    downs.ring_done()
    tails.ring_done()
    write(attended, attended_out)
    wo_turned[...] = wo[...].T
    write(wo_turned, wo_out)
    gate_ring.relay(0)
    gate_ring.relay(1)
    gate_ring.relay(2)
    gate_ring.relay(3)
    cots.own_chip()
    cots.x_chip()
    cots.z_chip()
    cots.d_chip()
    write(ca, cot_out)
    one, two = scatter.result()
    residual[:HALF, :] = tok[:HALF, :].astype(F32) + one
    residual[HALF:, :] = tok[HALF:, :].astype(F32) + two
    write(residual, residual_out)
    normed, _ = layer_norm_parts(residual[...])
    second[block_rows(near.me), :] = (normed * gains[2:3, :] + gains[3:4, :]).astype(BF)
    seconds.start()
    for half in range(2):
        wh_turned[half * 384 : (half + 1) * 384, :] = wv[half].T
    write(wh_turned, wh_out)
    for chip in range(4):
        first_turned[:, chip * CHIP : (chip + 1) * CHIP] = fa[chip * CHIP : (chip + 1) * CHIP, :].T
    write(first_turned, first_out)
    for j in range(4):
        up_ring.relay(j)
    seconds.first()
    seconds.second()
    downs.finish()
    write(wd, wd_out)
    for chip in range(4):
        rows = slice(chip * CHIP, (chip + 1) * CHIP)
        hg[:, rows] = dot_nt(wd[...], ca[rows, :])
    seconds.third()
    gate_ring.finish()
    up_ring.finish()
    tails.finish()
    write(wg, wg_out)

    def use(key):
        chip = near.chip[key]
        rows = chip_rows(chip)
        for s in range(2):
            made = dot_nt(wg[s * 2 : s * 2 + 2].reshape(2 * PAD, D), second[rows, :])
            h, g, u = silu_parts(made[:PAD], made[PAD:], hg[s * PAD : (s + 1) * PAD, rows])
            hidden[s * PAD : (s + 1) * PAD, rows] = h.astype(BF)
            grads[s * 2 * PAD : s * 2 * PAD + PAD, rows] = g.astype(BF)
            grads[s * 2 * PAD + PAD : (s + 1) * 2 * PAD, rows] = u.astype(BF)
        write(second.at[rows], second_out.at[rows])
        write(hidden.at[:, rows], hidden_out.at[:, rows])
        write(grads.at[:, rows], grads_out.at[:, rows])

    seconds.own_chip()
    use("o")
    seconds.x_chip()
    use("x")
    seconds.z_chip()
    use("z")
    seconds.d_chip()
    use("d")
    for group in (smalls, head_quad.copies, head_ring.copies, gate_quad.copies, up_quad.copies, vals.copies, firsts, cots, seconds):
        group.finish()
    for copy in written:
        copy.wait()


def forward_call(*args):
    narrow = shape((LEN, 256), BF)
    return pl.pallas_call(
        forward_kernel,
        out_shape=(
            shape((D, LEN), BF),
            shape((LEN, D), BF),
            narrow,
            narrow,
            narrow,
            narrow,
            shape((8, LEN), F32),
            shape((OWN, D), F32),
            shape((LEN, D), BF),
            shape((2 * PAD, LEN), BF),
            shape((4 * PAD, LEN), BF),
            shape((768, D), BF),
            shape((D, 256), BF),
            shape((4, PAD, D), BF),
            shape((2 * PAD, D), BF),
            shape((8, D), F32),
            shape((LEN, 128), F32),
            shape((LEN, 128), F32),
            shape((LEN, 128), F32),
            shape((8, LEN), jnp.int32),
        ),
        in_specs=[IN_VMEM] * 12,
        out_specs=(ANYWHERE,) * 6 + (IN_VMEM,) + (ANYWHERE,) * 8 + (IN_VMEM,) + (ANYWHERE,) * 3 + (IN_VMEM,),
        scratch_shapes=[
            pltpu.VMEM((LEN, D), BF),
            pltpu.VMEM((LEN, D), BF),
            pltpu.VMEM((2, D, 384), BF),
            pltpu.VMEM((256, D), BF),
            pltpu.VMEM((2 * PAD, D), BF),
            pltpu.VMEM((4, PAD, D), BF),
            pltpu.VMEM((LEN, 256), BF),
            pltpu.VMEM((LEN, 256), BF),
            pltpu.VMEM((LEN, 256), BF),
            pltpu.VMEM((LEN, 256), BF),
            pltpu.VMEM((4, 2, 128, CHIP), BF),
            pltpu.VMEM((2 * PAD, LEN), F32),
            pltpu.VMEM((LEN, D), BF),
            pltpu.VMEM((2 * PAD, LEN), BF),
            pltpu.VMEM((4 * PAD, LEN), BF),
            pltpu.VMEM((8, 8, 384), F32),
            pltpu.VMEM((8, 8, 384), F32),
            pltpu.VMEM((8, 768), F32),
            pltpu.VMEM((8, 384), F32),
            pltpu.VMEM((256, 384), BF),
            pltpu.VMEM((128, 256), BF),
            pltpu.VMEM((2, UNITS, 256), BF),
            pltpu.VMEM((UNITS, 256), BF),
            pltpu.VMEM((768, D), BF),
            pltpu.VMEM((D, 256), BF),
            pltpu.VMEM((D, LEN), BF),
            pltpu.VMEM((OWN, D), F32),
            pltpu.VMEM((LEN, 128), F32),
            pltpu.VMEM((LEN, 128), F32),
            pltpu.VMEM((LEN, 128), F32),
            *Scatter.scratch(),
            *sems(*[Gather.COPIES] * 3, 2, 6, 3, 12, 3, 12, 3, 12, *[1, 6, 8] * 4),
            DMA((27,)),
        ],
        compiler_params=params(1),
        cost_estimate=cost(40 * 10**9, 80 * 2**20),
        name="forward",
    )(*args)


ROWS = 3 * UNITS
A_ROWS = 608
B_ROWS = ROWS - A_ROWS


def back_kernel(
    residual_in, cot_own_in, gains_in, grads_in, second_in, hidden_in, cot_in, wo_in, wg_in, attended_in,
    residual_grad_out, attended_grad_out, norm_sums, a_sum, b_sum_out, grad_out_out,
    wo, wg, branch, grads, second, hidden, cots, attended, parts, b_land,
    residual, cot, gains, residual_grad, attended_grad, b_sum, grad_out, *rest,
):
    scatter_refs, a_refs, rest = rest[:10], rest[10:13], rest[13:]
    ga_send, ga_recv, ay_send, ay_recv, bz_send, bz_recv, w_sem, o_sem = rest
    near, far = Near(), Far()
    load = copy_all(
        [
            (wg_in, wg),
            (grads_in, grads),
            (second_in, second),
            (hidden_in, hidden),
            (cot_in, cots),
            (wo_in, wo),
            (attended_in, attended),
            (residual_in, residual),
            (cot_own_in, cot),
            (gains_in, gains),
        ],
        w_sem,
    )
    greet([near.dev["x"], near.dev["z"], near.dev["s"], far.partner, far.ring[1], far.ring[3]])
    a_rows, b_rows = pl.ds(0, A_ROWS), pl.ds(A_ROWS, B_ROWS)
    a = SumY(far, lambda k, j: parts.at[j % 2, a_rows, far.ahead(k, j // 2)], a_refs, ay_send, ay_recv)
    b = SumZ(
        far,
        lambda k, h, s: parts.at[s, b_rows, far.ahead(k, h)],
        lambda k, h: b_land.at[:, far.ahead(k, h)],
        lambda k, h: b_sum.at[:, far.ahead(k, h)],
        bz_send,
        bz_recv,
    )
    scatter = Scatter(near, scatter_refs)

    def make(chip):
        scatter.part[...] = dot_tn(grads[:, chip_rows(chip)], wg[...].reshape(4 * PAD, D))

    def gate_part(s):
        start = s * 2 * PAD
        parts[s, :UNITS, :] = dot(grads[start : start + UNITS, :], second[...]).astype(BF)

    def up_part(s):
        start = s * 2 * PAD + PAD
        parts[s, UNITS : 2 * UNITS, :] = dot(grads[start : start + UNITS, :], second[...]).astype(BF)

    def down_part(s):
        start = s * PAD
        parts[s, 2 * UNITS :, :] = dot(hidden[start : start + UNITS, :], cots[...]).astype(BF)

    load[0].wait()
    load[1].wait()
    scatter.produce("d", make)
    scatter.produce("z", make)
    scatter.far()
    scatter.produce("x", make)
    scatter.z_direct()
    for copy in load[2:5]:
        copy.wait()
    up_part(1)
    scatter.x_direct()
    gate_part(1)
    a.start(1)
    scatter.relays()
    scatter.produce("o", make)
    down_part(1)
    b.start_all()
    gate_part(0)
    up_part(0)
    a.start(0)
    a.relay(1)
    first, second_half = scatter.result()
    for copy in load[7:]:
        copy.wait()
    normed, inverse = layer_norm_parts(residual[...])
    upstream = jnp.concatenate([first, second_half], axis=0)
    part, gain_sum, shift_sum = norm_back(upstream, normed, inverse, gains[2:3, :])
    made = cot[...].astype(F32) + part
    residual_grad[...] = made
    written = copy_all([(residual_grad, residual_grad_out)], o_sem.at[pl.ds(0, 1)])
    norm_sums[...] = jnp.concatenate([gain_sum, shift_sum] * 4, axis=0)
    branch[block_rows(near.me), :] = made.astype(BF)
    gather = Gather(near, branch, ga_send, ga_recv)
    gather.start()
    load[5].wait()
    load[6].wait()
    down_part(0)
    a.relay(0)

    def use(key):
        rows = chip_rows(near.chip[key])
        attended_grad[rows, :] = dot(branch[rows, :], wo[...]).astype(BF)

    gather.run(use)
    written += copy_all([(attended_grad, attended_grad_out)], o_sem.at[pl.ds(1, 1)])
    grad_out[...] = dot_tn(attended[...], branch[...]).astype(BF)
    written += copy_all([(grad_out, grad_out_out)], o_sem.at[pl.ds(2, 1)])
    gather.finish()
    b.add()
    written += copy_all([(b_sum, b_sum_out)], o_sem.at[pl.ds(3, 1)])
    a.add(a_sum)
    for job in (a, b):
        job.copies.finish()
    for copy in written:
        copy.wait()


def back_call(*args):
    return pl.pallas_call(
        back_kernel,
        out_shape=(
            shape((OWN, D), F32),
            shape((LEN, 256), BF),
            shape((8, D), F32),
            shape((4, A_ROWS, 256), BF),
            shape((B_ROWS, D), BF),
            shape((256, D), BF),
        ),
        in_specs=[ANYWHERE] * 10,
        out_specs=(ANYWHERE,) * 2 + (IN_VMEM,) * 2 + (ANYWHERE,) * 2,
        scratch_shapes=[
            pltpu.VMEM((D, 256), BF),
            pltpu.VMEM((4, PAD, D), BF),
            pltpu.VMEM((LEN, D), BF),
            pltpu.VMEM((4 * PAD, LEN), BF),
            pltpu.VMEM((LEN, D), BF),
            pltpu.VMEM((2 * PAD, LEN), BF),
            pltpu.VMEM((LEN, D), BF),
            pltpu.VMEM((LEN, 256), BF),
            pltpu.VMEM((2, ROWS, D), BF),
            pltpu.VMEM((B_ROWS, D), BF),
            pltpu.VMEM((OWN, D), F32),
            pltpu.VMEM((OWN, D), BF),
            pltpu.VMEM((8, D), F32),
            pltpu.VMEM((OWN, D), F32),
            pltpu.VMEM((LEN, 256), BF),
            pltpu.VMEM((B_ROWS, D), BF),
            pltpu.VMEM((256, D), BF),
            *Scatter.scratch(),
            *SumY.scratch((A_ROWS, 256)),
            *sems(Gather.COPIES, SumY.COPIES, SumZ.COPIES),
            DMA((10,)),
            DMA((4,)),
        ],
        compiler_params=params(2),
        cost_estimate=cost(25 * 10**9, 60 * 2**20),
        name="back",
    )(*args)


def close_kernel(
    query_in, keys_in, values_in, attended_grad_in, log_sum_in, cos_in, up_in, sdown_in, lowest_in,
    residual_in, residual_grad_in, tok_in, gains_in, sums_in, a_in, b_in, grad_out_in, hidden_in, first_in, wd_in, wh_in,
    mixed_out, grad_tokens_out, norms, bias_grad, gate_up_out, down_out, output_out, heads_out,
    query, keys, values, attended_grad, log_sum, cos, sin_up, sin_down, lowest,
    residual, residual_grad, tok, gains, sums_two, a_sum, b_sum, grad_out,
    mixed, grad_tokens, gate_up, down, output, heads, kt, key_acc, value_acc, projected, wd, wh, hidden, first, head_part, bias_sum,
    a_zland, a_two, b_yland, b_two, o_zland, o_sum, o_yland, o_two,
    q_sum, q_zland, q_two, v_zland, v_sum, v_yland, v_two,
    a_xland, b_xland, o_xland, q_xland, v_xland, pack, pack_dp, pack_one, pack_chip, pack_two, pack_z, *rest,
):
    scatter_refs, more_refs, q_refs, rest = rest[:10], rest[10:15], rest[15:18], rest[18:]
    (
        az_send, az_recv, by_send, by_recv, oz_send, oz_recv, oy_send, oy_recv,
        qy_send, qy_recv, qz_send, qz_recv, vz_send, vz_recv, vy_send, vy_recv, x_send, x_recv, p_send, p_recv, w_sem, out_sem,
    ) = rest
    near, far = Near(), Far()
    flows = copy_all([(a_in, a_sum), (b_in, b_sum), (grad_out_in, grad_out)], w_sem.at[pl.ds(4, 3)])
    load = copy_all([(wd_in, wd), (hidden_in, hidden)], w_sem.at[pl.ds(0, 2)])
    early = copy_all(
        [
            (query_in, query),
            (keys_in, keys),
            (values_in, values),
            (attended_grad_in, attended_grad),
            (log_sum_in, log_sum),
            (cos_in, cos),
            (up_in, sin_up),
            (sdown_in, sin_down),
            (lowest_in, lowest),
        ],
        w_sem.at[pl.ds(7, 9)],
    )
    load += copy_all([(wh_in, wh), (first_in, first)], w_sem.at[pl.ds(2, 2)])
    late = copy_all(
        [
            (residual_in, residual),
            (residual_grad_in, residual_grad),
            (tok_in, tok),
            (gains_in, gains),
            (sums_in, sums_two),
        ],
        w_sem.at[pl.ds(16, 5)],
    )
    written = []

    def write(src, dst):
        written.extend(copy_all([(src, dst)], out_sem.at[pl.ds(len(written), 1)]))

    t = lax.axis_index("tensor")
    dp_peers = [{"dp": far.dp_of(i)} for i in range(1, 8)]
    chip_peers = [near.dev["s"], near.dev["x"], {"tensor": (t // 4) * 4 + 3 - t % 4}]
    z_peers = [far.partner, near.dev["z"], {"tensor": ((t // 4 + 2) % 4) * 4 + t % 4}]
    greet(dp_peers + chip_peers + z_peers)
    a = PairZ(far, az_send, az_recv)
    b = RingY(far, lambda k, h: b_sum.at[:, far.ahead(k, h)], b_yland, by_send, by_recv)
    o = SumZ(
        far,
        lambda k, h, s: grad_out.at[pl.ds(s * 128, 128), far.ahead(k, h)],
        lambda k, h: o_zland.at[:, far.ahead(k, h)],
        lambda k, h: o_sum.at[:, far.ahead(k, h)],
        oz_send,
        oz_recv,
    )
    o_y = RingY(far, lambda k, h: o_sum.at[:, far.ahead(k, h)], o_yland, oy_send, oy_recv)
    for copy in flows:
        copy.wait()
    b.start()
    a.start(a_sum, a_zland)
    o.start_all()
    xs = [SumX(far, x_send.at[pl.ds(i, 1)], x_recv.at[pl.ds(i, 1)]) for i in range(5)]
    packs = Copies(p_send, p_recv)

    key_acc[...] = jnp.zeros_like(key_acc)
    value_acc[...] = jnp.zeros_like(value_acc)
    scatter = Scatter(near, scatter_refs)
    load[0].wait()
    load[1].wait()

    def make(chip):
        scatter.part[...] = dot_tn(hidden[:, chip_rows(chip)], wd[...])

    def look(block, s):
        start, stop = window(block)
        rows = slice(block * QB, (block + 1) * QB)
        bias_t = mask_bias(lowest[0:1, rows], start, stop, block)
        lanes = slice(s * 128, (s + 1) * 128)
        q, k, v = query[rows, lanes], keys[start:stop, lanes], values[start:stop, lanes]
        grad, k_t = attended_grad[rows, lanes], kt[s, :, start:stop]
        halves, key_sum, value_sum = [], None, None
        for head_id in range(2):
            mine = head_lanes(QB, head_id)
            q_one = jnp.where(mine, q, jnp.zeros_like(q))
            g_one = jnp.where(mine, grad, jnp.zeros_like(grad))
            index = s * 2 + head_id
            probs = jnp.exp(dot_nt(k, q_one) + bias_t - log_sum[index : index + 1, rows])
            prob_grad = dot_nt(v, g_one)
            inner = jnp.sum(probs * prob_grad, axis=0, keepdims=True)
            score_grad = (probs * (prob_grad - inner)).astype(BF)
            made = dot(k_t, score_grad)
            halves.append(made[head_id * HD : (head_id + 1) * HD])
            key_part = dot(score_grad, q_one)
            value_part = dot(probs.astype(BF), g_one)
            key_sum = key_part if key_sum is None else key_sum + key_part
            value_sum = value_part if value_sum is None else value_sum + value_part
        query_grad = jnp.concatenate(halves, axis=0).T * HD ** (-0.5)
        query_grad = roll_rotate(query_grad, cos[rows, :], -sin_up[rows, :], -sin_down[rows, :])
        projected[rows, s * 384 : s * 384 + 128] = query_grad.astype(BF)
        key_acc[s, start:stop, :] += key_sum
        value_acc[s, start:stop, :] += value_sum

    def close_shard(s):
        made = roll_rotate(key_acc[s], cos[...], -sin_up[...], -sin_down[...])
        projected[:, s * 384 + 128 : s * 384 + 256] = made.astype(BF)
        projected[:, s * 384 + 256 : s * 384 + 384] = value_acc[s].astype(BF)

    scatter.produce("d", make)
    scatter.produce("z", make)
    scatter.far()
    scatter.produce("x", make)
    scatter.z_direct()
    scatter.x_direct()
    scatter.produce("o", make)
    def query_key_part(k, j):
        return head_part.at[far.ahead(k, j // 2), pl.ds((j % 2) * 384, Q_LANES)]

    q = SumY(far, query_key_part, q_refs, qy_send, qy_recv)
    v = SumZ(
        far,
        lambda k, h, s: head_part.at[far.ahead(k, h), pl.ds(s * 384 + Q_LANES, V_LANES)],
        lambda k, h: v_zland.at[far.ahead(k, h)],
        lambda k, h: v_sum.at[far.ahead(k, h)],
        vz_send,
        vz_recv,
    )
    q_z = PairZ(far, qz_send, qz_recv)
    v_y = RingY(far, lambda k, h: v_sum.at[far.ahead(k, h)], v_yland, vy_send, vy_recv)
    last = Scatter(near, Scatter.second(scatter_refs, more_refs))

    def make_last(chip):
        rows = chip_rows(chip)
        last.part[...] = dot(projected[rows, :], wh[...])

    def weight_part(k, h, s):
        rows, lanes = far.ahead(k, h), slice(s * 384, (s + 1) * 384)
        head_part[rows, lanes] = dot(first[rows, :], projected[:, lanes]).astype(BF)
        if s == 1:
            v.start(k, h)

    for copy in early:
        copy.wait()
    for s in range(2):
        kt[s] = keys[:, s * 128 : (s + 1) * 128].astype(F32).T.astype(BF)
    look(0, 1)
    scatter.relays()
    for block in range(1, 4):
        look(block, 1)
    close_shard(1)
    load[2].wait()
    load[3].wait()
    for k, h in ((2, 0), (2, 1), (1, 1), (3, 0)):
        weight_part(k, h, 1)
    q.start(1)
    for k, h in ((1, 0), (3, 1), (0, 0), (0, 1)):
        weight_part(k, h, 1)
    look(0, 0)
    a.add(a_two)
    xs[0].start(a_two, a_xland)
    look(1, 0)
    q.relay(1)
    b.add(b_two)
    xs[1].start(b_two, b_xland)
    look(2, 0)
    o.add()
    o_y.start()
    look(3, 0)
    close_shard(0)
    for k, h in ((2, 0), (2, 1), (1, 1), (3, 0)):
        weight_part(k, h, 0)
    q.start(0)
    for copy in late:
        copy.wait()
    one, two = scatter.result()
    mixed[:HALF, :] = residual[:HALF, :] + one
    mixed[HALF:, :] = residual[HALF:, :] + two
    write(mixed, mixed_out)
    last.produce("d", make_last)
    last.produce("z", make_last)
    last.far()
    last.produce("x", make_last)
    last.z_direct()
    for k, h in ((1, 0), (3, 1), (0, 0), (0, 1)):
        weight_part(k, h, 0)
    last.x_direct()
    last.relays()
    q.relay(0)
    last.produce("o", make_last)
    v.add()
    v_y.start()
    o_y.add(o_two)
    xs[2].start(o_two, o_xland)
    bias_sum[...] = jnp.broadcast_to(jnp.sum(projected[...].astype(F32), axis=0, keepdims=True), bias_sum.shape)
    normed, inverse = layer_norm_parts(tok[...].astype(F32))
    q.add(q_sum)
    q_z.start(q_sum, q_zland)
    one, two = last.result()
    part, gain_sum, shift_sum = norm_back(jnp.concatenate([one, two], axis=0), normed, inverse, gains[0:1, :])
    grad_tokens[...] = residual_grad[...] + part
    write(grad_tokens, grad_tokens_out)
    sums = jnp.concatenate([gain_sum, shift_sum, sums_two[0:2, :]], axis=0)
    pack[...] = jnp.zeros_like(pack)
    for d in range(8):
        pack[d, 0:4, :256] = sums[:, d * 256 : (d + 1) * 256]
        pack[d, 4:5, :] = bias_sum[0:1, :384]
        pack[d, 5:6, :] = bias_sum[0:1, 384:]
    for i, device in enumerate(dp_peers):
        packs.go(i, pack.at[far.dp_of(i + 1)], pack_dp.at[i], device)
    gate_up[:A_ROWS, :] = xs[0].add()
    made = xs[1].add()
    gate_up[A_ROWS:, :] = made[: 2 * UNITS - A_ROWS]
    down[...] = made[2 * UNITS - A_ROWS :]
    write(gate_up, gate_up_out)
    write(down, down_out)
    total = pack[far.dp(0, 0)]
    for i, device in enumerate(dp_peers):
        packs.take(i, pack_dp.at[i], device)
        total = total + pack_dp[i]
    pack_one[...] = total
    for i, device in enumerate(chip_peers):
        packs.go(7 + i, pack_one, pack_chip.at[i], device)
    v_y.add(v_two)
    xs[4].start(v_two, v_xland)
    q_z.add(q_two)
    xs[3].start(q_two, q_xland)
    output[...] = xs[2].add()
    write(output, output_out)
    for i, device in enumerate(chip_peers):
        packs.take(7 + i, pack_chip.at[i], device)
        total = jnp.concatenate([total[:4] + pack_chip[i, :4, :], total[4:]], axis=0)
    pack_two[...] = total
    for i, device in enumerate(z_peers):
        packs.go(10 + i, pack_two, pack_z.at[i], device)
    heads[2] = xs[4].add()
    made = xs[3].add()
    heads[0] = made[:, :128]
    heads[1] = made[:, 128:]
    write(heads, heads_out)
    own_bias = total[4:5]
    for i, device in enumerate(z_peers):
        packs.take(10 + i, pack_z.at[i], device)
        total = total + pack_z[i]
    own_bias = own_bias + pack_z[0, 5:6, :]
    dp, tensor = lax.axis_index("dp"), lax.axis_index("tensor")
    norms[...] = pltpu.roll(total[:, :256], 256 - tensor * 16, 1)[:, :128]
    own_bias = pltpu.roll(jnp.broadcast_to(own_bias, (8, 384)), 384 - dp * 8, 1)
    for i in range(6):
        bias_grad[i // 2, i % 2 : i % 2 + 1, :] = own_bias[0:1, i * HD : i * HD + 8]
    packs.finish()
    for job in [a, b, o, o_y, q, q_z, v, v_y] + xs:
        job.copies.finish()
    for copy in written:
        copy.wait()


def close_call(*args):
    def block(*lead):
        return pltpu.VMEM(lead, BF)

    return pl.pallas_call(
        close_kernel,
        out_shape=(
            shape((OWN, D), F32),
            shape((OWN, D), F32),
            shape((8, 128), F32),
            shape((3, 2, 8), F32),
            shape((2 * UNITS, 256), F32),
            shape((UNITS, 256), F32),
            shape((128, 256), F32),
            shape((3, 256, 128), F32),
        ),
        in_specs=[ANYWHERE] * 21,
        out_specs=(ANYWHERE,) * 2 + (IN_VMEM,) * 2 + (ANYWHERE,) * 4,
        scratch_shapes=[
            *[pltpu.VMEM((LEN, 256), BF)] * 4,
            pltpu.VMEM((8, LEN), F32),
            *[pltpu.VMEM((LEN, 128), F32)] * 3,
            pltpu.VMEM((8, LEN), jnp.int32),
            *[pltpu.VMEM((OWN, D), F32)] * 2,
            pltpu.VMEM((OWN, D), BF),
            *[pltpu.VMEM((8, D), F32)] * 2,
            block(4, A_ROWS, 256), block(B_ROWS, D), block(256, D),
            *[pltpu.VMEM((OWN, D), F32)] * 2,
            *[pltpu.VMEM(dims, F32) for dims in ((2 * UNITS, 256), (UNITS, 256), (128, 256), (3, 256, 128))],
            pltpu.VMEM((2, 128, LEN), BF),
            pltpu.VMEM((2, LEN, 128), F32),
            pltpu.VMEM((2, LEN, 128), F32),
            pltpu.VMEM((LEN, 768), BF),
            pltpu.VMEM((2 * PAD, D), BF),
            pltpu.VMEM((768, D), BF),
            pltpu.VMEM((2 * PAD, LEN), BF),
            pltpu.VMEM((D, LEN), BF),
            pltpu.VMEM((D, 768), BF),
            pltpu.VMEM((8, 768), F32),
            block(2, A_ROWS, 256), block(2, A_ROWS, 256),
            block(3, 2, B_ROWS, 256), block(2, B_ROWS, 256),
            block(128, D), block(128, D), block(3, 2, 128, 256), block(2, 128, 256),
            block(4, 256, Q_LANES), block(2, 256, Q_LANES), block(2, 256, Q_LANES),
            block(D, V_LANES), block(D, V_LANES), block(3, 2, 256, V_LANES), block(2, 256, V_LANES),
            block(A_ROWS, 256), block(B_ROWS, 256), block(128, 256), block(256, Q_LANES), block(256, V_LANES),
            *[pltpu.VMEM(lead + (8, 384), F32) for lead in ((8,), (7,), (), (3,), (), (3,))],
            *Scatter.scratch(),
            *Scatter.again(),
            *SumY.scratch((256, Q_LANES)),
            *sems(2, 6, 8, 6, 12, 2, 8, 6, 5, 13),
            DMA((21,)),
            DMA((6,)),
        ],
        compiler_params=params(3),
        cost_estimate=cost(25 * 10**9, 60 * 2**20),
        name="close",
    )(*args)


def results_kernel(*refs):
    n = len(refs) // 3
    ins, outs, held, (in_sem, out_sem) = refs[:n], refs[n : 2 * n], refs[2 * n : 3 * n], refs[3 * n :]
    copies = copy_all(zip(ins, held), in_sem)
    written = []
    for i in range(n):
        copies[i].wait()
        written.extend(copy_all([(held[i], outs[i])], out_sem.at[pl.ds(i, 1)]))
    for copy in written:
        copy.wait()


def results_call(*arrays):
    n = len(arrays)
    return pl.pallas_call(
        results_kernel,
        out_shape=tuple(shape(v.shape, v.dtype) for v in arrays),
        in_specs=[ANYWHERE] * n,
        out_specs=(ANYWHERE,) * n,
        scratch_shapes=[*[pltpu.VMEM(v.shape, v.dtype) for v in arrays], DMA((n,)), DMA((n,))],
        compiler_params=params(),
        cost_estimate=cost(0, 10 * 2**20),
        name="results",
    )(*arrays)


def per_device(
    tokens,
    segments,
    first_gain,
    first_shift,
    heads_weight,
    heads_bias,
    output_weight,
    second_gain,
    second_shift,
    gate_up_weight,
    down_weight,
    cotangent,
):
    (
        first_all, cot_all, query, keys, values, attended, log_sum, residual, second_all, hidden, grads,
        wh, wo, wg, wd, gains, cos, sin_up, sin_down, lowest,
    ) = forward_call(
        tokens,
        cotangent,
        segments,
        *[v.reshape(1, 256) for v in (first_gain, first_shift, second_gain, second_shift)],
        heads_weight.transpose(1, 0, 2),
        heads_bias,
        output_weight,
        gate_up_weight.transpose(1, 2, 0),
        down_weight,
    )
    residual_grad, attended_grad, sums_two, a, b, grad_out = back_call(
        residual, cotangent, gains, grads, second_all, hidden, cot_all, wo, wg, attended
    )
    mixed, grad_tokens, norms, bias_grad, gate_up, down, output, heads = close_call(
        query, keys, values, attended_grad, log_sum, cos, sin_up, sin_down, lowest,
        residual, residual_grad, tokens, gains, sums_two, a, b, grad_out, hidden, first_all, wd, wh,
    )
    mixed, grad_tokens, gate_up, down, output, heads, bias_grad = results_call(
        mixed, grad_tokens, gate_up, down, output, heads, bias_grad
    )
    return (
        mixed,
        grad_tokens,
        norms[0, :16],
        norms[1, :16],
        heads.transpose(1, 0, 2),
        bias_grad,
        output,
        norms[2, :16],
        norms[3, :16],
        gate_up.reshape(2, UNITS, 256).transpose(2, 0, 1),
        down,
    )


ALL = ("dp", "tensor")


def solution(mesh):
    return jax.shard_map(
        per_device,
        mesh=mesh,
        in_specs=(
            P(ALL, None),
            P("dp", None),
            P("dp"),
            P("dp"),
            P("dp", None, "tensor"),
            P(None, "tensor", "dp"),
            P("tensor", "dp"),
            P("dp"),
            P("dp"),
            P("dp", None, "tensor"),
            P("tensor", "dp"),
            P(ALL, None),
        ),
        out_specs=(
            P(ALL, None),
            P(ALL, None),
            P(ALL),
            P(ALL),
            P("dp", None, "tensor"),
            P(None, "tensor", "dp"),
            P("tensor", "dp"),
            P(ALL),
            P(ALL),
            P("dp", None, "tensor"),
            P("tensor", "dp"),
        ),
        check_vma=False,
    )
```

```python
import functools
import math

import jax
import jax.numpy as jnp
from jax import lax
from jax.experimental import pallas as pl
from jax.experimental.pallas import tpu as pltpu
from jax.sharding import PartitionSpec as P

D = 2048
HD = 64
ROT = 16
WINDOW = 512
LEN = 1024
OWN = 128
HALF = OWN // 2
CHIP = 2 * OWN
UNITS = 352
PAD = 384
QB = 256

NORM_EPS = 1e-05
BASE_FREQ = 10000.0
FAR_NEGATIVE = -1e30
BF = jnp.bfloat16
F32 = jnp.float32
MESH = pl.DeviceIdType.MESH
VMEM_LIMIT = 62 * 2**20
DMA = pltpu.SemaphoreType.DMA


def spot(z, x, c):
    return (z % 2) * 4 + x * 2 + c


class Near:
    def __init__(self):
        t = lax.axis_index("tensor")
        z, x, c = t // 4, (t // 2) % 2, t % 2
        oz = (z // 2) * 2 + (z + 1) % 2
        ox, oc = 1 - x, 1 - c
        self.c, self.oc = c, oc
        self.me = spot(z, x, c)
        self.dev = {
            "x": {"tensor": z * 4 + ox * 2 + c},
            "z": {"tensor": oz * 4 + x * 2 + c},
            "s": {"tensor": z * 4 + x * 2 + oc},
        }
        self.same = {"o": spot(z, x, c), "x": spot(z, ox, c), "z": spot(oz, x, c), "d": spot(oz, ox, c)}
        self.other = {
            "o": spot(z, x, oc),
            "x": spot(z, ox, oc),
            "z": spot(oz, x, oc),
            "d": spot(oz, ox, oc),
        }
        self.chip = {"o": (z % 2) * 2 + x, "x": (z % 2) * 2 + ox, "z": (oz % 2) * 2 + x, "d": (oz % 2) * 2 + ox}


def remote(src, dst, send, recv, device):
    return pltpu.make_async_remote_copy(
        src_ref=src, dst_ref=dst, send_sem=send, recv_sem=recv, device_id=device, device_id_type=MESH
    )


def greet(devices):
    barrier = pltpu.get_barrier_semaphore()
    for device in devices:
        pl.semaphore_signal(barrier, inc=1, device_id=device, device_id_type=MESH)
    pl.semaphore_wait(barrier, len(devices))


def block_rows(block, half=None):
    if half is None:
        return pl.ds(pl.multiple_of(block * OWN, OWN), OWN)
    return pl.ds(pl.multiple_of(block * OWN + half * HALF, HALF), HALF)


def chip_rows(chip):
    return pl.ds(pl.multiple_of(chip * CHIP, CHIP), CHIP)


class Gather:
    COPIES = 13

    def __init__(self, near, buf, send, recv):
        self.near, self.buf, self.send, self.recv = near, buf, send, recv
        self.sent = []

    def copy(self, index, block, half, to):
        view = self.buf.at[block_rows(block, half)]
        return remote(view, view, self.send.at[index], self.recv.at[index], self.near.dev[to])

    def go(self, index, block, half, to):
        copy = self.copy(index, block, half, to)
        copy.start()
        self.sent.append(copy)

    def take(self, index, block, half, to="s"):
        self.copy(index, block, half, to).wait_recv()

    def start(self):
        me = self.near.me
        self.go(0, me, 0, "z")
        self.go(1, me, 1, "x")
        self.go(4, me, None, "s")
        self.go(2, me, 0, "x")
        self.go(3, me, 1, "z")

    def first(self):
        same = self.near.same
        self.take(0, same["z"], 0)
        self.go(5, same["z"], 0, "x")
        self.go(7, same["z"], 0, "s")
        self.take(1, same["x"], 1)
        self.go(6, same["x"], 1, "z")
        self.go(8, same["x"], 1, "s")

    def second(self):
        same = self.near.same
        self.take(2, same["x"], 0)
        self.go(9, same["x"], 0, "s")
        self.take(3, same["z"], 1)
        self.go(10, same["z"], 1, "s")

    def third(self):
        same = self.near.same
        self.take(5, same["d"], 0)
        self.go(11, same["d"], 0, "s")
        self.take(6, same["d"], 1)
        self.go(12, same["d"], 1, "s")

    def own_chip(self):
        self.take(4, self.near.other["o"], None)

    def x_chip(self):
        self.take(8, self.near.other["x"], 1)
        self.take(9, self.near.other["x"], 0)

    def z_chip(self):
        self.take(7, self.near.other["z"], 0)
        self.take(10, self.near.other["z"], 1)

    def d_chip(self):
        self.take(11, self.near.other["d"], 0)
        self.take(12, self.near.other["d"], 1)

    def finish(self):
        for copy in self.sent:
            copy.wait_send()

    def run(self, use):
        self.own_chip()
        use("o")
        self.first()
        self.second()
        self.x_chip()
        use("x")
        self.third()
        self.z_chip()
        use("z")
        self.d_chip()
        use("d")


class Scatter:
    COPIES = 10

    @staticmethod
    def scratch(width=D):
        return [
            pltpu.VMEM((CHIP, width), F32),
            pltpu.VMEM((4, OWN, width), F32),
            pltpu.VMEM((4, OWN, width), BF),
            pltpu.VMEM((4, OWN, width), BF),
            pltpu.VMEM((OWN, width), BF),
            pltpu.VMEM((4, HALF, width), BF),
            pltpu.VMEM((2, HALF, width), BF),
            pltpu.VMEM((4, HALF, width), BF),
            DMA((Scatter.COPIES,)),
            DMA((Scatter.COPIES,)),
        ]

    @staticmethod
    def again(width=D):
        return [
            pltpu.VMEM((4, OWN, width), BF),
            pltpu.VMEM((2, HALF, width), BF),
            pltpu.VMEM((4, HALF, width), BF),
            DMA((Scatter.COPIES,)),
            DMA((Scatter.COPIES,)),
        ]

    @staticmethod
    def second(refs, more):
        return list(refs[:3]) + [more[0]] + list(refs[4:6]) + list(more[1:])

    KEYS = ("d", "z", "x", "o")

    def __init__(self, near, refs):
        self.near = near
        (
            self.part,
            self.mine,
            self.core_out,
            self.core_in,
            self.far_out,
            self.out,
            self.through,
            self.last,
            self.send,
            self.recv,
        ) = refs
        self.sent = []

    def copy(self, index, src, dst, to):
        return remote(src, dst, self.send.at[index], self.recv.at[index], self.near.dev[to])

    def go(self, index, src, dst, to):
        copy = self.copy(index, src, dst, to)
        copy.start()
        self.sent.append(copy)

    def take(self, index, dst, to="s"):
        self.copy(index, dst, dst, to).wait_recv()

    def produce(self, key, make):
        i = self.KEYS.index(key)
        make(self.near.chip[key])
        self.core_out[i] = self.part[block_rows(self.near.oc), :].astype(BF)
        self.go(i, self.core_out.at[i], self.core_in.at[i], "s")
        self.mine[i] = self.part[block_rows(self.near.c), :]

    def join(self, key):
        i = self.KEYS.index(key)
        self.take(i, self.core_in.at[i])

    def summed(self, key, half):
        i = self.KEYS.index(key)
        rows = slice(half * HALF, (half + 1) * HALF)
        return self.mine[i, rows, :] + self.core_in[i, rows, :].astype(F32)

    def far(self):
        self.join("d")
        self.far_out[:HALF, :] = self.summed("d", 0).astype(BF)
        self.go(4, self.far_out.at[pl.ds(0, HALF)], self.through.at[0], "z")
        self.far_out[HALF:, :] = self.summed("d", 1).astype(BF)
        self.go(5, self.far_out.at[pl.ds(HALF, HALF)], self.through.at[1], "x")

    def z_direct(self):
        self.join("z")
        self.out[0] = self.summed("z", 0).astype(BF)
        self.go(6, self.out.at[0], self.last.at[0], "z")

    def x_direct(self):
        self.join("x")
        self.out[1] = self.summed("x", 1).astype(BF)
        self.go(7, self.out.at[1], self.last.at[1], "x")

    def relays(self):
        self.take(4, self.through.at[0])
        self.out[2] = (self.summed("x", 0) + self.through[0].astype(F32)).astype(BF)
        self.go(8, self.out.at[2], self.last.at[2], "x")
        self.take(5, self.through.at[1])
        self.out[3] = (self.summed("z", 1) + self.through[1].astype(F32)).astype(BF)
        self.go(9, self.out.at[3], self.last.at[3], "z")

    def result(self):
        self.join("o")
        for index in range(4):
            self.take(6 + index, self.last.at[index])
        first = self.summed("o", 0) + self.last[0].astype(F32) + self.last[2].astype(F32)
        second = self.summed("o", 1) + self.last[1].astype(F32) + self.last[3].astype(F32)
        for copy in self.sent:
            copy.wait_send()
        self.sent = []
        return first, second

    def run(self, make):
        self.produce("d", make)
        self.produce("z", make)
        self.far()
        self.produce("x", make)
        self.z_direct()
        self.x_direct()
        self.relays()
        self.produce("o", make)
        return self.result()


def dot(left, right):
    return jnp.dot(left, right, preferred_element_type=F32)


def dot_nt(left, right):
    return lax.dot_general(left, right, (((1,), (1,)), ((), ())), preferred_element_type=F32)


def dot_tn(left, right):
    return lax.dot_general(left, right, (((0,), (0,)), ((), ())), preferred_element_type=F32)


def layer_norm_parts(values):
    centre = values - jnp.mean(values, axis=-1, keepdims=True)
    inverse = lax.rsqrt(jnp.mean(centre * centre, axis=-1, keepdims=True) + NORM_EPS)
    return (centre * inverse, inverse)


def norm_back(upstream, normed, inverse, gain):
    scaled = upstream * gain
    inner = (
        scaled
        - jnp.mean(scaled, axis=-1, keepdims=True)
        - normed * jnp.mean(scaled * normed, axis=-1, keepdims=True)
    )
    return (
        inner * inverse,
        jnp.sum(upstream * normed, axis=0, keepdims=True),
        jnp.sum(upstream, axis=0, keepdims=True),
    )


def params(collective=None):
    if collective is None:
        return pltpu.CompilerParams(vmem_limit_bytes=VMEM_LIMIT)
    return pltpu.CompilerParams(
        collective_id=collective, has_side_effects=True, vmem_limit_bytes=VMEM_LIMIT
    )


def cost(flops, moved):
    return pl.CostEstimate(flops=flops, bytes_accessed=moved, transcendentals=0)


IN_VMEM = pl.BlockSpec(memory_space=pltpu.VMEM)
ANYWHERE = pl.BlockSpec(memory_space=pl.ANY)


def shape(dims, dtype):
    return jax.ShapeDtypeStruct(dims, dtype)


def copy_all(pairs, sems):
    copies = [pltpu.make_async_copy(src, dst, sems.at[i]) for i, (src, dst) in enumerate(pairs)]
    for copy in copies:
        copy.start()
    return copies


class Far:
    def __init__(self):
        t, dp = lax.axis_index("tensor"), lax.axis_index("dp")
        self.h, self.y = dp // 4, dp % 4
        self.over = {"dp": (1 - self.h) * 4 + self.y}
        self.partner = {"tensor": (3 - t // 4) * 4 + t % 4}
        self.ring = {k: {"dp": self.h * 4 + (self.y + k) % 4} for k in (1, 2, 3)}

    def dp(self, k, h):
        return ((self.h + h) % 2) * 4 + (self.y - k + 4) % 4

    def dp_of(self, i):
        return (self.h + i // 4) % 2 * 4 + (self.y + i % 4) % 4

    def span(self, k, h):
        return pl.ds(pl.multiple_of(self.dp(k, h) * 256, 256), 256)

    def ahead(self, k, h):
        return pl.ds(pl.multiple_of((h * 4 + (self.y + k) % 4) * 256, 256), 256)


class Copies:
    def __init__(self, send, recv):
        self.send, self.recv, self.sent = send, recv, []

    def go(self, index, src, dst, device):
        copy = remote(src, dst, self.send.at[index], self.recv.at[index], device)
        copy.start()
        self.sent.append(copy)

    def take(self, index, dst, device):
        remote(dst, dst, self.send.at[index], self.recv.at[index], device).wait_recv()

    def finish(self):
        for copy in self.sent:
            copy.wait_send()
        self.sent = []


class Ring:
    def __init__(self, far, n, place, send, recv):
        self.far, self.n, self.place = far, n, place
        self.copies = Copies(send, recv)

    def start(self, j, src=None):
        own = self.place(0, j)
        src = own if src is None else src
        self.copies.go(j, src, own, self.far.ring[1])
        self.copies.go(self.n + j, src, own, self.far.ring[3])

    def relay(self, j):
        if j < self.n // 2:
            view = self.place(1, j)
            self.copies.take(j, view, self.far.ring[1])
            self.copies.go(2 * self.n + j, view, view, self.far.ring[1])
        else:
            view = self.place(3, j)
            self.copies.take(self.n + j, view, self.far.ring[3])
            self.copies.go(2 * self.n + j, view, view, self.far.ring[3])

    def near(self, j):
        if j < self.n // 2:
            self.copies.take(self.n + j, self.place(3, j), self.far.ring[3])
        else:
            self.copies.take(j, self.place(1, j), self.far.ring[1])

    def done(self, j):
        self.near(j)
        self.copies.take(2 * self.n + j, self.place(2, j), self.far.ring[1])

    def finish(self, near=True):
        for j in range(self.n):
            if near:
                self.near(j)
            self.copies.take(2 * self.n + j, self.place(2, j), self.far.ring[1])
        self.copies.finish()


class SumY:
    COPIES = 12

    @staticmethod
    def scratch(dims):
        return [
            pltpu.VMEM((4,) + dims, BF),
            pltpu.VMEM((4,) + dims, BF),
            pltpu.VMEM((2, 4) + dims, BF),
        ]

    def __init__(self, far, block, refs, send, recv):
        self.far, self.block = far, block
        self.through, self.out, self.last = refs
        self.copies = Copies(send, recv)

    def to(self, j):
        return self.far.ring[1] if j < 2 else self.far.ring[3]

    def start(self, s):
        for j in (s, 2 + s):
            self.copies.go(j, self.block(2, j), self.through.at[j], self.to(j))
        self.copies.go(4 + 2 + s, self.block(1, 2 + s), self.last.at[0, 2 + s], self.far.ring[1])
        self.copies.go(8 + s, self.block(3, s), self.last.at[1, s], self.far.ring[3])

    def relay(self, s):
        for j, k, side in ((s, 1, 0), (2 + s, 3, 1)):
            self.copies.take(j, self.through.at[j], self.to(j))
            self.out[j] = (self.block(k, j)[...].astype(F32) + self.through[j].astype(F32)).astype(BF)
            self.copies.go(4 + side * 4 + j, self.out.at[j], self.last.at[side, j], self.far.ring[k])

    def add(self, out):
        for j in range(4):
            total = self.block(0, j)[...].astype(F32)
            for side, k in ((0, 1), (1, 3)):
                self.copies.take(4 + side * 4 + j, self.last.at[side, j], self.far.ring[k])
                total = total + self.last[side, j].astype(F32)
            out[j] = total.astype(BF)


class PairZ:
    COPIES = 2

    def __init__(self, far, send, recv):
        self.far, self.copies = far, Copies(send, recv)

    def start(self, sums, land):
        self.sums, self.land = sums, land
        for h in range(2):
            self.copies.go(h, sums.at[h * 2 + 1], land.at[h], self.far.partner)

    def add(self, out):
        for h in range(2):
            self.copies.take(h, self.land.at[h], self.far.partner)
            out[h] = (self.sums[h * 2].astype(F32) + self.land[h].astype(F32)).astype(BF)


class SumZ:
    COPIES = 8

    def __init__(self, far, block, land, out, send, recv):
        self.far, self.block, self.land, self.out = far, block, land, out
        self.copies = Copies(send, recv)

    def start(self, k, h):
        self.copies.go(k * 2 + h, self.block(k, h, 1), self.land(k, h), self.far.partner)

    def start_all(self):
        for k in (2, 1, 3, 0):
            for h in range(2):
                self.start(k, h)

    def add(self):
        for k in (2, 1, 3, 0):
            for h in range(2):
                self.copies.take(k * 2 + h, self.land(k, h), self.far.partner)
                total = self.block(k, h, 0)[...].astype(F32) + self.land(k, h)[...].astype(F32)
                self.out(k, h)[...] = total.astype(BF)


class RingY:
    COPIES = 6

    def __init__(self, far, block, land, send, recv):
        self.far, self.block, self.land = far, block, land
        self.copies = Copies(send, recv)

    def start(self):
        for k in (2, 1, 3):
            for h in range(2):
                self.copies.go((k - 1) * 2 + h, self.block(k, h), self.land.at[k - 1, h], self.far.ring[k])

    def add(self, out):
        for h in range(2):
            total = self.block(0, h)[...].astype(F32)
            for k in (1, 2, 3):
                self.copies.take((k - 1) * 2 + h, self.land.at[k - 1, h], self.far.ring[k])
                total = total + self.land[k - 1, h].astype(F32)
            out[h] = total.astype(BF)


class SumX:
    def __init__(self, far, send, recv):
        self.far, self.copies = far, Copies(send, recv)

    def start(self, sums, land):
        self.sums, self.land = sums, land
        self.copies.go(0, sums.at[1 - self.far.h], land, self.far.over)

    def add(self):
        self.copies.take(0, self.land, self.far.over)
        return self.sums[self.far.h].astype(F32) + self.land[...].astype(F32)


def rotary_tables(starts, cos_out, up_out, down_out):
    index = lax.broadcasted_iota(jnp.int32, (8, LEN), 1)
    power = lax.broadcasted_iota(jnp.int32, (8, LEN), 0).astype(F32)
    angles = (index - starts).astype(F32) * jnp.exp(power * (-2.0 * math.log(BASE_FREQ) / ROT))
    cosine, sine = jnp.cos(angles), jnp.sin(angles)
    none, rest = jnp.zeros((8, LEN), F32), jnp.zeros((HD - ROT, LEN), F32)
    cos_out[...] = jnp.concatenate([cosine, cosine, rest + 1.0] * 2, axis=0).T
    up_out[...] = jnp.concatenate([-sine, none, rest] * 2, axis=0).T
    down_out[...] = jnp.concatenate([none, sine, rest] * 2, axis=0).T


def document_starts(seg):
    index = lax.broadcasted_iota(jnp.int32, (8, LEN), 1)
    new = (index == 0) | (pltpu.roll(seg, 1, 1) != seg)
    starts = jnp.where(new, index, 0)
    step = 1
    while step < LEN:
        starts = jnp.maximum(starts, jnp.where(index >= step, pltpu.roll(starts, step, 1), 0))
        step *= 2
    return starts


def roll_rotate(values, cos, sin_up, sin_down):
    return (
        values * cos + pltpu.roll(values, 128 - ROT // 2, 1) * sin_up + pltpu.roll(values, ROT // 2, 1) * sin_down
    )


def window(block):
    start = max(0, block * QB - WINDOW)
    return start, (block + 1) * QB


def mask_bias(lowest, start, stop, block):
    keys = lax.broadcasted_iota(jnp.int32, (stop - start, QB), 0) + start
    queries = lax.broadcasted_iota(jnp.int32, (stop - start, QB), 1) + block * QB
    return jnp.where((keys <= queries) & (keys >= lowest), 0.0, FAR_NEGATIVE)


def head_lanes(rows, head):
    lanes = lax.broadcasted_iota(jnp.int32, (rows, 128), 1)
    return (lanes >= HD) if head else (lanes < HD)


def silu_parts(gate, up, grad):
    sig = 1.0 / (1.0 + jnp.exp(-gate))
    silu = gate * sig
    return silu * up, grad * up * sig * (1.0 + gate * (1.0 - sig)), grad * silu


def sems(*counts):
    return [DMA((n,)) for n in counts for _ in range(2)]


class Quad:
    def __init__(self, far, place, send, recv):
        self.far, self.place = far, place
        self.copies = Copies(send, recv)

    def over(self, src):
        self.copies.go(0, src, self.place(0, 0), self.far.over)

    def partner(self, src):
        self.copies.go(1, src, self.place(0, 1), self.far.partner)

    def take_over(self):
        self.copies.take(0, self.place(0, 2), self.far.over)
        self.copies.go(2, self.place(0, 2), self.place(0, 3), self.far.partner)

    def take_partner(self):
        self.copies.take(1, self.place(0, 1), self.far.partner)

    def take_last(self):
        self.copies.take(2, self.place(0, 3), self.far.partner)


class Across:
    def __init__(self, far, place, send, recv):
        self.far, self.place = far, place
        self.copies = Copies(send, recv)

    def start(self, k, h, src=None):
        src = self.place(k, h, 0) if src is None else src
        self.copies.go(k * 2 + h, src, self.place(k, h, 1), self.far.partner)

    def finish(self):
        for k in range(4):
            for h in range(2):
                self.copies.take(k * 2 + h, self.place(k, h, 1), self.far.partner)
        self.copies.finish()


class ZLast:
    def __init__(self, far, place, refs):
        x_send, x_recv, r_send, r_recv, z_send, z_recv = refs
        self.far, self.place = far, place
        self.copies = Copies(x_send, x_recv)
        self.ring = Ring(far, 2, lambda k, j: place(k, j, 0), r_send, r_recv)
        self.across = Across(far, place, z_send, z_recv)

    def over(self, src):
        self.src = src
        self.copies.go(0, src, self.place(0, 0, 0), self.far.over)

    def take_over(self):
        self.copies.take(0, self.place(0, 1, 0), self.far.over)

    def partner(self):
        self.across.start(0, 0, self.src)
        self.across.start(0, 1)

    def start(self):
        self.ring.start(0, self.src)
        self.ring.start(1)

    def ring_done(self):
        self.ring.finish(near=False)
        self.across.start(2, 0)
        self.across.start(2, 1)

    def relay(self):
        self.ring.relay(0)
        self.ring.relay(1)
        self.ring.near(0)
        self.ring.near(1)
        for k in (1, 3):
            self.across.start(k, 0)
            self.across.start(k, 1)

    def finish(self):
        self.across.finish()
        self.copies.finish()


Q_LANES = 256
V_LANES = 384 - Q_LANES
UP_ROWS = 256


def bias_lanes(bias, dp):
    j = lax.broadcasted_iota(jnp.int32, (8, 384), 0)
    lane = lax.broadcasted_iota(jnp.int32, (8, 384), 1)
    pick = jnp.where(lane % HD == dp * 8 + j, 1.0, 0.0).astype(BF)
    total = jnp.zeros((1, 384), F32)
    lane = lax.broadcasted_iota(jnp.int32, (1, 384), 1)
    for p in range(3):
        for h in range(2):
            made = dot(bias[p, h : h + 1, :].astype(BF), pick)
            total = total + jnp.where(lane // HD == p * 2 + h, made, 0.0)
    return total


def forward_kernel(
    tok, cot, seg, gain_one, shift_one, gain_two, shift_two, head_in, bias_in, out_in, gate_in, down_in,
    first_out, cot_out, query_out, keys_out, values_out, attended_out, log_sum, residual_out, second_out, hidden_out,
    grads_out, wh_out, wo_out, wg_out, wd_out, gains, cos_out, up_out, sdown_out, lowest,
    fa, ca, wv, wo, wd, wg, query, keys, values, attended, vt, hg, second, hidden, grads, gbuf, gbuf_two, bias,
    small, head, outw, gate, down, wh_turned, wo_turned, first_turned, residual, cos, sin_up, sin_down, *rest,
):
    scatter_refs, rest = rest[:10], rest[10:]
    (
        ga_send, ga_recv, gc_send, gc_recv, gs_send, gs_recv, sm_send, sm_recv, sr_send, sr_recv,
        hq_send, hq_recv, hr_send, hr_recv, gq_send, gq_recv, gr_send, gr_recv, uq_send, uq_recv, ur_send, ur_recv,
    ) = rest[:22]
    out_refs, down_refs, tail_refs, value_refs, (out_sem,) = rest[22:28], rest[28:34], rest[34:40], rest[40:46], rest[46:]
    near, far = Near(), Far()
    greet([near.dev["x"], near.dev["z"], near.dev["s"], far.over, far.partner, far.ring[1], far.ring[3]])
    written = []

    def write(src, dst):
        copy = pltpu.make_async_copy(src, dst, out_sem.at[len(written)])
        copy.start()
        written.append(copy)

    def head_at(k, j):
        return wv.at[j % 2, far.span(k, j // 2), pl.ds(0, Q_LANES)]

    def value_at(k, h, s):
        return wv.at[s, far.span(k, h), pl.ds(Q_LANES, V_LANES)]

    def gate_at(k, j):
        return wg.at[(j % 2) * 2, pl.ds(0, UNITS), far.span(k, j // 2)]

    def up_at(k, j):
        return wg.at[(j % 2) * 2 + 1, pl.ds(0, UP_ROWS), far.span(k, j // 2)]

    def tail_at(k, h, s):
        return wg.at[s * 2 + 1, pl.ds(UP_ROWS, UNITS - UP_ROWS), far.span(k, h)]

    def out_at(k, h, s):
        return wo.at[pl.ds(s * 128, 128), far.span(k, h)]

    def down_at(k, h, s):
        return wd.at[pl.ds(s * PAD, UNITS), far.span(k, h)]

    smalls = Copies(sm_send, sm_recv)
    small_ring = Ring(far, 2, lambda k, j: gbuf.at[far.dp(k, j)], sr_send, sr_recv)
    head_quad, head_ring = Quad(far, head_at, hq_send, hq_recv), Ring(far, 4, head_at, hr_send, hr_recv)
    gate_quad, gate_ring = Quad(far, gate_at, gq_send, gq_recv), Ring(far, 4, gate_at, gr_send, gr_recv)
    up_quad, up_ring = Quad(far, up_at, uq_send, uq_recv), Ring(far, 4, up_at, ur_send, ur_recv)
    outs, downs, tails = ZLast(far, out_at, out_refs), ZLast(far, down_at, down_refs), ZLast(far, tail_at, tail_refs)
    vals = ZLast(far, value_at, value_refs)
    firsts = Gather(near, fa, ga_send, ga_recv)
    cots = Gather(near, ca, gc_send, gc_recv)
    seconds = Gather(near, second, gs_send, gs_recv)

    small[0:1, :256] = gain_one[...].astype(BF).astype(F32)
    small[1:2, :256] = shift_one[...].astype(BF).astype(F32)
    small[2:3, :256] = gain_two[...].astype(BF).astype(F32)
    small[3:4, :256] = shift_two[...].astype(BF).astype(F32)
    small[4:5, :] = bias_lanes(bias_in, lax.axis_index("dp"))
    for p in range(3):
        head[:, p * 128 : (p + 1) * 128] = head_in[p].astype(BF)
    smalls.go(0, small, gbuf.at[far.dp(0, 0)], far.over)
    small_ring.start(0, small)
    own_qk, own_v = head.at[:, pl.ds(0, Q_LANES)], head.at[:, pl.ds(Q_LANES, V_LANES)]
    head_quad.over(own_qk)
    head_quad.partner(own_qk)
    vals.over(own_v)
    vals.ring.start(0, own_v)
    head_ring.start(0, own_qk)
    outw[...] = out_in[...].astype(BF)
    down[...] = down_in[...].astype(BF)
    gate[...] = gate_in[...].astype(BF)
    up_own, tail_own = gate.at[1, pl.ds(0, UP_ROWS)], gate.at[1, pl.ds(UP_ROWS, UNITS - UP_ROWS)]
    outs.over(outw)
    downs.over(down)
    tails.over(tail_own)
    gbuf[far.dp(0, 0)] = small[...]
    normed, _ = layer_norm_parts(tok[...].astype(F32))
    smalls.take(0, gbuf.at[far.dp(0, 1)], far.over)
    small_ring.start(1)
    vals.take_over()
    vals.ring.start(1)
    vals.partner()
    head_quad.take_over()
    head_ring.start(2)
    small_ring.relay(0)
    small_ring.relay(1)
    small_ring.finish()
    for d in range(8):
        gains[:, d * 256 : (d + 1) * 256] = gbuf[d, :, :256]
    first = normed * gains[0:1, :] + gains[1:2, :]
    fa[block_rows(near.me), :] = first.astype(BF)
    firsts.start()
    vals.relay()
    head_ring.relay(0)
    head_ring.relay(2)
    head_quad.take_partner()
    head_ring.start(1)
    head_quad.take_last()
    head_ring.start(3)
    smalls.go(1, gbuf, gbuf_two, far.partner)
    gate_quad.partner(gate.at[0])
    up_quad.partner(up_own)
    wv[0, far.span(0, 0), :] = head[...]
    vals.ring_done()
    wo[:128, far.span(0, 0)] = outw[...]
    wd[:UNITS, far.span(0, 0)] = down[...]
    wg[0, :UNITS, far.span(0, 0)] = gate[0]
    wg[1, :UNITS, far.span(0, 0)] = gate[1]
    for i in range(4):
        wg[i, UNITS:, :] = jnp.zeros((PAD - UNITS, D), BF)
    for i in range(2):
        wd[i * PAD + UNITS : (i + 1) * PAD, :] = jnp.zeros((PAD - UNITS, D), BF)
    starts = document_starts(jnp.broadcast_to(seg[pl.ds(lax.axis_index("tensor") // 8, 1), :], (8, LEN)))
    index = lax.broadcasted_iota(jnp.int32, (8, LEN), 1)
    lowest[...] = jnp.maximum(starts, index - (WINDOW - 1))
    head_ring.relay(1)
    head_ring.relay(3)
    firsts.first()
    firsts.second()
    rotary_tables(starts, cos, sin_up, sin_down)
    for src, dst in ((cos, cos_out), (sin_up, up_out), (sin_down, sdown_out)):
        write(src, dst)
    smalls.take(1, gbuf_two, far.partner)
    bias[0:1, :384] = jnp.sum(gbuf[:, 4, :], axis=0, keepdims=True)
    bias[0:1, 384:] = jnp.sum(gbuf_two[:, 4, :], axis=0, keepdims=True)
    outs.take_over()
    outs.ring.start(0, outw)
    outs.ring.start(1)
    outs.partner()
    firsts.third()
    gate_quad.over(gate.at[0])
    up_quad.over(up_own)
    head_ring.done(0)
    head_ring.done(2)

    def project(chip, s):
        rows = chip_rows(chip)
        c, up, down = cos[rows, :], sin_up[rows, :], sin_down[rows, :]
        lanes = slice(s * 128, (s + 1) * 128)
        made = dot(fa[rows, :], wv[s]) + bias[0:1, s * 384 : (s + 1) * 384]
        query[rows, lanes] = (roll_rotate(made[:, :128], c, up, down) * HD ** (-0.5)).astype(BF)
        keys[rows, lanes] = roll_rotate(made[:, 128:256], c, up, down).astype(BF)
        values[rows, lanes] = made[:, 256:].astype(BF)
        vt[chip, s] = made[:, 256:].T.astype(BF)

    def look(block, s):
        start, stop = window(block)
        rows = slice(block * QB, (block + 1) * QB)
        bias_t = mask_bias(lowest[0:1, rows], start, stop, block)
        lanes = slice(s * 128, (s + 1) * 128)
        q, k = query[rows, lanes], keys[start:stop, lanes]
        v_t = jnp.concatenate([vt[i, s] for i in range(start // CHIP, stop // CHIP)], axis=1)
        halves = []
        for head_id in range(2):
            q_one = jnp.where(head_lanes(QB, head_id), q, jnp.zeros_like(q))
            scores = dot_nt(k, q_one) + bias_t
            top = jnp.max(scores, axis=0, keepdims=True)
            weights = jnp.exp(scores - top)
            total = jnp.sum(weights, axis=0, keepdims=True)
            made = dot(v_t, weights.astype(BF))
            halves.append(made[head_id * HD : (head_id + 1) * HD] * (1.0 / total))
            log_sum[s * 2 + head_id : s * 2 + head_id + 1, rows] = top + jnp.log(total)
        attended[rows, lanes] = jnp.concatenate(halves, axis=0).T.astype(BF)

    firsts.own_chip()
    project(near.chip["o"], 0)
    firsts.x_chip()
    project(near.chip["x"], 0)
    firsts.z_chip()
    project(near.chip["z"], 0)
    firsts.d_chip()
    project(near.chip["d"], 0)
    ca[block_rows(near.me), :] = cot[...]
    cots.start()
    look(0, 0)
    downs.ring.start(0, down)
    tails.ring.start(0, tail_own)
    outs.relay()
    look(1, 0)
    look(2, 0)
    gate_quad.take_over()
    up_quad.take_over()
    downs.take_over()
    downs.ring.start(1)
    downs.partner()
    tails.take_over()
    tails.ring.start(1)
    tails.partner()
    look(3, 0)
    head_ring.done(1)
    head_ring.done(3)
    vals.across.finish()
    gate_ring.start(0, gate.at[0])
    gate_ring.start(2)
    for key in "oxzd":
        project(near.chip[key], 1)
    outs.ring_done()
    for src, dst in ((query, query_out), (keys, keys_out), (values, values_out)):
        write(src, dst)
    look(0, 1)
    gate_quad.take_partner()
    gate_ring.start(1)
    look(1, 1)
    downs.relay()
    tails.relay()
    gate_quad.take_last()
    gate_ring.start(3)
    cots.first()
    cots.second()
    look(2, 1)
    up_quad.take_partner()
    up_quad.take_last()
    look(3, 1)
    cots.third()
    outs.finish()
    scatter = Scatter(near, scatter_refs)

    def make(chip):
        rows = chip_rows(chip)
        scatter.part[...] = dot(attended[rows, :], wo[...])

    scatter.produce("d", make)
    scatter.produce("z", make)
    scatter.far()
    scatter.produce("x", make)
    scatter.z_direct()
    scatter.x_direct()
    up_ring.start(0, up_own)
    up_ring.start(1)
    up_ring.start(2)
    up_ring.start(3)
    scatter.relays()
    scatter.produce("o", make)
    for half in range(2):
        wh_turned[half * 384 : (half + 1) * 384, :] = wv[half].T
    write(wh_turned, wh_out)
    for chip in range(4):
        first_turned[:, chip * CHIP : (chip + 1) * CHIP] = fa[chip * CHIP : (chip + 1) * CHIP, :].T
    write(first_turned, first_out)
    downs.ring_done()
    tails.ring_done()
    write(attended, attended_out)
    wo_turned[...] = wo[...].T
    write(wo_turned, wo_out)
    gate_ring.relay(0)
    gate_ring.relay(1)
    gate_ring.relay(2)
    gate_ring.relay(3)
    cots.own_chip()
    cots.x_chip()
    cots.z_chip()
    cots.d_chip()
    write(ca, cot_out)
    one, two = scatter.result()
    residual[:HALF, :] = tok[:HALF, :].astype(F32) + one
    residual[HALF:, :] = tok[HALF:, :].astype(F32) + two
    write(residual, residual_out)
    normed, _ = layer_norm_parts(residual[...])
    second[block_rows(near.me), :] = (normed * gains[2:3, :] + gains[3:4, :]).astype(BF)
    seconds.start()
    for j in range(4):
        up_ring.relay(j)
    seconds.first()
    seconds.second()
    downs.finish()
    write(wd, wd_out)
    for chip in range(4):
        rows = slice(chip * CHIP, (chip + 1) * CHIP)
        hg[:, rows] = dot_nt(wd[...], ca[rows, :])
    seconds.third()
    gate_ring.finish()
    up_ring.finish()
    tails.finish()
    write(wg, wg_out)

    def use(key):
        chip = near.chip[key]
        rows = chip_rows(chip)
        for s in range(2):
            made = dot_nt(wg[s * 2 : s * 2 + 2].reshape(2 * PAD, D), second[rows, :])
            h, g, u = silu_parts(made[:PAD], made[PAD:], hg[s * PAD : (s + 1) * PAD, rows])
            hidden[s * PAD : (s + 1) * PAD, rows] = h.astype(BF)
            grads[s * 2 * PAD : s * 2 * PAD + PAD, rows] = g.astype(BF)
            grads[s * 2 * PAD + PAD : (s + 1) * 2 * PAD, rows] = u.astype(BF)
        write(second.at[rows], second_out.at[rows])
        write(hidden.at[:, rows], hidden_out.at[:, rows])
        write(grads.at[:, rows], grads_out.at[:, rows])

    seconds.own_chip()
    use("o")
    seconds.x_chip()
    use("x")
    seconds.z_chip()
    use("z")
    seconds.d_chip()
    use("d")
    for group in (smalls, head_quad.copies, head_ring.copies, gate_quad.copies, up_quad.copies, vals.copies, firsts, cots, seconds):
        group.finish()
    for copy in written:
        copy.wait()


def forward_call(*args):
    narrow = shape((LEN, 256), BF)
    return pl.pallas_call(
        forward_kernel,
        out_shape=(
            shape((D, LEN), BF),
            shape((LEN, D), BF),
            narrow,
            narrow,
            narrow,
            narrow,
            shape((8, LEN), F32),
            shape((OWN, D), F32),
            shape((LEN, D), BF),
            shape((2 * PAD, LEN), BF),
            shape((4 * PAD, LEN), BF),
            shape((768, D), BF),
            shape((D, 256), BF),
            shape((4, PAD, D), BF),
            shape((2 * PAD, D), BF),
            shape((8, D), F32),
            shape((LEN, 128), F32),
            shape((LEN, 128), F32),
            shape((LEN, 128), F32),
            shape((8, LEN), jnp.int32),
        ),
        in_specs=[IN_VMEM] * 12,
        out_specs=(ANYWHERE,) * 6 + (IN_VMEM,) + (ANYWHERE,) * 8 + (IN_VMEM,) + (ANYWHERE,) * 3 + (IN_VMEM,),
        scratch_shapes=[
            pltpu.VMEM((LEN, D), BF),
            pltpu.VMEM((LEN, D), BF),
            pltpu.VMEM((2, D, 384), BF),
            pltpu.VMEM((256, D), BF),
            pltpu.VMEM((2 * PAD, D), BF),
            pltpu.VMEM((4, PAD, D), BF),
            pltpu.VMEM((LEN, 256), BF),
            pltpu.VMEM((LEN, 256), BF),
            pltpu.VMEM((LEN, 256), BF),
            pltpu.VMEM((LEN, 256), BF),
            pltpu.VMEM((4, 2, 128, CHIP), BF),
            pltpu.VMEM((2 * PAD, LEN), F32),
            pltpu.VMEM((LEN, D), BF),
            pltpu.VMEM((2 * PAD, LEN), BF),
            pltpu.VMEM((4 * PAD, LEN), BF),
            pltpu.VMEM((8, 8, 384), F32),
            pltpu.VMEM((8, 8, 384), F32),
            pltpu.VMEM((8, 768), F32),
            pltpu.VMEM((8, 384), F32),
            pltpu.VMEM((256, 384), BF),
            pltpu.VMEM((128, 256), BF),
            pltpu.VMEM((2, UNITS, 256), BF),
            pltpu.VMEM((UNITS, 256), BF),
            pltpu.VMEM((768, D), BF),
            pltpu.VMEM((D, 256), BF),
            pltpu.VMEM((D, LEN), BF),
            pltpu.VMEM((OWN, D), F32),
            pltpu.VMEM((LEN, 128), F32),
            pltpu.VMEM((LEN, 128), F32),
            pltpu.VMEM((LEN, 128), F32),
            *Scatter.scratch(),
            *sems(*[Gather.COPIES] * 3, 2, 6, 3, 12, 3, 12, 3, 12, *[1, 6, 8] * 4),
            DMA((27,)),
        ],
        compiler_params=params(1),
        cost_estimate=cost(40 * 10**9, 80 * 2**20),
        name="forward",
    )(*args)


ROWS = 3 * UNITS
A_ROWS = 608
B_ROWS = ROWS - A_ROWS


def back_kernel(
    residual_in, cot_own_in, gains_in, grads_in, second_in, hidden_in, cot_in, wo_in, wg_in, attended_in,
    residual_grad_out, attended_grad_out, norm_sums, a_sum, b_sum_out, grad_out_out,
    wo, wg, branch, grads, second, hidden, cots, attended, parts, b_land,
    residual, cot, gains, residual_grad, attended_grad, b_sum, grad_out, *rest,
):
    scatter_refs, a_refs, rest = rest[:10], rest[10:13], rest[13:]
    ga_send, ga_recv, ay_send, ay_recv, bz_send, bz_recv, w_sem, o_sem = rest
    near, far = Near(), Far()
    load = copy_all(
        [
            (wg_in, wg),
            (grads_in, grads),
            (second_in, second),
            (hidden_in, hidden),
            (cot_in, cots),
            (wo_in, wo),
            (attended_in, attended),
            (residual_in, residual),
            (cot_own_in, cot),
            (gains_in, gains),
        ],
        w_sem,
    )
    greet([near.dev["x"], near.dev["z"], near.dev["s"], far.partner, far.ring[1], far.ring[3]])
    a_rows, b_rows = pl.ds(0, A_ROWS), pl.ds(A_ROWS, B_ROWS)
    a = SumY(far, lambda k, j: parts.at[j % 2, a_rows, far.ahead(k, j // 2)], a_refs, ay_send, ay_recv)
    b = SumZ(
        far,
        lambda k, h, s: parts.at[s, b_rows, far.ahead(k, h)],
        lambda k, h: b_land.at[:, far.ahead(k, h)],
        lambda k, h: b_sum.at[:, far.ahead(k, h)],
        bz_send,
        bz_recv,
    )
    scatter = Scatter(near, scatter_refs)

    def make(chip):
        scatter.part[...] = dot_tn(grads[:, chip_rows(chip)], wg[...].reshape(4 * PAD, D))

    def gate_part(s):
        start = s * 2 * PAD
        parts[s, :UNITS, :] = dot(grads[start : start + UNITS, :], second[...]).astype(BF)

    def up_part(s):
        start = s * 2 * PAD + PAD
        parts[s, UNITS : 2 * UNITS, :] = dot(grads[start : start + UNITS, :], second[...]).astype(BF)

    def down_part(s):
        start = s * PAD
        parts[s, 2 * UNITS :, :] = dot(hidden[start : start + UNITS, :], cots[...]).astype(BF)

    for copy in load[1:5]:
        copy.wait()
    up_part(1)
    down_part(1)
    b.start_all()
    load[0].wait()
    scatter.produce("d", make)
    scatter.produce("z", make)
    scatter.far()
    gate_part(1)
    a.start(1)
    scatter.produce("x", make)
    scatter.z_direct()
    scatter.x_direct()
    scatter.relays()
    scatter.produce("o", make)
    gate_part(0)
    up_part(0)
    a.start(0)
    a.relay(1)
    first, second_half = scatter.result()
    for copy in load[7:]:
        copy.wait()
    normed, inverse = layer_norm_parts(residual[...])
    upstream = jnp.concatenate([first, second_half], axis=0)
    part, gain_sum, shift_sum = norm_back(upstream, normed, inverse, gains[2:3, :])
    made = cot[...].astype(F32) + part
    residual_grad[...] = made
    written = copy_all([(residual_grad, residual_grad_out)], o_sem.at[pl.ds(0, 1)])
    norm_sums[...] = jnp.concatenate([gain_sum, shift_sum] * 4, axis=0)
    branch[block_rows(near.me), :] = made.astype(BF)
    gather = Gather(near, branch, ga_send, ga_recv)
    gather.start()
    load[5].wait()
    load[6].wait()
    down_part(0)
    a.relay(0)

    def use(key):
        rows = chip_rows(near.chip[key])
        attended_grad[rows, :] = dot(branch[rows, :], wo[...]).astype(BF)

    gather.own_chip()
    use("o")
    gather.first()
    gather.second()
    gather.x_chip()
    use("x")
    gather.third()
    gather.z_chip()
    use("z")
    b.add()
    written += copy_all([(b_sum, b_sum_out)], o_sem.at[pl.ds(3, 1)])
    gather.d_chip()
    use("d")
    written += copy_all([(attended_grad, attended_grad_out)], o_sem.at[pl.ds(1, 1)])
    grad_out[...] = dot_tn(attended[...], branch[...]).astype(BF)
    written += copy_all([(grad_out, grad_out_out)], o_sem.at[pl.ds(2, 1)])
    gather.finish()
    a.add(a_sum)
    for job in (a, b):
        job.copies.finish()
    for copy in written:
        copy.wait()


def back_call(*args):
    return pl.pallas_call(
        back_kernel,
        out_shape=(
            shape((OWN, D), F32),
            shape((LEN, 256), BF),
            shape((8, D), F32),
            shape((4, A_ROWS, 256), BF),
            shape((B_ROWS, D), BF),
            shape((256, D), BF),
        ),
        in_specs=[ANYWHERE] * 10,
        out_specs=(ANYWHERE,) * 2 + (IN_VMEM,) * 2 + (ANYWHERE,) * 2,
        scratch_shapes=[
            pltpu.VMEM((D, 256), BF),
            pltpu.VMEM((4, PAD, D), BF),
            pltpu.VMEM((LEN, D), BF),
            pltpu.VMEM((4 * PAD, LEN), BF),
            pltpu.VMEM((LEN, D), BF),
            pltpu.VMEM((2 * PAD, LEN), BF),
            pltpu.VMEM((LEN, D), BF),
            pltpu.VMEM((LEN, 256), BF),
            pltpu.VMEM((2, ROWS, D), BF),
            pltpu.VMEM((B_ROWS, D), BF),
            pltpu.VMEM((OWN, D), F32),
            pltpu.VMEM((OWN, D), BF),
            pltpu.VMEM((8, D), F32),
            pltpu.VMEM((OWN, D), F32),
            pltpu.VMEM((LEN, 256), BF),
            pltpu.VMEM((B_ROWS, D), BF),
            pltpu.VMEM((256, D), BF),
            *Scatter.scratch(),
            *SumY.scratch((A_ROWS, 256)),
            *sems(Gather.COPIES, SumY.COPIES, SumZ.COPIES),
            DMA((10,)),
            DMA((4,)),
        ],
        compiler_params=params(2),
        cost_estimate=cost(25 * 10**9, 60 * 2**20),
        name="back",
    )(*args)


def close_kernel(
    query_in, keys_in, values_in, attended_grad_in, log_sum_in, cos_in, up_in, sdown_in, lowest_in,
    residual_in, residual_grad_in, tok_in, gains_in, sums_in, a_in, b_in, grad_out_in, hidden_in, first_in, wd_in, wh_in,
    mixed_out, grad_tokens_out, norms, bias_grad, gate_up_out, down_out, output_out, heads_out,
    query, keys, values, attended_grad, log_sum, cos, sin_up, sin_down, lowest,
    residual, residual_grad, tok, gains, sums_two, a_sum, b_sum, grad_out,
    mixed, grad_tokens, gate_up, down, output, heads, kt, key_acc, value_acc, projected, wd, wh, hidden, first, head_part, bias_sum,
    a_zland, a_two, b_yland, b_two, o_zland, o_sum, o_yland, o_two,
    q_sum, q_zland, q_two, v_zland, v_sum, v_yland, v_two,
    a_xland, b_xland, o_xland, q_xland, v_xland, pack, pack_dp, pack_one, pack_chip, pack_two, pack_z, *rest,
):
    scatter_refs, more_refs, q_refs, rest = rest[:10], rest[10:15], rest[15:18], rest[18:]
    (
        az_send, az_recv, by_send, by_recv, oz_send, oz_recv, oy_send, oy_recv,
        qy_send, qy_recv, qz_send, qz_recv, vz_send, vz_recv, vy_send, vy_recv, x_send, x_recv, p_send, p_recv, w_sem, out_sem,
    ) = rest
    near, far = Near(), Far()
    flows = copy_all([(a_in, a_sum), (b_in, b_sum), (grad_out_in, grad_out)], w_sem.at[pl.ds(4, 3)])
    load = copy_all([(wd_in, wd), (hidden_in, hidden)], w_sem.at[pl.ds(0, 2)])
    early = copy_all(
        [
            (query_in, query),
            (keys_in, keys),
            (values_in, values),
            (attended_grad_in, attended_grad),
            (log_sum_in, log_sum),
            (cos_in, cos),
            (up_in, sin_up),
            (sdown_in, sin_down),
            (lowest_in, lowest),
        ],
        w_sem.at[pl.ds(7, 9)],
    )
    load += copy_all([(wh_in, wh), (first_in, first)], w_sem.at[pl.ds(2, 2)])
    late = copy_all(
        [
            (residual_in, residual),
            (residual_grad_in, residual_grad),
            (tok_in, tok),
            (gains_in, gains),
            (sums_in, sums_two),
        ],
        w_sem.at[pl.ds(16, 5)],
    )
    written = []

    def write(src, dst):
        written.extend(copy_all([(src, dst)], out_sem.at[pl.ds(len(written), 1)]))

    t = lax.axis_index("tensor")
    dp_peers = [{"dp": far.dp_of(i)} for i in range(1, 8)]
    chip_peers = [near.dev["s"], near.dev["x"], {"tensor": (t // 4) * 4 + 3 - t % 4}]
    z_peers = [far.partner, near.dev["z"], {"tensor": ((t // 4 + 2) % 4) * 4 + t % 4}]
    greet(dp_peers + chip_peers + z_peers)
    a = PairZ(far, az_send, az_recv)
    b = RingY(far, lambda k, h: b_sum.at[:, far.ahead(k, h)], b_yland, by_send, by_recv)
    o = SumZ(
        far,
        lambda k, h, s: grad_out.at[pl.ds(s * 128, 128), far.ahead(k, h)],
        lambda k, h: o_zland.at[:, far.ahead(k, h)],
        lambda k, h: o_sum.at[:, far.ahead(k, h)],
        oz_send,
        oz_recv,
    )
    o_y = RingY(far, lambda k, h: o_sum.at[:, far.ahead(k, h)], o_yland, oy_send, oy_recv)
    for copy in flows:
        copy.wait()
    b.start()
    a.start(a_sum, a_zland)
    o.start_all()
    xs = [SumX(far, x_send.at[pl.ds(i, 1)], x_recv.at[pl.ds(i, 1)]) for i in range(5)]
    packs = Copies(p_send, p_recv)

    key_acc[...] = jnp.zeros_like(key_acc)
    value_acc[...] = jnp.zeros_like(value_acc)
    scatter = Scatter(near, scatter_refs)
    load[0].wait()
    load[1].wait()

    def make(chip):
        scatter.part[...] = dot_tn(hidden[:, chip_rows(chip)], wd[...])

    def look(block, s):
        start, stop = window(block)
        rows = slice(block * QB, (block + 1) * QB)
        bias_t = mask_bias(lowest[0:1, rows], start, stop, block)
        lanes = slice(s * 128, (s + 1) * 128)
        q, k, v = query[rows, lanes], keys[start:stop, lanes], values[start:stop, lanes]
        grad, k_t = attended_grad[rows, lanes], kt[s, :, start:stop]
        halves, key_sum, value_sum = [], None, None
        for head_id in range(2):
            mine = head_lanes(QB, head_id)
            q_one = jnp.where(mine, q, jnp.zeros_like(q))
            g_one = jnp.where(mine, grad, jnp.zeros_like(grad))
            index = s * 2 + head_id
            probs = jnp.exp(dot_nt(k, q_one) + bias_t - log_sum[index : index + 1, rows])
            prob_grad = dot_nt(v, g_one)
            inner = jnp.sum(probs * prob_grad, axis=0, keepdims=True)
            score_grad = (probs * (prob_grad - inner)).astype(BF)
            made = dot(k_t, score_grad)
            halves.append(made[head_id * HD : (head_id + 1) * HD])
            key_part = dot(score_grad, q_one)
            value_part = dot(probs.astype(BF), g_one)
            key_sum = key_part if key_sum is None else key_sum + key_part
            value_sum = value_part if value_sum is None else value_sum + value_part
        query_grad = jnp.concatenate(halves, axis=0).T * HD ** (-0.5)
        query_grad = roll_rotate(query_grad, cos[rows, :], -sin_up[rows, :], -sin_down[rows, :])
        projected[rows, s * 384 : s * 384 + 128] = query_grad.astype(BF)
        key_acc[s, start:stop, :] += key_sum
        value_acc[s, start:stop, :] += value_sum

    def close_shard(s):
        made = roll_rotate(key_acc[s], cos[...], -sin_up[...], -sin_down[...])
        projected[:, s * 384 + 128 : s * 384 + 256] = made.astype(BF)
        projected[:, s * 384 + 256 : s * 384 + 384] = value_acc[s].astype(BF)

    scatter.produce("d", make)
    scatter.produce("z", make)
    scatter.far()
    scatter.produce("x", make)
    scatter.z_direct()
    scatter.x_direct()
    scatter.produce("o", make)
    def query_key_part(k, j):
        return head_part.at[far.ahead(k, j // 2), pl.ds((j % 2) * 384, Q_LANES)]

    q = SumY(far, query_key_part, q_refs, qy_send, qy_recv)
    v = SumZ(
        far,
        lambda k, h, s: head_part.at[far.ahead(k, h), pl.ds(s * 384 + Q_LANES, V_LANES)],
        lambda k, h: v_zland.at[far.ahead(k, h)],
        lambda k, h: v_sum.at[far.ahead(k, h)],
        vz_send,
        vz_recv,
    )
    q_z = PairZ(far, qz_send, qz_recv)
    v_y = RingY(far, lambda k, h: v_sum.at[far.ahead(k, h)], v_yland, vy_send, vy_recv)
    last = Scatter(near, Scatter.second(scatter_refs, more_refs))

    def make_last(chip):
        rows = chip_rows(chip)
        last.part[...] = dot(projected[rows, :], wh[...])

    def weight_part(k, h, s):
        rows, lanes = far.ahead(k, h), slice(s * 384, (s + 1) * 384)
        head_part[rows, lanes] = dot(first[rows, :], projected[:, lanes]).astype(BF)
        if s == 1:
            v.start(k, h)

    for copy in early:
        copy.wait()
    for s in range(2):
        kt[s] = keys[:, s * 128 : (s + 1) * 128].astype(F32).T.astype(BF)
    look(0, 1)
    scatter.relays()
    for block in range(1, 4):
        look(block, 1)
    close_shard(1)
    load[2].wait()
    load[3].wait()
    for k, h in ((2, 0), (2, 1), (1, 1), (3, 0)):
        weight_part(k, h, 1)
    q.start(1)
    for k, h in ((1, 0), (3, 1), (0, 0), (0, 1)):
        weight_part(k, h, 1)
    look(0, 0)
    a.add(a_two)
    xs[0].start(a_two, a_xland)
    look(1, 0)
    q.relay(1)
    b.add(b_two)
    xs[1].start(b_two, b_xland)
    look(2, 0)
    o.add()
    o_y.start()
    look(3, 0)
    close_shard(0)
    for k, h in ((2, 0), (2, 1), (1, 1), (3, 0)):
        weight_part(k, h, 0)
    q.start(0)
    for copy in late:
        copy.wait()
    one, two = scatter.result()
    mixed[:HALF, :] = residual[:HALF, :] + one
    mixed[HALF:, :] = residual[HALF:, :] + two
    write(mixed, mixed_out)
    last.produce("d", make_last)
    last.produce("z", make_last)
    last.far()
    last.produce("x", make_last)
    last.z_direct()
    for k, h in ((1, 0), (3, 1), (0, 0), (0, 1)):
        weight_part(k, h, 0)
    last.x_direct()
    last.relays()
    q.relay(0)
    last.produce("o", make_last)
    v.add()
    v_y.start()
    o_y.add(o_two)
    xs[2].start(o_two, o_xland)
    bias_sum[...] = jnp.broadcast_to(jnp.sum(projected[...].astype(F32), axis=0, keepdims=True), bias_sum.shape)
    normed, inverse = layer_norm_parts(tok[...].astype(F32))
    q.add(q_sum)
    q_z.start(q_sum, q_zland)
    one, two = last.result()
    part, gain_sum, shift_sum = norm_back(jnp.concatenate([one, two], axis=0), normed, inverse, gains[0:1, :])
    grad_tokens[...] = residual_grad[...] + part
    write(grad_tokens, grad_tokens_out)
    sums = jnp.concatenate([gain_sum, shift_sum, sums_two[0:2, :]], axis=0)
    pack[...] = jnp.zeros_like(pack)
    for d in range(8):
        pack[d, 0:4, :256] = sums[:, d * 256 : (d + 1) * 256]
        pack[d, 4:5, :] = bias_sum[0:1, :384]
        pack[d, 5:6, :] = bias_sum[0:1, 384:]
    for i, device in enumerate(dp_peers):
        packs.go(i, pack.at[far.dp_of(i + 1)], pack_dp.at[i], device)
    gate_up[:A_ROWS, :] = xs[0].add()
    made = xs[1].add()
    gate_up[A_ROWS:, :] = made[: 2 * UNITS - A_ROWS]
    down[...] = made[2 * UNITS - A_ROWS :]
    write(gate_up, gate_up_out)
    write(down, down_out)
    total = pack[far.dp(0, 0)]
    for i, device in enumerate(dp_peers):
        packs.take(i, pack_dp.at[i], device)
        total = total + pack_dp[i]
    pack_one[...] = total
    for i, device in enumerate(chip_peers):
        packs.go(7 + i, pack_one, pack_chip.at[i], device)
    v_y.add(v_two)
    xs[4].start(v_two, v_xland)
    q_z.add(q_two)
    xs[3].start(q_two, q_xland)
    output[...] = xs[2].add()
    write(output, output_out)
    for i, device in enumerate(chip_peers):
        packs.take(7 + i, pack_chip.at[i], device)
        total = jnp.concatenate([total[:4] + pack_chip[i, :4, :], total[4:]], axis=0)
    pack_two[...] = total
    for i, device in enumerate(z_peers):
        packs.go(10 + i, pack_two, pack_z.at[i], device)
    heads[2] = xs[4].add()
    made = xs[3].add()
    heads[0] = made[:, :128]
    heads[1] = made[:, 128:]
    write(heads, heads_out)
    own_bias = total[4:5]
    for i, device in enumerate(z_peers):
        packs.take(10 + i, pack_z.at[i], device)
        total = total + pack_z[i]
    own_bias = own_bias + pack_z[0, 5:6, :]
    dp, tensor = lax.axis_index("dp"), lax.axis_index("tensor")
    norms[...] = pltpu.roll(total[:, :256], 256 - tensor * 16, 1)[:, :128]
    own_bias = pltpu.roll(jnp.broadcast_to(own_bias, (8, 384)), 384 - dp * 8, 1)
    for i in range(6):
        bias_grad[i // 2, i % 2 : i % 2 + 1, :] = own_bias[0:1, i * HD : i * HD + 8]
    packs.finish()
    for job in [a, b, o, o_y, q, q_z, v, v_y] + xs:
        job.copies.finish()
    for copy in written:
        copy.wait()


def close_call(*args):
    def block(*lead):
        return pltpu.VMEM(lead, BF)

    return pl.pallas_call(
        close_kernel,
        out_shape=(
            shape((OWN, D), F32),
            shape((OWN, D), F32),
            shape((8, 128), F32),
            shape((3, 2, 8), F32),
            shape((2 * UNITS, 256), F32),
            shape((UNITS, 256), F32),
            shape((128, 256), F32),
            shape((3, 256, 128), F32),
        ),
        in_specs=[ANYWHERE] * 21,
        out_specs=(ANYWHERE,) * 2 + (IN_VMEM,) * 2 + (ANYWHERE,) * 4,
        scratch_shapes=[
            *[pltpu.VMEM((LEN, 256), BF)] * 4,
            pltpu.VMEM((8, LEN), F32),
            *[pltpu.VMEM((LEN, 128), F32)] * 3,
            pltpu.VMEM((8, LEN), jnp.int32),
            *[pltpu.VMEM((OWN, D), F32)] * 2,
            pltpu.VMEM((OWN, D), BF),
            *[pltpu.VMEM((8, D), F32)] * 2,
            block(4, A_ROWS, 256), block(B_ROWS, D), block(256, D),
            *[pltpu.VMEM((OWN, D), F32)] * 2,
            *[pltpu.VMEM(dims, F32) for dims in ((2 * UNITS, 256), (UNITS, 256), (128, 256), (3, 256, 128))],
            pltpu.VMEM((2, 128, LEN), BF),
            pltpu.VMEM((2, LEN, 128), F32),
            pltpu.VMEM((2, LEN, 128), F32),
            pltpu.VMEM((LEN, 768), BF),
            pltpu.VMEM((2 * PAD, D), BF),
            pltpu.VMEM((768, D), BF),
            pltpu.VMEM((2 * PAD, LEN), BF),
            pltpu.VMEM((D, LEN), BF),
            pltpu.VMEM((D, 768), BF),
            pltpu.VMEM((8, 768), F32),
            block(2, A_ROWS, 256), block(2, A_ROWS, 256),
            block(3, 2, B_ROWS, 256), block(2, B_ROWS, 256),
            block(128, D), block(128, D), block(3, 2, 128, 256), block(2, 128, 256),
            block(4, 256, Q_LANES), block(2, 256, Q_LANES), block(2, 256, Q_LANES),
            block(D, V_LANES), block(D, V_LANES), block(3, 2, 256, V_LANES), block(2, 256, V_LANES),
            block(A_ROWS, 256), block(B_ROWS, 256), block(128, 256), block(256, Q_LANES), block(256, V_LANES),
            *[pltpu.VMEM(lead + (8, 384), F32) for lead in ((8,), (7,), (), (3,), (), (3,))],
            *Scatter.scratch(),
            *Scatter.again(),
            *SumY.scratch((256, Q_LANES)),
            *sems(2, 6, 8, 6, 12, 2, 8, 6, 5, 13),
            DMA((21,)),
            DMA((6,)),
        ],
        compiler_params=params(3),
        cost_estimate=cost(25 * 10**9, 60 * 2**20),
        name="close",
    )(*args)


def results_kernel(*refs):
    n = len(refs) // 3
    ins, outs, held, (in_sem, out_sem) = refs[:n], refs[n : 2 * n], refs[2 * n : 3 * n], refs[3 * n :]
    copies = copy_all(zip(ins, held), in_sem)
    written = []
    for i in range(n):
        copies[i].wait()
        written.extend(copy_all([(held[i], outs[i])], out_sem.at[pl.ds(i, 1)]))
    for copy in written:
        copy.wait()


def results_call(*arrays):
    n = len(arrays)
    return pl.pallas_call(
        results_kernel,
        out_shape=tuple(shape(v.shape, v.dtype) for v in arrays),
        in_specs=[ANYWHERE] * n,
        out_specs=(ANYWHERE,) * n,
        scratch_shapes=[*[pltpu.VMEM(v.shape, v.dtype) for v in arrays], DMA((n,)), DMA((n,))],
        compiler_params=params(),
        cost_estimate=cost(0, 10 * 2**20),
        name="results",
    )(*arrays)


def per_device(
    tokens,
    segments,
    first_gain,
    first_shift,
    heads_weight,
    heads_bias,
    output_weight,
    second_gain,
    second_shift,
    gate_up_weight,
    down_weight,
    cotangent,
):
    (
        first_all, cot_all, query, keys, values, attended, log_sum, residual, second_all, hidden, grads,
        wh, wo, wg, wd, gains, cos, sin_up, sin_down, lowest,
    ) = forward_call(
        tokens,
        cotangent,
        segments,
        *[v.reshape(1, 256) for v in (first_gain, first_shift, second_gain, second_shift)],
        heads_weight.transpose(1, 0, 2),
        heads_bias,
        output_weight,
        gate_up_weight.transpose(1, 2, 0),
        down_weight,
    )
    residual_grad, attended_grad, sums_two, a, b, grad_out = back_call(
        residual, cotangent, gains, grads, second_all, hidden, cot_all, wo, wg, attended
    )
    mixed, grad_tokens, norms, bias_grad, gate_up, down, output, heads = close_call(
        query, keys, values, attended_grad, log_sum, cos, sin_up, sin_down, lowest,
        residual, residual_grad, tokens, gains, sums_two, a, b, grad_out, hidden, first_all, wd, wh,
    )
    mixed, grad_tokens, gate_up, down, output, heads, bias_grad = results_call(
        mixed, grad_tokens, gate_up, down, output, heads, bias_grad
    )
    return (
        mixed,
        grad_tokens,
        norms[0, :16],
        norms[1, :16],
        heads.transpose(1, 0, 2),
        bias_grad,
        output,
        norms[2, :16],
        norms[3, :16],
        gate_up.reshape(2, UNITS, 256).transpose(2, 0, 1),
        down,
    )


ALL = ("dp", "tensor")


def solution(mesh):
    return jax.shard_map(
        per_device,
        mesh=mesh,
        in_specs=(
            P(ALL, None),
            P("dp", None),
            P("dp"),
            P("dp"),
            P("dp", None, "tensor"),
            P(None, "tensor", "dp"),
            P("tensor", "dp"),
            P("dp"),
            P("dp"),
            P("dp", None, "tensor"),
            P("tensor", "dp"),
            P(ALL, None),
        ),
        out_specs=(
            P(ALL, None),
            P(ALL, None),
            P(ALL),
            P(ALL),
            P("dp", None, "tensor"),
            P(None, "tensor", "dp"),
            P("tensor", "dp"),
            P(ALL),
            P(ALL),
            P("dp", None, "tensor"),
            P("tensor", "dp"),
        ),
        check_vma=False,
    )
```

```python
import functools
import math

import jax
import jax.numpy as jnp
from jax import lax
from jax.experimental import pallas as pl
from jax.experimental.pallas import tpu as pltpu
from jax.sharding import PartitionSpec as P

D = 2048
HD = 64
ROT = 16
WINDOW = 512
LEN = 1024
OWN = 128
HALF = OWN // 2
CHIP = 2 * OWN
UNITS = 352
PAD = 384
QB = 256

NORM_EPS = 1e-05
BASE_FREQ = 10000.0
FAR_NEGATIVE = -1e30
BF = jnp.bfloat16
F32 = jnp.float32
MESH = pl.DeviceIdType.MESH
VMEM_LIMIT = 62 * 2**20
DMA = pltpu.SemaphoreType.DMA


def spot(z, x, c):
    return (z % 2) * 4 + x * 2 + c


class Near:
    def __init__(self):
        t = lax.axis_index("tensor")
        z, x, c = t // 4, (t // 2) % 2, t % 2
        oz = (z // 2) * 2 + (z + 1) % 2
        ox, oc = 1 - x, 1 - c
        self.c, self.oc = c, oc
        self.me = spot(z, x, c)
        self.dev = {
            "x": {"tensor": z * 4 + ox * 2 + c},
            "z": {"tensor": oz * 4 + x * 2 + c},
            "s": {"tensor": z * 4 + x * 2 + oc},
        }
        self.same = {"o": spot(z, x, c), "x": spot(z, ox, c), "z": spot(oz, x, c), "d": spot(oz, ox, c)}
        self.other = {
            "o": spot(z, x, oc),
            "x": spot(z, ox, oc),
            "z": spot(oz, x, oc),
            "d": spot(oz, ox, oc),
        }
        self.chip = {"o": (z % 2) * 2 + x, "x": (z % 2) * 2 + ox, "z": (oz % 2) * 2 + x, "d": (oz % 2) * 2 + ox}


def remote(src, dst, send, recv, device):
    return pltpu.make_async_remote_copy(
        src_ref=src, dst_ref=dst, send_sem=send, recv_sem=recv, device_id=device, device_id_type=MESH
    )


def greet(devices):
    barrier = pltpu.get_barrier_semaphore()
    for device in devices:
        pl.semaphore_signal(barrier, inc=1, device_id=device, device_id_type=MESH)
    pl.semaphore_wait(barrier, len(devices))


def block_rows(block, half=None):
    if half is None:
        return pl.ds(pl.multiple_of(block * OWN, OWN), OWN)
    return pl.ds(pl.multiple_of(block * OWN + half * HALF, HALF), HALF)


def chip_rows(chip):
    return pl.ds(pl.multiple_of(chip * CHIP, CHIP), CHIP)


class Gather:
    COPIES = 13

    def __init__(self, near, buf, send, recv):
        self.near, self.buf, self.send, self.recv = near, buf, send, recv
        self.sent = []

    def copy(self, index, block, half, to):
        view = self.buf.at[block_rows(block, half)]
        return remote(view, view, self.send.at[index], self.recv.at[index], self.near.dev[to])

    def go(self, index, block, half, to):
        copy = self.copy(index, block, half, to)
        copy.start()
        self.sent.append(copy)

    def take(self, index, block, half, to="s"):
        self.copy(index, block, half, to).wait_recv()

    def start(self):
        me = self.near.me
        self.go(0, me, 0, "z")
        self.go(1, me, 1, "x")
        self.go(4, me, None, "s")
        self.go(2, me, 0, "x")
        self.go(3, me, 1, "z")

    def first(self):
        same = self.near.same
        self.take(0, same["z"], 0)
        self.go(5, same["z"], 0, "x")
        self.go(7, same["z"], 0, "s")
        self.take(1, same["x"], 1)
        self.go(6, same["x"], 1, "z")
        self.go(8, same["x"], 1, "s")

    def second(self):
        same = self.near.same
        self.take(2, same["x"], 0)
        self.go(9, same["x"], 0, "s")
        self.take(3, same["z"], 1)
        self.go(10, same["z"], 1, "s")

    def third(self):
        same = self.near.same
        self.take(5, same["d"], 0)
        self.go(11, same["d"], 0, "s")
        self.take(6, same["d"], 1)
        self.go(12, same["d"], 1, "s")

    def own_chip(self):
        self.take(4, self.near.other["o"], None)

    def x_chip(self):
        self.take(8, self.near.other["x"], 1)
        self.take(9, self.near.other["x"], 0)

    def z_chip(self):
        self.take(7, self.near.other["z"], 0)
        self.take(10, self.near.other["z"], 1)

    def d_chip(self):
        self.take(11, self.near.other["d"], 0)
        self.take(12, self.near.other["d"], 1)

    def finish(self):
        for copy in self.sent:
            copy.wait_send()

    def run(self, use):
        self.own_chip()
        use("o")
        self.first()
        self.second()
        self.x_chip()
        use("x")
        self.third()
        self.z_chip()
        use("z")
        self.d_chip()
        use("d")


class Scatter:
    COPIES = 10

    @staticmethod
    def scratch(width=D):
        return [
            pltpu.VMEM((CHIP, width), F32),
            pltpu.VMEM((4, OWN, width), F32),
            pltpu.VMEM((4, OWN, width), BF),
            pltpu.VMEM((4, OWN, width), BF),
            pltpu.VMEM((OWN, width), BF),
            pltpu.VMEM((4, HALF, width), BF),
            pltpu.VMEM((2, HALF, width), BF),
            pltpu.VMEM((4, HALF, width), BF),
            DMA((Scatter.COPIES,)),
            DMA((Scatter.COPIES,)),
        ]

    @staticmethod
    def again(width=D):
        return [
            pltpu.VMEM((4, OWN, width), BF),
            pltpu.VMEM((2, HALF, width), BF),
            pltpu.VMEM((4, HALF, width), BF),
            DMA((Scatter.COPIES,)),
            DMA((Scatter.COPIES,)),
        ]

    @staticmethod
    def second(refs, more):
        return list(refs[:3]) + [more[0]] + list(refs[4:6]) + list(more[1:])

    KEYS = ("d", "z", "x", "o")

    def __init__(self, near, refs):
        self.near = near
        (
            self.part,
            self.mine,
            self.core_out,
            self.core_in,
            self.far_out,
            self.out,
            self.through,
            self.last,
            self.send,
            self.recv,
        ) = refs
        self.sent = []

    def copy(self, index, src, dst, to):
        return remote(src, dst, self.send.at[index], self.recv.at[index], self.near.dev[to])

    def go(self, index, src, dst, to):
        copy = self.copy(index, src, dst, to)
        copy.start()
        self.sent.append(copy)

    def take(self, index, dst, to="s"):
        self.copy(index, dst, dst, to).wait_recv()

    def produce(self, key, make):
        i = self.KEYS.index(key)
        make(self.near.chip[key])
        self.core_out[i] = self.part[block_rows(self.near.oc), :].astype(BF)
        self.go(i, self.core_out.at[i], self.core_in.at[i], "s")
        self.mine[i] = self.part[block_rows(self.near.c), :]

    def join(self, key):
        i = self.KEYS.index(key)
        self.take(i, self.core_in.at[i])

    def summed(self, key, half):
        i = self.KEYS.index(key)
        rows = slice(half * HALF, (half + 1) * HALF)
        return self.mine[i, rows, :] + self.core_in[i, rows, :].astype(F32)

    def far(self):
        self.join("d")
        self.far_out[:HALF, :] = self.summed("d", 0).astype(BF)
        self.go(4, self.far_out.at[pl.ds(0, HALF)], self.through.at[0], "z")
        self.far_out[HALF:, :] = self.summed("d", 1).astype(BF)
        self.go(5, self.far_out.at[pl.ds(HALF, HALF)], self.through.at[1], "x")

    def z_direct(self):
        self.join("z")
        self.out[0] = self.summed("z", 0).astype(BF)
        self.go(6, self.out.at[0], self.last.at[0], "z")

    def x_direct(self):
        self.join("x")
        self.out[1] = self.summed("x", 1).astype(BF)
        self.go(7, self.out.at[1], self.last.at[1], "x")

    def relays(self):
        self.take(4, self.through.at[0])
        self.out[2] = (self.summed("x", 0) + self.through[0].astype(F32)).astype(BF)
        self.go(8, self.out.at[2], self.last.at[2], "x")
        self.take(5, self.through.at[1])
        self.out[3] = (self.summed("z", 1) + self.through[1].astype(F32)).astype(BF)
        self.go(9, self.out.at[3], self.last.at[3], "z")

    def result(self):
        self.join("o")
        for index in range(4):
            self.take(6 + index, self.last.at[index])
        first = self.summed("o", 0) + self.last[0].astype(F32) + self.last[2].astype(F32)
        second = self.summed("o", 1) + self.last[1].astype(F32) + self.last[3].astype(F32)
        for copy in self.sent:
            copy.wait_send()
        self.sent = []
        return first, second

    def run(self, make):
        self.produce("d", make)
        self.produce("z", make)
        self.far()
        self.produce("x", make)
        self.z_direct()
        self.x_direct()
        self.relays()
        self.produce("o", make)
        return self.result()


def dot(left, right):
    return jnp.dot(left, right, preferred_element_type=F32)


def dot_nt(left, right):
    return lax.dot_general(left, right, (((1,), (1,)), ((), ())), preferred_element_type=F32)


def dot_tn(left, right):
    return lax.dot_general(left, right, (((0,), (0,)), ((), ())), preferred_element_type=F32)


def layer_norm_parts(values):
    centre = values - jnp.mean(values, axis=-1, keepdims=True)
    inverse = lax.rsqrt(jnp.mean(centre * centre, axis=-1, keepdims=True) + NORM_EPS)
    return (centre * inverse, inverse)


def norm_back(upstream, normed, inverse, gain):
    scaled = upstream * gain
    inner = (
        scaled
        - jnp.mean(scaled, axis=-1, keepdims=True)
        - normed * jnp.mean(scaled * normed, axis=-1, keepdims=True)
    )
    return (
        inner * inverse,
        jnp.sum(upstream * normed, axis=0, keepdims=True),
        jnp.sum(upstream, axis=0, keepdims=True),
    )


def params(collective=None):
    if collective is None:
        return pltpu.CompilerParams(vmem_limit_bytes=VMEM_LIMIT)
    return pltpu.CompilerParams(
        collective_id=collective, has_side_effects=True, vmem_limit_bytes=VMEM_LIMIT
    )


def cost(flops, moved):
    return pl.CostEstimate(flops=flops, bytes_accessed=moved, transcendentals=0)


IN_VMEM = pl.BlockSpec(memory_space=pltpu.VMEM)
ANYWHERE = pl.BlockSpec(memory_space=pl.ANY)


def shape(dims, dtype):
    return jax.ShapeDtypeStruct(dims, dtype)


def copy_all(pairs, sems):
    copies = [pltpu.make_async_copy(src, dst, sems.at[i]) for i, (src, dst) in enumerate(pairs)]
    for copy in copies:
        copy.start()
    return copies


class Far:
    def __init__(self):
        t, dp = lax.axis_index("tensor"), lax.axis_index("dp")
        self.h, self.y = dp // 4, dp % 4
        self.over = {"dp": (1 - self.h) * 4 + self.y}
        self.partner = {"tensor": (3 - t // 4) * 4 + t % 4}
        self.ring = {k: {"dp": self.h * 4 + (self.y + k) % 4} for k in (1, 2, 3)}

    def dp(self, k, h):
        return ((self.h + h) % 2) * 4 + (self.y - k + 4) % 4

    def dp_of(self, i):
        return (self.h + i // 4) % 2 * 4 + (self.y + i % 4) % 4

    def span(self, k, h):
        return pl.ds(pl.multiple_of(self.dp(k, h) * 256, 256), 256)

    def ahead(self, k, h):
        return pl.ds(pl.multiple_of((h * 4 + (self.y + k) % 4) * 256, 256), 256)


class Copies:
    def __init__(self, send, recv):
        self.send, self.recv, self.sent = send, recv, []

    def go(self, index, src, dst, device):
        copy = remote(src, dst, self.send.at[index], self.recv.at[index], device)
        copy.start()
        self.sent.append(copy)

    def take(self, index, dst, device):
        remote(dst, dst, self.send.at[index], self.recv.at[index], device).wait_recv()

    def finish(self):
        for copy in self.sent:
            copy.wait_send()
        self.sent = []


class Ring:
    def __init__(self, far, n, place, send, recv):
        self.far, self.n, self.place = far, n, place
        self.copies = Copies(send, recv)

    def start(self, j, src=None):
        own = self.place(0, j)
        src = own if src is None else src
        self.copies.go(j, src, own, self.far.ring[1])
        self.copies.go(self.n + j, src, own, self.far.ring[3])

    def relay(self, j):
        if j < self.n // 2:
            view = self.place(1, j)
            self.copies.take(j, view, self.far.ring[1])
            self.copies.go(2 * self.n + j, view, view, self.far.ring[1])
        else:
            view = self.place(3, j)
            self.copies.take(self.n + j, view, self.far.ring[3])
            self.copies.go(2 * self.n + j, view, view, self.far.ring[3])

    def near(self, j):
        if j < self.n // 2:
            self.copies.take(self.n + j, self.place(3, j), self.far.ring[3])
        else:
            self.copies.take(j, self.place(1, j), self.far.ring[1])

    def done(self, j):
        self.near(j)
        self.copies.take(2 * self.n + j, self.place(2, j), self.far.ring[1])

    def finish(self, near=True):
        for j in range(self.n):
            if near:
                self.near(j)
            self.copies.take(2 * self.n + j, self.place(2, j), self.far.ring[1])
        self.copies.finish()


class SumY:
    COPIES = 12

    @staticmethod
    def scratch(dims):
        return [
            pltpu.VMEM((4,) + dims, BF),
            pltpu.VMEM((4,) + dims, BF),
            pltpu.VMEM((2, 4) + dims, BF),
        ]

    def __init__(self, far, block, refs, send, recv):
        self.far, self.block = far, block
        self.through, self.out, self.last = refs
        self.copies = Copies(send, recv)

    def to(self, j):
        return self.far.ring[1] if j < 2 else self.far.ring[3]

    def start(self, s):
        for j in (s, 2 + s):
            self.copies.go(j, self.block(2, j), self.through.at[j], self.to(j))
        self.copies.go(4 + 2 + s, self.block(1, 2 + s), self.last.at[0, 2 + s], self.far.ring[1])
        self.copies.go(8 + s, self.block(3, s), self.last.at[1, s], self.far.ring[3])

    def relay(self, s):
        for j, k, side in ((s, 1, 0), (2 + s, 3, 1)):
            self.copies.take(j, self.through.at[j], self.to(j))
            self.out[j] = (self.block(k, j)[...].astype(F32) + self.through[j].astype(F32)).astype(BF)
            self.copies.go(4 + side * 4 + j, self.out.at[j], self.last.at[side, j], self.far.ring[k])

    def add(self, out):
        for j in range(4):
            total = self.block(0, j)[...].astype(F32)
            for side, k in ((0, 1), (1, 3)):
                self.copies.take(4 + side * 4 + j, self.last.at[side, j], self.far.ring[k])
                total = total + self.last[side, j].astype(F32)
            out[j] = total.astype(BF)


class PairZ:
    COPIES = 2

    def __init__(self, far, send, recv):
        self.far, self.copies = far, Copies(send, recv)

    def start(self, sums, land):
        self.sums, self.land = sums, land
        for h in range(2):
            self.copies.go(h, sums.at[h * 2 + 1], land.at[h], self.far.partner)

    def add(self, out):
        for h in range(2):
            self.copies.take(h, self.land.at[h], self.far.partner)
            out[h] = (self.sums[h * 2].astype(F32) + self.land[h].astype(F32)).astype(BF)


class SumZ:
    COPIES = 8

    def __init__(self, far, block, land, out, send, recv):
        self.far, self.block, self.land, self.out = far, block, land, out
        self.copies = Copies(send, recv)

    def start(self, k, h):
        self.copies.go(k * 2 + h, self.block(k, h, 1), self.land(k, h), self.far.partner)

    def start_all(self):
        for k in (2, 1, 3, 0):
            for h in range(2):
                self.start(k, h)

    def add(self):
        for k in (2, 1, 3, 0):
            for h in range(2):
                self.copies.take(k * 2 + h, self.land(k, h), self.far.partner)
                total = self.block(k, h, 0)[...].astype(F32) + self.land(k, h)[...].astype(F32)
                self.out(k, h)[...] = total.astype(BF)


class RingY:
    COPIES = 6

    def __init__(self, far, block, land, send, recv):
        self.far, self.block, self.land = far, block, land
        self.copies = Copies(send, recv)

    def start(self):
        for k in (2, 1, 3):
            for h in range(2):
                self.copies.go((k - 1) * 2 + h, self.block(k, h), self.land.at[k - 1, h], self.far.ring[k])

    def add(self, out):
        for h in range(2):
            total = self.block(0, h)[...].astype(F32)
            for k in (1, 2, 3):
                self.copies.take((k - 1) * 2 + h, self.land.at[k - 1, h], self.far.ring[k])
                total = total + self.land[k - 1, h].astype(F32)
            out[h] = total.astype(BF)


class SumX:
    def __init__(self, far, send, recv):
        self.far, self.copies = far, Copies(send, recv)

    def start(self, sums, land):
        self.sums, self.land = sums, land
        self.copies.go(0, sums.at[1 - self.far.h], land, self.far.over)

    def add(self):
        self.copies.take(0, self.land, self.far.over)
        return self.sums[self.far.h].astype(F32) + self.land[...].astype(F32)


def rotary_tables(starts, cos_out, up_out, down_out):
    index = lax.broadcasted_iota(jnp.int32, (8, LEN), 1)
    power = lax.broadcasted_iota(jnp.int32, (8, LEN), 0).astype(F32)
    angles = (index - starts).astype(F32) * jnp.exp(power * (-2.0 * math.log(BASE_FREQ) / ROT))
    cosine, sine = jnp.cos(angles), jnp.sin(angles)
    none, rest = jnp.zeros((8, LEN), F32), jnp.zeros((HD - ROT, LEN), F32)
    cos_out[...] = jnp.concatenate([cosine, cosine, rest + 1.0] * 2, axis=0).T
    up_out[...] = jnp.concatenate([-sine, none, rest] * 2, axis=0).T
    down_out[...] = jnp.concatenate([none, sine, rest] * 2, axis=0).T


def document_starts(seg):
    index = lax.broadcasted_iota(jnp.int32, (8, LEN), 1)
    new = (index == 0) | (pltpu.roll(seg, 1, 1) != seg)
    starts = jnp.where(new, index, 0)
    step = 1
    while step < LEN:
        starts = jnp.maximum(starts, jnp.where(index >= step, pltpu.roll(starts, step, 1), 0))
        step *= 2
    return starts


def roll_rotate(values, cos, sin_up, sin_down):
    return (
        values * cos + pltpu.roll(values, 128 - ROT // 2, 1) * sin_up + pltpu.roll(values, ROT // 2, 1) * sin_down
    )


def window(block):
    start = max(0, block * QB - WINDOW)
    return start, (block + 1) * QB


def mask_bias(lowest, start, stop, block):
    keys = lax.broadcasted_iota(jnp.int32, (stop - start, QB), 0) + start
    queries = lax.broadcasted_iota(jnp.int32, (stop - start, QB), 1) + block * QB
    return jnp.where((keys <= queries) & (keys >= lowest), 0.0, FAR_NEGATIVE)


def head_lanes(rows, head):
    lanes = lax.broadcasted_iota(jnp.int32, (rows, 128), 1)
    return (lanes >= HD) if head else (lanes < HD)


def silu_parts(gate, up, grad):
    sig = 1.0 / (1.0 + jnp.exp(-gate))
    silu = gate * sig
    return silu * up, grad * up * sig * (1.0 + gate * (1.0 - sig)), grad * silu


def sems(*counts):
    return [DMA((n,)) for n in counts for _ in range(2)]


class Quad:
    def __init__(self, far, place, send, recv):
        self.far, self.place = far, place
        self.copies = Copies(send, recv)

    def over(self, src):
        self.copies.go(0, src, self.place(0, 0), self.far.over)

    def partner(self, src):
        self.copies.go(1, src, self.place(0, 1), self.far.partner)

    def take_over(self):
        self.copies.take(0, self.place(0, 2), self.far.over)
        self.copies.go(2, self.place(0, 2), self.place(0, 3), self.far.partner)

    def take_partner(self):
        self.copies.take(1, self.place(0, 1), self.far.partner)

    def take_last(self):
        self.copies.take(2, self.place(0, 3), self.far.partner)


class Across:
    def __init__(self, far, place, send, recv):
        self.far, self.place = far, place
        self.copies = Copies(send, recv)

    def start(self, k, h, src=None):
        src = self.place(k, h, 0) if src is None else src
        self.copies.go(k * 2 + h, src, self.place(k, h, 1), self.far.partner)

    def finish(self):
        for k in range(4):
            for h in range(2):
                self.copies.take(k * 2 + h, self.place(k, h, 1), self.far.partner)
        self.copies.finish()


class ZLast:
    def __init__(self, far, place, refs):
        x_send, x_recv, r_send, r_recv, z_send, z_recv = refs
        self.far, self.place = far, place
        self.copies = Copies(x_send, x_recv)
        self.ring = Ring(far, 2, lambda k, j: place(k, j, 0), r_send, r_recv)
        self.across = Across(far, place, z_send, z_recv)

    def over(self, src):
        self.src = src
        self.copies.go(0, src, self.place(0, 0, 0), self.far.over)

    def take_over(self):
        self.copies.take(0, self.place(0, 1, 0), self.far.over)

    def partner(self):
        self.across.start(0, 0, self.src)
        self.across.start(0, 1)

    def start(self):
        self.ring.start(0, self.src)
        self.ring.start(1)

    def ring_done(self):
        self.ring.finish(near=False)
        self.across.start(2, 0)
        self.across.start(2, 1)

    def relay(self):
        self.ring.relay(0)
        self.ring.relay(1)
        self.ring.near(0)
        self.ring.near(1)
        for k in (1, 3):
            self.across.start(k, 0)
            self.across.start(k, 1)

    def finish(self):
        self.across.finish()
        self.copies.finish()


Q_LANES = 256
V_LANES = 384 - Q_LANES


def bias_lanes(bias, dp):
    j = lax.broadcasted_iota(jnp.int32, (8, 384), 0)
    lane = lax.broadcasted_iota(jnp.int32, (8, 384), 1)
    pick = jnp.where(lane % HD == dp * 8 + j, 1.0, 0.0).astype(BF)
    total = jnp.zeros((1, 384), F32)
    lane = lax.broadcasted_iota(jnp.int32, (1, 384), 1)
    for p in range(3):
        for h in range(2):
            made = dot(bias[p, h : h + 1, :].astype(BF), pick)
            total = total + jnp.where(lane // HD == p * 2 + h, made, 0.0)
    return total


def forward_kernel(
    tok, cot, seg, gain_one, shift_one, gain_two, shift_two, head_in, bias_in, out_in, gate_in, down_in,
    first_out, cot_out, query_out, keys_out, values_out, attended_out, log_sum, residual_out, second_out, hidden_out,
    grads_out, wh_out, wo_out, wg_out, wd_out, gains, cos_out, up_out, sdown_out, lowest,
    fa, ca, wv, wo, wd, wg, query, keys, values, attended, vt, hg, second, hidden, grads, gbuf, gbuf_two, bias,
    small, head, outw, gate, down, wh_turned, wo_turned, first_turned, residual, cos, sin_up, sin_down, *rest,
):
    scatter_refs, rest = rest[:10], rest[10:]
    (
        ga_send, ga_recv, gc_send, gc_recv, gs_send, gs_recv, sm_send, sm_recv, sr_send, sr_recv,
        hq_send, hq_recv, hr_send, hr_recv, gq_send, gq_recv, gr_send, gr_recv,
    ) = rest[:18]
    out_refs, down_refs, value_refs, (out_sem,) = rest[18:24], rest[24:30], rest[30:36], rest[36:]
    near, far = Near(), Far()
    greet([near.dev["x"], near.dev["z"], near.dev["s"], far.over, far.partner, far.ring[1], far.ring[3]])
    written = []

    def write(src, dst):
        copy = pltpu.make_async_copy(src, dst, out_sem.at[len(written)])
        copy.start()
        written.append(copy)

    def head_at(k, j):
        return wv.at[j % 2, far.span(k, j // 2), pl.ds(0, Q_LANES)]

    def value_at(k, h, s):
        return wv.at[s, far.span(k, h), pl.ds(Q_LANES, V_LANES)]

    def gate_at(k, j):
        return wg.at[pl.ds((j % 2) * 2, 2), pl.ds(0, UNITS), far.span(k, j // 2)]

    def out_at(k, h, s):
        return wo.at[pl.ds(s * 128, 128), far.span(k, h)]

    def down_at(k, h, s):
        return wd.at[pl.ds(s * PAD, UNITS), far.span(k, h)]

    smalls = Copies(sm_send, sm_recv)
    small_ring = Ring(far, 2, lambda k, j: gbuf.at[far.dp(k, j)], sr_send, sr_recv)
    head_quad, head_ring = Quad(far, head_at, hq_send, hq_recv), Ring(far, 4, head_at, hr_send, hr_recv)
    gate_quad, gate_ring = Quad(far, gate_at, gq_send, gq_recv), Ring(far, 4, gate_at, gr_send, gr_recv)
    outs, downs = ZLast(far, out_at, out_refs), ZLast(far, down_at, down_refs)
    vals = ZLast(far, value_at, value_refs)
    firsts = Gather(near, fa, ga_send, ga_recv)
    cots = Gather(near, ca, gc_send, gc_recv)
    seconds = Gather(near, second, gs_send, gs_recv)

    small[0:1, :256] = gain_one[...].astype(BF).astype(F32)
    small[1:2, :256] = shift_one[...].astype(BF).astype(F32)
    small[2:3, :256] = gain_two[...].astype(BF).astype(F32)
    small[3:4, :256] = shift_two[...].astype(BF).astype(F32)
    small[4:5, :] = bias_lanes(bias_in, lax.axis_index("dp"))
    for p in range(3):
        head[:, p * 128 : (p + 1) * 128] = head_in[p].astype(BF)
    smalls.go(0, small, gbuf.at[far.dp(0, 0)], far.over)
    small_ring.start(0, small)
    own_qk, own_v = head.at[:, pl.ds(0, Q_LANES)], head.at[:, pl.ds(Q_LANES, V_LANES)]
    head_quad.over(own_qk)
    head_quad.partner(own_qk)
    vals.over(own_v)
    vals.ring.start(0, own_v)
    head_ring.start(0, own_qk)
    outw[...] = out_in[...].astype(BF)
    down[...] = down_in[...].astype(BF)
    gate[...] = gate_in[...].astype(BF)
    outs.over(outw)
    downs.over(down)
    gbuf[far.dp(0, 0)] = small[...]
    normed, _ = layer_norm_parts(tok[...].astype(F32))
    smalls.take(0, gbuf.at[far.dp(0, 1)], far.over)
    small_ring.start(1)
    vals.take_over()
    vals.ring.start(1)
    vals.partner()
    head_quad.take_over()
    head_ring.start(2)
    small_ring.relay(0)
    small_ring.relay(1)
    small_ring.finish()
    for d in range(8):
        gains[:, d * 256 : (d + 1) * 256] = gbuf[d, :, :256]
    first = normed * gains[0:1, :] + gains[1:2, :]
    fa[block_rows(near.me), :] = first.astype(BF)
    firsts.start()
    vals.relay()
    head_ring.relay(0)
    head_ring.relay(2)
    head_quad.take_partner()
    head_ring.start(1)
    head_quad.take_last()
    head_ring.start(3)
    smalls.go(1, gbuf, gbuf_two, far.partner)
    gate_quad.partner(gate)
    wv[0, far.span(0, 0), :] = head[...]
    vals.ring_done()
    wo[:128, far.span(0, 0)] = outw[...]
    wd[:UNITS, far.span(0, 0)] = down[...]
    wg[0, :UNITS, far.span(0, 0)] = gate[0]
    wg[1, :UNITS, far.span(0, 0)] = gate[1]
    for i in range(4):
        wg[i, UNITS:, :] = jnp.zeros((PAD - UNITS, D), BF)
    for i in range(2):
        wd[i * PAD + UNITS : (i + 1) * PAD, :] = jnp.zeros((PAD - UNITS, D), BF)
    starts = document_starts(jnp.broadcast_to(seg[pl.ds(lax.axis_index("tensor") // 8, 1), :], (8, LEN)))
    index = lax.broadcasted_iota(jnp.int32, (8, LEN), 1)
    lowest[...] = jnp.maximum(starts, index - (WINDOW - 1))
    head_ring.relay(1)
    head_ring.relay(3)
    firsts.first()
    firsts.second()
    rotary_tables(starts, cos, sin_up, sin_down)
    for src, dst in ((cos, cos_out), (sin_up, up_out), (sin_down, sdown_out)):
        write(src, dst)
    smalls.take(1, gbuf_two, far.partner)
    bias[0:1, :384] = jnp.sum(gbuf[:, 4, :], axis=0, keepdims=True)
    bias[0:1, 384:] = jnp.sum(gbuf_two[:, 4, :], axis=0, keepdims=True)
    outs.take_over()
    outs.ring.start(0, outw)
    outs.ring.start(1)
    outs.partner()
    firsts.third()
    gate_quad.over(gate)
    head_ring.done(0)
    head_ring.done(2)

    def project(chip, s):
        rows = chip_rows(chip)
        c, up, down = cos[rows, :], sin_up[rows, :], sin_down[rows, :]
        lanes = slice(s * 128, (s + 1) * 128)
        made = dot(fa[rows, :], wv[s]) + bias[0:1, s * 384 : (s + 1) * 384]
        query[rows, lanes] = (roll_rotate(made[:, :128], c, up, down) * HD ** (-0.5)).astype(BF)
        keys[rows, lanes] = roll_rotate(made[:, 128:256], c, up, down).astype(BF)
        values[rows, lanes] = made[:, 256:].astype(BF)
        vt[chip, s] = made[:, 256:].T.astype(BF)

    def look(block, s):
        start, stop = window(block)
        rows = slice(block * QB, (block + 1) * QB)
        bias_t = mask_bias(lowest[0:1, rows], start, stop, block)
        lanes = slice(s * 128, (s + 1) * 128)
        q, k = query[rows, lanes], keys[start:stop, lanes]
        v_t = jnp.concatenate([vt[i, s] for i in range(start // CHIP, stop // CHIP)], axis=1)
        halves = []
        for head_id in range(2):
            q_one = jnp.where(head_lanes(QB, head_id), q, jnp.zeros_like(q))
            scores = dot_nt(k, q_one) + bias_t
            top = jnp.max(scores, axis=0, keepdims=True)
            weights = jnp.exp(scores - top)
            total = jnp.sum(weights, axis=0, keepdims=True)
            made = dot(v_t, weights.astype(BF))
            halves.append(made[head_id * HD : (head_id + 1) * HD] * (1.0 / total))
            log_sum[s * 2 + head_id : s * 2 + head_id + 1, rows] = top + jnp.log(total)
        attended[rows, lanes] = jnp.concatenate(halves, axis=0).T.astype(BF)

    firsts.own_chip()
    project(near.chip["o"], 0)
    firsts.x_chip()
    project(near.chip["x"], 0)
    firsts.z_chip()
    project(near.chip["z"], 0)
    firsts.d_chip()
    project(near.chip["d"], 0)
    ca[block_rows(near.me), :] = cot[...]
    cots.start()
    look(0, 0)
    downs.ring.start(0, down)
    outs.relay()
    look(1, 0)
    look(2, 0)
    gate_quad.take_over()
    downs.take_over()
    downs.ring.start(1)
    downs.partner()
    look(3, 0)
    head_ring.done(1)
    head_ring.done(3)
    vals.across.finish()
    gate_ring.start(0, gate)
    gate_ring.start(2)
    for key in "oxzd":
        project(near.chip[key], 1)
    outs.ring_done()
    for src, dst in ((query, query_out), (keys, keys_out), (values, values_out)):
        write(src, dst)
    look(0, 1)
    gate_quad.take_partner()
    gate_ring.start(1)
    look(1, 1)
    downs.relay()
    gate_quad.take_last()
    gate_ring.start(3)
    cots.first()
    cots.second()
    look(2, 1)
    look(3, 1)
    cots.third()
    outs.finish()
    scatter = Scatter(near, scatter_refs)

    def make(chip):
        rows = chip_rows(chip)
        scatter.part[...] = dot(attended[rows, :], wo[...])

    scatter.produce("d", make)
    scatter.produce("z", make)
    scatter.far()
    scatter.produce("x", make)
    scatter.z_direct()
    scatter.x_direct()
    scatter.relays()
    scatter.produce("o", make)
    for half in range(2):
        wh_turned[half * 384 : (half + 1) * 384, :] = wv[half].T
    write(wh_turned, wh_out)
    for chip in range(4):
        first_turned[:, chip * CHIP : (chip + 1) * CHIP] = fa[chip * CHIP : (chip + 1) * CHIP, :].T
    write(first_turned, first_out)
    downs.ring_done()
    write(attended, attended_out)
    wo_turned[...] = wo[...].T
    write(wo_turned, wo_out)
    gate_ring.relay(0)
    gate_ring.relay(1)
    gate_ring.relay(2)
    gate_ring.relay(3)
    cots.own_chip()
    cots.x_chip()
    cots.z_chip()
    cots.d_chip()
    write(ca, cot_out)
    one, two = scatter.result()
    residual[:HALF, :] = tok[:HALF, :].astype(F32) + one
    residual[HALF:, :] = tok[HALF:, :].astype(F32) + two
    write(residual, residual_out)
    normed, _ = layer_norm_parts(residual[...])
    second[block_rows(near.me), :] = (normed * gains[2:3, :] + gains[3:4, :]).astype(BF)
    seconds.start()
    seconds.first()
    seconds.second()
    downs.finish()
    write(wd, wd_out)
    for chip in range(4):
        rows = slice(chip * CHIP, (chip + 1) * CHIP)
        hg[:, rows] = dot_nt(wd[...], ca[rows, :])
    seconds.third()
    gate_ring.finish()
    write(wg, wg_out)

    def use(key):
        chip = near.chip[key]
        rows = chip_rows(chip)
        for s in range(2):
            made = dot_nt(wg[s * 2 : s * 2 + 2].reshape(2 * PAD, D), second[rows, :])
            h, g, u = silu_parts(made[:PAD], made[PAD:], hg[s * PAD : (s + 1) * PAD, rows])
            hidden[s * PAD : (s + 1) * PAD, rows] = h.astype(BF)
            grads[s * 2 * PAD : s * 2 * PAD + PAD, rows] = g.astype(BF)
            grads[s * 2 * PAD + PAD : (s + 1) * 2 * PAD, rows] = u.astype(BF)
        write(second.at[rows], second_out.at[rows])
        write(hidden.at[:, rows], hidden_out.at[:, rows])
        write(grads.at[:, rows], grads_out.at[:, rows])

    seconds.own_chip()
    use("o")
    seconds.x_chip()
    use("x")
    seconds.z_chip()
    use("z")
    seconds.d_chip()
    use("d")
    for group in (smalls, head_quad.copies, head_ring.copies, gate_quad.copies, vals.copies, firsts, cots, seconds):
        group.finish()
    for copy in written:
        copy.wait()


def forward_call(*args):
    narrow = shape((LEN, 256), BF)
    return pl.pallas_call(
        forward_kernel,
        out_shape=(
            shape((D, LEN), BF),
            shape((LEN, D), BF),
            narrow,
            narrow,
            narrow,
            narrow,
            shape((8, LEN), F32),
            shape((OWN, D), F32),
            shape((LEN, D), BF),
            shape((2 * PAD, LEN), BF),
            shape((4 * PAD, LEN), BF),
            shape((768, D), BF),
            shape((D, 256), BF),
            shape((4, PAD, D), BF),
            shape((2 * PAD, D), BF),
            shape((8, D), F32),
            shape((LEN, 128), F32),
            shape((LEN, 128), F32),
            shape((LEN, 128), F32),
            shape((8, LEN), jnp.int32),
        ),
        in_specs=[IN_VMEM] * 12,
        out_specs=(ANYWHERE,) * 6 + (IN_VMEM,) + (ANYWHERE,) * 8 + (IN_VMEM,) + (ANYWHERE,) * 3 + (IN_VMEM,),
        scratch_shapes=[
            pltpu.VMEM((LEN, D), BF),
            pltpu.VMEM((LEN, D), BF),
            pltpu.VMEM((2, D, 384), BF),
            pltpu.VMEM((256, D), BF),
            pltpu.VMEM((2 * PAD, D), BF),
            pltpu.VMEM((4, PAD, D), BF),
            pltpu.VMEM((LEN, 256), BF),
            pltpu.VMEM((LEN, 256), BF),
            pltpu.VMEM((LEN, 256), BF),
            pltpu.VMEM((LEN, 256), BF),
            pltpu.VMEM((4, 2, 128, CHIP), BF),
            pltpu.VMEM((2 * PAD, LEN), F32),
            pltpu.VMEM((LEN, D), BF),
            pltpu.VMEM((2 * PAD, LEN), BF),
            pltpu.VMEM((4 * PAD, LEN), BF),
            pltpu.VMEM((8, 8, 384), F32),
            pltpu.VMEM((8, 8, 384), F32),
            pltpu.VMEM((8, 768), F32),
            pltpu.VMEM((8, 384), F32),
            pltpu.VMEM((256, 384), BF),
            pltpu.VMEM((128, 256), BF),
            pltpu.VMEM((2, UNITS, 256), BF),
            pltpu.VMEM((UNITS, 256), BF),
            pltpu.VMEM((768, D), BF),
            pltpu.VMEM((D, 256), BF),
            pltpu.VMEM((D, LEN), BF),
            pltpu.VMEM((OWN, D), F32),
            pltpu.VMEM((LEN, 128), F32),
            pltpu.VMEM((LEN, 128), F32),
            pltpu.VMEM((LEN, 128), F32),
            *Scatter.scratch(),
            *sems(*[Gather.COPIES] * 3, 2, 6, 3, 12, 3, 12, *[1, 6, 8] * 3),
            DMA((27,)),
        ],
        compiler_params=params(1),
        cost_estimate=cost(40 * 10**9, 80 * 2**20),
        name="forward",
    )(*args)


ROWS = 3 * UNITS
A_ROWS = 608
B_ROWS = ROWS - A_ROWS


def back_kernel(
    residual_in, cot_own_in, gains_in, grads_in, second_in, hidden_in, cot_in, wo_in, wg_in, attended_in,
    residual_grad_out, attended_grad_out, norm_sums, a_sum, b_sum_out, grad_out_out,
    wo, wg, branch, grads, second, hidden, cots, attended, parts, b_land,
    residual, cot, gains, residual_grad, attended_grad, b_sum, grad_out, *rest,
):
    scatter_refs, a_refs, rest = rest[:10], rest[10:13], rest[13:]
    ga_send, ga_recv, ay_send, ay_recv, bz_send, bz_recv, w_sem, o_sem = rest
    near, far = Near(), Far()
    load = copy_all(
        [
            (wg_in, wg),
            (grads_in, grads),
            (second_in, second),
            (hidden_in, hidden),
            (cot_in, cots),
            (wo_in, wo),
            (attended_in, attended),
            (residual_in, residual),
            (cot_own_in, cot),
            (gains_in, gains),
        ],
        w_sem,
    )
    greet([near.dev["x"], near.dev["z"], near.dev["s"], far.partner, far.ring[1], far.ring[3]])
    a_rows, b_rows = pl.ds(0, A_ROWS), pl.ds(A_ROWS, B_ROWS)
    a = SumY(far, lambda k, j: parts.at[j % 2, a_rows, far.ahead(k, j // 2)], a_refs, ay_send, ay_recv)
    b = SumZ(
        far,
        lambda k, h, s: parts.at[s, b_rows, far.ahead(k, h)],
        lambda k, h: b_land.at[:, far.ahead(k, h)],
        lambda k, h: b_sum.at[:, far.ahead(k, h)],
        bz_send,
        bz_recv,
    )
    scatter = Scatter(near, scatter_refs)

    def make(chip):
        scatter.part[...] = dot_tn(grads[:, chip_rows(chip)], wg[...].reshape(4 * PAD, D))

    def gate_part(s):
        start = s * 2 * PAD
        parts[s, :UNITS, :] = dot(grads[start : start + UNITS, :], second[...]).astype(BF)

    def up_part(s):
        start = s * 2 * PAD + PAD
        parts[s, UNITS : 2 * UNITS, :] = dot(grads[start : start + UNITS, :], second[...]).astype(BF)

    def down_part(s):
        start = s * PAD
        parts[s, 2 * UNITS :, :] = dot(hidden[start : start + UNITS, :], cots[...]).astype(BF)

    for copy in load[1:5]:
        copy.wait()
    up_part(1)
    down_part(1)
    b.start_all()
    load[0].wait()
    scatter.produce("d", make)
    scatter.produce("z", make)
    scatter.far()
    gate_part(1)
    a.start(1)
    scatter.produce("x", make)
    scatter.z_direct()
    scatter.x_direct()
    scatter.relays()
    scatter.produce("o", make)
    gate_part(0)
    up_part(0)
    a.start(0)
    a.relay(1)
    first, second_half = scatter.result()
    for copy in load[7:]:
        copy.wait()
    normed, inverse = layer_norm_parts(residual[...])
    upstream = jnp.concatenate([first, second_half], axis=0)
    part, gain_sum, shift_sum = norm_back(upstream, normed, inverse, gains[2:3, :])
    made = cot[...].astype(F32) + part
    residual_grad[...] = made
    written = copy_all([(residual_grad, residual_grad_out)], o_sem.at[pl.ds(0, 1)])
    norm_sums[...] = jnp.concatenate([gain_sum, shift_sum] * 4, axis=0)
    branch[block_rows(near.me), :] = made.astype(BF)
    gather = Gather(near, branch, ga_send, ga_recv)
    gather.start()
    load[5].wait()
    load[6].wait()
    down_part(0)
    a.relay(0)

    def use(key):
        rows = chip_rows(near.chip[key])
        attended_grad[rows, :] = dot(branch[rows, :], wo[...]).astype(BF)

    gather.own_chip()
    use("o")
    gather.first()
    gather.second()
    gather.x_chip()
    use("x")
    gather.third()
    gather.z_chip()
    use("z")
    b.add()
    written += copy_all([(b_sum, b_sum_out)], o_sem.at[pl.ds(3, 1)])
    gather.d_chip()
    use("d")
    written += copy_all([(attended_grad, attended_grad_out)], o_sem.at[pl.ds(1, 1)])
    grad_out[...] = dot_tn(attended[...], branch[...]).astype(BF)
    written += copy_all([(grad_out, grad_out_out)], o_sem.at[pl.ds(2, 1)])
    gather.finish()
    a.add(a_sum)
    for job in (a, b):
        job.copies.finish()
    for copy in written:
        copy.wait()


def back_call(*args):
    return pl.pallas_call(
        back_kernel,
        out_shape=(
            shape((OWN, D), F32),
            shape((LEN, 256), BF),
            shape((8, D), F32),
            shape((4, A_ROWS, 256), BF),
            shape((B_ROWS, D), BF),
            shape((256, D), BF),
        ),
        in_specs=[ANYWHERE] * 10,
        out_specs=(ANYWHERE,) * 2 + (IN_VMEM,) * 2 + (ANYWHERE,) * 2,
        scratch_shapes=[
            pltpu.VMEM((D, 256), BF),
            pltpu.VMEM((4, PAD, D), BF),
            pltpu.VMEM((LEN, D), BF),
            pltpu.VMEM((4 * PAD, LEN), BF),
            pltpu.VMEM((LEN, D), BF),
            pltpu.VMEM((2 * PAD, LEN), BF),
            pltpu.VMEM((LEN, D), BF),
            pltpu.VMEM((LEN, 256), BF),
            pltpu.VMEM((2, ROWS, D), BF),
            pltpu.VMEM((B_ROWS, D), BF),
            pltpu.VMEM((OWN, D), F32),
            pltpu.VMEM((OWN, D), BF),
            pltpu.VMEM((8, D), F32),
            pltpu.VMEM((OWN, D), F32),
            pltpu.VMEM((LEN, 256), BF),
            pltpu.VMEM((B_ROWS, D), BF),
            pltpu.VMEM((256, D), BF),
            *Scatter.scratch(),
            *SumY.scratch((A_ROWS, 256)),
            *sems(Gather.COPIES, SumY.COPIES, SumZ.COPIES),
            DMA((10,)),
            DMA((4,)),
        ],
        compiler_params=params(2),
        cost_estimate=cost(25 * 10**9, 60 * 2**20),
        name="back",
    )(*args)


def close_kernel(
    query_in, keys_in, values_in, attended_grad_in, log_sum_in, cos_in, up_in, sdown_in, lowest_in,
    residual_in, residual_grad_in, tok_in, gains_in, sums_in, a_in, b_in, grad_out_in, hidden_in, first_in, wd_in, wh_in,
    mixed_out, grad_tokens_out, norms, bias_grad, gate_up_out, down_out, output_out, heads_out,
    query, keys, values, attended_grad, log_sum, cos, sin_up, sin_down, lowest,
    residual, residual_grad, tok, gains, sums_two, a_sum, b_sum, grad_out,
    mixed, grad_tokens, gate_up, down, output, heads, kt, key_acc, value_acc, projected, wd, wh, hidden, first, head_part, bias_sum,
    a_zland, a_two, b_yland, b_two, o_zland, o_sum, o_yland, o_two,
    q_sum, q_zland, q_two, v_zland, v_sum, v_yland, v_two,
    a_xland, b_xland, o_xland, q_xland, v_xland, pack, pack_dp, pack_one, pack_chip, pack_two, pack_z, *rest,
):
    scatter_refs, more_refs, q_refs, rest = rest[:10], rest[10:15], rest[15:18], rest[18:]
    (
        az_send, az_recv, by_send, by_recv, oz_send, oz_recv, oy_send, oy_recv,
        qy_send, qy_recv, qz_send, qz_recv, vz_send, vz_recv, vy_send, vy_recv, x_send, x_recv, p_send, p_recv, w_sem, out_sem,
    ) = rest
    near, far = Near(), Far()
    flows = copy_all([(a_in, a_sum), (b_in, b_sum), (grad_out_in, grad_out)], w_sem.at[pl.ds(4, 3)])
    load = copy_all([(wd_in, wd), (hidden_in, hidden)], w_sem.at[pl.ds(0, 2)])
    early = copy_all(
        [
            (query_in, query),
            (keys_in, keys),
            (values_in, values),
            (attended_grad_in, attended_grad),
            (log_sum_in, log_sum),
            (cos_in, cos),
            (up_in, sin_up),
            (sdown_in, sin_down),
            (lowest_in, lowest),
        ],
        w_sem.at[pl.ds(7, 9)],
    )
    load += copy_all([(wh_in, wh), (first_in, first)], w_sem.at[pl.ds(2, 2)])
    late = copy_all(
        [
            (residual_in, residual),
            (residual_grad_in, residual_grad),
            (tok_in, tok),
            (gains_in, gains),
            (sums_in, sums_two),
        ],
        w_sem.at[pl.ds(16, 5)],
    )
    written = []

    def write(src, dst):
        written.extend(copy_all([(src, dst)], out_sem.at[pl.ds(len(written), 1)]))

    t = lax.axis_index("tensor")
    dp_peers = [{"dp": far.dp_of(i)} for i in range(1, 8)]
    chip_peers = [near.dev["s"], near.dev["x"], {"tensor": (t // 4) * 4 + 3 - t % 4}]
    z_peers = [far.partner, near.dev["z"], {"tensor": ((t // 4 + 2) % 4) * 4 + t % 4}]
    greet(dp_peers + chip_peers + z_peers)
    a = PairZ(far, az_send, az_recv)
    b = RingY(far, lambda k, h: b_sum.at[:, far.ahead(k, h)], b_yland, by_send, by_recv)
    o = SumZ(
        far,
        lambda k, h, s: grad_out.at[pl.ds(s * 128, 128), far.ahead(k, h)],
        lambda k, h: o_zland.at[:, far.ahead(k, h)],
        lambda k, h: o_sum.at[:, far.ahead(k, h)],
        oz_send,
        oz_recv,
    )
    o_y = RingY(far, lambda k, h: o_sum.at[:, far.ahead(k, h)], o_yland, oy_send, oy_recv)
    for copy in flows:
        copy.wait()
    b.start()
    a.start(a_sum, a_zland)
    o.start_all()
    xs = [SumX(far, x_send.at[pl.ds(i, 1)], x_recv.at[pl.ds(i, 1)]) for i in range(5)]
    packs = Copies(p_send, p_recv)

    key_acc[...] = jnp.zeros_like(key_acc)
    value_acc[...] = jnp.zeros_like(value_acc)
    scatter = Scatter(near, scatter_refs)
    load[0].wait()
    load[1].wait()

    def make(chip):
        scatter.part[...] = dot_tn(hidden[:, chip_rows(chip)], wd[...])

    def look(block, s):
        start, stop = window(block)
        rows = slice(block * QB, (block + 1) * QB)
        bias_t = mask_bias(lowest[0:1, rows], start, stop, block)
        lanes = slice(s * 128, (s + 1) * 128)
        q, k, v = query[rows, lanes], keys[start:stop, lanes], values[start:stop, lanes]
        grad, k_t = attended_grad[rows, lanes], kt[s, :, start:stop]
        halves, key_sum, value_sum = [], None, None
        for head_id in range(2):
            mine = head_lanes(QB, head_id)
            q_one = jnp.where(mine, q, jnp.zeros_like(q))
            g_one = jnp.where(mine, grad, jnp.zeros_like(grad))
            index = s * 2 + head_id
            probs = jnp.exp(dot_nt(k, q_one) + bias_t - log_sum[index : index + 1, rows])
            prob_grad = dot_nt(v, g_one)
            inner = jnp.sum(probs * prob_grad, axis=0, keepdims=True)
            score_grad = (probs * (prob_grad - inner)).astype(BF)
            made = dot(k_t, score_grad)
            halves.append(made[head_id * HD : (head_id + 1) * HD])
            key_part = dot(score_grad, q_one)
            value_part = dot(probs.astype(BF), g_one)
            key_sum = key_part if key_sum is None else key_sum + key_part
            value_sum = value_part if value_sum is None else value_sum + value_part
        query_grad = jnp.concatenate(halves, axis=0).T * HD ** (-0.5)
        query_grad = roll_rotate(query_grad, cos[rows, :], -sin_up[rows, :], -sin_down[rows, :])
        projected[rows, s * 384 : s * 384 + 128] = query_grad.astype(BF)
        key_acc[s, start:stop, :] += key_sum
        value_acc[s, start:stop, :] += value_sum

    def close_shard(s):
        made = roll_rotate(key_acc[s], cos[...], -sin_up[...], -sin_down[...])
        projected[:, s * 384 + 128 : s * 384 + 256] = made.astype(BF)
        projected[:, s * 384 + 256 : s * 384 + 384] = value_acc[s].astype(BF)

    scatter.produce("d", make)
    scatter.produce("z", make)
    scatter.far()
    scatter.produce("x", make)
    scatter.z_direct()
    scatter.x_direct()
    scatter.produce("o", make)
    def query_key_part(k, j):
        return head_part.at[far.ahead(k, j // 2), pl.ds((j % 2) * 384, Q_LANES)]

    q = SumY(far, query_key_part, q_refs, qy_send, qy_recv)
    v = SumZ(
        far,
        lambda k, h, s: head_part.at[far.ahead(k, h), pl.ds(s * 384 + Q_LANES, V_LANES)],
        lambda k, h: v_zland.at[far.ahead(k, h)],
        lambda k, h: v_sum.at[far.ahead(k, h)],
        vz_send,
        vz_recv,
    )
    q_z = PairZ(far, qz_send, qz_recv)
    v_y = RingY(far, lambda k, h: v_sum.at[far.ahead(k, h)], v_yland, vy_send, vy_recv)
    last = Scatter(near, Scatter.second(scatter_refs, more_refs))

    def make_last(chip):
        rows = chip_rows(chip)
        last.part[...] = dot(projected[rows, :], wh[...])

    def weight_part(k, h, s):
        rows, lanes = far.ahead(k, h), slice(s * 384, (s + 1) * 384)
        head_part[rows, lanes] = dot(first[rows, :], projected[:, lanes]).astype(BF)
        if s == 1:
            v.start(k, h)

    for copy in early:
        copy.wait()
    for s in range(2):
        kt[s] = keys[:, s * 128 : (s + 1) * 128].astype(F32).T.astype(BF)
    look(0, 1)
    scatter.relays()
    for block in range(1, 4):
        look(block, 1)
    close_shard(1)
    load[2].wait()
    load[3].wait()
    for k, h in ((2, 0), (2, 1), (1, 1), (3, 0)):
        weight_part(k, h, 1)
    q.start(1)
    for k, h in ((1, 0), (3, 1), (0, 0), (0, 1)):
        weight_part(k, h, 1)
    look(0, 0)
    a.add(a_two)
    xs[0].start(a_two, a_xland)
    look(1, 0)
    q.relay(1)
    b.add(b_two)
    xs[1].start(b_two, b_xland)
    look(2, 0)
    o.add()
    o_y.start()
    look(3, 0)
    close_shard(0)
    for k, h in ((2, 0), (2, 1), (1, 1), (3, 0)):
        weight_part(k, h, 0)
    q.start(0)
    for copy in late:
        copy.wait()
    one, two = scatter.result()
    mixed[:HALF, :] = residual[:HALF, :] + one
    mixed[HALF:, :] = residual[HALF:, :] + two
    write(mixed, mixed_out)
    last.produce("d", make_last)
    last.produce("z", make_last)
    last.far()
    last.produce("x", make_last)
    last.z_direct()
    for k, h in ((1, 0), (3, 1), (0, 0), (0, 1)):
        weight_part(k, h, 0)
    last.x_direct()
    last.relays()
    q.relay(0)
    last.produce("o", make_last)
    v.add()
    v_y.start()
    o_y.add(o_two)
    xs[2].start(o_two, o_xland)
    bias_sum[...] = jnp.broadcast_to(jnp.sum(projected[...].astype(F32), axis=0, keepdims=True), bias_sum.shape)
    normed, inverse = layer_norm_parts(tok[...].astype(F32))
    q.add(q_sum)
    q_z.start(q_sum, q_zland)
    one, two = last.result()
    part, gain_sum, shift_sum = norm_back(jnp.concatenate([one, two], axis=0), normed, inverse, gains[0:1, :])
    grad_tokens[...] = residual_grad[...] + part
    write(grad_tokens, grad_tokens_out)
    sums = jnp.concatenate([gain_sum, shift_sum, sums_two[0:2, :]], axis=0)
    pack[...] = jnp.zeros_like(pack)
    for d in range(8):
        pack[d, 0:4, :256] = sums[:, d * 256 : (d + 1) * 256]
        pack[d, 4:5, :] = bias_sum[0:1, :384]
        pack[d, 5:6, :] = bias_sum[0:1, 384:]
    for i, device in enumerate(dp_peers):
        packs.go(i, pack.at[far.dp_of(i + 1)], pack_dp.at[i], device)
    gate_up[:A_ROWS, :] = xs[0].add()
    made = xs[1].add()
    gate_up[A_ROWS:, :] = made[: 2 * UNITS - A_ROWS]
    down[...] = made[2 * UNITS - A_ROWS :]
    write(gate_up, gate_up_out)
    write(down, down_out)
    total = pack[far.dp(0, 0)]
    for i, device in enumerate(dp_peers):
        packs.take(i, pack_dp.at[i], device)
        total = total + pack_dp[i]
    pack_one[...] = total
    for i, device in enumerate(chip_peers):
        packs.go(7 + i, pack_one, pack_chip.at[i], device)
    v_y.add(v_two)
    xs[4].start(v_two, v_xland)
    q_z.add(q_two)
    xs[3].start(q_two, q_xland)
    output[...] = xs[2].add()
    write(output, output_out)
    for i, device in enumerate(chip_peers):
        packs.take(7 + i, pack_chip.at[i], device)
        total = jnp.concatenate([total[:4] + pack_chip[i, :4, :], total[4:]], axis=0)
    pack_two[...] = total
    for i, device in enumerate(z_peers):
        packs.go(10 + i, pack_two, pack_z.at[i], device)
    heads[2] = xs[4].add()
    made = xs[3].add()
    heads[0] = made[:, :128]
    heads[1] = made[:, 128:]
    write(heads, heads_out)
    own_bias = total[4:5]
    for i, device in enumerate(z_peers):
        packs.take(10 + i, pack_z.at[i], device)
        total = total + pack_z[i]
    own_bias = own_bias + pack_z[0, 5:6, :]
    dp, tensor = lax.axis_index("dp"), lax.axis_index("tensor")
    norms[...] = pltpu.roll(total[:, :256], 256 - tensor * 16, 1)[:, :128]
    own_bias = pltpu.roll(jnp.broadcast_to(own_bias, (8, 384)), 384 - dp * 8, 1)
    for i in range(6):
        bias_grad[i // 2, i % 2 : i % 2 + 1, :] = own_bias[0:1, i * HD : i * HD + 8]
    packs.finish()
    for job in [a, b, o, o_y, q, q_z, v, v_y] + xs:
        job.copies.finish()
    for copy in written:
        copy.wait()


def close_call(*args):
    def block(*lead):
        return pltpu.VMEM(lead, BF)

    return pl.pallas_call(
        close_kernel,
        out_shape=(
            shape((OWN, D), F32),
            shape((OWN, D), F32),
            shape((8, 128), F32),
            shape((3, 2, 8), F32),
            shape((2 * UNITS, 256), F32),
            shape((UNITS, 256), F32),
            shape((128, 256), F32),
            shape((3, 256, 128), F32),
        ),
        in_specs=[ANYWHERE] * 21,
        out_specs=(ANYWHERE,) * 2 + (IN_VMEM,) * 2 + (ANYWHERE,) * 4,
        scratch_shapes=[
            *[pltpu.VMEM((LEN, 256), BF)] * 4,
            pltpu.VMEM((8, LEN), F32),
            *[pltpu.VMEM((LEN, 128), F32)] * 3,
            pltpu.VMEM((8, LEN), jnp.int32),
            *[pltpu.VMEM((OWN, D), F32)] * 2,
            pltpu.VMEM((OWN, D), BF),
            *[pltpu.VMEM((8, D), F32)] * 2,
            block(4, A_ROWS, 256), block(B_ROWS, D), block(256, D),
            *[pltpu.VMEM((OWN, D), F32)] * 2,
            *[pltpu.VMEM(dims, F32) for dims in ((2 * UNITS, 256), (UNITS, 256), (128, 256), (3, 256, 128))],
            pltpu.VMEM((2, 128, LEN), BF),
            pltpu.VMEM((2, LEN, 128), F32),
            pltpu.VMEM((2, LEN, 128), F32),
            pltpu.VMEM((LEN, 768), BF),
            pltpu.VMEM((2 * PAD, D), BF),
            pltpu.VMEM((768, D), BF),
            pltpu.VMEM((2 * PAD, LEN), BF),
            pltpu.VMEM((D, LEN), BF),
            pltpu.VMEM((D, 768), BF),
            pltpu.VMEM((8, 768), F32),
            block(2, A_ROWS, 256), block(2, A_ROWS, 256),
            block(3, 2, B_ROWS, 256), block(2, B_ROWS, 256),
            block(128, D), block(128, D), block(3, 2, 128, 256), block(2, 128, 256),
            block(4, 256, Q_LANES), block(2, 256, Q_LANES), block(2, 256, Q_LANES),
            block(D, V_LANES), block(D, V_LANES), block(3, 2, 256, V_LANES), block(2, 256, V_LANES),
            block(A_ROWS, 256), block(B_ROWS, 256), block(128, 256), block(256, Q_LANES), block(256, V_LANES),
            *[pltpu.VMEM(lead + (8, 384), F32) for lead in ((8,), (7,), (), (3,), (), (3,))],
            *Scatter.scratch(),
            *Scatter.again(),
            *SumY.scratch((256, Q_LANES)),
            *sems(2, 6, 8, 6, 12, 2, 8, 6, 5, 13),
            DMA((21,)),
            DMA((6,)),
        ],
        compiler_params=params(3),
        cost_estimate=cost(25 * 10**9, 60 * 2**20),
        name="close",
    )(*args)


def results_kernel(*refs):
    n = len(refs) // 3
    ins, outs, held, (in_sem, out_sem) = refs[:n], refs[n : 2 * n], refs[2 * n : 3 * n], refs[3 * n :]
    copies = copy_all(zip(ins, held), in_sem)
    written = []
    for i in range(n):
        copies[i].wait()
        written.extend(copy_all([(held[i], outs[i])], out_sem.at[pl.ds(i, 1)]))
    for copy in written:
        copy.wait()


def results_call(*arrays):
    n = len(arrays)
    return pl.pallas_call(
        results_kernel,
        out_shape=tuple(shape(v.shape, v.dtype) for v in arrays),
        in_specs=[ANYWHERE] * n,
        out_specs=(ANYWHERE,) * n,
        scratch_shapes=[*[pltpu.VMEM(v.shape, v.dtype) for v in arrays], DMA((n,)), DMA((n,))],
        compiler_params=params(),
        cost_estimate=cost(0, 10 * 2**20),
        name="results",
    )(*arrays)


def per_device(
    tokens,
    segments,
    first_gain,
    first_shift,
    heads_weight,
    heads_bias,
    output_weight,
    second_gain,
    second_shift,
    gate_up_weight,
    down_weight,
    cotangent,
):
    (
        first_all, cot_all, query, keys, values, attended, log_sum, residual, second_all, hidden, grads,
        wh, wo, wg, wd, gains, cos, sin_up, sin_down, lowest,
    ) = forward_call(
        tokens,
        cotangent,
        segments,
        *[v.reshape(1, 256) for v in (first_gain, first_shift, second_gain, second_shift)],
        heads_weight.transpose(1, 0, 2),
        heads_bias,
        output_weight,
        gate_up_weight.transpose(1, 2, 0),
        down_weight,
    )
    residual_grad, attended_grad, sums_two, a, b, grad_out = back_call(
        residual, cotangent, gains, grads, second_all, hidden, cot_all, wo, wg, attended
    )
    mixed, grad_tokens, norms, bias_grad, gate_up, down, output, heads = close_call(
        query, keys, values, attended_grad, log_sum, cos, sin_up, sin_down, lowest,
        residual, residual_grad, tokens, gains, sums_two, a, b, grad_out, hidden, first_all, wd, wh,
    )
    mixed, grad_tokens, gate_up, down, output, heads, bias_grad = results_call(
        mixed, grad_tokens, gate_up, down, output, heads, bias_grad
    )
    return (
        mixed,
        grad_tokens,
        norms[0, :16],
        norms[1, :16],
        heads.transpose(1, 0, 2),
        bias_grad,
        output,
        norms[2, :16],
        norms[3, :16],
        gate_up.reshape(2, UNITS, 256).transpose(2, 0, 1),
        down,
    )


ALL = ("dp", "tensor")


def solution(mesh):
    return jax.shard_map(
        per_device,
        mesh=mesh,
        in_specs=(
            P(ALL, None),
            P("dp", None),
            P("dp"),
            P("dp"),
            P("dp", None, "tensor"),
            P(None, "tensor", "dp"),
            P("tensor", "dp"),
            P("dp"),
            P("dp"),
            P("dp", None, "tensor"),
            P("tensor", "dp"),
            P(ALL, None),
        ),
        out_specs=(
            P(ALL, None),
            P(ALL, None),
            P(ALL),
            P(ALL),
            P("dp", None, "tensor"),
            P(None, "tensor", "dp"),
            P("tensor", "dp"),
            P(ALL),
            P(ALL),
            P("dp", None, "tensor"),
            P("tensor", "dp"),
        ),
        check_vma=False,
    )
```
